32 devices in a mesh: dp: 2 (over y), row: 4 (over x, core), col: 4 (over z).
Axes of the slice: x: 2, y: 2, z: 4, core: 2. Of those that a mesh axis runs over, the one named last changes fastest.
Arguments:
- hidden_in: bfloat16 [4096, 2048], P(('dp', 'col'), 'row'), may hold values from -6 to 6
- segment_ids: int32 [4096], P(('dp', 'row')), may hold values from 0 to 8, never falling along the last dimension, each value on 1 to 1000 neighbouring positions
- attn_gain: float32 [2048], replicated, may hold values from 0.1 to 1.9
- w_query: bfloat16 [2048, 2048], P('row', 'col'), may hold values from -0.125 to 0.125
- key_projection: bfloat16 [2048, 1024], P('row', 'col'), may hold values from -0.125 to 0.125
- value_projection: bfloat16 [2048, 1024], P('row', 'col'), may hold values from -0.125 to 0.125
- query_gain: float32 [128], replicated, may hold values from 0.1 to 1.9
- key_norm_gain: float32 [128], replicated, may hold values from 0.1 to 1.9
- w_out: bfloat16 [2048, 2048], P('col', 'row'), may hold values from -1 to 1
- ffn_gain: float32 [2048], replicated, may hold values from 0.1 to 1.9
- w_gate: bfloat16 [2048, 6144], P('row', 'col'), may hold values from -0.125 to 0.125
- w_up: bfloat16 [2048, 6144], P('row', 'col'), may hold values from -0.125 to 0.125
- w_down: bfloat16 [6144, 2048], P('col', 'row'), may hold values from -0.078125 to 0.078125
- out_grad: bfloat16 [4096, 2048], P(('dp', 'col'), 'row'), may hold values from -6 to 6
Outputs:
- layer_out: bfloat16 [4096, 2048], P(('dp', 'col'), 'row')
- in_grad: float32 [4096, 2048], P(('dp', 'col'), 'row')
- attn_gain_grad: float32 [2048], replicated
- w_query_grad: float32 [2048, 2048], P('row', 'col')
- w_key_grad: float32 [2048, 1024], P('row', 'col')
- w_value_grad: float32 [2048, 1024], P('row', 'col')
- query_gain_grad: float32 [128], replicated
- key_gain_grad: float32 [128], replicated
- w_out_grad: float32 [2048, 2048], P('col', 'row')
- ffn_gain_grad: float32 [2048], replicated
- w_gate_grad: float32 [2048, 6144], P('row', 'col')
- w_up_grad: float32 [2048, 6144], P('row', 'col')
- w_down_grad: float32 [6144, 2048], P('col', 'row')
The draws below stay inside these ranges and needn't reach their ends.
Inputs may be any that keep to these rules, and one draw needn't show every extreme that they name: `segment_ids`: document numbers never fall along the tokens; each document covers 1 to 1000 consecutive tokens, one exactly 1000.
All inputs are finite; a program needn't handle non-finite values.
Results may differ from the reference program's by a relative error of at most 0.014.
Values may be sent and summed in bfloat16 or wider, within the bound.
A program may use at most 192 MiB of HBM per device.

```python
import math
import jax
import jax.numpy as jnp
import numpy as np
from jax import lax

MODEL_WIDTH = 2048
QUERY_HEADS = 16
KEY_VALUE_HEADS = 8
HEAD_SIZE = 128
FF = 6144
PACKED_TOKENS = 512
SEG_MOST = 1000
TOKENS = 4096
SEGS = 9


def level_of(key, extent, cuts, least, top_value):
    def one(dim, blocks):
        steps = jax.random.uniform(jax.random.fold_in(jax.random.fold_in(key, 6), dim), (blocks,), jnp.float32, least / len(cuts), top_value / len(cuts))
        return jnp.repeat(jnp.exp(steps), extent[dim] // blocks).reshape((-1,) + (1,) * (len(extent) - dim - 1))

    level = one(*cuts[0])
    for cut in cuts[1:]:
        level = level * one(*cut)
    return level


def length_profile(count, total, bound, skew):
    weights = [(1 << 20) // math.isqrt(rank ** skew) + 1 for rank in range(2, count + 1)]
    rest, holding = total - bound - (count - 1), [1] * (count - 1)
    while rest > 0:
        movable = [i for i in range(count - 1) if holding[i] < bound]
        mass, left = sum([weights[i] for i in movable]), rest
        for i in movable:
            extra = min(bound - holding[i], max(1, left * weights[i] // mass), rest)
            holding[i] = holding[i] + extra
            rest = rest - extra
    return np.array([bound] + holding)


def uneven(key, amount, total, most, skew):
    if amount == 2:
        one = jax.random.randint(key, (), max(1, total - most), min(most, total - 1) + 1)
        return jnp.stack([one, total - one])
    tallies = jnp.asarray(length_profile(amount, total, most, skew), jnp.int32)
    twos = (amount - 1) // 2
    donor, receiver = tallies[1:1 + 2 * twos:2], tallies[2:2 + 2 * twos:2]
    margin = jnp.minimum(donor - 1, most - receiver)
    shifted = jax.random.randint(jax.random.fold_in(key, 1), (twos,), 0, 1 << 20) % (margin + 1)
    tallies = tallies.at[1:1 + 2 * twos:2].set(donor - shifted).at[2:2 + 2 * twos:2].set(receiver + shifted)
    return tallies[jax.random.permutation(jax.random.fold_in(key, 2), amount)]


def normal_values(own_key, extent, scale, reach, cuts=(), kind=jnp.bfloat16):
    entries = scale * jax.random.normal(own_key, extent, jnp.float32)
    if cuts:
        entries = entries * level_of(own_key, extent, cuts, -0.22, 0.18)
    return jnp.clip(entries, -reach, reach).astype(kind)


def setup_inputs(seed: int = 0) -> dict:
    key_list = jax.random.split(jax.random.key(seed), 15)
    return {
        "hidden_in": normal_values(key_list[0], (TOKENS, MODEL_WIDTH), 1.0, 6.0, ((0, 8), (1, 4))),
        "segment_ids": jnp.searchsorted(jnp.cumsum(uneven(key_list[1], SEGS, TOKENS, SEG_MOST, 1)), jnp.arange(TOKENS), side="right").astype(jnp.int32),
        "attn_gain": jnp.clip(1.0 + 0.18 * jax.random.normal(key_list[2], (MODEL_WIDTH,), jnp.float32), 0.1, 1.9),
        "w_query": normal_values(key_list[3], (MODEL_WIDTH, QUERY_HEADS * HEAD_SIZE), MODEL_WIDTH ** -0.5, 0.125, ((0, 4), (1, 4))),
        "key_projection": normal_values(key_list[4], (MODEL_WIDTH, KEY_VALUE_HEADS * HEAD_SIZE), MODEL_WIDTH ** -0.5, 0.125, ((0, 4), (1, 4))),
        "value_projection": normal_values(key_list[5], (MODEL_WIDTH, KEY_VALUE_HEADS * HEAD_SIZE), MODEL_WIDTH ** -0.5, 0.125, ((0, 4), (1, 4))),
        "query_gain": jnp.clip(1.0 + 0.18 * jax.random.normal(key_list[6], (HEAD_SIZE,), jnp.float32), 0.1, 1.9),
        "key_norm_gain": jnp.clip(1.0 + 0.18 * jax.random.normal(key_list[7], (HEAD_SIZE,), jnp.float32), 0.1, 1.9),
        "w_out": normal_values(key_list[8], (QUERY_HEADS * HEAD_SIZE, MODEL_WIDTH), (QUERY_HEADS * HEAD_SIZE // 64) ** -0.5, 1.0, ((0, 4), (1, 4))),
        "ffn_gain": jnp.clip(1.0 + 0.18 * jax.random.normal(key_list[9], (MODEL_WIDTH,), jnp.float32), 0.1, 1.9),
        "w_gate": normal_values(key_list[10], (MODEL_WIDTH, FF), MODEL_WIDTH ** -0.5, 0.125, ((0, 4), (1, 4))),
        "w_up": normal_values(key_list[11], (MODEL_WIDTH, FF), MODEL_WIDTH ** -0.5, 0.125, ((0, 4), (1, 4))),
        "w_down": normal_values(key_list[12], (FF, MODEL_WIDTH), FF ** -0.5, 0.078125, ((0, 4), (1, 4))),
        "out_grad": normal_values(key_list[13], (TOKENS, MODEL_WIDTH), 1.0, 6.0, ((0, 8), (1, 4))),
    }


EPSILON = 1e-06
THETA = 1000000.0
MASKED = -1e+30

@jax.custom_vjp
def lower_precision(v):
    return lax.optimization_barrier(v.astype(jnp.bfloat16)).astype(jnp.float32)

@jax.custom_vjp
def lower_precision_backward(v):
    return v

def low_keep(v):
    return (lower_precision(v), None)

def low_pass(kept, grad):
    return (grad,)

def back_keep(v):
    return (v, None)

def back_low(kept, grad):
    return (lower_precision(grad),)
lower_precision.defvjp(low_keep, low_pass)
lower_precision_backward.defvjp(back_keep, back_low)

def matrix_multiply(left_op, right_op):
    return jnp.dot(left_op, right_op, precision=lax.Precision.HIGHEST, preferred_element_type=jnp.float32)

def inverse_root_mean(operand):
    return lax.rsqrt(lax.optimization_barrier(jnp.mean(operand * operand, axis=-1, keepdims=True)) + EPSILON)

def rope_tables(sequence_length, width):
    positions = jnp.arange(sequence_length).astype(jnp.float32)
    rates = jnp.power(THETA, -jnp.arange(width // 2).astype(jnp.float32) * 2.0 / width)
    angles = positions[:, None] * rates[None, :]
    return (jnp.cos(angles), jnp.sin(angles))

def apply_rotation(operand, cosine_table, sine_values):
    half_width = operand.shape[-1] // 2
    leading = operand[..., :half_width]
    trailing = operand[..., half_width:]
    cos_part = cosine_table[:, None, :]
    sin_part = sine_values[:, None, :]
    return jnp.concatenate([leading * cos_part - trailing * sin_part, trailing * cos_part + leading * sin_part], axis=-1)

def attend(pieces):
    query_rows, heads_of_keys, heads_of_values, segment = pieces
    sequence_length = query_rows.shape[0]
    grouped_heads = query_rows.reshape(sequence_length, KEY_VALUE_HEADS, QUERY_HEADS // KEY_VALUE_HEADS, HEAD_SIZE)
    scores = jnp.einsum('qkgd,pkd->kgqp', grouped_heads, heads_of_keys, precision=lax.Precision.HIGHEST) * (1.0 / math.sqrt(HEAD_SIZE))
    scores = lower_precision_backward(scores)
    places = jnp.arange(sequence_length)
    allowed = (places[None, :] <= places[:, None]) & (segment[None, :] == segment[:, None])
    scores = jnp.where(allowed[None, None], scores, MASKED)
    row_top = lax.optimization_barrier(jnp.max(scores, axis=-1, keepdims=True))
    expo_vals = jnp.exp(scores - row_top)
    attn_probs = lower_precision(expo_vals / lax.optimization_barrier(jnp.sum(expo_vals, axis=-1, keepdims=True)))
    mixed_out = jnp.einsum('kgqp,pkd->qkgd', attn_probs, heads_of_values, precision=lax.Precision.HIGHEST)
    return mixed_out.reshape(sequence_length, QUERY_HEADS * HEAD_SIZE)

def layer_forward(stream, segment, params):
    attn_gain, w_query, key_projection, value_projection, query_gain, key_norm_gain, w_out, ffn_gain, w_gate, w_up, w_down = params
    count_of_rows = stream.shape[0]
    sequence_count = count_of_rows // PACKED_TOKENS
    normalized = lower_precision(stream * inverse_root_mean(stream) * attn_gain)
    query_rows = lower_precision_backward(matrix_multiply(normalized, w_query)).reshape(count_of_rows, QUERY_HEADS, HEAD_SIZE)
    heads_of_keys = lower_precision_backward(matrix_multiply(normalized, key_projection)).reshape(count_of_rows, KEY_VALUE_HEADS, HEAD_SIZE)
    heads_of_values = lower_precision(lower_precision_backward(matrix_multiply(normalized, value_projection))).reshape(sequence_count, PACKED_TOKENS, KEY_VALUE_HEADS, HEAD_SIZE)
    cosine_table, sine_values = rope_tables(PACKED_TOKENS, HEAD_SIZE)
    q_rot = lower_precision(apply_rotation((query_rows * inverse_root_mean(query_rows) * query_gain).reshape(sequence_count, PACKED_TOKENS, QUERY_HEADS, HEAD_SIZE), cosine_table, sine_values))
    rotated_keys = lower_precision(apply_rotation((heads_of_keys * inverse_root_mean(heads_of_keys) * key_norm_gain).reshape(sequence_count, PACKED_TOKENS, KEY_VALUE_HEADS, HEAD_SIZE), cosine_table, sine_values))
    mixed_out = lax.map(jax.checkpoint(attend), (q_rot, rotated_keys, heads_of_values, segment.reshape(sequence_count, PACKED_TOKENS)))
    mixed_out = lower_precision(lower_precision_backward(mixed_out.reshape(count_of_rows, QUERY_HEADS * HEAD_SIZE)))
    attn_out = lower_precision_backward(matrix_multiply(mixed_out, w_out))
    hidden = stream + attn_out
    ffn_in = lower_precision(hidden * inverse_root_mean(hidden) * ffn_gain)
    gate_pre = lower_precision_backward(matrix_multiply(ffn_in, w_gate))
    upward = lower_precision_backward(matrix_multiply(ffn_in, w_up))
    inner_act = lower_precision(jax.nn.silu(gate_pre) * upward)
    return hidden + lower_precision_backward(matrix_multiply(inner_act, w_down))

def reference(hidden_in, segment_ids, attn_gain, w_query, key_projection, value_projection, query_gain, key_norm_gain, w_out, ffn_gain, w_gate, w_up, w_down, out_grad):
    params = (attn_gain.astype(jnp.float32), w_query.astype(jnp.float32), key_projection.astype(jnp.float32), value_projection.astype(jnp.float32), query_gain.astype(jnp.float32), key_norm_gain.astype(jnp.float32), w_out.astype(jnp.float32), ffn_gain.astype(jnp.float32), w_gate.astype(jnp.float32), w_up.astype(jnp.float32), w_down.astype(jnp.float32))
    per_block = max(1, min(TOKENS // PACKED_TOKENS, 4096 // PACKED_TOKENS))
    span_rows = per_block * PACKED_TOKENS
    blocks = TOKENS // span_rows
    streams = hidden_in.astype(jnp.float32).reshape(blocks, span_rows, MODEL_WIDTH)
    segments = segment_ids.reshape(blocks, span_rows)
    cotangents = out_grad.astype(jnp.float32).reshape(blocks, span_rows, MODEL_WIDTH)

    def step_block(totals, inputs_block):
        stream, segment, cotangent = inputs_block

        def forward(operand, weights):
            return layer_forward(operand, segment, weights)
        output, pullback = jax.vjp(forward, stream, params)
        in_part, weight_parts = pullback(cotangent)
        return (jax.tree.map(jnp.add, totals, weight_parts), (output.astype(jnp.bfloat16), in_part))
    zeros = jax.tree.map(jnp.zeros_like, params)
    totals, (outputs, in_parts) = lax.scan(step_block, zeros, (streams, segments, cotangents))
    return (outputs.reshape(TOKENS, MODEL_WIDTH), in_parts.reshape(TOKENS, MODEL_WIDTH), totals[0], totals[1], totals[2], totals[3], totals[4], totals[5], totals[6], totals[7], totals[8], totals[9], totals[10])
```

```python
import functools
import math

import jax
import jax.numpy as jnp
import numpy as np
from jax import lax
from jax.experimental import pallas as pl
from jax.experimental.pallas import tpu as pltpu
from jax.sharding import PartitionSpec as P

HEAD_SIZE = 128
EPSILON = 1e-06
THETA = 1000000.0
MASKED = -1e30
MESH = pl.DeviceIdType.MESH
BF16 = jnp.bfloat16
F32 = jnp.float32
VMEM_LIMIT = 60 << 20


def place():
    row = lax.axis_index("row")
    col = lax.axis_index("col")
    chip = lax.div(row, 2)
    core = lax.rem(row, 2)
    return row, col, chip, core, chip * 2 + (1 - core), (1 - chip) * 2 + core


def to(**where):
    return dict(device_id=where, device_id_type=MESH)


def greet(col, mate, across):
    gate = pltpu.get_barrier_semaphore()
    pl.semaphore_signal(gate, inc=1, **to(row=mate))
    pl.semaphore_signal(gate, inc=1, **to(row=across))

    @pl.when(col > 0)
    def _():
        pl.semaphore_signal(gate, inc=1, **to(col=col - 1))

    @pl.when(col < 3)
    def _():
        pl.semaphore_signal(gate, inc=1, **to(col=col + 1))

    ends = jnp.where(col > 0, 1, 0) + jnp.where(col < 3, 1, 0)
    pl.semaphore_wait(gate, 2 + ends)


def remote(src, dst, sends, recvs, **where):
    return pltpu.make_async_remote_copy(
        src_ref=src, dst_ref=dst, send_sem=sends, recv_sem=recvs, **to(**where)
    )


def times(left, ref, cols, flipped):
    if flipped:
        return lax.dot_general(
            left, ref[cols, :], (((1,), (1,)), ((), ())), preferred_element_type=F32
        )
    return jnp.dot(left, ref[:, cols], preferred_element_type=F32)


def in_rows(count, step, body):
    def one(i, _):
        body(pl.ds(pl.multiple_of(i * step, step), step))
        return 0

    lax.fori_loop(0, count // step, one, 0)


def cols_rows_kernel(whole, parts, tile, *refs):
    n_w = len(parts)
    x_ref = refs[0]
    w_refs = refs[1 : 1 + n_w]
    out_ref, wide_out = refs[1 + n_w : 3 + n_w]
    (wide, product, keep, a_send, a_recv, b_send, c_recv, d_send, d_recv) = refs[3 + n_w : 12 + n_w]
    (z_send, z_recv, local, m_send, m_recv, x_send, x_recv) = refs[12 + n_w :]
    row, col, chip, core, mate, across = place()
    spot_a = (1 - chip) * 2 + (1 - core)
    spot_b = across
    spot_c = mate
    spot_d = row
    width = sum(p[1] for p in parts)

    wide[col] = x_ref[...]
    greet(col, mate, across)

    def mate_copy(src, dst, lane, spot):
        return remote(src, dst, m_send.at[lane, spot], m_recv.at[lane, spot], row=mate)

    def across_copy(src, dst, spot):
        return remote(src, dst, x_send.at[spot], x_recv.at[spot], row=across)

    def up(s):
        return remote(wide.at[s], wide.at[s], z_send.at[0, s], z_recv.at[s], col=col + 1)

    def down(s):
        return remote(wide.at[s], wide.at[s], z_send.at[1, s], z_recv.at[s], col=col - 1)

    def keep_wide(s):
        return pltpu.make_async_copy(wide.at[s], wide_out.at[s], local.at[s])

    def at_step(i):
        dist = lax.div(i + 1, 2)
        s = jnp.where(lax.rem(i, 2) == 1, col - dist, col + dist)
        return dist, s, (s >= 0) & (s <= 3)

    def multiply(s, handle):
        for w_ref, (base, size, flipped) in zip(w_refs, parts):

            def one(j, _, w_ref=w_ref, base=base, flipped=flipped):
                cols = pl.ds(pl.multiple_of(j * tile, tile), tile)
                spot = pl.ds(pl.multiple_of(base + j * tile, tile), tile)
                handle(times(wide[s], w_ref, cols, flipped), spot)
                return 0

            lax.fori_loop(0, size // tile, one, 0)

    def step(i, _):
        dist, s, valid = at_step(i)

        @pl.when(valid)
        def _():
            @pl.when(dist > 0)
            def _():
                up(s).wait_recv()

            @pl.when((s <= col) & (col < 3))
            def _():
                up(s).start()

            @pl.when((s >= col) & (col > 0))
            def _():
                down(s).start()

            keep_wide(s).start()
            if whole:

                def store(value, spot):
                    product[:, spot] = value

                multiply(s, store)

                @pl.when(s == spot_a)
                def _():
                    def cast(rows):
                        a_send[0, rows] = product[rows, :].astype(BF16)

                    in_rows(512, 64, cast)
                    mate_copy(a_send.at[0], a_recv.at[0], 0, 0).start()

                @pl.when(s == spot_c)
                def _():
                    def cast(rows):
                        d_send[0, rows] = product[rows, :].astype(BF16)

                    in_rows(512, 64, cast)
                    mate_copy(d_send.at[0], d_recv.at[0], 1, 0).start()

                @pl.when(s == spot_b)
                def _():
                    mate_copy(a_send.at[0], a_recv.at[0], 0, 0).wait_recv()

                    def add(rows):
                        b_send[0, rows] = (product[rows, :] + a_recv[0, rows].astype(F32)).astype(
                            BF16
                        )

                    in_rows(512, 64, add)
                    across_copy(b_send.at[0], c_recv.at[0], 0).start()

                @pl.when(s == spot_d)
                def _():
                    def store_own(rows):
                        out_ref[0, rows] = product[rows, :]

                    in_rows(512, 64, store_own)

            else:

                def quarter(q):
                    return pl.ds(pl.multiple_of(q * 128, 128), 128)

                def split(value, spot):
                    product[...] = value
                    a_send[s, :, spot] = product[quarter(spot_a), :].astype(BF16)
                    keep[:, spot] = product[quarter(spot_b), :]
                    d_send[s, :, spot] = product[quarter(spot_c), :].astype(BF16)
                    out_ref[s, :, spot] = product[quarter(spot_d), :]

                multiply(s, split)
                mate_copy(a_send.at[s], a_recv.at[s], 0, s).start()
                mate_copy(d_send.at[s], d_recv.at[s], 1, s).start()
                mate_copy(a_send.at[s], a_recv.at[s], 0, s).wait_recv()

                def add(rows):
                    b_send[s, rows] = (keep[rows, :] + a_recv[s, rows].astype(F32)).astype(BF16)

                in_rows(128, 16, add)
                across_copy(b_send.at[s], c_recv.at[s], s).start()

        return 0

    lax.fori_loop(0, 7, step, 0)

    def finish(s):
        mate_copy(d_send.at[s], d_recv.at[s], 1, s).wait_recv()
        across_copy(b_send.at[s], c_recv.at[s], s).wait_recv()

        def add(rows):
            out_ref[s, rows] += d_recv[s, rows].astype(F32) + c_recv[s, rows].astype(F32)

        in_rows(out_ref.shape[1], 16, add)
        mate_copy(a_send.at[s], a_recv.at[s], 0, s).wait_send()
        mate_copy(d_send.at[s], d_recv.at[s], 1, s).wait_send()
        across_copy(b_send.at[s], c_recv.at[s], s).wait_send()

    def last(i, _):
        dist, s, valid = at_step(i)

        @pl.when(valid)
        def _():
            if not whole:
                finish(s)

            @pl.when((s <= col) & (col < 3))
            def _():
                up(s).wait_send()

            @pl.when((s >= col) & (col > 0))
            def _():
                down(s).wait_send()

            keep_wide(s).wait()

        return 0

    lax.fori_loop(0, 7, last, 0)
    if whole:
        finish(0)


def cols_rows(name, number, x, weights, flipped, whole, tile):
    tokens = x.shape[0]
    parts, base = [], 0
    for w in weights:
        size = w.shape[0] if flipped else w.shape[1]
        parts.append((base, size, flipped))
        base += size
    if whole:
        lead, rows, span, kept = 1, tokens, (tokens, base), (8, 128)
    else:
        lead, rows, span, kept = 4, tokens // 4, (tokens, tile), (tokens // 4, base)
    moved = pltpu.VMEM((lead, rows, base), BF16)
    out, wide = pl.pallas_call(
        functools.partial(cols_rows_kernel, whole, tuple(parts), tile),
        out_shape=(
            jax.ShapeDtypeStruct((lead, rows, base), F32),
            jax.ShapeDtypeStruct((4, tokens, x.shape[1]), BF16),
        ),
        in_specs=[pl.BlockSpec(memory_space=pltpu.VMEM)] * (1 + len(weights)),
        out_specs=(pl.BlockSpec(memory_space=pltpu.VMEM), pl.BlockSpec(memory_space=pl.ANY)),
        scratch_shapes=[
            pltpu.VMEM((4, tokens, x.shape[1]), BF16),
            pltpu.VMEM(span, F32),
            pltpu.VMEM(kept, F32),
        ]
        + [moved] * 6
        + [
            pltpu.SemaphoreType.DMA((2, 4)),
            pltpu.SemaphoreType.DMA((4,)),
            pltpu.SemaphoreType.DMA((4,)),
            pltpu.SemaphoreType.DMA((2, lead)),
            pltpu.SemaphoreType.DMA((2, lead)),
            pltpu.SemaphoreType.DMA((lead,)),
            pltpu.SemaphoreType.DMA((lead,)),
        ],
        compiler_params=pltpu.CompilerParams(
            collective_id=number, has_side_effects=True, vmem_limit_bytes=VMEM_LIMIT
        ),
        cost_estimate=pl.CostEstimate(
            flops=8 * tokens * x.shape[1] * base, bytes_accessed=8 * tokens * base, transcendentals=0
        ),
        name=name,
    )(x, *weights)
    return out.reshape(tokens, base), wide.reshape(4 * tokens, x.shape[1])


def rows_cols_kernel(whole, parts, flipped, tile, *refs):
    n_w = len(parts)
    a_ref = refs[0]
    w_refs = refs[1 : 1 + n_w]
    out_ref, wide_out = refs[1 + n_w : 3 + n_w]
    (wide, product, sent, from_below, from_above) = refs[3 + n_w : 8 + n_w]
    (z_send, z_recv, local, own_sem, m_send, m_recv, x_send, x_recv, f_send, f_recv) = refs[8 + n_w :]
    row, col, chip, core, mate, across = place()
    diag = (1 - chip) * 2 + (1 - core)
    half = product.shape[0] // 2

    def order(j):
        first = jnp.where(col < 2, 3, 0)
        second = jnp.where(col < 2, 2, 1)
        third = jnp.where(lax.rem(col, 2) == 0, col + 1, col - 1)
        return jnp.where(j == 0, first, jnp.where(j == 1, second, jnp.where(j == 2, third, col)))

    def slot(s, q):
        return wide.at[q] if whole else wide.at[s, q]

    def own(s):
        return a_ref if whole else a_ref.at[s]

    def to_mate(s):
        return remote(own(s), slot(s, row), m_send.at[s], m_recv.at[s], row=mate)

    def to_across(s):
        return remote(own(s), slot(s, row), x_send.at[s], x_recv.at[s], row=across)

    def pass_on(s):
        return remote(slot(s, across), slot(s, across), f_send.at[s], f_recv.at[s], row=mate)

    def from_mate(s):
        return remote(slot(s, mate), slot(s, mate), m_send.at[s], m_recv.at[s], row=mate)

    def from_across(s):
        return remote(slot(s, across), slot(s, across), x_send.at[s], x_recv.at[s], row=across)

    def from_diag(s):
        return remote(slot(s, diag), slot(s, diag), f_send.at[s], f_recv.at[s], row=mate)

    def keep_wide(s):
        return pltpu.make_async_copy(wide.at[s], wide_out.at[s], local.at[s])

    def move_own(s):
        return pltpu.make_async_copy(own(s), slot(s, row), own_sem.at[s])

    def piece(ref, s, h):
        return ref.at[s, pl.ds(h * half, half)]

    def up(s, h):
        return remote(piece(sent, s, h), piece(from_below, s, h), z_send.at[s, h], z_recv.at[0, s, h], col=col + 1)

    def down(s, h):
        return remote(piece(sent, s, h), piece(from_above, s, h), z_send.at[s, h], z_recv.at[1, s, h], col=col - 1)

    greet(col, mate, across)
    if whole:
        to_across(0).start()
        to_mate(0).start()
        move_own(0).start()
        from_across(0).wait_recv()
        pass_on(0).start()
        from_mate(0).wait_recv()
        move_own(0).wait()
        from_diag(0).wait_recv()
    else:
        for j in range(2):
            to_across(order(j)).start()
        for j in range(4):
            to_mate(order(j)).start()
            move_own(order(j)).start()

    def multiply(left, rows):
        for t in range(product.shape[1] // tile):
            cols = pl.ds(t * tile, tile)
            total = None
            for w_ref, (base, size) in zip(w_refs, parts):
                term = times(left(base, size), w_ref, cols, flipped)
                total = term if total is None else total + term
            product[rows, cols] = total

    def step(j, _):
        s = order(j)
        if whole:
            keep_wide(s).start()
            multiply(lambda base, size: wide[s, :, pl.ds(base, size)], slice(None))
        else:

            @pl.when(j < 2)
            def _():
                to_across(order(j + 2)).start()

            def pair(first):
                def left(base, size):
                    two = wide[s, pl.ds(first, 2), :, pl.ds(base, size)]
                    return two.reshape(2 * two.shape[1], size)

                multiply(left, pl.ds(pl.multiple_of(first * (half // 2), half), half))

            from_mate(s).wait_recv()
            move_own(s).wait()
            pair(chip * 2)
            from_across(s).wait_recv()
            pass_on(s).start()
            from_diag(s).wait_recv()
            pair((1 - chip) * 2)
            keep_wide(s).start()

        for h in range(2):
            span = half

            def add_in(ref, h=h):
                def add(rows):
                    here = pl.ds(pl.multiple_of(h * span + rows.start, rows.size), rows.size)
                    product[here, :] += ref[s, here].astype(F32)

                in_rows(span, 64, add)

            def cast(rows, h=h):
                here = pl.ds(pl.multiple_of(h * span + rows.start, rows.size), rows.size)
                sent[s, here] = product[here, :].astype(BF16)

            @pl.when((s >= col) & (col > 0))
            def _():
                up(s, h).wait_recv()
                add_in(from_below)

            @pl.when((s <= col) & (col < 3))
            def _():
                down(s, h).wait_recv()
                add_in(from_above)

            @pl.when(s > col)
            def _():
                in_rows(span, 64, cast)
                up(s, h).start()

            @pl.when(s < col)
            def _():
                in_rows(span, 64, cast)
                down(s, h).start()

        return 0

    lax.fori_loop(0, 4, step, 0)
    out_ref[...] = product[...]

    def last(s, _):
        for h in range(2):

            @pl.when(s > col)
            def _():
                up(s, h).wait_send()

            @pl.when(s < col)
            def _():
                down(s, h).wait_send()

        if not whole:
            to_mate(s).wait_send()
            to_across(s).wait_send()
            pass_on(s).wait_send()
        keep_wide(s).wait()
        return 0

    lax.fori_loop(0, 4, last, 0)
    if whole:
        to_mate(0).wait_send()
        to_across(0).wait_send()
        pass_on(0).wait_send()


def rows_cols(name, number, a, weights, flipped, whole, tile=256):
    tokens, wide_size = a.shape
    parts, base = [], 0
    for w in weights:
        size = w.shape[1] if flipped else w.shape[0]
        parts.append((base, size))
        base += size
    feats = weights[0].shape[0] if flipped else weights[0].shape[1]
    if whole:
        slots, lead, given = (4, tokens, base), 1, a
    else:
        slots, lead, given = (4, 4, tokens // 4, base), 4, a.reshape(4, tokens // 4, base)
    chain = pltpu.VMEM((4, tokens, feats), BF16)
    out, wide = pl.pallas_call(
        functools.partial(rows_cols_kernel, whole, tuple(parts), flipped, tile),
        out_shape=(
            jax.ShapeDtypeStruct((tokens, feats), F32),
            jax.ShapeDtypeStruct(slots, BF16),
        ),
        in_specs=[pl.BlockSpec(memory_space=pltpu.VMEM)] * (1 + len(weights)),
        out_specs=(pl.BlockSpec(memory_space=pltpu.VMEM), pl.BlockSpec(memory_space=pl.ANY)),
        scratch_shapes=[
            pltpu.VMEM(slots, BF16),
            pltpu.VMEM((tokens, feats), F32),
            chain,
            chain,
            chain,
            pltpu.SemaphoreType.DMA((4, 2)),
            pltpu.SemaphoreType.DMA((2, 4, 2)),
            pltpu.SemaphoreType.DMA((4,)),
            pltpu.SemaphoreType.DMA((lead,)),
        ]
        + [pltpu.SemaphoreType.DMA((lead,))] * 6,
        compiler_params=pltpu.CompilerParams(
            collective_id=number, has_side_effects=True, vmem_limit_bytes=VMEM_LIMIT
        ),
        cost_estimate=pl.CostEstimate(
            flops=8 * tokens * feats * base, bytes_accessed=8 * tokens * base, transcendentals=0
        ),
        name=name,
    )(given, *weights)
    return out, wide.reshape(4 * tokens, base)


def turn_tables(length):
    rates = THETA ** (-np.arange(HEAD_SIZE // 2) * 2.0 / HEAD_SIZE)
    angles = np.arange(length)[:, None] * rates[None, :]
    cos, sin = np.cos(angles), np.sin(angles)
    return (
        np.concatenate([cos, cos], axis=1).astype(np.float32),
        np.concatenate([-sin, sin], axis=1).astype(np.float32),
    )


def swap_halves(value):
    return pltpu.roll(value, HEAD_SIZE // 2, 1)


def head(ref, index):
    return ref[:, index * HEAD_SIZE : (index + 1) * HEAD_SIZE]


def root_scale(raw):
    return lax.rsqrt(jnp.mean(raw * raw, axis=1, keepdims=True) + EPSILON)


def attend_kernel(q_heads, groups, qkv, seg_col, seg_row, cos, sin, q_gain, k_gain, o, qa, ka, va, probs):
    kv = q_heads // groups
    tokens = qkv.shape[0]
    half = tokens // 2

    def turned(index, gain):
        raw = head(qkv, index)
        normed = raw * root_scale(raw) * gain[...]
        return (normed * cos[...] + swap_halves(normed) * sin[...]).astype(BF16)

    for i in range(q_heads):
        qa[:, i * HEAD_SIZE : (i + 1) * HEAD_SIZE] = turned(i, q_gain)
    for i in range(kv):
        ka[:, i * HEAD_SIZE : (i + 1) * HEAD_SIZE] = turned(q_heads + i, k_gain)
        va[:, i * HEAD_SIZE : (i + 1) * HEAD_SIZE] = head(qkv, q_heads + kv + i).astype(BF16)
    for block in range(2):
        rows = slice(block * half, (block + 1) * half)
        keys = (block + 1) * half
        spot = lax.broadcasted_iota(jnp.int32, (half, keys), 0) + block * half
        other = lax.broadcasted_iota(jnp.int32, (half, keys), 1)
        allowed = (other <= spot) & (seg_col[rows, :] == seg_row[:, :keys])
        for i in range(q_heads):
            j = i // groups
            dots = lax.dot_general(
                head(qa, i)[rows], head(ka, j)[:keys], (((1,), (1,)), ((), ())), preferred_element_type=F32
            ) * (1.0 / math.sqrt(HEAD_SIZE))
            scores = jnp.where(allowed, dots, MASKED)
            expo = jnp.exp(scores - jnp.max(scores, axis=1, keepdims=True))
            p = expo / jnp.sum(expo, axis=1, keepdims=True)
            probs[i, rows, :keys] = p
            mixed = jnp.dot(p.astype(BF16), head(va, j)[:keys], preferred_element_type=F32)
            o[rows, i * HEAD_SIZE : (i + 1) * HEAD_SIZE] = mixed.astype(BF16)


def attend_back_kernel(
    q_heads, groups, grad, qkv, qa, ka, va, probs, cos, sin, q_gain, k_gain, out, q_part, k_part, dq, dk, dv
):
    kv = q_heads // groups
    tokens = qkv.shape[0]
    half = tokens // 2
    scale = 1.0 / math.sqrt(HEAD_SIZE)
    dk[...] = jnp.zeros_like(dk)
    dv[...] = jnp.zeros_like(dv)

    def across_rows(left, right):
        return lax.dot_general(left, right, (((0,), (0,)), ((), ())), preferred_element_type=F32)

    for block in range(2):
        rows = slice(block * half, (block + 1) * half)
        keys = (block + 1) * half
        for i in range(q_heads):
            j = i // groups
            spot = slice(j * HEAD_SIZE, (j + 1) * HEAD_SIZE)
            p = probs[i, rows, :keys]
            g = head(grad, i)[rows].astype(BF16)
            dv[:keys, spot] += across_rows(p.astype(BF16), g)
            dp = lax.dot_general(
                g, head(va, j)[:keys], (((1,), (1,)), ((), ())), preferred_element_type=F32
            )
            ds = (p * (dp - jnp.sum(p * dp, axis=1, keepdims=True))).astype(BF16)
            dq[rows, i * HEAD_SIZE : (i + 1) * HEAD_SIZE] = (
                jnp.dot(ds, head(ka, j)[:keys], preferred_element_type=F32) * scale
            )
            dk[:keys, spot] += across_rows(ds, head(qa, i)[rows]) * scale

    def back(turned, index, gain):
        raw = head(qkv, index)
        scales = root_scale(raw)
        normed = turned * cos[...] - swap_halves(turned) * sin[...]
        part = jnp.sum(normed * raw * scales, axis=0, keepdims=True)
        weighted = normed * gain[...]
        inner = jnp.sum(weighted * raw, axis=1, keepdims=True)
        result = scales * weighted - raw * (scales * scales * scales) * inner * (1.0 / HEAD_SIZE)
        out[:, index * HEAD_SIZE : (index + 1) * HEAD_SIZE] = result.astype(BF16)
        return part

    q_part[...] = sum(back(head(dq, i), i, q_gain) for i in range(q_heads))
    k_part[...] = sum(back(head(dk, i), q_heads + i, k_gain) for i in range(kv))
    for i in range(kv):
        spot = (q_heads + kv + i) * HEAD_SIZE
        out[:, spot : spot + HEAD_SIZE] = head(dv, i).astype(BF16)


def local_call(kernel, name, shapes, scratch, *args):
    return pl.pallas_call(
        kernel,
        out_shape=shapes,
        scratch_shapes=scratch,
        compiler_params=pltpu.CompilerParams(vmem_limit_bytes=VMEM_LIMIT),
        name=name,
    )(*args)


def token_sums(operand):
    return lax.psum(operand, "row")


def outer(left_op, right_op):
    return lax.dot_general(left_op, right_op, (((0,), (0,)), ((), ())), preferred_element_type=F32)


def shards(
    pairs,
    hidden_in,
    segment_ids,
    attn_gain,
    w_query,
    key_projection,
    value_projection,
    query_gain,
    key_norm_gain,
    w_out,
    ffn_gain,
    w_gate,
    w_up,
    w_down,
    out_grad,
):
    tokens, slice_width = hidden_in.shape
    model_width = attn_gain.shape[0]
    offset = lax.axis_index("row") * slice_width
    gain_one = lax.dynamic_slice_in_dim(attn_gain, offset, slice_width)
    gain_two = lax.dynamic_slice_in_dim(ffn_gain, offset, slice_width)
    q_width = w_query.shape[1]
    k_width = key_projection.shape[1]
    q_heads = q_width // HEAD_SIZE
    groups = q_width // k_width
    ff = w_gate.shape[1]

    def over_pairs(part):
        if pairs == 2:
            other = lax.ppermute(part.astype(BF16), "dp", [(0, 1), (1, 0)])
            return part + other.astype(F32)
        return lax.psum(part, "dp")

    stream = hidden_in.astype(F32)
    scale_one = lax.rsqrt(token_sums(jnp.sum(stream * stream, axis=1)) / model_width + EPSILON)[:, None]
    normalized = (stream * scale_one * gain_one).astype(BF16)
    qkv, normed_wide = cols_rows(
        "qkv", 0, normalized, [w_query, key_projection, value_projection], False, True, 256
    )
    cos, sin = turn_tables(tokens)
    q_gain, k_gain = query_gain[None, :], key_norm_gain[None, :]
    mixed, q_turned, k_turned, values, probs = local_call(
        functools.partial(attend_kernel, q_heads, groups),
        "attend",
        (
            jax.ShapeDtypeStruct((tokens, q_width), BF16),
            jax.ShapeDtypeStruct((tokens, q_width), BF16),
            jax.ShapeDtypeStruct((tokens, k_width), BF16),
            jax.ShapeDtypeStruct((tokens, k_width), BF16),
            jax.ShapeDtypeStruct((q_heads, tokens, tokens), F32),
        ),
        [],
        qkv, segment_ids[:, None], segment_ids[None, :], cos, sin, q_gain, k_gain,
    )
    attn_out, mixed_wide = rows_cols("out", 1, mixed, [w_out], False, True)
    hidden = stream + attn_out
    scale_two = lax.rsqrt(token_sums(jnp.sum(hidden * hidden, axis=1)) / model_width + EPSILON)[:, None]
    ffn_in = (hidden * scale_two * gain_two).astype(BF16)
    gate_up, ffn_wide = cols_rows("gate_up", 2, ffn_in, [w_gate, w_up], False, False, 512)
    grad_inner, grad_wide = cols_rows("down_back", 3, out_grad, [w_down], True, False, 512)
    gate_pre, upward = gate_up[:, :ff], gate_up[:, ff:]
    sigmoid_gate = jax.nn.sigmoid(gate_pre)
    activated = gate_pre * sigmoid_gate
    inner_act = (activated * upward).astype(BF16)
    grad_gate = grad_inner * upward * (sigmoid_gate * (1.0 + gate_pre * (1.0 - sigmoid_gate)))
    grad_up = grad_inner * activated
    grad_ffn = jnp.concatenate([grad_gate, grad_up], axis=1).astype(BF16)
    grad_ffn_in, ffn_grad_wide = rows_cols("ffn_back", 4, grad_ffn, [w_gate, w_up], True, False)
    down_out, inner_wide = rows_cols("down", 5, inner_act, [w_down], False, False)
    layer_out = (hidden + down_out).astype(BF16)
    down_grad = over_pairs(outer(inner_wide, grad_wide))
    gate_grad = over_pairs(outer(ffn_wide, ffn_grad_wide[:, :ff]))
    up_grad = over_pairs(outer(ffn_wide, ffn_grad_wide[:, ff:]))
    grad_out = out_grad.astype(F32)
    weighted_two = grad_ffn_in * gain_two
    gain_two_part = jnp.sum(grad_ffn_in * hidden * scale_two, axis=0)
    dot_two = token_sums(jnp.sum(weighted_two * hidden, axis=1))[:, None]
    grad_hidden = grad_out + scale_two * weighted_two - hidden * scale_two**3 * dot_two / model_width
    grad_attn = grad_hidden.astype(BF16)
    grad_mixed, attn_grad_wide = cols_rows("out_back", 6, grad_attn, [w_out], True, True, 256)
    out_weight_grad = over_pairs(outer(mixed_wide, attn_grad_wide))
    grad_qkv, q_gain_part, k_gain_part = local_call(
        functools.partial(attend_back_kernel, q_heads, groups),
        "attend_back",
        (
            jax.ShapeDtypeStruct((tokens, q_width + 2 * k_width), BF16),
            jax.ShapeDtypeStruct((1, HEAD_SIZE), F32),
            jax.ShapeDtypeStruct((1, HEAD_SIZE), F32),
        ),
        [
            pltpu.VMEM((tokens, q_width), F32),
            pltpu.VMEM((tokens, k_width), F32),
            pltpu.VMEM((tokens, k_width), F32),
        ],
        grad_mixed, qkv, q_turned, k_turned, values, probs, cos, sin, q_gain, k_gain,
    )
    grad_normed, qkv_grad_wide = rows_cols(
        "qkv_back", 7, grad_qkv, [w_query, key_projection, value_projection], True, True
    )
    qkv_grad = over_pairs(outer(normed_wide, qkv_grad_wide))
    weighted_one = grad_normed * gain_one
    gain_one_part = jnp.sum(grad_normed * stream * scale_one, axis=0)
    dot_one = token_sums(jnp.sum(weighted_one * stream, axis=1))[:, None]
    in_grad = grad_hidden + scale_one * weighted_one - stream * scale_one**3 * dot_one / model_width

    def full(part):
        return lax.dynamic_update_slice_in_dim(jnp.zeros((model_width,), F32), part, offset, 0)

    attn_gain_grad, ffn_gain_grad, query_gain_grad, key_gain_grad = lax.psum(
        (full(gain_one_part), full(gain_two_part), q_gain_part[0], k_gain_part[0]), ("dp", "row", "col")
    )
    return (
        layer_out,
        in_grad,
        attn_gain_grad,
        qkv_grad[:, :q_width],
        qkv_grad[:, q_width : q_width + k_width],
        qkv_grad[:, q_width + k_width :],
        query_gain_grad,
        key_gain_grad,
        out_weight_grad,
        ffn_gain_grad,
        gate_grad,
        up_grad,
        down_grad,
    )


def solution(mesh):
    acts, grid, flip, none = P(("dp", "col"), "row"), P("row", "col"), P("col", "row"), P()
    return jax.shard_map(
        functools.partial(shards, mesh.shape["dp"]),
        mesh=mesh,
        in_specs=(
            acts, P(("dp", "row")), none, grid, grid, grid, none, none, flip, none, grid, grid, flip, acts,
        ),
        out_specs=(
            acts, acts, none, grid, grid, grid, none, none, flip, none, grid, grid, flip,
        ),
        check_vma=False,
    )
```

```python
import functools
import math

import jax
import jax.numpy as jnp
import numpy as np
from jax import lax
from jax.experimental import pallas as pl
from jax.experimental.pallas import tpu as pltpu
from jax.sharding import PartitionSpec as P

HEAD_SIZE = 128
EPSILON = 1e-06
THETA = 1000000.0
MASKED = -1e30
MESH = pl.DeviceIdType.MESH
BF16 = jnp.bfloat16
F32 = jnp.float32
VMEM_LIMIT = 60 << 20


def place():
    row = lax.axis_index("row")
    col = lax.axis_index("col")
    chip = lax.div(row, 2)
    core = lax.rem(row, 2)
    return row, col, chip, core, chip * 2 + (1 - core), (1 - chip) * 2 + core


def to(**where):
    return dict(device_id=where, device_id_type=MESH)


def greet(col, mate, across):
    gate = pltpu.get_barrier_semaphore()
    pl.semaphore_signal(gate, inc=1, **to(row=mate))
    pl.semaphore_signal(gate, inc=1, **to(row=across))

    @pl.when(col > 0)
    def _():
        pl.semaphore_signal(gate, inc=1, **to(col=col - 1))

    @pl.when(col < 3)
    def _():
        pl.semaphore_signal(gate, inc=1, **to(col=col + 1))

    ends = jnp.where(col > 0, 1, 0) + jnp.where(col < 3, 1, 0)
    pl.semaphore_wait(gate, 2 + ends)


def times(left, ref, cols, flipped):
    if flipped:
        return lax.dot_general(
            left, ref[cols, :], (((1,), (1,)), ((), ())), preferred_element_type=F32
        )
    return jnp.dot(left, ref[:, cols], preferred_element_type=F32)


class Ends:
    def __init__(self):
        self.row = lax.axis_index("row")
        self.col = lax.axis_index("col")
        self.chip = lax.div(self.row, 2)
        self.core = lax.rem(self.row, 2)
        self.mate = self.chip * 2 + (1 - self.core)
        self.across = (1 - self.chip) * 2 + self.core
        self.diag = (1 - self.chip) * 2 + (1 - self.core)
        self.end = (self.col == 0) | (self.col == 3)

    def greet(self, pairs=0):
        gate = pltpu.get_barrier_semaphore()
        pl.semaphore_signal(gate, inc=1, **to(row=self.mate))
        pl.semaphore_signal(gate, inc=1, **to(row=self.across))
        if pairs == 2:
            pl.semaphore_signal(gate, inc=1, **to(dp=1 - lax.axis_index("dp")))

        @pl.when(self.col > 0)
        def _():
            pl.semaphore_signal(gate, inc=1, **to(col=self.col - 1))

        @pl.when(self.col < 3)
        def _():
            pl.semaphore_signal(gate, inc=1, **to(col=self.col + 1))

        ends = jnp.where(self.col > 0, 1, 0) + jnp.where(self.col < 3, 1, 0)
        pl.semaphore_wait(gate, (3 if pairs == 2 else 2) + ends)


def remote(src, dst, sends, recvs, **where):
    return pltpu.make_async_remote_copy(
        src_ref=src, dst_ref=dst, send_sem=sends, recv_sem=recvs, **to(**where)
    )


def in_rows(count, step, body, first=0):
    def one(i, _):
        body(pl.ds(pl.multiple_of(first + i * step, step), step))
        return 0

    lax.fori_loop(0, count // step, one, 0)


class ColGather:
    def __init__(self, at, wide, sends, recvs):
        self.at, self.wide, self.sends, self.recvs = at, wide, sends, recvs

    def up(self, s):
        return remote(self.wide.at[s], self.wide.at[s], self.sends.at[0, s], self.recvs.at[s], col=self.at.col + 1)

    def down(self, s):
        return remote(self.wide.at[s], self.wide.at[s], self.sends.at[1, s], self.recvs.at[s], col=self.at.col - 1)

    def both(self, dist, body):
        if dist == 0:
            body(self.at.col)
            return
        below, above = self.at.col - dist, self.at.col + dist
        pl.when(below >= 0)(lambda: body(below))
        pl.when(above <= 3)(lambda: body(above))

    def loop(self, dist, body):
        if dist == 0:
            body(self.at.col)
            return

        def one(side, _):
            s = jnp.where(side == 0, self.at.col - dist, self.at.col + dist)
            pl.when((s >= 0) & (s <= 3))(lambda: body(s))
            return 0

        lax.fori_loop(0, 2, one, 0)

    def arrive(self, dist):
        def take(s):
            if dist:
                self.up(s).wait_recv()

            @pl.when((s <= self.at.col) & (self.at.col < 3))
            def _():
                self.up(s).start()

            @pl.when((s >= self.at.col) & (self.at.col > 0))
            def _():
                self.down(s).start()

        self.loop(dist, take)

    def close(self):
        def one(s, _):
            @pl.when((s <= self.at.col) & (self.at.col < 3))
            def _():
                self.up(s).wait_send()

            @pl.when((s >= self.at.col) & (self.at.col > 0))
            def _():
                self.down(s).wait_send()

            return 0

        lax.fori_loop(0, 4, one, 0)


class RowSumWhole:
    def __init__(self, at, product, out, a_send, a_recv, b_send, c_recv, d_send, d_recv, m_send, m_recv, x_send, x_recv):
        self.at, self.product, self.out = at, product, out
        self.b_send, self.c_recv, self.a_recv, self.d_recv = b_send, c_recv, a_recv, d_recv
        self.a_send, self.d_send = a_send, d_send
        self.a = remote(a_send, a_recv, m_send.at[0], m_recv.at[0], row=at.mate)
        self.d = remote(d_send, d_recv, m_send.at[1], m_recv.at[1], row=at.mate)
        self.b = remote(b_send, c_recv, x_send.at[0], x_recv.at[0], row=at.across)

    def give(self, s):
        at, product = self.at, self.product
        rows = product.shape[0]

        def cast(ref):
            def one(here):
                ref[here] = product[here, :].astype(BF16)

            in_rows(rows, 64, one)

        @pl.when(s == at.diag)
        def _():
            cast(self.a_send)
            self.a.start()

        @pl.when(s == at.mate)
        def _():
            cast(self.d_send)
            self.d.start()

        @pl.when(s == at.across)
        def _():
            self.a.wait_recv()

            def one(here):
                self.b_send[here] = (product[here, :] + self.a_recv[here].astype(F32)).astype(BF16)

            in_rows(rows, 64, one)
            self.b.start()

        @pl.when(s == at.row)
        def _():
            def one(here):
                self.out[here] = product[here, :]

            in_rows(rows, 64, one)

    def finish(self):
        self.d.wait_recv()
        self.b.wait_recv()

        def one(here):
            self.out[here] += self.d_recv[here].astype(F32) + self.c_recv[here].astype(F32)

        in_rows(self.out.shape[0], 64, one)

    def close(self):
        self.a.wait_send()
        self.b.wait_send()
        self.d.wait_send()


class RowSumQuarter:
    def __init__(self, at, chunk, keep, a_send, a_recv, b_send, c_recv, d_send, d_recv, m_send, m_recv, x_send, x_recv):
        self.at, self.chunk, self.keep = at, chunk, keep
        self.a_send, self.a_recv, self.b_send, self.c_recv = a_send, a_recv, b_send, c_recv
        self.d_send, self.d_recv = d_send, d_recv
        self.sems = (m_send, m_recv, x_send, x_recv)

    def a(self, s):
        m_send, m_recv, _, _ = self.sems
        return remote(self.a_send.at[s], self.a_recv.at[s], m_send.at[0, s], m_recv.at[0, s], row=self.at.mate)

    def d(self, s):
        m_send, m_recv, _, _ = self.sems
        return remote(self.d_send.at[s], self.d_recv.at[s], m_send.at[1, s], m_recv.at[1, s], row=self.at.mate)

    def b(self, s):
        _, _, x_send, x_recv = self.sems
        return remote(self.b_send.at[s], self.c_recv.at[s], x_send.at[s], x_recv.at[s], row=self.at.across)

    def split(self, s, value, spot, own):
        at, chunk = self.at, self.chunk
        chunk[...] = value

        def quarter(q):
            return chunk[pl.ds(pl.multiple_of(q * 128, 128), 128), :]

        self.a_send[s, :, spot] = quarter(at.diag).astype(BF16)
        self.keep[:, spot] = quarter(at.across)
        self.d_send[s, :, spot] = quarter(at.mate).astype(BF16)
        own[s, :, spot] = quarter(at.row)

    def give(self, s):
        self.a(s).start()
        self.d(s).start()
        self.a(s).wait_recv()

        def one(here):
            self.b_send[s, here] = (self.keep[here, :] + self.a_recv[s, here].astype(F32)).astype(BF16)

        in_rows(128, 16, one)
        self.b(s).start()

    def finish(self, s):
        self.d(s).wait_recv()
        self.b(s).wait_recv()

    def close(self):
        def one(s, _):
            self.a(s).wait_send()
            self.b(s).wait_send()
            self.d(s).wait_send()
            return 0

        lax.fori_loop(0, 4, one, 0)


class RowGather:
    def __init__(self, at, own, slot, sems):
        self.at, self.own, self.slot = at, own, slot
        self.m_send, self.m_recv, self.x_send, self.x_recv, self.f_send, self.f_recv, self.local = sems

    def to_mate(self, s):
        return remote(self.own(s), self.slot(s, self.at.row), self.m_send.at[s], self.m_recv.at[s], row=self.at.mate)

    def to_across(self, s):
        return remote(self.own(s), self.slot(s, self.at.row), self.x_send.at[s], self.x_recv.at[s], row=self.at.across)

    def pass_on(self, s):
        here = self.slot(s, self.at.across)
        return remote(here, here, self.f_send.at[s], self.f_recv.at[s], row=self.at.mate)

    def move_own(self, s):
        return pltpu.make_async_copy(self.own(s), self.slot(s, self.at.row), self.local.at[s])

    def near(self, s):
        self.to_mate(s).start()
        self.move_own(s).start()

    def wait_near(self, s):
        here = self.slot(s, self.at.mate)
        remote(here, here, self.m_send.at[s], self.m_recv.at[s], row=self.at.mate).wait_recv()
        self.move_own(s).wait()

    def take_across(self, s):
        here = self.slot(s, self.at.across)
        remote(here, here, self.x_send.at[s], self.x_recv.at[s], row=self.at.across).wait_recv()
        self.pass_on(s).start()

    def wait_diag(self, s):
        here = self.slot(s, self.at.diag)
        remote(here, here, self.f_send.at[s], self.f_recv.at[s], row=self.at.mate).wait_recv()

    def close(self, count):
        def one(s, _):
            self.to_mate(s).wait_send()
            self.to_across(s).wait_send()
            self.pass_on(s).wait_send()
            return 0

        lax.fori_loop(0, count, one, 0)


class ColSum:
    def __init__(self, at, product, sent, got, extra, sends, recvs, extra_recvs):
        self.at, self.product, self.sent, self.got, self.extra = at, product, sent, got, extra
        self.sends, self.recvs, self.extra_recvs = sends, recvs, extra_recvs
        self.half = product.shape[0] // 2

    def part(self, h):
        return pl.ds(h * self.half, self.half)

    def up(self, s, h):
        return remote(
            self.sent.at[s, self.part(h)], self.got.at[s, self.part(h)],
            self.sends.at[s, h], self.recvs.at[s, h], col=self.at.col + 1,
        )

    def down(self, s, h):
        return remote(
            self.sent.at[s, self.part(h)], self.got.at[s, self.part(h)],
            self.sends.at[s, h], self.recvs.at[s, h], col=self.at.col - 1,
        )

    def last_down(self, s, h):
        return remote(
            self.sent.at[s, self.part(h)], self.extra.at[self.part(h)],
            self.sends.at[s, h], self.extra_recvs.at[h], col=self.at.col - 1,
        )

    def step(self, s):
        col, product = self.at.col, self.product
        for h in range(2):
            @pl.when(((s >= col) & (col > 0)) | ((s < col) & (col < 3)))
            def _():
                self.up(s, h).wait_recv()

                def add(here):
                    product[here, :] += self.got[s, here].astype(F32)

                in_rows(self.half, 64, add, h * self.half)

            @pl.when((s == col) & (col < 3))
            def _():
                self.last_down(s, h).wait_recv()

                def add(here):
                    product[here, :] += self.extra[here].astype(F32)

                in_rows(self.half, 64, add, h * self.half)

            @pl.when(s != col)
            def _():
                def cast(here):
                    self.sent[s, here] = product[here, :].astype(BF16)

                in_rows(self.half, 64, cast, h * self.half)

            pl.when(s > col)(lambda: self.up(s, h).start())
            pl.when(s < col - 1)(lambda: self.down(s, h).start())
            pl.when(s == col - 1)(lambda: self.last_down(s, h).start())

    def close(self):
        def one(s, _):
            for h in range(2):
                pl.when(s != self.at.col)(lambda: self.up(s, h).wait_send())
            return 0

        lax.fori_loop(0, 4, one, 0)


def far_first(col, j):
    first = jnp.where(col < 2, 3, 0)
    second = jnp.where(col < 2, 2, 1)
    third = jnp.where(lax.rem(col, 2) == 0, col + 1, col - 1)
    return (first, second, third, col)[j]


def near_first(at, j):
    first, second, partner, _ = [far_first(at.col, i) for i in range(4)]
    mine = lax.div(at.col, 2) == at.chip
    return (
        jnp.where(mine, partner, first),
        jnp.where(mine, first, second),
        jnp.where(mine, second, partner),
        at.col,
    )[j]


def cols_rows_kernel(whole, parts, tile, *refs):
    n_w = len(parts)
    x_ref = refs[0]
    w_refs = refs[1 : 1 + n_w]
    out_ref, wide_out = refs[1 + n_w : 3 + n_w]
    (wide, product, keep, a_send, a_recv, b_send, c_recv, d_send, d_recv) = refs[3 + n_w : 12 + n_w]
    (z_send, z_recv, local, m_send, m_recv, x_send, x_recv) = refs[12 + n_w :]
    row, col, chip, core, mate, across = place()
    spot_a = (1 - chip) * 2 + (1 - core)
    spot_b = across
    spot_c = mate
    spot_d = row
    width = sum(p[1] for p in parts)

    wide[col] = x_ref[...]
    greet(col, mate, across)

    def mate_copy(src, dst, lane, spot):
        return remote(src, dst, m_send.at[lane, spot], m_recv.at[lane, spot], row=mate)

    def across_copy(src, dst, spot):
        return remote(src, dst, x_send.at[spot], x_recv.at[spot], row=across)

    def up(s):
        return remote(wide.at[s], wide.at[s], z_send.at[0, s], z_recv.at[s], col=col + 1)

    def down(s):
        return remote(wide.at[s], wide.at[s], z_send.at[1, s], z_recv.at[s], col=col - 1)

    def keep_wide(s):
        return pltpu.make_async_copy(wide.at[s], wide_out.at[s], local.at[s])

    def at_step(dist, side):
        s = jnp.where(side == 0, col - dist, col + dist)
        return s, (s >= 0) & (s <= 3) & ((dist > 0) | (side == 0))

    def both(dist, body):
        def one(side, _):
            s, valid = at_step(dist, side)
            pl.when(valid)(lambda: body(s))
            return 0

        lax.fori_loop(0, 2, one, 0)

    def multiply(s, handle):
        for w_ref, (base, size, flipped) in zip(w_refs, parts):

            def one(j, _, w_ref=w_ref, base=base, flipped=flipped):
                cols = pl.ds(pl.multiple_of(j * tile, tile), tile)
                spot = pl.ds(pl.multiple_of(base + j * tile, tile), tile)
                handle(times(wide[s], w_ref, cols, flipped), spot)
                return 0

            lax.fori_loop(0, size // tile, one, 0)

    def step(dist, _):
        def arrive(s):
            @pl.when(dist > 0)
            def _():
                up(s).wait_recv()

            @pl.when((s <= col) & (col < 3))
            def _():
                up(s).start()

            @pl.when((s >= col) & (col > 0))
            def _():
                down(s).start()

            keep_wide(s).start()

        def work(s):
            if whole:

                def store(value, spot):
                    product[:, spot] = value

                multiply(s, store)

                @pl.when(s == spot_a)
                def _():
                    def cast(rows):
                        a_send[0, rows] = product[rows, :].astype(BF16)

                    in_rows(512, 64, cast)
                    mate_copy(a_send.at[0], a_recv.at[0], 0, 0).start()

                @pl.when(s == spot_c)
                def _():
                    def cast(rows):
                        d_send[0, rows] = product[rows, :].astype(BF16)

                    in_rows(512, 64, cast)
                    mate_copy(d_send.at[0], d_recv.at[0], 1, 0).start()

                @pl.when(s == spot_b)
                def _():
                    mate_copy(a_send.at[0], a_recv.at[0], 0, 0).wait_recv()

                    def add(rows):
                        b_send[0, rows] = (product[rows, :] + a_recv[0, rows].astype(F32)).astype(
                            BF16
                        )

                    in_rows(512, 64, add)
                    across_copy(b_send.at[0], c_recv.at[0], 0).start()

                @pl.when(s == spot_d)
                def _():
                    def store_own(rows):
                        out_ref[0, rows] = product[rows, :]

                    in_rows(512, 64, store_own)

            else:

                def quarter(q):
                    return pl.ds(pl.multiple_of(q * 128, 128), 128)

                def split(value, spot):
                    product[...] = value
                    a_send[s, :, spot] = product[quarter(spot_a), :].astype(BF16)
                    keep[:, spot] = product[quarter(spot_b), :]
                    d_send[s, :, spot] = product[quarter(spot_c), :].astype(BF16)
                    out_ref[s, :, spot] = product[quarter(spot_d), :]

                multiply(s, split)
                mate_copy(a_send.at[s], a_recv.at[s], 0, s).start()
                mate_copy(d_send.at[s], d_recv.at[s], 1, s).start()
                mate_copy(a_send.at[s], a_recv.at[s], 0, s).wait_recv()

                def add(rows):
                    b_send[s, rows] = (keep[rows, :] + a_recv[s, rows].astype(F32)).astype(BF16)

                in_rows(128, 16, add)
                across_copy(b_send.at[s], c_recv.at[s], s).start()

        both(dist, arrive)
        both(dist, work)
        return 0

    lax.fori_loop(0, 4, step, 0)

    def finish(s):
        mate_copy(d_send.at[s], d_recv.at[s], 1, s).wait_recv()
        across_copy(b_send.at[s], c_recv.at[s], s).wait_recv()

        def add(rows):
            out_ref[s, rows] += d_recv[s, rows].astype(F32) + c_recv[s, rows].astype(F32)

        in_rows(out_ref.shape[1], 16, add)
        mate_copy(a_send.at[s], a_recv.at[s], 0, s).wait_send()
        mate_copy(d_send.at[s], d_recv.at[s], 1, s).wait_send()
        across_copy(b_send.at[s], c_recv.at[s], s).wait_send()

    def last(dist, _):
        def close(s):
            if not whole:
                finish(s)

            @pl.when((s <= col) & (col < 3))
            def _():
                up(s).wait_send()

            @pl.when((s >= col) & (col > 0))
            def _():
                down(s).wait_send()

            keep_wide(s).wait()

        both(dist, close)
        return 0

    lax.fori_loop(0, 4, last, 0)
    if whole:
        finish(0)


def cols_rows(name, number, x, weights, flipped, whole, tile):
    tokens = x.shape[0]
    parts, base = [], 0
    for w in weights:
        size = w.shape[0] if flipped else w.shape[1]
        parts.append((base, size, flipped))
        base += size
    if whole:
        lead, rows, span, kept = 1, tokens, (tokens, base), (8, 128)
    else:
        lead, rows, span, kept = 4, tokens // 4, (tokens, tile), (tokens // 4, base)
    moved = pltpu.VMEM((lead, rows, base), BF16)
    out, wide = pl.pallas_call(
        functools.partial(cols_rows_kernel, whole, tuple(parts), tile),
        out_shape=(
            jax.ShapeDtypeStruct((lead, rows, base), F32),
            jax.ShapeDtypeStruct((4, tokens, x.shape[1]), BF16),
        ),
        in_specs=[pl.BlockSpec(memory_space=pltpu.VMEM)] * (1 + len(weights)),
        out_specs=(pl.BlockSpec(memory_space=pltpu.VMEM), pl.BlockSpec(memory_space=pl.ANY)),
        scratch_shapes=[
            pltpu.VMEM((4, tokens, x.shape[1]), BF16),
            pltpu.VMEM(span, F32),
            pltpu.VMEM(kept, F32),
        ]
        + [moved] * 6
        + [
            pltpu.SemaphoreType.DMA((2, 4)),
            pltpu.SemaphoreType.DMA((4,)),
            pltpu.SemaphoreType.DMA((4,)),
            pltpu.SemaphoreType.DMA((2, lead)),
            pltpu.SemaphoreType.DMA((2, lead)),
            pltpu.SemaphoreType.DMA((lead,)),
            pltpu.SemaphoreType.DMA((lead,)),
        ],
        compiler_params=pltpu.CompilerParams(
            collective_id=number, has_side_effects=True, vmem_limit_bytes=VMEM_LIMIT
        ),
        cost_estimate=pl.CostEstimate(
            flops=8 * tokens * x.shape[1] * base, bytes_accessed=8 * tokens * base, transcendentals=0
        ),
        name=name,
    )(x, *weights)
    return out.reshape(tokens, base), wide.reshape(4 * tokens, x.shape[1])


def rows_cols_kernel(whole, parts, flipped, tile, *refs):
    n_w = len(parts)
    a_ref = refs[0]
    w_refs = refs[1 : 1 + n_w]
    out_ref, wide_out = refs[1 + n_w : 3 + n_w]
    (wide, product, sent, from_below, from_above) = refs[3 + n_w : 8 + n_w]
    (z_send, z_recv, local, own_sem, m_send, m_recv, x_send, x_recv, f_send, f_recv) = refs[8 + n_w :]
    row, col, chip, core, mate, across = place()
    diag = (1 - chip) * 2 + (1 - core)
    half = product.shape[0] // 2

    def order(j):
        first = jnp.where(col < 2, 3, 0)
        second = jnp.where(col < 2, 2, 1)
        third = jnp.where(lax.rem(col, 2) == 0, col + 1, col - 1)
        return jnp.where(j == 0, first, jnp.where(j == 1, second, jnp.where(j == 2, third, col)))

    def slot(s, q):
        return wide.at[q] if whole else wide.at[s, q]

    def own(s):
        return a_ref if whole else a_ref.at[s]

    def to_mate(s):
        return remote(own(s), slot(s, row), m_send.at[s], m_recv.at[s], row=mate)

    def to_across(s):
        return remote(own(s), slot(s, row), x_send.at[s], x_recv.at[s], row=across)

    def pass_on(s):
        return remote(slot(s, across), slot(s, across), f_send.at[s], f_recv.at[s], row=mate)

    def from_mate(s):
        return remote(slot(s, mate), slot(s, mate), m_send.at[s], m_recv.at[s], row=mate)

    def from_across(s):
        return remote(slot(s, across), slot(s, across), x_send.at[s], x_recv.at[s], row=across)

    def from_diag(s):
        return remote(slot(s, diag), slot(s, diag), f_send.at[s], f_recv.at[s], row=mate)

    def keep_wide(s):
        return pltpu.make_async_copy(wide.at[s], wide_out.at[s], local.at[s])

    def move_own(s):
        return pltpu.make_async_copy(own(s), slot(s, row), own_sem.at[s])

    def piece(ref, s, h):
        return ref.at[s, pl.ds(h * half, half)]

    def up(s, h):
        return remote(piece(sent, s, h), piece(from_below, s, h), z_send.at[s, h], z_recv.at[0, s, h], col=col + 1)

    def down(s, h):
        return remote(piece(sent, s, h), piece(from_above, s, h), z_send.at[s, h], z_recv.at[1, s, h], col=col - 1)

    greet(col, mate, across)
    if whole:
        to_across(0).start()
        to_mate(0).start()
        move_own(0).start()
        from_across(0).wait_recv()
        pass_on(0).start()
        from_mate(0).wait_recv()
        move_own(0).wait()
        from_diag(0).wait_recv()
    else:
        for j in range(2):
            to_across(order(j)).start()
        for j in range(4):
            to_mate(order(j)).start()
            move_own(order(j)).start()

    def multiply(left, rows):
        for t in range(product.shape[1] // tile):
            cols = pl.ds(t * tile, tile)
            total = None
            for w_ref, (base, size) in zip(w_refs, parts):
                term = times(left(base, size), w_ref, cols, flipped)
                total = term if total is None else total + term
            product[rows, cols] = total

    def step(j, _):
        s = order(j)
        if whole:
            keep_wide(s).start()
            multiply(lambda base, size: wide[s, :, pl.ds(base, size)], slice(None))
        else:

            @pl.when(j < 2)
            def _():
                to_across(order(j + 2)).start()

            def pair(first):
                def left(base, size):
                    two = wide[s, pl.ds(first, 2), :, pl.ds(base, size)]
                    return two.reshape(2 * two.shape[1], size)

                multiply(left, pl.ds(pl.multiple_of(first * (half // 2), half), half))

            from_mate(s).wait_recv()
            move_own(s).wait()
            pair(chip * 2)
            from_across(s).wait_recv()
            pass_on(s).start()
            from_diag(s).wait_recv()
            pair((1 - chip) * 2)
            keep_wide(s).start()

        for h in range(2):
            span = half

            def add_in(ref, h=h):
                def add(rows):
                    here = pl.ds(pl.multiple_of(h * span + rows.start, rows.size), rows.size)
                    product[here, :] += ref[s, here].astype(F32)

                in_rows(span, 64, add)

            def cast(rows, h=h):
                here = pl.ds(pl.multiple_of(h * span + rows.start, rows.size), rows.size)
                sent[s, here] = product[here, :].astype(BF16)

            @pl.when((s >= col) & (col > 0))
            def _():
                up(s, h).wait_recv()
                add_in(from_below)

            @pl.when((s <= col) & (col < 3))
            def _():
                down(s, h).wait_recv()
                add_in(from_above)

            @pl.when(s > col)
            def _():
                in_rows(span, 64, cast)

                @pl.when(s < 3)
                def _():
                    up(s + 1, h).wait_send()

                up(s, h).start()

            @pl.when(s < col)
            def _():
                in_rows(span, 64, cast)

                @pl.when(s > 0)
                def _():
                    down(s - 1, h).wait_send()

                down(s, h).start()

        return 0

    lax.fori_loop(0, 4, step, 0)
    out_ref[...] = product[...]

    def last(s, _):
        for h in range(2):

            @pl.when(s == col + 1)
            def _():
                up(s, h).wait_send()

            @pl.when(s == col - 1)
            def _():
                down(s, h).wait_send()

        if not whole:
            to_mate(s).wait_send()
            to_across(s).wait_send()
            pass_on(s).wait_send()
        keep_wide(s).wait()
        return 0

    lax.fori_loop(0, 4, last, 0)
    if whole:
        to_mate(0).wait_send()
        to_across(0).wait_send()
        pass_on(0).wait_send()


def rows_cols(name, number, a, weights, flipped, whole, tile=256):
    tokens, wide_size = a.shape
    parts, base = [], 0
    for w in weights:
        size = w.shape[1] if flipped else w.shape[0]
        parts.append((base, size))
        base += size
    feats = weights[0].shape[0] if flipped else weights[0].shape[1]
    if whole:
        slots, lead, given = (4, tokens, base), 1, a
    else:
        slots, lead, given = (4, 4, tokens // 4, base), 4, a.reshape(4, tokens // 4, base)
    chain = pltpu.VMEM((4, tokens, feats), BF16)
    out, wide = pl.pallas_call(
        functools.partial(rows_cols_kernel, whole, tuple(parts), flipped, tile),
        out_shape=(
            jax.ShapeDtypeStruct((tokens, feats), F32),
            jax.ShapeDtypeStruct(slots, BF16),
        ),
        in_specs=[pl.BlockSpec(memory_space=pltpu.VMEM)] * (1 + len(weights)),
        out_specs=(pl.BlockSpec(memory_space=pltpu.VMEM), pl.BlockSpec(memory_space=pl.ANY)),
        scratch_shapes=[
            pltpu.VMEM(slots, BF16),
            pltpu.VMEM((tokens, feats), F32),
            chain,
            chain,
            chain,
            pltpu.SemaphoreType.DMA((4, 2)),
            pltpu.SemaphoreType.DMA((2, 4, 2)),
            pltpu.SemaphoreType.DMA((4,)),
            pltpu.SemaphoreType.DMA((lead,)),
        ]
        + [pltpu.SemaphoreType.DMA((lead,))] * 6,
        compiler_params=pltpu.CompilerParams(
            collective_id=number, has_side_effects=True, vmem_limit_bytes=VMEM_LIMIT
        ),
        cost_estimate=pl.CostEstimate(
            flops=8 * tokens * feats * base, bytes_accessed=8 * tokens * base, transcendentals=0
        ),
        name=name,
    )(given, *weights)
    return out, wide.reshape(4 * tokens, base)


def turn_tables(length):
    rates = THETA ** (-np.arange(HEAD_SIZE // 2) * 2.0 / HEAD_SIZE)
    angles = np.arange(length)[:, None] * rates[None, :]
    cos, sin = np.cos(angles), np.sin(angles)
    return (
        np.concatenate([cos, cos], axis=1).astype(np.float32),
        np.concatenate([-sin, sin], axis=1).astype(np.float32),
    )


def swap_halves(value):
    return pltpu.roll(value, HEAD_SIZE // 2, 1)


def head(ref, index):
    return ref[:, index * HEAD_SIZE : (index + 1) * HEAD_SIZE]


def root_scale(raw):
    return lax.rsqrt(jnp.mean(raw * raw, axis=1, keepdims=True) + EPSILON)


def attend_kernel(q_heads, groups, qkv, seg_col, seg_row, cos, sin, q_gain, k_gain, o, qa, ka, va, probs):
    kv = q_heads // groups
    tokens = qkv.shape[0]
    half = tokens // 2

    def turned(index, gain):
        raw = head(qkv, index)
        normed = raw * root_scale(raw) * gain[...]
        return (normed * cos[...] + swap_halves(normed) * sin[...]).astype(BF16)

    for i in range(q_heads):
        qa[:, i * HEAD_SIZE : (i + 1) * HEAD_SIZE] = turned(i, q_gain)
    for i in range(kv):
        ka[:, i * HEAD_SIZE : (i + 1) * HEAD_SIZE] = turned(q_heads + i, k_gain)
        va[:, i * HEAD_SIZE : (i + 1) * HEAD_SIZE] = head(qkv, q_heads + kv + i).astype(BF16)
    for block in range(2):
        rows = slice(block * half, (block + 1) * half)
        keys = (block + 1) * half
        spot = lax.broadcasted_iota(jnp.int32, (half, keys), 0) + block * half
        other = lax.broadcasted_iota(jnp.int32, (half, keys), 1)
        allowed = (other <= spot) & (seg_col[rows, :] == seg_row[:, :keys])
        for i in range(q_heads):
            j = i // groups
            dots = lax.dot_general(
                head(qa, i)[rows], head(ka, j)[:keys], (((1,), (1,)), ((), ())), preferred_element_type=F32
            ) * (1.0 / math.sqrt(HEAD_SIZE))
            scores = jnp.where(allowed, dots, MASKED)
            expo = jnp.exp(scores - jnp.max(scores, axis=1, keepdims=True))
            p = expo / jnp.sum(expo, axis=1, keepdims=True)
            probs[i, rows, :keys] = p.astype(BF16)
            mixed = jnp.dot(p.astype(BF16), head(va, j)[:keys], preferred_element_type=F32)
            o[rows, i * HEAD_SIZE : (i + 1) * HEAD_SIZE] = mixed.astype(BF16)


def across_rows(left, right):
    return lax.dot_general(left, right, (((0,), (0,)), ((), ())), preferred_element_type=F32)


def attend_back(q_heads, groups, grad, qkv, qa, ka, va, probs, cos, sin, q_gain, k_gain, out, q_part, k_part, dq, dk, dv):
    kv = q_heads // groups
    tokens = qkv.shape[0]
    half = tokens // 2
    scale = 1.0 / math.sqrt(HEAD_SIZE)
    dk[...] = jnp.zeros_like(dk)
    dv[...] = jnp.zeros_like(dv)
    for block in range(2):
        rows = slice(block * half, (block + 1) * half)
        keys = (block + 1) * half
        for i in range(q_heads):
            j = i // groups
            spot = slice(j * HEAD_SIZE, (j + 1) * HEAD_SIZE)
            pb = probs[i, rows, :keys]
            p = pb.astype(F32)
            g = head(grad, i)[rows].astype(BF16)
            dv[:keys, spot] += across_rows(pb.astype(BF16), g)
            dp = lax.dot_general(
                g, head(va, j)[:keys], (((1,), (1,)), ((), ())), preferred_element_type=F32
            )
            ds = (p * (dp - jnp.sum(p * dp, axis=1, keepdims=True))).astype(BF16)
            dq[rows, i * HEAD_SIZE : (i + 1) * HEAD_SIZE] = (
                jnp.dot(ds, head(ka, j)[:keys], preferred_element_type=F32) * scale
            )
            dk[:keys, spot] += across_rows(ds, head(qa, i)[rows]) * scale

    def back(turned, index, gain):
        raw = head(qkv, index)
        scales = root_scale(raw)
        normed = turned * cos[...] - swap_halves(turned) * sin[...]
        part = jnp.sum(normed * raw * scales, axis=0, keepdims=True)
        weighted = normed * gain[...]
        inner = jnp.sum(weighted * raw, axis=1, keepdims=True)
        result = scales * weighted - raw * (scales * scales * scales) * inner * (1.0 / HEAD_SIZE)
        out[:, index * HEAD_SIZE : (index + 1) * HEAD_SIZE] = result.astype(BF16)
        return part

    q_part[...] = sum(back(head(dq, i), i, q_gain) for i in range(q_heads))
    k_part[...] = sum(back(head(dk, i), q_heads + i, k_gain) for i in range(kv))
    for i in range(kv):
        spot = (q_heads + kv + i) * HEAD_SIZE
        out[:, spot : spot + HEAD_SIZE] = head(dv, i).astype(BF16)


def tail_kernel(pairs, q_heads, groups, *refs):
    refs = list(refs)

    def take(count):
        found = refs[:count]
        del refs[:count]
        return found

    (da, act, w_out, w_down, w_query, w_key, w_value, qkv, qa, ka, va, probs, cos, sin, q_gain, k_gain) = take(16)
    (gy_wide, mixed_wide, normed_wide, gate_n, up_n) = take(5)
    (dxn, down_out, q_part, k_part, down_n, out_n, qkv_n) = take(7)
    others = take(5) if pairs == 2 else []
    (da_wide, act_wide, dqkv, dqkv_wide, held, product, grad_mixed, dq, dk, dv, n_down, n_out, n_qkv) = take(13)
    moved = take(6)
    down_bufs, dxn_bufs = take(3), take(3)
    (g_send, g_recv, local, y_send, y_recv) = take(5)
    moved_sems = take(4)
    act_sems, dqkv_sems = take(7), take(7)
    down_sems, dxn_sems = take(3), take(3)

    at = Ends()
    at.greet(pairs)

    def pair_copy(src, index):
        return remote(src, others[index], y_send.at[index], y_recv.at[index], dp=1 - lax.axis_index("dp"))

    narrow = (gate_n, up_n, n_down, n_out, n_qkv)

    def to_pair(index):
        if pairs == 2:
            pair_copy(narrow[index], index).start()

    def load(index, src):
        return pltpu.make_async_copy(src, held, local.at[index])

    def keep(index, src, dst):
        return pltpu.make_async_copy(src, dst, local.at[3 + index])

    to_pair(0)
    to_pair(1)
    load(0, gy_wide).start()
    gather = ColGather(at, da_wide, g_send, g_recv)
    row_sum = RowSumWhole(at, product, grad_mixed, *moved, *moved_sems)
    acts = RowGather(at, lambda s: act.at[s], lambda s, q: act_wide.at[s, q], act_sems)
    grads = RowGather(at, lambda s: dqkv, lambda s, q: dqkv_wide.at[q], dqkv_sems)
    down_sum = ColSum(at, product, *down_bufs, *down_sems)
    dxn_sum = ColSum(at, product, *dxn_bufs, *dxn_sems)

    da_wide[at.col] = da[...]
    gather.arrive(0)
    for j in range(2):
        acts.to_across(far_first(at.col, j)).start()
    for j in range(4):
        acts.near(far_first(at.col, j))

    def back_out(s):
        product[...] = lax.dot_general(
            da_wide[s], w_out[...], (((1,), (1,)), ((), ())), preferred_element_type=F32
        )
        row_sum.give(s)

    def take_act(j):
        s = far_first(at.col, j)
        if j < 2:
            acts.to_across(far_first(at.col, j + 2)).start()
        acts.wait_near(s)
        acts.take_across(s)
        acts.wait_diag(s)

    def act_rows(s, cols):
        return act_wide[s, :, :, cols].reshape(product.shape[0], cols.size)

    def down_step(j):
        s = far_first(at.col, j)
        product[...] = jnp.dot(
            act_rows(s, pl.ds(0, act.shape[2])), w_down[...], preferred_element_type=F32
        )
        down_sum.step(s)

    def dxn_step(j):
        s = near_first(at, j)
        total, base = None, 0
        for w in (w_query, w_key, w_value):
            size = w.shape[1]
            term = lax.dot_general(
                dqkv_wide[s, :, pl.ds(base, size)], w[...], (((1,), (1,)), ((), ())), preferred_element_type=F32
            )
            total = term if total is None else total + term
            base += size
        product[...] = total
        dxn_sum.step(s)

    def weight_grad(out, left, right):
        def block(here):
            total = None
            for s in range(4):
                term = across_rows(left(s, here), right(s))
                total = term if total is None else total + term
            out[here, :] = total.astype(BF16)

        in_rows(out.shape[0], 256, block)

    gather.loop(0, back_out)
    take_act(0)
    gather.arrive(1)
    gather.loop(1, back_out)
    down_step(0)
    gather.arrive(2)
    gather.loop(2, back_out)
    take_act(1)
    down_step(1)
    gather.arrive(3)
    gather.loop(3, back_out)

    @pl.when(at.end)
    def _():
        take_act(2)
        down_step(2)

    row_sum.finish()
    attend_back(
        q_heads, groups, grad_mixed, qkv, qa, ka, va, probs, cos, sin, q_gain, k_gain,
        dqkv, q_part, k_part, dq, dk, dv,
    )
    grads.to_across(0).start()
    grads.near(0)
    grads.wait_near(0)

    @pl.when(at.end)
    def _():
        dxn_step(0)

    @pl.when(jnp.logical_not(at.end))
    def _():
        take_act(2)
        down_step(2)

    take_act(3)
    load(0, gy_wide).wait()
    weight_grad(n_down, act_rows, lambda s: held[s])
    to_pair(2)
    keep(0, n_down, down_n).start()
    load(1, mixed_wide).start()

    @pl.when(jnp.logical_not(at.end))
    def _():
        dxn_step(0)

    load(1, mixed_wide).wait()
    weight_grad(n_out, lambda s, here: held[s, :, here], lambda s: da_wide[s])
    to_pair(3)
    keep(1, n_out, out_n).start()
    load(2, normed_wide).start()
    grads.take_across(0)
    grads.wait_diag(0)

    @pl.when(at.end)
    def _():
        dxn_step(1)
        dxn_step(2)

    load(2, normed_wide).wait()
    weight_grad(n_qkv, lambda s, here: held[s, :, here], lambda s: dqkv_wide[s])
    to_pair(4)
    keep(2, n_qkv, qkv_n).start()

    @pl.when(jnp.logical_not(at.end))
    def _():
        dxn_step(1)
        dxn_step(2)

    down_step(3)
    down_out[...] = product[...]
    dxn_step(3)
    dxn[...] = product[...]

    gather.close()
    row_sum.close()
    acts.close(4)
    grads.close(1)
    down_sum.close()
    dxn_sum.close()
    keep(0, n_down, down_n).wait()
    keep(1, n_out, out_n).wait()
    keep(2, n_qkv, qkv_n).wait()
    if pairs == 2:
        for index in range(5):
            pair_copy(narrow[index], index).wait()


def tail(pairs, q_heads, groups, number, da, act, w_out, w_down, w_qkv, saved, tables, wides, narrow):
    tokens, feats = da.shape
    ff = act.shape[1]
    width = saved[0].shape[1]
    dma = pltpu.SemaphoreType.DMA
    act = act.reshape(4, tokens // 4, ff)
    any_spec, vmem = pl.BlockSpec(memory_space=pl.ANY), pl.BlockSpec(memory_space=pltpu.VMEM)
    wides = [w.reshape(4, tokens, feats) for w in wides]
    shapes = [
        jax.ShapeDtypeStruct((tokens, feats), F32),
        jax.ShapeDtypeStruct((tokens, feats), F32),
        jax.ShapeDtypeStruct((1, HEAD_SIZE), F32),
        jax.ShapeDtypeStruct((1, HEAD_SIZE), F32),
    ]
    own = [
        jax.ShapeDtypeStruct((ff, feats), BF16),
        jax.ShapeDtypeStruct((w_out.shape[0], feats), BF16),
        jax.ShapeDtypeStruct((feats, width), BF16),
    ]
    others = [jax.ShapeDtypeStruct(n.shape, BF16) for n in narrow] + own if pairs == 2 else []
    chain = [
        pltpu.VMEM((4, tokens, feats), BF16), pltpu.VMEM((4, tokens, feats), BF16), pltpu.VMEM((tokens, feats), BF16),
    ]
    chain_sems = [dma((4, 2)), dma((4, 2)), dma((2,))]
    k_width = saved[2].shape[1]
    out = pl.pallas_call(
        functools.partial(tail_kernel, pairs, q_heads, groups),
        out_shape=tuple(shapes + own + others),
        in_specs=[vmem] * 16 + [any_spec] * 5,
        out_specs=tuple([vmem] * 4 + [any_spec] * (3 + len(others))),
        scratch_shapes=[
            pltpu.VMEM((4, tokens, feats), BF16),
            pltpu.VMEM((4, 4, tokens // 4, ff), BF16),
            pltpu.VMEM((tokens, width), BF16),
            pltpu.VMEM((4, tokens, width), BF16),
            pltpu.VMEM((4, tokens, feats), BF16),
            pltpu.VMEM((tokens, feats), F32),
            pltpu.VMEM((tokens, w_out.shape[0]), F32),
            pltpu.VMEM((tokens, w_out.shape[0]), F32),
            pltpu.VMEM((tokens, k_width), F32),
            pltpu.VMEM((tokens, k_width), F32),
            pltpu.VMEM((ff, feats), BF16),
            pltpu.VMEM((w_out.shape[0], feats), BF16),
            pltpu.VMEM((feats, width), BF16),
        ]
        + [pltpu.VMEM((tokens, w_out.shape[0]), BF16)] * 6
        + chain * 2
        + [dma((2, 4)), dma((4,)), dma((6,)), dma((5,)), dma((5,))]
        + [dma((2,)), dma((2,)), dma((1,)), dma((1,))]
        + [dma((4,))] * 7
        + [dma((1,))] * 7
        + chain_sems * 2,
        compiler_params=pltpu.CompilerParams(
            collective_id=number, has_side_effects=True, vmem_limit_bytes=VMEM_LIMIT
        ),
        name="tail",
    )(da, act, w_out, w_down, *w_qkv, *saved, *tables, *wides, *narrow)
    return out[:4], out[4:7], out[7:]


def local_call(kernel, name, shapes, scratch, *args):
    return pl.pallas_call(
        kernel,
        out_shape=shapes,
        scratch_shapes=scratch,
        compiler_params=pltpu.CompilerParams(vmem_limit_bytes=VMEM_LIMIT),
        name=name,
    )(*args)


def token_sums(operand):
    return lax.psum(operand, "row")


def outer(left_op, right_op):
    return lax.dot_general(left_op, right_op, (((0,), (0,)), ((), ())), preferred_element_type=F32)


def shards(
    pairs,
    hidden_in,
    segment_ids,
    attn_gain,
    w_query,
    key_projection,
    value_projection,
    query_gain,
    key_norm_gain,
    w_out,
    ffn_gain,
    w_gate,
    w_up,
    w_down,
    out_grad,
):
    tokens, slice_width = hidden_in.shape
    model_width = attn_gain.shape[0]
    offset = lax.axis_index("row") * slice_width
    gain_one = lax.dynamic_slice_in_dim(attn_gain, offset, slice_width)
    gain_two = lax.dynamic_slice_in_dim(ffn_gain, offset, slice_width)
    q_width = w_query.shape[1]
    k_width = key_projection.shape[1]
    q_heads = q_width // HEAD_SIZE
    groups = q_width // k_width
    ff = w_gate.shape[1]

    def narrow_outer(left_op, right_op):
        return outer(left_op, right_op).astype(BF16)

    stream = hidden_in.astype(F32)
    scale_one = lax.rsqrt(token_sums(jnp.sum(stream * stream, axis=1)) / model_width + EPSILON)[:, None]
    normalized = (stream * scale_one * gain_one).astype(BF16)
    qkv, normed_wide = cols_rows(
        "qkv", 0, normalized, [w_query, key_projection, value_projection], False, True, 256
    )
    cos, sin = turn_tables(tokens)
    q_gain, k_gain = query_gain[None, :], key_norm_gain[None, :]
    mixed, q_turned, k_turned, values, probs = local_call(
        functools.partial(attend_kernel, q_heads, groups),
        "attend",
        (
            jax.ShapeDtypeStruct((tokens, q_width), BF16),
            jax.ShapeDtypeStruct((tokens, q_width), BF16),
            jax.ShapeDtypeStruct((tokens, k_width), BF16),
            jax.ShapeDtypeStruct((tokens, k_width), BF16),
            jax.ShapeDtypeStruct((q_heads, tokens, tokens), BF16),
        ),
        [],
        qkv, segment_ids[:, None], segment_ids[None, :], cos, sin, q_gain, k_gain,
    )
    attn_out, mixed_wide = rows_cols("out", 1, mixed, [w_out], False, True)
    hidden = stream + attn_out
    scale_two = lax.rsqrt(token_sums(jnp.sum(hidden * hidden, axis=1)) / model_width + EPSILON)[:, None]
    ffn_in = (hidden * scale_two * gain_two).astype(BF16)
    gate_up, ffn_wide = cols_rows("gate_up", 2, ffn_in, [w_gate, w_up], False, False, 512)
    grad_inner, grad_wide = cols_rows("down_back", 3, out_grad, [w_down], True, False, 512)
    gate_pre, upward = gate_up[:, :ff], gate_up[:, ff:]
    sigmoid_gate = jax.nn.sigmoid(gate_pre)
    activated = gate_pre * sigmoid_gate
    inner_act = (activated * upward).astype(BF16)
    grad_gate = grad_inner * upward * (sigmoid_gate * (1.0 + gate_pre * (1.0 - sigmoid_gate)))
    grad_up = grad_inner * activated
    grad_ffn = jnp.concatenate([grad_gate, grad_up], axis=1).astype(BF16)
    grad_ffn_in, ffn_grad_wide = rows_cols("ffn_back", 4, grad_ffn, [w_gate, w_up], True, False)
    gate_n = narrow_outer(ffn_wide, ffn_grad_wide[:, :ff])
    up_n = narrow_outer(ffn_wide, ffn_grad_wide[:, ff:])
    grad_out = out_grad.astype(F32)
    weighted_two = grad_ffn_in * gain_two
    gain_two_part = jnp.sum(grad_ffn_in * hidden * scale_two, axis=0)
    dot_two = token_sums(jnp.sum(weighted_two * hidden, axis=1))[:, None]
    grad_hidden = grad_out + scale_two * weighted_two - hidden * scale_two**3 * dot_two / model_width
    grad_attn = grad_hidden.astype(BF16)
    (grad_normed, down_out, q_gain_part, k_gain_part), own, others = tail(
        pairs, q_heads, groups, 5, grad_attn, inner_act, w_out, w_down,
        (w_query, key_projection, value_projection),
        (qkv, q_turned, k_turned, values, probs),
        (cos, sin, q_gain, k_gain),
        (grad_wide, mixed_wide, normed_wide),
        (gate_n, up_n),
    )
    parts = (gate_n, up_n, *own)
    if pairs == 2:
        sums = [a.astype(F32) + b.astype(F32) for a, b in zip(parts, others)]
    else:
        sums = lax.psum(tuple(part.astype(F32) for part in parts), "dp")
    gate_grad, up_grad, down_grad, out_weight_grad, qkv_grad = sums
    layer_out = (hidden + down_out).astype(BF16)
    weighted_one = grad_normed * gain_one
    gain_one_part = jnp.sum(grad_normed * stream * scale_one, axis=0)
    dot_one = token_sums(jnp.sum(weighted_one * stream, axis=1))[:, None]
    in_grad = grad_hidden + scale_one * weighted_one - stream * scale_one**3 * dot_one / model_width

    def full(part):
        return lax.dynamic_update_slice_in_dim(jnp.zeros((model_width,), F32), part, offset, 0)

    attn_gain_grad, ffn_gain_grad, query_gain_grad, key_gain_grad = lax.psum(
        (full(gain_one_part), full(gain_two_part), q_gain_part[0], k_gain_part[0]), ("dp", "row", "col")
    )
    return (
        layer_out,
        in_grad,
        attn_gain_grad,
        qkv_grad[:, :q_width],
        qkv_grad[:, q_width : q_width + k_width],
        qkv_grad[:, q_width + k_width :],
        query_gain_grad,
        key_gain_grad,
        out_weight_grad,
        ffn_gain_grad,
        gate_grad,
        up_grad,
        down_grad,
    )


def solution(mesh):
    acts, grid, flip, none = P(("dp", "col"), "row"), P("row", "col"), P("col", "row"), P()
    return jax.shard_map(
        functools.partial(shards, mesh.shape["dp"]),
        mesh=mesh,
        in_specs=(
            acts, P(("dp", "row")), none, grid, grid, grid, none, none, flip, none, grid, grid, flip, acts,
        ),
        out_specs=(
            acts, acts, none, grid, grid, grid, none, none, flip, none, grid, grid, flip,
        ),
        check_vma=False,
    )
```

```python
import functools
import math

import jax
import jax.numpy as jnp
import numpy as np
from jax import lax
from jax.experimental import pallas as pl
from jax.experimental.pallas import tpu as pltpu
from jax.sharding import PartitionSpec as P

HEAD_SIZE = 128
EPSILON = 1e-06
THETA = 1000000.0
MASKED = -1e30
MESH = pl.DeviceIdType.MESH
BF16 = jnp.bfloat16
F32 = jnp.float32
VMEM_LIMIT = 60 << 20


def place():
    row = lax.axis_index("row")
    col = lax.axis_index("col")
    chip = lax.div(row, 2)
    core = lax.rem(row, 2)
    return row, col, chip, core, chip * 2 + (1 - core), (1 - chip) * 2 + core


def to(**where):
    return dict(device_id=where, device_id_type=MESH)


def greet(col, mate, across):
    gate = pltpu.get_barrier_semaphore()
    pl.semaphore_signal(gate, inc=1, **to(row=mate))
    pl.semaphore_signal(gate, inc=1, **to(row=across))

    @pl.when(col > 0)
    def _():
        pl.semaphore_signal(gate, inc=1, **to(col=col - 1))

    @pl.when(col < 3)
    def _():
        pl.semaphore_signal(gate, inc=1, **to(col=col + 1))

    ends = jnp.where(col > 0, 1, 0) + jnp.where(col < 3, 1, 0)
    pl.semaphore_wait(gate, 2 + ends)


def times(left, ref, cols, flipped):
    if flipped:
        return lax.dot_general(
            left, ref[cols, :], (((1,), (1,)), ((), ())), preferred_element_type=F32
        )
    return jnp.dot(left, ref[:, cols], preferred_element_type=F32)


class Ends:
    def __init__(self):
        self.row = lax.axis_index("row")
        self.col = lax.axis_index("col")
        self.chip = lax.div(self.row, 2)
        self.core = lax.rem(self.row, 2)
        self.mate = self.chip * 2 + (1 - self.core)
        self.across = (1 - self.chip) * 2 + self.core
        self.diag = (1 - self.chip) * 2 + (1 - self.core)
        self.end = (self.col == 0) | (self.col == 3)

    def greet(self, pairs=0, line=False):
        gate = pltpu.get_barrier_semaphore()
        count = 3
        for peer in (self.mate, self.across, self.diag):
            pl.semaphore_signal(gate, inc=1, **to(row=peer))
        for step in range(1, pairs):
            pl.semaphore_signal(gate, inc=1, **to(dp=self.pair(pairs, step)))
            count += 1
        if line:
            for step in range(1, 4):
                pl.semaphore_signal(gate, inc=1, **to(col=lax.rem(self.col + step, 4)))
                count += 1
        else:

            @pl.when(self.col > 0)
            def _():
                pl.semaphore_signal(gate, inc=1, **to(col=self.col - 1))

            @pl.when(self.col < 3)
            def _():
                pl.semaphore_signal(gate, inc=1, **to(col=self.col + 1))

            count += jnp.where(self.col > 0, 1, 0) + jnp.where(self.col < 3, 1, 0)
        pl.semaphore_wait(gate, count)

    def pair(self, pairs, step):
        return lax.rem(lax.axis_index("dp") + step, pairs)


class RowTotal:
    def __init__(self, at, own, got, sends, recvs):
        self.own, self.got = own, got
        self.copies = [
            remote(own, got.at[i], sends.at[i], recvs.at[i], row=peer)
            for i, peer in enumerate((at.mate, at.across, at.diag))
        ]

    def start(self, column):
        self.own[...] = jnp.broadcast_to(column, (column.shape[0], 128)).T[:8, :]
        for copy in self.copies:
            copy.start()

    def finish(self):
        for copy in self.copies:
            copy.wait()
        total = (self.own[...] + self.got[0]) + (self.got[1] + self.got[2])
        return jnp.concatenate([total] * 16, axis=0).T[:, :1]


def row_total_scratch(tokens):
    return [pltpu.VMEM((8, tokens), F32), pltpu.VMEM((3, 8, tokens), F32)]


def row_total_sems():
    return [pltpu.SemaphoreType.DMA((3,)), pltpu.SemaphoreType.DMA((3,))]


def remote(src, dst, sends, recvs, **where):
    return pltpu.make_async_remote_copy(
        src_ref=src, dst_ref=dst, send_sem=sends, recv_sem=recvs, **to(**where)
    )


def in_rows(count, step, body, first=0):
    def one(i, _):
        body(pl.ds(pl.multiple_of(first + i * step, step), step))
        return 0

    lax.fori_loop(0, count // step, one, 0)


class ColGather:
    def __init__(self, at, wide, sends, recvs):
        self.at, self.wide, self.sends, self.recvs = at, wide, sends, recvs

    def up(self, s):
        return remote(self.wide.at[s], self.wide.at[s], self.sends.at[0, s], self.recvs.at[s], col=self.at.col + 1)

    def down(self, s):
        return remote(self.wide.at[s], self.wide.at[s], self.sends.at[1, s], self.recvs.at[s], col=self.at.col - 1)

    def both(self, dist, body):
        if dist == 0:
            body(self.at.col)
            return
        below, above = self.at.col - dist, self.at.col + dist
        pl.when(below >= 0)(lambda: body(below))
        pl.when(above <= 3)(lambda: body(above))

    def loop(self, dist, body):
        if dist == 0:
            body(self.at.col)
            return

        def one(side, _):
            s = jnp.where(side == 0, self.at.col - dist, self.at.col + dist)
            pl.when((s >= 0) & (s <= 3))(lambda: body(s))
            return 0

        lax.fori_loop(0, 2, one, 0)

    def arrive(self, dist):
        def take(s):
            if dist:
                self.up(s).wait_recv()

            @pl.when((s <= self.at.col) & (self.at.col < 3))
            def _():
                self.up(s).start()

            @pl.when((s >= self.at.col) & (self.at.col > 0))
            def _():
                self.down(s).start()

        self.loop(dist, take)

    def close(self):
        def one(s, _):
            @pl.when((s <= self.at.col) & (self.at.col < 3))
            def _():
                self.up(s).wait_send()

            @pl.when((s >= self.at.col) & (self.at.col > 0))
            def _():
                self.down(s).wait_send()

            return 0

        lax.fori_loop(0, 4, one, 0)


class RowSumWhole:
    def __init__(self, at, product, out, a_send, a_recv, b_send, c_recv, d_send, d_recv, m_send, m_recv, x_send, x_recv):
        self.at, self.product, self.out = at, product, out
        self.b_send, self.c_recv, self.a_recv, self.d_recv = b_send, c_recv, a_recv, d_recv
        self.a_send, self.d_send = a_send, d_send
        self.a = remote(a_send, a_recv, m_send.at[0], m_recv.at[0], row=at.mate)
        self.d = remote(d_send, d_recv, m_send.at[1], m_recv.at[1], row=at.mate)
        self.b = remote(b_send, c_recv, x_send.at[0], x_recv.at[0], row=at.across)

    def give(self, s):
        at, product = self.at, self.product
        rows = product.shape[0]

        def cast(ref):
            def one(here):
                ref[here] = product[here, :].astype(BF16)

            in_rows(rows, 64, one)

        @pl.when(s == at.diag)
        def _():
            cast(self.a_send)
            self.a.start()

        @pl.when(s == at.mate)
        def _():
            cast(self.d_send)
            self.d.start()

        @pl.when(s == at.across)
        def _():
            self.a.wait_recv()

            def one(here):
                self.b_send[here] = (product[here, :] + self.a_recv[here].astype(F32)).astype(BF16)

            in_rows(rows, 64, one)
            self.b.start()

        @pl.when(s == at.row)
        def _():
            def one(here):
                self.out[here] = product[here, :]

            in_rows(rows, 64, one)

    def finish(self):
        self.d.wait_recv()
        self.b.wait_recv()

        def one(here):
            self.out[here] += self.d_recv[here].astype(F32) + self.c_recv[here].astype(F32)

        in_rows(self.out.shape[0], 64, one)

    def close(self):
        self.a.wait_send()
        self.b.wait_send()
        self.d.wait_send()


class RowSumQuarter:
    def __init__(self, at, chunk, keep, a_send, a_recv, b_send, c_recv, d_send, d_recv, m_send, m_recv, x_send, x_recv):
        self.at, self.chunk, self.keep = at, chunk, keep
        self.a_send, self.a_recv, self.b_send, self.c_recv = a_send, a_recv, b_send, c_recv
        self.d_send, self.d_recv = d_send, d_recv
        self.sems = (m_send, m_recv, x_send, x_recv)

    def a(self, s):
        m_send, m_recv, _, _ = self.sems
        return remote(self.a_send.at[s], self.a_recv.at[s], m_send.at[0, s], m_recv.at[0, s], row=self.at.mate)

    def d(self, s):
        m_send, m_recv, _, _ = self.sems
        return remote(self.d_send.at[s], self.d_recv.at[s], m_send.at[1, s], m_recv.at[1, s], row=self.at.mate)

    def b(self, s):
        _, _, x_send, x_recv = self.sems
        return remote(self.b_send.at[s], self.c_recv.at[s], x_send.at[s], x_recv.at[s], row=self.at.across)

    def split(self, s, value, spot, own):
        at, chunk = self.at, self.chunk
        chunk[...] = value

        def quarter(q):
            return chunk[pl.ds(pl.multiple_of(q * 128, 128), 128), :]

        self.a_send[s, :, spot] = quarter(at.diag).astype(BF16)
        self.keep[:, spot] = quarter(at.across)
        self.d_send[s, :, spot] = quarter(at.mate).astype(BF16)
        own[s, :, spot] = quarter(at.row)

    def give(self, s):
        self.a(s).start()
        self.d(s).start()
        self.a(s).wait_recv()

        def one(here):
            self.b_send[s, here] = (self.keep[here, :] + self.a_recv[s, here].astype(F32)).astype(BF16)

        in_rows(128, 16, one)
        self.b(s).start()

    def finish(self, s):
        self.d(s).wait_recv()
        self.b(s).wait_recv()

    def close(self):
        def one(s, _):
            self.a(s).wait_send()
            self.b(s).wait_send()
            self.d(s).wait_send()
            return 0

        lax.fori_loop(0, 4, one, 0)


class RowGather:
    def __init__(self, at, own, slot, sems):
        self.at, self.own, self.slot = at, own, slot
        self.m_send, self.m_recv, self.x_send, self.x_recv, self.f_send, self.f_recv, self.local = sems

    def to_mate(self, s):
        return remote(self.own(s), self.slot(s, self.at.row), self.m_send.at[s], self.m_recv.at[s], row=self.at.mate)

    def to_across(self, s):
        return remote(self.own(s), self.slot(s, self.at.row), self.x_send.at[s], self.x_recv.at[s], row=self.at.across)

    def pass_on(self, s):
        here = self.slot(s, self.at.across)
        return remote(here, here, self.f_send.at[s], self.f_recv.at[s], row=self.at.mate)

    def move_own(self, s):
        return pltpu.make_async_copy(self.own(s), self.slot(s, self.at.row), self.local.at[s])

    def near(self, s):
        self.to_mate(s).start()
        self.move_own(s).start()

    def wait_near(self, s):
        here = self.slot(s, self.at.mate)
        remote(here, here, self.m_send.at[s], self.m_recv.at[s], row=self.at.mate).wait_recv()
        self.move_own(s).wait()

    def take_across(self, s):
        here = self.slot(s, self.at.across)
        remote(here, here, self.x_send.at[s], self.x_recv.at[s], row=self.at.across).wait_recv()
        self.pass_on(s).start()

    def wait_diag(self, s):
        here = self.slot(s, self.at.diag)
        remote(here, here, self.f_send.at[s], self.f_recv.at[s], row=self.at.mate).wait_recv()

    def close(self, count):
        def one(s, _):
            self.to_mate(s).wait_send()
            self.to_across(s).wait_send()
            self.pass_on(s).wait_send()
            return 0

        lax.fori_loop(0, count, one, 0)


class ColSum:
    def __init__(self, at, product, sent, got, extra, sends, recvs, extra_recvs):
        self.at, self.product, self.sent, self.got, self.extra = at, product, sent, got, extra
        self.sends, self.recvs, self.extra_recvs = sends, recvs, extra_recvs
        self.half = product.shape[0] // 2

    def part(self, h):
        return pl.ds(h * self.half, self.half)

    def up(self, s, h):
        return remote(
            self.sent.at[s, self.part(h)], self.got.at[s, self.part(h)],
            self.sends.at[s, h], self.recvs.at[s, h], col=self.at.col + 1,
        )

    def down(self, s, h):
        return remote(
            self.sent.at[s, self.part(h)], self.got.at[s, self.part(h)],
            self.sends.at[s, h], self.recvs.at[s, h], col=self.at.col - 1,
        )

    def last_down(self, s, h):
        return remote(
            self.sent.at[s, self.part(h)], self.extra.at[self.part(h)],
            self.sends.at[s, h], self.extra_recvs.at[h], col=self.at.col - 1,
        )

    def step(self, s):
        col, product = self.at.col, self.product
        for h in range(2):
            @pl.when(((s >= col) & (col > 0)) | ((s < col) & (col < 3)))
            def _():
                self.up(s, h).wait_recv()

                def add(here):
                    product[here, :] += self.got[s, here].astype(F32)

                in_rows(self.half, 64, add, h * self.half)

            @pl.when((s == col) & (col < 3))
            def _():
                self.last_down(s, h).wait_recv()

                def add(here):
                    product[here, :] += self.extra[here].astype(F32)

                in_rows(self.half, 64, add, h * self.half)

            @pl.when(s != col)
            def _():
                def cast(here):
                    self.sent[s, here] = product[here, :].astype(BF16)

                in_rows(self.half, 64, cast, h * self.half)

            pl.when(s > col)(lambda: self.up(s, h).start())
            pl.when(s < col - 1)(lambda: self.down(s, h).start())
            pl.when(s == col - 1)(lambda: self.last_down(s, h).start())

    def close(self):
        def one(s, _):
            for h in range(2):
                pl.when(s != self.at.col)(lambda: self.up(s, h).wait_send())
            return 0

        lax.fori_loop(0, 4, one, 0)


def far_first(col, j):
    first = jnp.where(col < 2, 3, 0)
    second = jnp.where(col < 2, 2, 1)
    third = jnp.where(lax.rem(col, 2) == 0, col + 1, col - 1)
    return (first, second, third, col)[j]


def near_first(at, j):
    first, second, partner, _ = [far_first(at.col, i) for i in range(4)]
    mine = lax.div(at.col, 2) == at.chip
    return (
        jnp.where(mine, partner, first),
        jnp.where(mine, first, second),
        jnp.where(mine, second, partner),
        at.col,
    )[j]


def cols_rows_kernel(whole, parts, tile, *refs):
    n_w = len(parts)
    x_ref = refs[0]
    w_refs = refs[1 : 1 + n_w]
    out_ref, wide_out = refs[1 + n_w : 3 + n_w]
    (wide, product, keep, a_send, a_recv, b_send, c_recv, d_send, d_recv) = refs[3 + n_w : 12 + n_w]
    (z_send, z_recv, local, m_send, m_recv, x_send, x_recv) = refs[12 + n_w :]
    row, col, chip, core, mate, across = place()
    spot_a = (1 - chip) * 2 + (1 - core)
    spot_b = across
    spot_c = mate
    spot_d = row
    width = sum(p[1] for p in parts)

    wide[col] = x_ref[...]
    greet(col, mate, across)

    def mate_copy(src, dst, lane, spot):
        return remote(src, dst, m_send.at[lane, spot], m_recv.at[lane, spot], row=mate)

    def across_copy(src, dst, spot):
        return remote(src, dst, x_send.at[spot], x_recv.at[spot], row=across)

    def up(s):
        return remote(wide.at[s], wide.at[s], z_send.at[0, s], z_recv.at[s], col=col + 1)

    def down(s):
        return remote(wide.at[s], wide.at[s], z_send.at[1, s], z_recv.at[s], col=col - 1)

    def keep_wide(s):
        return pltpu.make_async_copy(wide.at[s], wide_out.at[s], local.at[s])

    def at_step(dist, side):
        s = jnp.where(side == 0, col - dist, col + dist)
        return s, (s >= 0) & (s <= 3) & ((dist > 0) | (side == 0))

    def both(dist, body):
        def one(side, _):
            s, valid = at_step(dist, side)
            pl.when(valid)(lambda: body(s))
            return 0

        lax.fori_loop(0, 2, one, 0)

    def multiply(s, handle):
        for w_ref, (base, size, flipped) in zip(w_refs, parts):

            def one(j, _, w_ref=w_ref, base=base, flipped=flipped):
                cols = pl.ds(pl.multiple_of(j * tile, tile), tile)
                spot = pl.ds(pl.multiple_of(base + j * tile, tile), tile)
                handle(times(wide[s], w_ref, cols, flipped), spot)
                return 0

            lax.fori_loop(0, size // tile, one, 0)

    def step(dist, _):
        def arrive(s):
            @pl.when(dist > 0)
            def _():
                up(s).wait_recv()

            @pl.when((s <= col) & (col < 3))
            def _():
                up(s).start()

            @pl.when((s >= col) & (col > 0))
            def _():
                down(s).start()

            keep_wide(s).start()

        def work(s):
            if whole:

                def store(value, spot):
                    product[:, spot] = value

                multiply(s, store)

                @pl.when(s == spot_a)
                def _():
                    def cast(rows):
                        a_send[0, rows] = product[rows, :].astype(BF16)

                    in_rows(512, 64, cast)
                    mate_copy(a_send.at[0], a_recv.at[0], 0, 0).start()

                @pl.when(s == spot_c)
                def _():
                    def cast(rows):
                        d_send[0, rows] = product[rows, :].astype(BF16)

                    in_rows(512, 64, cast)
                    mate_copy(d_send.at[0], d_recv.at[0], 1, 0).start()

                @pl.when(s == spot_b)
                def _():
                    mate_copy(a_send.at[0], a_recv.at[0], 0, 0).wait_recv()

                    def add(rows):
                        b_send[0, rows] = (product[rows, :] + a_recv[0, rows].astype(F32)).astype(
                            BF16
                        )

                    in_rows(512, 64, add)
                    across_copy(b_send.at[0], c_recv.at[0], 0).start()

                @pl.when(s == spot_d)
                def _():
                    def store_own(rows):
                        out_ref[0, rows] = product[rows, :]

                    in_rows(512, 64, store_own)

            else:

                def quarter(q):
                    return pl.ds(pl.multiple_of(q * 128, 128), 128)

                def split(value, spot):
                    product[...] = value
                    a_send[s, :, spot] = product[quarter(spot_a), :].astype(BF16)
                    keep[:, spot] = product[quarter(spot_b), :]
                    d_send[s, :, spot] = product[quarter(spot_c), :].astype(BF16)
                    out_ref[s, :, spot] = product[quarter(spot_d), :]

                multiply(s, split)
                mate_copy(a_send.at[s], a_recv.at[s], 0, s).start()
                mate_copy(d_send.at[s], d_recv.at[s], 1, s).start()
                mate_copy(a_send.at[s], a_recv.at[s], 0, s).wait_recv()

                def add(rows):
                    b_send[s, rows] = (keep[rows, :] + a_recv[s, rows].astype(F32)).astype(BF16)

                in_rows(128, 16, add)
                across_copy(b_send.at[s], c_recv.at[s], s).start()

        both(dist, arrive)
        both(dist, work)
        return 0

    lax.fori_loop(0, 4, step, 0)

    def finish(s):
        mate_copy(d_send.at[s], d_recv.at[s], 1, s).wait_recv()
        across_copy(b_send.at[s], c_recv.at[s], s).wait_recv()

        def add(rows):
            out_ref[s, rows] += d_recv[s, rows].astype(F32) + c_recv[s, rows].astype(F32)

        in_rows(out_ref.shape[1], 16, add)
        mate_copy(a_send.at[s], a_recv.at[s], 0, s).wait_send()
        mate_copy(d_send.at[s], d_recv.at[s], 1, s).wait_send()
        across_copy(b_send.at[s], c_recv.at[s], s).wait_send()

    def last(dist, _):
        def close(s):
            if not whole:
                finish(s)

            @pl.when((s <= col) & (col < 3))
            def _():
                up(s).wait_send()

            @pl.when((s >= col) & (col > 0))
            def _():
                down(s).wait_send()

            keep_wide(s).wait()

        both(dist, close)
        return 0

    lax.fori_loop(0, 4, last, 0)
    if whole:
        finish(0)


def cols_rows(name, number, x, weights, flipped, whole, tile):
    tokens = x.shape[0]
    parts, base = [], 0
    for w in weights:
        size = w.shape[0] if flipped else w.shape[1]
        parts.append((base, size, flipped))
        base += size
    if whole:
        lead, rows, span, kept = 1, tokens, (tokens, base), (8, 128)
    else:
        lead, rows, span, kept = 4, tokens // 4, (tokens, tile), (tokens // 4, base)
    moved = pltpu.VMEM((lead, rows, base), BF16)
    out, wide = pl.pallas_call(
        functools.partial(cols_rows_kernel, whole, tuple(parts), tile),
        out_shape=(
            jax.ShapeDtypeStruct((lead, rows, base), F32),
            jax.ShapeDtypeStruct((4, tokens, x.shape[1]), BF16),
        ),
        in_specs=[pl.BlockSpec(memory_space=pltpu.VMEM)] * (1 + len(weights)),
        out_specs=(pl.BlockSpec(memory_space=pltpu.VMEM), pl.BlockSpec(memory_space=pl.ANY)),
        scratch_shapes=[
            pltpu.VMEM((4, tokens, x.shape[1]), BF16),
            pltpu.VMEM(span, F32),
            pltpu.VMEM(kept, F32),
        ]
        + [moved] * 6
        + [
            pltpu.SemaphoreType.DMA((2, 4)),
            pltpu.SemaphoreType.DMA((4,)),
            pltpu.SemaphoreType.DMA((4,)),
            pltpu.SemaphoreType.DMA((2, lead)),
            pltpu.SemaphoreType.DMA((2, lead)),
            pltpu.SemaphoreType.DMA((lead,)),
            pltpu.SemaphoreType.DMA((lead,)),
        ],
        compiler_params=pltpu.CompilerParams(
            collective_id=number, has_side_effects=True, vmem_limit_bytes=VMEM_LIMIT
        ),
        cost_estimate=pl.CostEstimate(
            flops=8 * tokens * x.shape[1] * base, bytes_accessed=8 * tokens * base, transcendentals=0
        ),
        name=name,
    )(x, *weights)
    return out.reshape(tokens, base), wide.reshape(4 * tokens, x.shape[1])


def rows_cols_kernel(whole, parts, flipped, tile, *refs):
    n_w = len(parts)
    a_ref = refs[0]
    w_refs = refs[1 : 1 + n_w]
    out_ref, wide_out = refs[1 + n_w : 3 + n_w]
    (wide, product, sent, from_below, from_above) = refs[3 + n_w : 8 + n_w]
    (z_send, z_recv, local, own_sem, m_send, m_recv, x_send, x_recv, f_send, f_recv) = refs[8 + n_w :]
    row, col, chip, core, mate, across = place()
    diag = (1 - chip) * 2 + (1 - core)
    half = product.shape[0] // 2

    def order(j):
        first = jnp.where(col < 2, 3, 0)
        second = jnp.where(col < 2, 2, 1)
        third = jnp.where(lax.rem(col, 2) == 0, col + 1, col - 1)
        return jnp.where(j == 0, first, jnp.where(j == 1, second, jnp.where(j == 2, third, col)))

    def slot(s, q):
        return wide.at[q] if whole else wide.at[s, q]

    def own(s):
        return a_ref if whole else a_ref.at[s]

    def to_mate(s):
        return remote(own(s), slot(s, row), m_send.at[s], m_recv.at[s], row=mate)

    def to_across(s):
        return remote(own(s), slot(s, row), x_send.at[s], x_recv.at[s], row=across)

    def pass_on(s):
        return remote(slot(s, across), slot(s, across), f_send.at[s], f_recv.at[s], row=mate)

    def from_mate(s):
        return remote(slot(s, mate), slot(s, mate), m_send.at[s], m_recv.at[s], row=mate)

    def from_across(s):
        return remote(slot(s, across), slot(s, across), x_send.at[s], x_recv.at[s], row=across)

    def from_diag(s):
        return remote(slot(s, diag), slot(s, diag), f_send.at[s], f_recv.at[s], row=mate)

    def keep_wide(s):
        return pltpu.make_async_copy(wide.at[s], wide_out.at[s], local.at[s])

    def move_own(s):
        return pltpu.make_async_copy(own(s), slot(s, row), own_sem.at[s])

    def piece(ref, s, h):
        return ref.at[s, pl.ds(h * half, half)]

    def up(s, h):
        return remote(piece(sent, s, h), piece(from_below, s, h), z_send.at[s, h], z_recv.at[0, s, h], col=col + 1)

    def down(s, h):
        return remote(piece(sent, s, h), piece(from_above, s, h), z_send.at[s, h], z_recv.at[1, s, h], col=col - 1)

    greet(col, mate, across)
    if whole:
        to_across(0).start()
        to_mate(0).start()
        move_own(0).start()
        from_across(0).wait_recv()
        pass_on(0).start()
        from_mate(0).wait_recv()
        move_own(0).wait()
        from_diag(0).wait_recv()
    else:
        for j in range(2):
            to_across(order(j)).start()
        for j in range(4):
            to_mate(order(j)).start()
            move_own(order(j)).start()

    def multiply(left, rows):
        for t in range(product.shape[1] // tile):
            cols = pl.ds(t * tile, tile)
            total = None
            for w_ref, (base, size) in zip(w_refs, parts):
                term = times(left(base, size), w_ref, cols, flipped)
                total = term if total is None else total + term
            product[rows, cols] = total

    def step(j, _):
        s = order(j)
        if whole:
            keep_wide(s).start()
            multiply(lambda base, size: wide[s, :, pl.ds(base, size)], slice(None))
        else:

            @pl.when(j < 2)
            def _():
                to_across(order(j + 2)).start()

            def pair(first):
                def left(base, size):
                    two = wide[s, pl.ds(first, 2), :, pl.ds(base, size)]
                    return two.reshape(2 * two.shape[1], size)

                multiply(left, pl.ds(pl.multiple_of(first * (half // 2), half), half))

            from_mate(s).wait_recv()
            move_own(s).wait()
            pair(chip * 2)
            from_across(s).wait_recv()
            pass_on(s).start()
            from_diag(s).wait_recv()
            pair((1 - chip) * 2)
            keep_wide(s).start()

        for h in range(2):
            span = half

            def add_in(ref, h=h):
                def add(rows):
                    here = pl.ds(pl.multiple_of(h * span + rows.start, rows.size), rows.size)
                    product[here, :] += ref[s, here].astype(F32)

                in_rows(span, 64, add)

            def cast(rows, h=h):
                here = pl.ds(pl.multiple_of(h * span + rows.start, rows.size), rows.size)
                sent[s, here] = product[here, :].astype(BF16)

            @pl.when((s >= col) & (col > 0))
            def _():
                up(s, h).wait_recv()
                add_in(from_below)

            @pl.when((s <= col) & (col < 3))
            def _():
                down(s, h).wait_recv()
                add_in(from_above)

            @pl.when(s > col)
            def _():
                in_rows(span, 64, cast)

                @pl.when(s < 3)
                def _():
                    up(s + 1, h).wait_send()

                up(s, h).start()

            @pl.when(s < col)
            def _():
                in_rows(span, 64, cast)

                @pl.when(s > 0)
                def _():
                    down(s - 1, h).wait_send()

                down(s, h).start()

        return 0

    lax.fori_loop(0, 4, step, 0)
    out_ref[...] = product[...]

    def last(s, _):
        for h in range(2):

            @pl.when(s == col + 1)
            def _():
                up(s, h).wait_send()

            @pl.when(s == col - 1)
            def _():
                down(s, h).wait_send()

        if not whole:
            to_mate(s).wait_send()
            to_across(s).wait_send()
            pass_on(s).wait_send()
        keep_wide(s).wait()
        return 0

    lax.fori_loop(0, 4, last, 0)
    if whole:
        to_mate(0).wait_send()
        to_across(0).wait_send()
        pass_on(0).wait_send()


def rows_cols(name, number, a, weights, flipped, whole, tile=256):
    tokens, wide_size = a.shape
    parts, base = [], 0
    for w in weights:
        size = w.shape[1] if flipped else w.shape[0]
        parts.append((base, size))
        base += size
    feats = weights[0].shape[0] if flipped else weights[0].shape[1]
    if whole:
        slots, lead, given = (4, tokens, base), 1, a
    else:
        slots, lead, given = (4, 4, tokens // 4, base), 4, a.reshape(4, tokens // 4, base)
    chain = pltpu.VMEM((4, tokens, feats), BF16)
    out, wide = pl.pallas_call(
        functools.partial(rows_cols_kernel, whole, tuple(parts), flipped, tile),
        out_shape=(
            jax.ShapeDtypeStruct((tokens, feats), F32),
            jax.ShapeDtypeStruct(slots, BF16),
        ),
        in_specs=[pl.BlockSpec(memory_space=pltpu.VMEM)] * (1 + len(weights)),
        out_specs=(pl.BlockSpec(memory_space=pltpu.VMEM), pl.BlockSpec(memory_space=pl.ANY)),
        scratch_shapes=[
            pltpu.VMEM(slots, BF16),
            pltpu.VMEM((tokens, feats), F32),
            chain,
            chain,
            chain,
            pltpu.SemaphoreType.DMA((4, 2)),
            pltpu.SemaphoreType.DMA((2, 4, 2)),
            pltpu.SemaphoreType.DMA((4,)),
            pltpu.SemaphoreType.DMA((lead,)),
        ]
        + [pltpu.SemaphoreType.DMA((lead,))] * 6,
        compiler_params=pltpu.CompilerParams(
            collective_id=number, has_side_effects=True, vmem_limit_bytes=VMEM_LIMIT
        ),
        cost_estimate=pl.CostEstimate(
            flops=8 * tokens * feats * base, bytes_accessed=8 * tokens * base, transcendentals=0
        ),
        name=name,
    )(given, *weights)
    return out, wide.reshape(4 * tokens, base)


def turn_tables(length):
    rates = THETA ** (-np.arange(HEAD_SIZE // 2) * 2.0 / HEAD_SIZE)
    angles = np.arange(length)[:, None] * rates[None, :]
    cos, sin = np.cos(angles), np.sin(angles)
    return (
        np.concatenate([cos, cos], axis=1).astype(np.float32),
        np.concatenate([-sin, sin], axis=1).astype(np.float32),
    )


def swap_halves(value):
    return pltpu.roll(value, HEAD_SIZE // 2, 1)


def head(ref, index):
    return ref[:, index * HEAD_SIZE : (index + 1) * HEAD_SIZE]


def root_scale(raw):
    return lax.rsqrt(jnp.mean(raw * raw, axis=1, keepdims=True) + EPSILON)


def attend(q_heads, groups, qkv, seg_col, seg_row, cos, sin, q_gain, k_gain, o, qa, ka, va, probs):
    kv = q_heads // groups
    tokens = qkv.shape[0]
    half = tokens // 2

    def turned(index, gain):
        raw = head(qkv, index)
        normed = raw * root_scale(raw) * gain[...]
        return (normed * cos[...] + swap_halves(normed) * sin[...]).astype(BF16)

    for i in range(q_heads):
        qa[:, i * HEAD_SIZE : (i + 1) * HEAD_SIZE] = turned(i, q_gain)
    for i in range(kv):
        ka[:, i * HEAD_SIZE : (i + 1) * HEAD_SIZE] = turned(q_heads + i, k_gain)
        va[:, i * HEAD_SIZE : (i + 1) * HEAD_SIZE] = head(qkv, q_heads + kv + i).astype(BF16)
    for block in range(2):
        rows = slice(block * half, (block + 1) * half)
        keys = (block + 1) * half
        spot = lax.broadcasted_iota(jnp.int32, (half, keys), 0) + block * half
        other = lax.broadcasted_iota(jnp.int32, (half, keys), 1)
        allowed = (other <= spot) & (seg_col[rows, :] == seg_row[:, :keys])
        for i in range(q_heads):
            j = i // groups
            dots = lax.dot_general(
                head(qa, i)[rows], head(ka, j)[:keys], (((1,), (1,)), ((), ())), preferred_element_type=F32
            ) * (1.0 / math.sqrt(HEAD_SIZE))
            scores = jnp.where(allowed, dots, MASKED)
            expo = jnp.exp(scores - jnp.max(scores, axis=1, keepdims=True))
            p = expo / jnp.sum(expo, axis=1, keepdims=True)
            probs[i, rows, :keys] = p.astype(BF16)
            mixed = jnp.dot(p.astype(BF16), head(va, j)[:keys], preferred_element_type=F32)
            o[rows, i * HEAD_SIZE : (i + 1) * HEAD_SIZE] = mixed.astype(BF16)


def front_kernel(q_heads, groups, model_width, *refs):
    refs = list(refs)

    def take(count):
        found = refs[:count]
        del refs[:count]
        return found

    (x_ref, gy, w_query, w_key, w_value, w_out, w_down, seg_col, seg_row, cos, sin, q_gain, k_gain, gain_one, gain_two) = take(15)
    (scale_one, hidden, scale_two, ffn_in, dact, qkv, qa, ka, va, probs) = take(10)
    (xn_out, gy_out, mixed_out) = take(3)
    (xn_wide, gy_wide, mixed_wide, mixed, product, chunk, keep) = take(7)
    total_bufs = take(2)
    second_bufs = take(2)
    moved = take(6)
    moved_q = take(6)
    chain = take(3)
    x_sems, gy_sems = take(2), take(2)
    (local,) = take(1)
    moved_sems, moved_q_sems = take(4), take(4)
    mixed_sems = take(7)
    chain_sems = take(3)
    total_sems, second_sems = take(2), take(2)

    at = Ends()
    tokens, feats = x_ref.shape
    first_total = RowTotal(at, *total_bufs, *total_sems)
    second_total = RowTotal(at, *second_bufs, *second_sems)
    x_gather = ColGather(at, xn_wide, *x_sems)
    gy_gather = ColGather(at, gy_wide, *gy_sems)
    row_sum = RowSumWhole(at, product, qkv, *moved, *moved_sems)
    quarter_sum = RowSumQuarter(at, chunk, keep, *moved_q, *moved_q_sems)
    mixes = RowGather(at, lambda s: mixed, lambda s, q: mixed_wide.at[q], mixed_sems)
    out_sum = ColSum(at, hidden, *chain, *chain_sems)

    gy_wide[at.col] = gy[...]
    at.greet()
    stream = x_ref[...].astype(F32)
    first_total.start(jnp.sum(stream * stream, axis=1, keepdims=True))
    scale = lax.rsqrt(first_total.finish() / model_width + EPSILON)
    scale_one[...] = scale
    xn_wide[at.col] = (x_ref[...].astype(F32) * scale * gain_one[...]).astype(BF16)

    def project(s):
        base = 0
        for w in (w_query, w_key, w_value):
            size = w.shape[1]
            product[:, base : base + size] = jnp.dot(xn_wide[s], w[...], preferred_element_type=F32)
            base += size
        row_sum.give(s)

    def back_down(s):
        size = chunk.shape[1]

        def one(j, _):
            cols = pl.ds(pl.multiple_of(j * size, size), size)
            value = lax.dot_general(
                gy_wide[s], w_down[cols, :], (((1,), (1,)), ((), ())), preferred_element_type=F32
            )
            quarter_sum.split(s, value, cols, dact)
            return 0

        lax.fori_loop(0, w_down.shape[0] // size, one, 0)
        quarter_sum.give(s)

    def end_down(s):
        quarter_sum.finish(s)

        def add(here):
            dact[s, here] += moved_q[3][s, here].astype(F32) + moved_q[5][s, here].astype(F32)

        in_rows(128, 16, add)

    def send_gy(dist):
        @pl.when((at.col == dist) & (at.col < 3))
        def _():
            gy_gather.up(at.col).start()

        @pl.when((at.col == 3 - dist) & (at.col > 0))
        def _():
            gy_gather.down(at.col).start()

    def out_step(j):
        s = near_first(at, j)
        hidden[...] = jnp.dot(mixed_wide[s], w_out[...], preferred_element_type=F32)
        out_sum.step(s)

    mid = jnp.logical_not(at.end)
    x_gather.arrive(0)
    send_gy(0)
    x_gather.loop(0, project)
    back_down(at.col)
    for dist in range(1, 4):
        x_gather.arrive(dist)
        send_gy(dist)
        x_gather.loop(dist, project)

    @pl.when(mid)
    def _():
        gy_gather.arrive(1)

    row_sum.finish()
    attend(q_heads, groups, qkv, seg_col, seg_row, cos, sin, q_gain, k_gain, mixed, qa, ka, va, probs)
    mixes.to_across(0).start()
    mixes.near(0)

    @pl.when(mid)
    def _():
        gy_gather.arrive(2)

    mixes.wait_near(0)

    @pl.when(at.end)
    def _():
        out_step(0)
        gy_gather.arrive(1)

    gy_gather.loop(1, back_down)
    mixes.take_across(0)
    mixes.wait_diag(0)

    @pl.when(at.end)
    def _():
        out_step(1)
        out_step(2)
        gy_gather.arrive(2)

    @pl.when(mid)
    def _():
        out_step(0)

    gy_gather.loop(2, back_down)

    @pl.when(mid)
    def _():
        out_step(1)
        out_step(2)

    @pl.when(at.end)
    def _():
        gy_gather.arrive(3)

    gy_gather.loop(3, back_down)
    wides = [
        pltpu.make_async_copy(src, dst, local.at[i])
        for i, (src, dst) in enumerate(((xn_wide, xn_out), (gy_wide, gy_out), (mixed_wide, mixed_out)))
    ]
    for copy in wides:
        copy.start()
    for dist in range(3):
        gy_gather.loop(dist, end_down)
    out_step(3)

    def residual(here):
        hidden[here, :] += x_ref[here, :].astype(F32)

    in_rows(tokens, 64, residual)
    value = hidden[...]
    second_total.start(jnp.sum(value * value, axis=1, keepdims=True))
    gy_gather.loop(3, end_down)
    scale = lax.rsqrt(second_total.finish() / model_width + EPSILON)
    scale_two[...] = scale
    ffn_in[...] = (hidden[...] * scale * gain_two[...]).astype(BF16)

    x_gather.close()
    gy_gather.close()
    row_sum.close()
    quarter_sum.close()
    mixes.close(1)
    out_sum.close()
    for copy in wides:
        copy.wait()


def chain_scratch(tokens, feats):
    return [
        pltpu.VMEM((4, tokens, feats), BF16), pltpu.VMEM((4, tokens, feats), BF16), pltpu.VMEM((tokens, feats), BF16),
    ]


def chain_sems():
    dma = pltpu.SemaphoreType.DMA
    return [dma((4, 2)), dma((4, 2)), dma((2,))]


def front(q_heads, groups, model_width, number, x, gy, weights, segments, tables, gains):
    tokens, feats = x.shape
    w_query, w_key, w_value, w_out, w_down = weights
    width = w_query.shape[1] + w_key.shape[1] + w_value.shape[1]
    q_width, k_width, ff = w_query.shape[1], w_key.shape[1], w_down.shape[0]
    dma = pltpu.SemaphoreType.DMA
    any_spec, vmem = pl.BlockSpec(memory_space=pl.ANY), pl.BlockSpec(memory_space=pltpu.VMEM)
    shape = jax.ShapeDtypeStruct
    wide = pltpu.VMEM((4, tokens, feats), BF16)
    return pl.pallas_call(
        functools.partial(front_kernel, q_heads, groups, model_width),
        out_shape=(
            shape((tokens, 1), F32),
            shape((tokens, feats), F32),
            shape((tokens, 1), F32),
            shape((tokens, feats), BF16),
            shape((4, tokens // 4, ff), F32),
            shape((tokens, width), F32),
            shape((tokens, q_width), BF16),
            shape((tokens, k_width), BF16),
            shape((tokens, k_width), BF16),
            shape((q_heads, tokens, tokens), BF16),
            shape((4, tokens, feats), BF16),
            shape((4, tokens, feats), BF16),
            shape((4, tokens, q_width), BF16),
        ),
        in_specs=[vmem] * 15,
        out_specs=tuple([vmem] * 10 + [any_spec] * 3),
        scratch_shapes=[
            wide,
            wide,
            pltpu.VMEM((4, tokens, q_width), BF16),
            pltpu.VMEM((tokens, q_width), BF16),
            pltpu.VMEM((tokens, width), F32),
            pltpu.VMEM((tokens, 512), F32),
            pltpu.VMEM((tokens // 4, ff), F32),
        ]
        + row_total_scratch(tokens) * 2
        + [pltpu.VMEM((tokens, width), BF16)] * 6
        + [pltpu.VMEM((4, tokens // 4, ff), BF16)] * 6
        + chain_scratch(tokens, feats)
        + [dma((2, 4)), dma((4,))] * 2
        + [dma((3,))]
        + [dma((2,)), dma((2,)), dma((1,)), dma((1,))]
        + [dma((2, 4)), dma((2, 4)), dma((4,)), dma((4,))]
        + [dma((1,))] * 7
        + chain_sems()
        + row_total_sems() * 2,
        compiler_params=pltpu.CompilerParams(
            collective_id=number, has_side_effects=True, vmem_limit_bytes=VMEM_LIMIT
        ),
        name="front",
    )(x, gy, *weights, *segments, *tables, *gains)


def across_rows(left, right):
    return lax.dot_general(left, right, (((0,), (0,)), ((), ())), preferred_element_type=F32)


def attend_back(q_heads, groups, grad, qkv, qa, ka, va, probs, cos, sin, q_gain, k_gain, out, q_part, k_part, dq, dk, dv):
    kv = q_heads // groups
    tokens = qkv.shape[0]
    half = tokens // 2
    scale = 1.0 / math.sqrt(HEAD_SIZE)
    dk[...] = jnp.zeros_like(dk)
    dv[...] = jnp.zeros_like(dv)
    for block in range(2):
        rows = slice(block * half, (block + 1) * half)
        keys = (block + 1) * half
        for i in range(q_heads):
            j = i // groups
            spot = slice(j * HEAD_SIZE, (j + 1) * HEAD_SIZE)
            pb = probs[i, rows, :keys]
            p = pb.astype(F32)
            g = head(grad, i)[rows].astype(BF16)
            dv[:keys, spot] += across_rows(pb.astype(BF16), g)
            dp = lax.dot_general(
                g, head(va, j)[:keys], (((1,), (1,)), ((), ())), preferred_element_type=F32
            )
            ds = (p * (dp - jnp.sum(p * dp, axis=1, keepdims=True))).astype(BF16)
            dq[rows, i * HEAD_SIZE : (i + 1) * HEAD_SIZE] = (
                jnp.dot(ds, head(ka, j)[:keys], preferred_element_type=F32) * scale
            )
            dk[:keys, spot] += across_rows(ds, head(qa, i)[rows]) * scale

    def back(turned, index, gain):
        raw = head(qkv, index)
        scales = root_scale(raw)
        normed = turned * cos[...] - swap_halves(turned) * sin[...]
        part = jnp.sum(normed * raw * scales, axis=0, keepdims=True)
        weighted = normed * gain[...]
        inner = jnp.sum(weighted * raw, axis=1, keepdims=True)
        result = scales * weighted - raw * (scales * scales * scales) * inner * (1.0 / HEAD_SIZE)
        out[:, index * HEAD_SIZE : (index + 1) * HEAD_SIZE] = result.astype(BF16)
        return part

    q_part[...] = sum(back(head(dq, i), i, q_gain) for i in range(q_heads))
    k_part[...] = sum(back(head(dk, i), q_heads + i, k_gain) for i in range(kv))
    for i in range(kv):
        spot = (q_heads + kv + i) * HEAD_SIZE
        out[:, spot : spot + HEAD_SIZE] = head(dv, i).astype(BF16)


def tail_kernel(pairs, q_heads, groups, *refs):
    refs = list(refs)

    def take(count):
        found = refs[:count]
        del refs[:count]
        return found

    (act, w_out, w_down, w_query, w_key, w_value, qkv, qa, ka, va, probs, cos, sin, q_gain, k_gain) = take(15)
    (dhn, hidden, scale_two, gain_two, gy, x_ref, scale_one, gain_one) = take(8)
    (gy_wide, mixed_wide, normed_wide, gate_n, up_n) = take(5)
    (in_grad, layer_out, one_grad, two_grad, q_grad, k_grad, down_n, out_n, qkv_n) = take(9)
    others = take(5) if pairs == 2 else []
    (da_wide, act_wide, dqkv, dqkv_wide, held, product, grad_mixed, dq, dk, dv, n_down, n_out, n_qkv) = take(13)
    (dh, q_part, k_part, packet, packet_got, by_row, summed, summed_got) = take(8)
    first_bufs, last_bufs = take(2), take(2)
    moved = take(6)
    down_bufs, dxn_bufs = take(3), take(3)
    (g_send, g_recv, local, y_send, y_recv) = take(5)
    moved_sems = take(4)
    act_sems, dqkv_sems = take(7), take(7)
    down_sems, dxn_sems = take(3), take(3)
    first_sems, last_sems = take(2), take(2)
    (p_send, p_recv, r_send, r_recv, s_send, s_recv) = take(6)

    at = Ends()
    model_width = 4 * dhn.shape[1]
    first_total = RowTotal(at, *first_bufs, *first_sems)
    last_total = RowTotal(at, *last_bufs, *last_sems)
    at.greet(pairs, True)

    def pair_copy(src, index):
        return remote(src, others[index], y_send.at[index], y_recv.at[index], dp=1 - lax.axis_index("dp"))

    narrow = (gate_n, up_n, n_down, n_out, n_qkv)

    def to_pair(index):
        if pairs == 2:
            pair_copy(narrow[index], index).start()

    def load(index, src):
        return pltpu.make_async_copy(src, held, local.at[index])

    def keep(index, src, dst):
        return pltpu.make_async_copy(src, dst, local.at[3 + index])

    to_pair(0)
    to_pair(1)
    load(0, gy_wide).start()
    gather = ColGather(at, da_wide, g_send, g_recv)
    row_sum = RowSumWhole(at, product, grad_mixed, *moved, *moved_sems)
    acts = RowGather(at, lambda s: act.at[s], lambda s, q: act_wide.at[s, q], act_sems)
    grads = RowGather(at, lambda s: dqkv, lambda s, q: dqkv_wide.at[q], dqkv_sems)
    down_sum = ColSum(at, product, *down_bufs, *down_sems)
    dxn_sum = ColSum(at, product, *dxn_bufs, *dxn_sems)

    weighted = dhn[...] * gain_two[...]
    first_total.start(jnp.sum(weighted * hidden[...], axis=1, keepdims=True))
    for j in range(2):
        acts.to_across(far_first(at.col, j)).start()
    for j in range(4):
        acts.near(far_first(at.col, j))
    scale = scale_two[...]
    packet[...] = jnp.zeros_like(packet)
    packet[1:2, :] = jnp.sum(dhn[...] * hidden[...] * scale, axis=0, keepdims=True)
    inner = first_total.finish()
    dh[...] = (
        gy[...].astype(F32)
        + scale * (dhn[...] * gain_two[...])
        - hidden[...] * (scale * scale * scale * inner * (1.0 / model_width))
    )
    da_wide[at.col] = dh[...].astype(BF16)
    gather.arrive(0)

    def back_out(s):
        product[...] = lax.dot_general(
            da_wide[s], w_out[...], (((1,), (1,)), ((), ())), preferred_element_type=F32
        )
        row_sum.give(s)

    def take_act(j):
        s = far_first(at.col, j)
        if j < 2:
            acts.to_across(far_first(at.col, j + 2)).start()
        acts.wait_near(s)
        acts.take_across(s)
        acts.wait_diag(s)

    def act_rows(s, cols):
        return act_wide[s, :, :, cols].reshape(product.shape[0], cols.size)

    def down_step(j):
        s = far_first(at.col, j)
        product[...] = jnp.dot(
            act_rows(s, pl.ds(0, act.shape[2])), w_down[...], preferred_element_type=F32
        )
        down_sum.step(s)

    def dxn_step(j):
        s = near_first(at, j)
        total, base = None, 0
        for w in (w_query, w_key, w_value):
            size = w.shape[1]
            term = lax.dot_general(
                dqkv_wide[s, :, pl.ds(base, size)], w[...], (((1,), (1,)), ((), ())), preferred_element_type=F32
            )
            total = term if total is None else total + term
            base += size
        product[...] = total
        dxn_sum.step(s)

    def weight_grad(out, left, right):
        def block(here):
            total = None
            for s in range(4):
                term = across_rows(left(s, here), right(s))
                total = term if total is None else total + term
            out[here, :] = total.astype(BF16)

        in_rows(out.shape[0], 256, block)

    gather.loop(0, back_out)
    take_act(0)
    gather.arrive(1)
    gather.loop(1, back_out)
    down_step(0)
    gather.arrive(2)
    gather.loop(2, back_out)
    take_act(1)
    down_step(1)
    gather.arrive(3)
    gather.loop(3, back_out)

    @pl.when(at.end)
    def _():
        take_act(2)
        down_step(2)

    row_sum.finish()
    attend_back(
        q_heads, groups, grad_mixed, qkv, qa, ka, va, probs, cos, sin, q_gain, k_gain,
        dqkv, q_part, k_part, dq, dk, dv,
    )
    grads.to_across(0).start()
    grads.near(0)
    grads.wait_near(0)

    @pl.when(at.end)
    def _():
        dxn_step(0)

    @pl.when(jnp.logical_not(at.end))
    def _():
        take_act(2)
        down_step(2)

    take_act(3)
    load(0, gy_wide).wait()
    weight_grad(n_down, act_rows, lambda s: held[s])
    to_pair(2)
    keep(0, n_down, down_n).start()
    load(1, mixed_wide).start()

    @pl.when(jnp.logical_not(at.end))
    def _():
        dxn_step(0)

    load(1, mixed_wide).wait()
    weight_grad(n_out, lambda s, here: held[s, :, here], lambda s: da_wide[s])
    to_pair(3)
    keep(1, n_out, out_n).start()
    load(2, normed_wide).start()
    grads.take_across(0)
    grads.wait_diag(0)

    @pl.when(at.end)
    def _():
        dxn_step(1)
        dxn_step(2)

    load(2, normed_wide).wait()
    weight_grad(n_qkv, lambda s, here: held[s, :, here], lambda s: dqkv_wide[s])
    to_pair(4)
    keep(2, n_qkv, qkv_n).start()

    @pl.when(jnp.logical_not(at.end))
    def _():
        dxn_step(1)
        dxn_step(2)

    down_step(3)
    layer_out[...] = (hidden[...] + product[...]).astype(BF16)
    dxn_step(3)
    scale = scale_one[...]
    last_total.start(
        jnp.sum(product[...] * gain_one[...] * x_ref[...].astype(F32), axis=1, keepdims=True)
    )
    packet[0:1, :] = jnp.sum(product[...] * x_ref[...].astype(F32) * scale, axis=0, keepdims=True)
    packet[2:3, :HEAD_SIZE] = q_part[...]
    packet[2:3, HEAD_SIZE : 2 * HEAD_SIZE] = k_part[...]

    def to_line(step):
        return remote(
            packet, packet_got.at[step - 1], p_send.at[step - 1], p_recv.at[step - 1],
            col=lax.rem(at.col + step, 4),
        )

    def to_row(index, peer):
        return remote(by_row.at[at.row], by_row.at[at.row], r_send.at[index], r_recv.at[index], row=peer)

    def from_row(index, peer):
        return remote(by_row.at[peer], by_row.at[peer], r_send.at[index], r_recv.at[index], row=peer)

    def to_peer(step):
        return remote(
            summed, summed_got.at[step - 1], s_send.at[step - 1], s_recv.at[step - 1], dp=at.pair(pairs, step)
        )

    for step in range(1, 4):
        to_line(step).start()
    inner = last_total.finish()
    in_grad[...] = (
        dh[...]
        + scale * (product[...] * gain_one[...])
        - x_ref[...].astype(F32) * (scale * scale * scale * inner * (1.0 / model_width))
    )
    for step in range(1, 4):
        to_line(step).wait()
    by_row[at.row] = (packet[...] + packet_got[0]) + (packet_got[1] + packet_got[2])
    peers = (at.mate, at.across, at.diag)
    for index, peer in enumerate(peers):
        to_row(index, peer).start()
    for index, peer in enumerate(peers):
        from_row(index, peer).wait_recv()
        to_row(index, peer).wait_send()
    summed[...] = jnp.zeros_like(summed)
    for r in range(4):
        summed[r : r + 1, :] = by_row[r, 0:1, :]
        summed[4 + r : 5 + r, :] = by_row[r, 1:2, :]
    summed[8:9, :] = (by_row[0, 2:3, :] + by_row[1, 2:3, :]) + (by_row[2, 2:3, :] + by_row[3, 2:3, :])
    for step in range(1, pairs):
        to_peer(step).start()
    for step in range(1, pairs):
        to_peer(step).wait()
    total = summed[...]
    for step in range(1, pairs):
        total = total + summed_got[step - 1]
    one_grad[...] = total[0:4, :]
    two_grad[...] = total[4:8, :]
    q_grad[...] = total[8:9, :HEAD_SIZE]
    k_grad[...] = total[8:9, HEAD_SIZE : 2 * HEAD_SIZE]

    gather.close()
    row_sum.close()
    acts.close(4)
    grads.close(1)
    down_sum.close()
    dxn_sum.close()
    keep(0, n_down, down_n).wait()
    keep(1, n_out, out_n).wait()
    keep(2, n_qkv, qkv_n).wait()
    if pairs == 2:
        for index in range(5):
            pair_copy(narrow[index], index).wait()


def tail(pairs, q_heads, groups, number, act, weights, saved, tables, norms, wides, narrow):
    tokens, feats = norms[0].shape
    w_out, w_down = weights[:2]
    ff = w_down.shape[0]
    width = saved[0].shape[1]
    q_width, k_width = saved[1].shape[1], saved[2].shape[1]
    dma = pltpu.SemaphoreType.DMA
    any_spec, vmem = pl.BlockSpec(memory_space=pl.ANY), pl.BlockSpec(memory_space=pltpu.VMEM)
    shape = jax.ShapeDtypeStruct
    shapes = [
        shape((tokens, feats), F32),
        shape((tokens, feats), BF16),
        shape((4, feats), F32),
        shape((4, feats), F32),
        shape((1, HEAD_SIZE), F32),
        shape((1, HEAD_SIZE), F32),
    ]
    own = [shape((ff, feats), BF16), shape((q_width, feats), BF16), shape((feats, width), BF16)]
    others = [shape(n.shape, BF16) for n in narrow] + own if pairs == 2 else []
    packet = pltpu.VMEM((8, feats), F32)
    operands = (act, *weights, *saved, *tables, *norms)
    out = pl.pallas_call(
        functools.partial(tail_kernel, pairs, q_heads, groups),
        out_shape=tuple(shapes + own + others),
        in_specs=[vmem] * len(operands) + [any_spec] * 5,
        out_specs=tuple([vmem] * 6 + [any_spec] * (3 + len(others))),
        scratch_shapes=[
            pltpu.VMEM((4, tokens, feats), BF16),
            pltpu.VMEM((4, 4, tokens // 4, ff), BF16),
            pltpu.VMEM((tokens, width), BF16),
            pltpu.VMEM((4, tokens, width), BF16),
            pltpu.VMEM((4, tokens, feats), BF16),
            pltpu.VMEM((tokens, feats), F32),
            pltpu.VMEM((tokens, q_width), F32),
            pltpu.VMEM((tokens, q_width), F32),
            pltpu.VMEM((tokens, k_width), F32),
            pltpu.VMEM((tokens, k_width), F32),
            pltpu.VMEM((ff, feats), BF16),
            pltpu.VMEM((q_width, feats), BF16),
            pltpu.VMEM((feats, width), BF16),
            pltpu.VMEM((tokens, feats), F32),
            pltpu.VMEM((1, HEAD_SIZE), F32),
            pltpu.VMEM((1, HEAD_SIZE), F32),
            packet,
            pltpu.VMEM((3, 8, feats), F32),
            pltpu.VMEM((4, 8, feats), F32),
            pltpu.VMEM((16, feats), F32),
            pltpu.VMEM((max(pairs - 1, 1), 16, feats), F32),
        ]
        + row_total_scratch(tokens) * 2
        + [pltpu.VMEM((tokens, q_width), BF16)] * 6
        + chain_scratch(tokens, feats) * 2
        + [dma((2, 4)), dma((4,)), dma((6,)), dma((5,)), dma((5,))]
        + [dma((2,)), dma((2,)), dma((1,)), dma((1,))]
        + [dma((4,))] * 7
        + [dma((1,))] * 7
        + chain_sems() * 2
        + row_total_sems() * 2
        + [dma((3,))] * 4
        + [dma((max(pairs - 1, 1),))] * 2,
        compiler_params=pltpu.CompilerParams(
            collective_id=number, has_side_effects=True, vmem_limit_bytes=VMEM_LIMIT
        ),
        name="tail",
    )(*operands, *wides, *narrow)
    return out[:6], out[6:9], out[9:]


def outer(left_op, right_op):
    return lax.dot_general(left_op, right_op, (((0,), (0,)), ((), ())), preferred_element_type=F32)


def shards(
    pairs,
    hidden_in,
    segment_ids,
    attn_gain,
    w_query,
    key_projection,
    value_projection,
    query_gain,
    key_norm_gain,
    w_out,
    ffn_gain,
    w_gate,
    w_up,
    w_down,
    out_grad,
):
    tokens, slice_width = hidden_in.shape
    model_width = attn_gain.shape[0]
    offset = lax.axis_index("row") * slice_width
    gain_one = lax.dynamic_slice_in_dim(attn_gain, offset, slice_width)
    gain_two = lax.dynamic_slice_in_dim(ffn_gain, offset, slice_width)
    q_width = w_query.shape[1]
    k_width = key_projection.shape[1]
    q_heads = q_width // HEAD_SIZE
    groups = q_width // k_width
    ff = w_gate.shape[1]

    def narrow_outer(left_op, right_op):
        return outer(left_op, right_op).astype(BF16)

    tables = (*turn_tables(tokens), query_gain[None, :], key_norm_gain[None, :])
    (scale_one, hidden, scale_two, ffn_in, grad_inner, qkv, q_turned, k_turned, values, probs, xn_wide, gy_wide, mixed_wide) = front(
        q_heads, groups, model_width, 0, hidden_in, out_grad,
        (w_query, key_projection, value_projection, w_out, w_down),
        (segment_ids[:, None], segment_ids[None, :]),
        tables,
        (gain_one[None, :], gain_two[None, :]),
    )
    gate_up, ffn_wide = cols_rows("gate_up", 1, ffn_in, [w_gate, w_up], False, False, 512)
    gate_pre, upward = gate_up[:, :ff], gate_up[:, ff:]
    grad_inner = grad_inner.reshape(tokens, ff)
    sigmoid_gate = jax.nn.sigmoid(gate_pre)
    activated = gate_pre * sigmoid_gate
    inner_act = (activated * upward).astype(BF16)
    grad_gate = grad_inner * upward * (sigmoid_gate * (1.0 + gate_pre * (1.0 - sigmoid_gate)))
    grad_up = grad_inner * activated
    grad_ffn = jnp.concatenate([grad_gate, grad_up], axis=1).astype(BF16)
    grad_ffn_in, ffn_grad_wide = rows_cols("ffn_back", 2, grad_ffn, [w_gate, w_up], True, False)
    gate_n = narrow_outer(ffn_wide, ffn_grad_wide[:, :ff])
    up_n = narrow_outer(ffn_wide, ffn_grad_wide[:, ff:])
    (in_grad, layer_out, one_grad, two_grad, q_gain_grad, k_gain_grad), own, others = tail(
        pairs, q_heads, groups, 3, inner_act.reshape(4, tokens // 4, ff),
        (w_out, w_down, w_query, key_projection, value_projection),
        (qkv, q_turned, k_turned, values, probs),
        tables,
        (grad_ffn_in, hidden, scale_two, gain_two[None, :], out_grad, hidden_in, scale_one, gain_one[None, :]),
        (gy_wide, mixed_wide, xn_wide),
        (gate_n, up_n),
    )
    parts = (gate_n, up_n, *own)
    if pairs == 2:
        sums = [a.astype(F32) + b.astype(F32) for a, b in zip(parts, others)]
    else:
        sums = lax.psum(tuple(part.astype(F32) for part in parts), "dp")
    gate_grad, up_grad, down_grad, out_weight_grad, qkv_grad = sums
    return (
        layer_out,
        in_grad,
        one_grad.reshape(-1),
        qkv_grad[:, :q_width],
        qkv_grad[:, q_width : q_width + k_width],
        qkv_grad[:, q_width + k_width :],
        q_gain_grad.reshape(-1),
        k_gain_grad.reshape(-1),
        out_weight_grad,
        two_grad.reshape(-1),
        gate_grad,
        up_grad,
        down_grad,
    )


def solution(mesh):
    acts, grid, flip, none = P(("dp", "col"), "row"), P("row", "col"), P("col", "row"), P()
    return jax.shard_map(
        functools.partial(shards, mesh.shape["dp"]),
        mesh=mesh,
        in_specs=(
            acts, P(("dp", "row")), none, grid, grid, grid, none, none, flip, none, grid, grid, flip, acts,
        ),
        out_specs=(
            acts, acts, none, grid, grid, grid, none, none, flip, none, grid, grid, flip,
        ),
        check_vma=False,
    )
```

```python
import functools
import math

import jax
import jax.numpy as jnp
import numpy as np
from jax import lax
from jax.experimental import pallas as pl
from jax.experimental.pallas import tpu as pltpu
from jax.sharding import PartitionSpec as P

HEAD_SIZE = 128
EPSILON = 1e-06
THETA = 1000000.0
MASKED = -1e30
MESH = pl.DeviceIdType.MESH
BF16 = jnp.bfloat16
F32 = jnp.float32
VMEM_LIMIT = 60 << 20


def to(**where):
    return dict(device_id=where, device_id_type=MESH)


class Ends:
    def __init__(self):
        self.row = lax.axis_index("row")
        self.col = lax.axis_index("col")
        self.chip = lax.div(self.row, 2)
        self.core = lax.rem(self.row, 2)
        self.mate = self.chip * 2 + (1 - self.core)
        self.across = (1 - self.chip) * 2 + self.core
        self.diag = (1 - self.chip) * 2 + (1 - self.core)
        self.end = (self.col == 0) | (self.col == 3)

    def greet(self, pairs=0, line=False):
        gate = pltpu.get_barrier_semaphore()
        count = 3
        for peer in (self.mate, self.across, self.diag):
            pl.semaphore_signal(gate, inc=1, **to(row=peer))
        for step in range(1, pairs):
            pl.semaphore_signal(gate, inc=1, **to(dp=self.pair(pairs, step)))
            count += 1
        if line:
            for step in range(1, 4):
                pl.semaphore_signal(gate, inc=1, **to(col=lax.rem(self.col + step, 4)))
                count += 1
        else:

            @pl.when(self.col > 0)
            def _():
                pl.semaphore_signal(gate, inc=1, **to(col=self.col - 1))

            @pl.when(self.col < 3)
            def _():
                pl.semaphore_signal(gate, inc=1, **to(col=self.col + 1))

            count += jnp.where(self.col > 0, 1, 0) + jnp.where(self.col < 3, 1, 0)
        pl.semaphore_wait(gate, count)

    def pair(self, pairs, step):
        return lax.rem(lax.axis_index("dp") + step, pairs)


class RowTotal:
    def __init__(self, at, own, got, sends, recvs):
        self.own, self.got = own, got
        self.copies = [
            remote(own, got.at[i], sends.at[i], recvs.at[i], row=peer)
            for i, peer in enumerate((at.mate, at.across, at.diag))
        ]

    def start(self, column):
        self.own[...] = jnp.broadcast_to(column, (column.shape[0], 128)).T[:8, :]
        for copy in self.copies:
            copy.start()

    def finish(self):
        for copy in self.copies:
            copy.wait()
        total = (self.own[...] + self.got[0]) + (self.got[1] + self.got[2])
        return jnp.concatenate([total] * 16, axis=0).T[:, :1]


def row_total_scratch(tokens):
    return [pltpu.VMEM((8, tokens), F32), pltpu.VMEM((3, 8, tokens), F32)]


def row_total_sems():
    return [pltpu.SemaphoreType.DMA((3,)), pltpu.SemaphoreType.DMA((3,))]


def remote(src, dst, sends, recvs, **where):
    return pltpu.make_async_remote_copy(
        src_ref=src, dst_ref=dst, send_sem=sends, recv_sem=recvs, **to(**where)
    )


def in_rows(count, step, body, first=0):
    def one(i, _):
        body(pl.ds(pl.multiple_of(first + i * step, step), step))
        return 0

    lax.fori_loop(0, count // step, one, 0)


class ColGather:
    def __init__(self, at, wide, sends, recvs):
        self.at, self.wide, self.sends, self.recvs = at, wide, sends, recvs
        self.half = wide.shape[1] // 2

    def copy(self, s, h, side, col):
        part = self.wide.at[s, pl.ds(h * self.half, self.half)]
        return remote(part, part, self.sends.at[side, s, h], self.recvs.at[s, h], col=col)

    def up(self, s, h):
        return self.copy(s, h, 0, self.at.col + 1)

    def down(self, s, h):
        return self.copy(s, h, 1, self.at.col - 1)

    def loop(self, dist, body):
        if dist == 0:
            body(self.at.col)
            return

        def one(side, _):
            s = jnp.where(side == 0, self.at.col - dist, self.at.col + dist)
            pl.when((s >= 0) & (s <= 3))(lambda: body(s))
            return 0

        lax.fori_loop(0, 2, one, 0)

    def arrive(self, dist):
        for h in range(2):

            def take(s, h=h):
                if dist:
                    self.up(s, h).wait_recv()

                @pl.when((s <= self.at.col) & (self.at.col < 3))
                def _():
                    self.up(s, h).start()

                @pl.when((s >= self.at.col) & (self.at.col > 0))
                def _():
                    self.down(s, h).start()

            self.loop(dist, take)

    def send_up(self):
        for h in range(2):
            self.up(self.at.col, h).start()

    def send_down(self):
        for h in range(2):
            self.down(self.at.col, h).start()

    def close(self):
        def one(s, _):
            for h in range(2):

                @pl.when((s <= self.at.col) & (self.at.col < 3))
                def _():
                    self.up(s, h).wait_send()

                @pl.when((s >= self.at.col) & (self.at.col > 0))
                def _():
                    self.down(s, h).wait_send()

            return 0

        lax.fori_loop(0, 4, one, 0)


class RowSumWhole:
    def __init__(self, at, product, out, a_send, a_recv, c_recv, d_send, d_recv, m_send, m_recv, x_send, x_recv):
        self.at, self.product, self.out = at, product, out
        self.a_send, self.a_recv, self.c_recv, self.d_send, self.d_recv = a_send, a_recv, c_recv, d_send, d_recv
        self.m_send, self.m_recv, self.x_send, self.x_recv = m_send, m_recv, x_send, x_recv
        self.half = product.shape[0] // 2
        self.d = remote(d_send, d_recv, m_send.at[2], m_recv.at[2], row=at.mate)

    def a(self, i):
        return remote(self.a_send.at[i], self.a_recv.at[i], self.m_send.at[i], self.m_recv.at[i], row=self.at.mate)

    def b(self, i, s):
        core = self.at.core
        return remote(self.a_recv.at[i], self.c_recv.at[core], self.x_send.at[i], self.x_recv.at[core], row=s)

    def part(self, core, here):
        return pl.ds(pl.multiple_of(core * self.half + here.start, here.size), here.size)

    def give(self, s):
        at, product, half = self.at, self.product, self.half
        i = lax.rem(s, 2)
        ours = lax.div(s, 2) == at.chip

        @pl.when(jnp.logical_not(ours))
        def _():
            def cast(here):
                self.a_send[i, here] = product[self.part(1 - at.core, here), :].astype(BF16)

            in_rows(half, 64, cast)
            self.a(i).start()
            self.a(i).wait_recv()

            def add(here):
                total = product[self.part(at.core, here), :] + self.a_recv[i, here].astype(F32)
                self.a_recv[i, here] = total.astype(BF16)

            in_rows(half, 64, add)
            self.b(i, s).start()

        @pl.when(ours & (i != at.core))
        def _():
            def cast(here):
                self.d_send[here] = product[here, :].astype(BF16)

            in_rows(2 * half, 64, cast)
            self.d.start()

        @pl.when(s == at.row)
        def _():
            def store(here):
                self.out[here] = product[here, :]

            in_rows(2 * half, 64, store)

    def finish(self):
        self.d.wait_recv()
        for h in range(2):
            here = self.c_recv.at[h]
            remote(here, here, self.x_send.at[h], self.x_recv.at[h], row=self.at.across).wait_recv()

            def add(rows, h=h):
                spot = pl.ds(pl.multiple_of(h * self.half + rows.start, rows.size), rows.size)
                self.out[spot] += self.d_recv[spot].astype(F32) + self.c_recv[h, rows].astype(F32)

            in_rows(self.half, 64, add)

    def close(self):
        self.d.wait_send()
        for i in range(2):
            self.a(i).wait_send()
            self.b(i, self.at.across).wait_send()


def row_sum_scratch(tokens, width):
    half = pltpu.VMEM((2, tokens // 2, width), BF16)
    full = pltpu.VMEM((tokens, width), BF16)
    return [half, half, half, full, full]


def row_sum_sems():
    dma = pltpu.SemaphoreType.DMA
    return [dma((3,)), dma((3,)), dma((2,)), dma((2,))]


class RowSumQuarter:
    def __init__(self, at, chunk, keep, a_send, a_recv, c_recv, d_send, d_recv, m_send, m_recv, x_send, x_recv):
        self.at, self.chunk, self.keep = at, chunk, keep
        self.a_send, self.a_recv, self.c_recv = a_send, a_recv, c_recv
        self.d_send, self.d_recv = d_send, d_recv
        self.sems = (m_send, m_recv, x_send, x_recv)

    def a(self, s):
        m_send, m_recv, _, _ = self.sems
        return remote(self.a_send.at[s], self.a_recv.at[s], m_send.at[0, s], m_recv.at[0, s], row=self.at.mate)

    def d(self, s):
        m_send, m_recv, _, _ = self.sems
        return remote(self.d_send.at[s], self.d_recv.at[s], m_send.at[1, s], m_recv.at[1, s], row=self.at.mate)

    def b(self, s):
        _, _, x_send, x_recv = self.sems
        return remote(self.a_recv.at[s], self.c_recv.at[s], x_send.at[s], x_recv.at[s], row=self.at.across)

    def split(self, s, value, spot, own):
        at, chunk = self.at, self.chunk
        chunk[...] = value

        def quarter(q):
            return chunk[pl.ds(pl.multiple_of(q * 128, 128), 128), :]

        self.a_send[s, :, spot] = quarter(at.diag).astype(BF16)
        self.keep[:, spot] = quarter(at.across)
        self.d_send[s, :, spot] = quarter(at.mate).astype(BF16)
        own[s, :, spot] = quarter(at.row).astype(own.dtype)

    def give(self, s):
        self.a(s).start()
        self.d(s).start()
        self.a(s).wait_recv()

        def one(here):
            self.a_recv[s, here] = (self.keep[here, :] + self.a_recv[s, here].astype(F32)).astype(BF16)

        in_rows(128, 16, one)
        self.b(s).start()

    def finish(self, s):
        self.d(s).wait_recv()
        self.b(s).wait_recv()

    def close(self):
        def one(s, _):
            self.a(s).wait_send()
            self.b(s).wait_send()
            self.d(s).wait_send()
            return 0

        lax.fori_loop(0, 4, one, 0)


class RowGather:
    def __init__(self, at, own, slot, sems):
        self.at, self.own, self.slot = at, own, slot
        self.m_send, self.m_recv, self.x_send, self.x_recv, self.f_send, self.f_recv, self.local = (*sems, None)[:7]

    def to_mate(self, s):
        return remote(self.own(s), self.slot(s, self.at.row), self.m_send.at[s], self.m_recv.at[s], row=self.at.mate)

    def to_across(self, s):
        return remote(self.own(s), self.slot(s, self.at.row), self.x_send.at[s], self.x_recv.at[s], row=self.at.across)

    def pass_on(self, s):
        here = self.slot(s, self.at.across)
        return remote(here, here, self.f_send.at[s], self.f_recv.at[s], row=self.at.mate)

    def move_own(self, s):
        return pltpu.make_async_copy(self.own(s), self.slot(s, self.at.row), self.local.at[s])

    def near(self, s):
        self.to_mate(s).start()
        if self.local is not None:
            self.move_own(s).start()

    def wait_near(self, s):
        here = self.slot(s, self.at.mate)
        remote(here, here, self.m_send.at[s], self.m_recv.at[s], row=self.at.mate).wait_recv()
        if self.local is not None:
            self.move_own(s).wait()

    def take_across(self, s):
        here = self.slot(s, self.at.across)
        remote(here, here, self.x_send.at[s], self.x_recv.at[s], row=self.at.across).wait_recv()
        self.pass_on(s).start()

    def wait_diag(self, s):
        here = self.slot(s, self.at.diag)
        remote(here, here, self.f_send.at[s], self.f_recv.at[s], row=self.at.mate).wait_recv()

    def close(self, count):
        def one(s, _):
            self.to_mate(s).wait_send()
            self.to_across(s).wait_send()
            self.pass_on(s).wait_send()
            return 0

        lax.fori_loop(0, count, one, 0)


class ColSum:
    def __init__(self, at, product, sent, got, extra, sends, recvs, extra_recvs):
        self.at, self.product, self.sent, self.got, self.extra = at, product, sent, got, extra
        self.sends, self.recvs, self.extra_recvs = sends, recvs, extra_recvs
        self.half = product.shape[0] // 2

    def part(self, h):
        return pl.ds(h * self.half, self.half)

    def up(self, s, h):
        return remote(
            self.sent.at[s, self.part(h)], self.got.at[s, self.part(h)],
            self.sends.at[s, h], self.recvs.at[s, h], col=self.at.col + 1,
        )

    def down(self, s, h):
        return remote(
            self.sent.at[s, self.part(h)], self.got.at[s, self.part(h)],
            self.sends.at[s, h], self.recvs.at[s, h], col=self.at.col - 1,
        )

    def last_down(self, s, h):
        return remote(
            self.sent.at[s, self.part(h)], self.extra.at[self.part(h)],
            self.sends.at[s, h], self.extra_recvs.at[h], col=self.at.col - 1,
        )

    def step(self, s):
        col, product = self.at.col, self.product
        for h in range(2):
            @pl.when(((s >= col) & (col > 0)) | ((s < col) & (col < 3)))
            def _():
                self.up(s, h).wait_recv()

                def add(here):
                    product[here, :] += self.got[s, here].astype(F32)

                in_rows(self.half, 64, add, h * self.half)

            @pl.when((s == col) & (col < 3))
            def _():
                self.last_down(s, h).wait_recv()

                def add(here):
                    product[here, :] += self.extra[here].astype(F32)

                in_rows(self.half, 64, add, h * self.half)

            @pl.when(s != col)
            def _():
                def cast(here):
                    self.sent[s, here] = product[here, :].astype(BF16)

                in_rows(self.half, 64, cast, h * self.half)

            pl.when(s > col)(lambda: self.up(s, h).start())
            pl.when(s < col - 1)(lambda: self.down(s, h).start())
            pl.when(s == col - 1)(lambda: self.last_down(s, h).start())

    def close(self):
        def one(s, _):
            for h in range(2):
                pl.when(s != self.at.col)(lambda: self.up(s, h).wait_send())
            return 0

        lax.fori_loop(0, 4, one, 0)


def far_first(col, j):
    first = jnp.where(col < 2, 3, 0)
    second = jnp.where(col < 2, 2, 1)
    third = jnp.where(lax.rem(col, 2) == 0, col + 1, col - 1)
    return (first, second, third, col)[j]


def near_first(at, j):
    first, second, partner, _ = [far_first(at.col, i) for i in range(4)]
    mine = lax.div(at.col, 2) == at.chip
    return (
        jnp.where(mine, partner, first),
        jnp.where(mine, first, second),
        jnp.where(mine, second, partner),
        at.col,
    )[j]


def turn_tables(length):
    rates = THETA ** (-np.arange(HEAD_SIZE // 2) * 2.0 / HEAD_SIZE)
    angles = np.arange(length)[:, None] * rates[None, :]
    cos, sin = np.cos(angles), np.sin(angles)
    return (
        np.concatenate([cos, cos], axis=1).astype(np.float32),
        np.concatenate([-sin, sin], axis=1).astype(np.float32),
    )


def swap_halves(value):
    return pltpu.roll(value, HEAD_SIZE // 2, 1)


def head(ref, index):
    return ref[:, index * HEAD_SIZE : (index + 1) * HEAD_SIZE]


def root_scale(raw):
    return lax.rsqrt(jnp.mean(raw * raw, axis=1, keepdims=True) + EPSILON)


def attend(q_heads, groups, qkv, seg_col, seg_row, cos, sin, q_gain, k_gain, o, qa, ka, va, probs):
    kv = q_heads // groups
    tokens = qkv.shape[0]
    half = tokens // 2

    def turned(index, gain):
        raw = head(qkv, index)
        normed = raw * root_scale(raw) * gain[...]
        return (normed * cos[...] + swap_halves(normed) * sin[...]).astype(BF16)

    for i in range(q_heads):
        qa[:, i * HEAD_SIZE : (i + 1) * HEAD_SIZE] = turned(i, q_gain)
    for i in range(kv):
        ka[:, i * HEAD_SIZE : (i + 1) * HEAD_SIZE] = turned(q_heads + i, k_gain)
        va[:, i * HEAD_SIZE : (i + 1) * HEAD_SIZE] = head(qkv, q_heads + kv + i).astype(BF16)
    for block in range(2):
        rows = slice(block * half, (block + 1) * half)
        keys = (block + 1) * half
        spot = lax.broadcasted_iota(jnp.int32, (half, keys), 0) + block * half
        other = lax.broadcasted_iota(jnp.int32, (half, keys), 1)
        allowed = (other <= spot) & (seg_col[rows, :] == seg_row[:, :keys])
        for i in range(q_heads):
            j = i // groups
            dots = lax.dot_general(
                head(qa, i)[rows], head(ka, j)[:keys], (((1,), (1,)), ((), ())), preferred_element_type=F32
            ) * (1.0 / math.sqrt(HEAD_SIZE))
            scores = jnp.where(allowed, dots, MASKED)
            expo = jnp.exp(scores - jnp.max(scores, axis=1, keepdims=True))
            p = expo / jnp.sum(expo, axis=1, keepdims=True)
            probs[i, rows, :keys] = p.astype(BF16)
            mixed = jnp.dot(p.astype(BF16), head(va, j)[:keys], preferred_element_type=F32)
            o[rows, i * HEAD_SIZE : (i + 1) * HEAD_SIZE] = mixed.astype(BF16)


def front_kernel(q_heads, groups, model_width, *refs):
    refs = list(refs)

    def take(count):
        found = refs[:count]
        del refs[:count]
        return found

    (x_ref, gy, w_query, w_key, w_value, w_out, w_down, seg_col, seg_row, cos, sin, q_gain, k_gain, gain_one, gain_two) = take(15)
    (scale_one, hidden, scale_two, ffn_in, dact, qkv, qa, ka, va, probs) = take(10)
    (xn_out, gy_out, mixed_out) = take(3)
    (xn_wide, gy_wide, mixed_wide, mixed, product, chunk, keep) = take(7)
    total_bufs = take(2)
    second_bufs = take(2)
    moved = take(5)
    moved_q = take(5)
    chain = take(3)
    x_sems, gy_sems = take(2), take(2)
    (local,) = take(1)
    moved_sems, moved_q_sems = take(4), take(4)
    mixed_sems = take(7)
    chain_sems = take(3)
    total_sems, second_sems = take(2), take(2)

    at = Ends()
    tokens, feats = x_ref.shape
    first_total = RowTotal(at, *total_bufs, *total_sems)
    second_total = RowTotal(at, *second_bufs, *second_sems)
    x_gather = ColGather(at, xn_wide, *x_sems)
    gy_gather = ColGather(at, gy_wide, *gy_sems)
    row_sum = RowSumWhole(at, product, qkv, *moved, *moved_sems)
    quarter_sum = RowSumQuarter(at, chunk, keep, *moved_q, *moved_q_sems)
    mixes = RowGather(at, lambda s: mixed, lambda s, q: mixed_wide.at[q], mixed_sems)
    out_sum = ColSum(at, hidden, *chain, *chain_sems)

    gy_wide[at.col] = gy[...]
    at.greet()
    stream = x_ref[...].astype(F32)
    first_total.start(jnp.sum(stream * stream, axis=1, keepdims=True))
    scale = lax.rsqrt(first_total.finish() / model_width + EPSILON)
    scale_one[...] = scale
    xn_wide[at.col] = (x_ref[...].astype(F32) * scale * gain_one[...]).astype(BF16)

    def project(s):
        base = 0
        for w in (w_query, w_key, w_value):
            size = w.shape[1]
            product[:, base : base + size] = jnp.dot(xn_wide[s], w[...], preferred_element_type=F32)
            base += size
        row_sum.give(s)

    def back_down(s):
        size = chunk.shape[1]

        def one(j, _):
            cols = pl.ds(pl.multiple_of(j * size, size), size)
            value = lax.dot_general(
                gy_wide[s], w_down[cols, :], (((1,), (1,)), ((), ())), preferred_element_type=F32
            )
            quarter_sum.split(s, value, cols, dact)
            return 0

        lax.fori_loop(0, w_down.shape[0] // size, one, 0)
        quarter_sum.give(s)

    def end_down(s):
        quarter_sum.finish(s)

        def add(here):
            dact[s, here] += moved_q[2][s, here].astype(F32) + moved_q[4][s, here].astype(F32)

        in_rows(128, 16, add)

    def send_gy(dist):
        @pl.when((at.col == dist) & (at.col < 3))
        def _():
            gy_gather.send_up()

        @pl.when((at.col == 3 - dist) & (at.col > 0))
        def _():
            gy_gather.send_down()

    def out_step(j):
        s = near_first(at, j)
        hidden[...] = jnp.dot(mixed_wide[s], w_out[...], preferred_element_type=F32)
        out_sum.step(s)

    mid = jnp.logical_not(at.end)
    x_gather.arrive(0)
    send_gy(0)
    x_gather.loop(0, project)
    back_down(at.col)
    for dist in range(1, 4):
        x_gather.arrive(dist)
        send_gy(dist)
        x_gather.loop(dist, project)

    @pl.when(mid)
    def _():
        gy_gather.arrive(1)

    row_sum.finish()
    attend(q_heads, groups, qkv, seg_col, seg_row, cos, sin, q_gain, k_gain, mixed, qa, ka, va, probs)
    mixes.to_across(0).start()
    mixes.near(0)

    @pl.when(mid)
    def _():
        gy_gather.arrive(2)

    mixes.wait_near(0)

    @pl.when(at.end)
    def _():
        out_step(0)
        gy_gather.arrive(1)

    gy_gather.loop(1, back_down)
    mixes.take_across(0)
    mixes.wait_diag(0)

    @pl.when(at.end)
    def _():
        out_step(1)
        out_step(2)
        gy_gather.arrive(2)

    @pl.when(mid)
    def _():
        out_step(0)

    gy_gather.loop(2, back_down)

    @pl.when(mid)
    def _():
        out_step(1)
        out_step(2)

    @pl.when(at.end)
    def _():
        gy_gather.arrive(3)

    gy_gather.loop(3, back_down)
    wides = [
        pltpu.make_async_copy(src, dst, local.at[i])
        for i, (src, dst) in enumerate(((xn_wide, xn_out), (gy_wide, gy_out), (mixed_wide, mixed_out)))
    ]
    for copy in wides:
        copy.start()
    for dist in range(3):
        gy_gather.loop(dist, end_down)
    out_step(3)

    def residual(here):
        hidden[here, :] += x_ref[here, :].astype(F32)

    in_rows(tokens, 64, residual)
    value = hidden[...]
    second_total.start(jnp.sum(value * value, axis=1, keepdims=True))
    gy_gather.loop(3, end_down)
    scale = lax.rsqrt(second_total.finish() / model_width + EPSILON)
    scale_two[...] = scale
    ffn_in[...] = (hidden[...] * scale * gain_two[...]).astype(BF16)

    x_gather.close()
    gy_gather.close()
    row_sum.close()
    quarter_sum.close()
    mixes.close(1)
    out_sum.close()
    for copy in wides:
        copy.wait()


def col_gather_sems():
    return [pltpu.SemaphoreType.DMA((2, 4, 2)), pltpu.SemaphoreType.DMA((4, 2))]


def chain_scratch(tokens, feats):
    return [
        pltpu.VMEM((4, tokens, feats), BF16), pltpu.VMEM((4, tokens, feats), BF16), pltpu.VMEM((tokens, feats), BF16),
    ]


def chain_sems():
    dma = pltpu.SemaphoreType.DMA
    return [dma((4, 2)), dma((4, 2)), dma((2,))]


def front(q_heads, groups, model_width, number, x, gy, weights, segments, tables, gains):
    tokens, feats = x.shape
    w_query, w_key, w_value, w_out, w_down = weights
    width = w_query.shape[1] + w_key.shape[1] + w_value.shape[1]
    q_width, k_width, ff = w_query.shape[1], w_key.shape[1], w_down.shape[0]
    dma = pltpu.SemaphoreType.DMA
    any_spec, vmem = pl.BlockSpec(memory_space=pl.ANY), pl.BlockSpec(memory_space=pltpu.VMEM)
    shape = jax.ShapeDtypeStruct
    wide = pltpu.VMEM((4, tokens, feats), BF16)
    return pl.pallas_call(
        functools.partial(front_kernel, q_heads, groups, model_width),
        out_shape=(
            shape((tokens, 1), F32),
            shape((tokens, feats), F32),
            shape((tokens, 1), F32),
            shape((tokens, feats), BF16),
            shape((4, tokens // 4, ff), F32),
            shape((tokens, width), F32),
            shape((tokens, q_width), BF16),
            shape((tokens, k_width), BF16),
            shape((tokens, k_width), BF16),
            shape((q_heads, tokens, tokens), BF16),
            shape((4, tokens, feats), BF16),
            shape((4, tokens, feats), BF16),
            shape((4, tokens, q_width), BF16),
        ),
        in_specs=[vmem] * 15,
        out_specs=tuple([vmem] * 10 + [any_spec] * 3),
        scratch_shapes=[
            wide,
            wide,
            pltpu.VMEM((4, tokens, q_width), BF16),
            pltpu.VMEM((tokens, q_width), BF16),
            pltpu.VMEM((tokens, width), F32),
            pltpu.VMEM((tokens, 512), F32),
            pltpu.VMEM((tokens // 4, ff), F32),
        ]
        + row_total_scratch(tokens) * 2
        + row_sum_scratch(tokens, width)
        + [pltpu.VMEM((4, tokens // 4, ff), BF16)] * 5
        + chain_scratch(tokens, feats)
        + col_gather_sems() * 2
        + [dma((3,))]
        + row_sum_sems()
        + [dma((2, 4)), dma((2, 4)), dma((4,)), dma((4,))]
        + [dma((1,))] * 7
        + chain_sems()
        + row_total_sems() * 2,
        compiler_params=pltpu.CompilerParams(
            collective_id=number, has_side_effects=True, vmem_limit_bytes=VMEM_LIMIT
        ),
        name="front",
    )(x, gy, *weights, *segments, *tables, *gains)


def across_rows(left, right):
    return lax.dot_general(left, right, (((0,), (0,)), ((), ())), preferred_element_type=F32)


def attend_back(q_heads, groups, grad, qkv, qa, ka, va, probs, cos, sin, q_gain, k_gain, out, q_part, k_part, dq, dk, dv):
    kv = q_heads // groups
    tokens = qkv.shape[0]
    half = tokens // 2
    scale = 1.0 / math.sqrt(HEAD_SIZE)
    dk[...] = jnp.zeros_like(dk)
    dv[...] = jnp.zeros_like(dv)
    for block in range(2):
        rows = slice(block * half, (block + 1) * half)
        keys = (block + 1) * half
        for i in range(q_heads):
            j = i // groups
            spot = slice(j * HEAD_SIZE, (j + 1) * HEAD_SIZE)
            pb = probs[i, rows, :keys]
            p = pb.astype(F32)
            g = head(grad, i)[rows].astype(BF16)
            dv[:keys, spot] += across_rows(pb.astype(BF16), g)
            dp = lax.dot_general(
                g, head(va, j)[:keys], (((1,), (1,)), ((), ())), preferred_element_type=F32
            )
            ds = (p * (dp - jnp.sum(p * dp, axis=1, keepdims=True))).astype(BF16)
            dq[rows, i * HEAD_SIZE : (i + 1) * HEAD_SIZE] = (
                jnp.dot(ds, head(ka, j)[:keys], preferred_element_type=F32) * scale
            )
            dk[:keys, spot] += across_rows(ds, head(qa, i)[rows]) * scale

    def back(turned, index, gain):
        raw = head(qkv, index)
        scales = root_scale(raw)
        normed = turned * cos[...] - swap_halves(turned) * sin[...]
        part = jnp.sum(normed * raw * scales, axis=0, keepdims=True)
        weighted = normed * gain[...]
        inner = jnp.sum(weighted * raw, axis=1, keepdims=True)
        result = scales * weighted - raw * (scales * scales * scales) * inner * (1.0 / HEAD_SIZE)
        out[:, index * HEAD_SIZE : (index + 1) * HEAD_SIZE] = result.astype(BF16)
        return part

    q_part[...] = sum(back(head(dq, i), i, q_gain) for i in range(q_heads))
    k_part[...] = sum(back(head(dk, i), q_heads + i, k_gain) for i in range(kv))
    for i in range(kv):
        spot = (q_heads + kv + i) * HEAD_SIZE
        out[:, spot : spot + HEAD_SIZE] = head(dv, i).astype(BF16)


def weight_grad(out, left, right):
    def block(here):
        total = None
        for s in range(4):
            term = across_rows(left(s, here), right(s))
            total = term if total is None else total + term
        out[here, :] = total.astype(BF16)

    in_rows(out.shape[0], 256, block)


def middle_kernel(pairs, *refs):
    refs = list(refs)

    def take(count):
        found = refs[:count]
        del refs[:count]
        return found

    (hn, w_gate, w_up, dact) = take(4)
    (dhn, act, gate_n, up_n) = take(4)
    others = take(1) if pairs == 2 else []
    (hn_wide, chunk, keep, own, gate_wide, up_wide, n_gate, n_up) = take(8)
    moved = take(5)
    chain = take(3)
    hn_sems = take(2)
    moved_sems = take(4)
    gate_sems, up_sems = take(6), take(6)
    chain_sems_ = take(3)
    (local, y_send, y_recv) = take(3)

    at = Ends()
    ff = w_gate.shape[1]
    quarter = act.shape[1]
    gather = ColGather(at, hn_wide, *hn_sems)
    row_sum = RowSumQuarter(at, chunk, keep, *moved, *moved_sems)
    gates = RowGather(at, lambda s: gate_wide.at[s, at.row], lambda s, q: gate_wide.at[s, q], gate_sems)
    ups = RowGather(at, lambda s: up_wide.at[s, at.row], lambda s, q: up_wide.at[s, q], up_sems)
    back_sum = ColSum(at, dhn, *chain, *chain_sems_)

    hn_wide[at.col] = hn[...]
    at.greet(pairs if pairs == 2 else 0)

    def project(s):
        size = chunk.shape[1]
        for w, base in ((w_gate, 0), (w_up, ff)):

            def one(j, _, w=w, base=base):
                cols = pl.ds(pl.multiple_of(j * size, size), size)
                spot = pl.ds(pl.multiple_of(base + j * size, size), size)
                row_sum.split(s, jnp.dot(hn_wide[s], w[:, cols], preferred_element_type=F32), spot, own)
                return 0

            lax.fori_loop(0, ff // size, one, 0)
        row_sum.give(s)

    def hidden_units(s):
        row_sum.finish(s)
        size = chunk.shape[1]

        def some(j, _):
            cols = pl.ds(pl.multiple_of(j * size, size), size)
            later = pl.ds(pl.multiple_of(ff + j * size, size), size)

            def one(here):
                def whole(spot):
                    c_recv, d_recv = moved[2], moved[4]
                    return (
                        own[s, here, spot].astype(F32)
                        + d_recv[s, here, spot].astype(F32)
                        + c_recv[s, here, spot].astype(F32)
                    )

                gate, up = whole(cols), whole(later)
                grad = dact[s, here, cols]
                sigmoid = jax.nn.sigmoid(gate)
                silu = gate * sigmoid
                act[s, here, cols] = (silu * up).astype(BF16)
                gate_wide[s, at.row, here, cols] = (
                    grad * up * (sigmoid * (1.0 + gate * (1.0 - sigmoid)))
                ).astype(BF16)
                up_wide[s, at.row, here, cols] = (grad * silu).astype(BF16)

            in_rows(quarter, 16, one)
            return 0

        lax.fori_loop(0, ff // size, some, 0)
        gates.to_across(s).start()
        gates.near(s)
        ups.near(s)

    def rows_of(ref, s):
        return ref[s].reshape(4 * quarter, ff)

    def back(j):
        s = far_first(at.col, j)
        contract = (((1,), (1,)), ((), ()))
        dhn[...] = lax.dot_general(
            rows_of(gate_wide, s), w_gate[...], contract, preferred_element_type=F32
        ) + lax.dot_general(rows_of(up_wide, s), w_up[...], contract, preferred_element_type=F32)

    def arrive(some, j):
        s = far_first(at.col, j)
        some.wait_near(s)
        some.take_across(s)
        some.wait_diag(s)

    def left(s, here):
        return hn_wide[s, :, here]

    mid = jnp.logical_not(at.end)
    gather.arrive(0)
    gather.loop(0, project)
    gather.arrive(1)
    gather.loop(1, project)
    gather.arrive(2)
    gather.loop(2, project)
    gather.loop(0, hidden_units)
    gather.arrive(3)
    gather.loop(3, project)
    for dist in range(1, 4):
        gather.loop(dist, hidden_units)
    for j in range(4):
        ups.to_across(far_first(at.col, j)).start()
    for j in range(4):
        arrive(gates, j)
    weight_grad(n_gate, left, lambda s: rows_of(gate_wide, s))
    pair = remote(n_gate, others[0], y_send.at[0], y_recv.at[0], dp=at.pair(2, 1)) if pairs == 2 else None
    if pairs == 2:
        pair.start()
    keep_gate = pltpu.make_async_copy(n_gate, gate_n, local.at[0])
    keep_gate.start()
    arrive(ups, 0)
    for j in range(3):
        back(j)
        pl.when(at.end)(lambda: back_sum.step(far_first(at.col, j)))
        arrive(ups, j + 1)
        pl.when(mid)(lambda: back_sum.step(far_first(at.col, j)))
    weight_grad(n_up, left, lambda s: rows_of(up_wide, s))
    keep_up = pltpu.make_async_copy(n_up, up_n, local.at[1])
    keep_up.start()
    back(3)
    back_sum.step(at.col)

    gather.close()
    row_sum.close()
    gates.close(4)
    ups.close(4)
    back_sum.close()
    keep_gate.wait()
    keep_up.wait()
    if pairs == 2:
        pair.wait()


def middle(pairs, number, hn, w_gate, w_up, dact):
    tokens, feats = hn.shape
    ff = w_gate.shape[1]
    quarter = tokens // 4
    dma = pltpu.SemaphoreType.DMA
    any_spec, vmem = pl.BlockSpec(memory_space=pl.ANY), pl.BlockSpec(memory_space=pltpu.VMEM)
    shape = jax.ShapeDtypeStruct
    narrow = shape((feats, ff), BF16)
    others = 1 if pairs == 2 else 0
    out = pl.pallas_call(
        functools.partial(middle_kernel, pairs),
        out_shape=tuple(
            [shape((tokens, feats), F32), shape((4, quarter, ff), BF16), narrow, narrow] + [narrow] * others
        ),
        in_specs=[vmem] * 4,
        out_specs=tuple([vmem] * 2 + [any_spec] * (2 + others)),
        scratch_shapes=[
            pltpu.VMEM((4, tokens, feats), BF16),
            pltpu.VMEM((tokens, 512), F32),
            pltpu.VMEM((quarter, 2 * ff), F32),
            pltpu.VMEM((4, quarter, 2 * ff), BF16),
            pltpu.VMEM((4, 4, quarter, ff), BF16),
            pltpu.VMEM((4, 4, quarter, ff), BF16),
            pltpu.VMEM((feats, ff), BF16),
            pltpu.VMEM((feats, ff), BF16),
        ]
        + [pltpu.VMEM((4, quarter, 2 * ff), BF16)] * 5
        + chain_scratch(tokens, feats)
        + col_gather_sems()
        + [dma((2, 4)), dma((2, 4)), dma((4,)), dma((4,))]
        + [dma((4,))] * 12
        + chain_sems()
        + [dma((2,)), dma((1,)), dma((1,))],
        compiler_params=pltpu.CompilerParams(
            collective_id=number, has_side_effects=True, vmem_limit_bytes=VMEM_LIMIT
        ),
        name="middle",
    )(hn, w_gate, w_up, dact)
    return out[:4], out[4:]


def tail_kernel(pairs, q_heads, groups, *refs):
    refs = list(refs)

    def take(count):
        found = refs[:count]
        del refs[:count]
        return found

    (act, w_out, w_down, w_query, w_key, w_value, qkv, qa, ka, va, probs, cos, sin, q_gain, k_gain) = take(15)
    (dhn, hidden, scale_two, gain_two, gy, x_ref, scale_one, gain_one) = take(8)
    (gy_wide, mixed_wide, normed_wide, up_n) = take(4)
    (in_grad, layer_out, one_grad, two_grad, q_grad, k_grad, down_n, out_n, qkv_n) = take(9)
    others = take(4) if pairs == 2 else []
    (da_wide, act_wide, dqkv, dqkv_wide, held, product, grad_mixed, dq, dk, dv, n_down, n_out, n_qkv) = take(13)
    (dh, q_part, k_part, packet, packet_got, by_row, summed, summed_got) = take(8)
    first_bufs, last_bufs = take(2), take(2)
    moved = take(5)
    down_bufs, dxn_bufs = take(3), take(3)
    (g_send, g_recv, local, y_send, y_recv) = take(5)
    moved_sems = take(4)
    act_sems, dqkv_sems = take(7), take(7)
    down_sems, dxn_sems = take(3), take(3)
    first_sems, last_sems = take(2), take(2)
    (p_send, p_recv, r_send, r_recv, s_send, s_recv) = take(6)

    at = Ends()
    model_width = 4 * dhn.shape[1]
    first_total = RowTotal(at, *first_bufs, *first_sems)
    last_total = RowTotal(at, *last_bufs, *last_sems)
    at.greet(pairs, True)

    def pair_copy(src, index):
        return remote(src, others[index], y_send.at[index], y_recv.at[index], dp=1 - lax.axis_index("dp"))

    narrow = (up_n, n_down, n_out, n_qkv)

    def to_pair(index):
        if pairs == 2:
            pair_copy(narrow[index], index).start()

    def load(index, src):
        return pltpu.make_async_copy(src, held, local.at[index])

    def keep(index, src, dst):
        return pltpu.make_async_copy(src, dst, local.at[3 + index])

    to_pair(0)
    load(0, gy_wide).start()
    gather = ColGather(at, da_wide, g_send, g_recv)
    row_sum = RowSumWhole(at, product, grad_mixed, *moved, *moved_sems)
    acts = RowGather(at, lambda s: act.at[s], lambda s, q: act_wide.at[s, q], act_sems)
    grads = RowGather(at, lambda s: dqkv, lambda s, q: dqkv_wide.at[q], dqkv_sems)
    down_sum = ColSum(at, product, *down_bufs, *down_sems)
    dxn_sum = ColSum(at, product, *dxn_bufs, *dxn_sems)

    weighted = dhn[...] * gain_two[...]
    first_total.start(jnp.sum(weighted * hidden[...], axis=1, keepdims=True))
    for j in range(2):
        acts.to_across(far_first(at.col, j)).start()
    for j in range(4):
        acts.near(far_first(at.col, j))
    scale = scale_two[...]
    packet[...] = jnp.zeros_like(packet)
    packet[1:2, :] = jnp.sum(dhn[...] * hidden[...] * scale, axis=0, keepdims=True)
    inner = first_total.finish()
    dh[...] = (
        gy[...].astype(F32)
        + scale * (dhn[...] * gain_two[...])
        - hidden[...] * (scale * scale * scale * inner * (1.0 / model_width))
    )
    da_wide[at.col] = dh[...].astype(BF16)
    gather.arrive(0)

    def back_out(s):
        product[...] = lax.dot_general(
            da_wide[s], w_out[...], (((1,), (1,)), ((), ())), preferred_element_type=F32
        )
        row_sum.give(s)

    def take_act(j):
        s = far_first(at.col, j)
        if j < 2:
            acts.to_across(far_first(at.col, j + 2)).start()
        acts.wait_near(s)
        acts.take_across(s)
        acts.wait_diag(s)

    def act_rows(s, cols):
        return act_wide[s, :, :, cols].reshape(product.shape[0], cols.size)

    def down_step(j):
        s = far_first(at.col, j)
        product[...] = jnp.dot(
            act_rows(s, pl.ds(0, act.shape[2])), w_down[...], preferred_element_type=F32
        )
        down_sum.step(s)

    def dxn_step(j):
        s = near_first(at, j)
        total, base = None, 0
        for w in (w_query, w_key, w_value):
            size = w.shape[1]
            term = lax.dot_general(
                dqkv_wide[s, :, pl.ds(base, size)], w[...], (((1,), (1,)), ((), ())), preferred_element_type=F32
            )
            total = term if total is None else total + term
            base += size
        product[...] = total
        dxn_sum.step(s)

    gather.loop(0, back_out)
    take_act(0)
    gather.arrive(1)
    gather.loop(1, back_out)
    down_step(0)
    gather.arrive(2)
    gather.loop(2, back_out)
    take_act(1)
    down_step(1)
    gather.arrive(3)
    gather.loop(3, back_out)

    @pl.when(at.end)
    def _():
        take_act(2)
        down_step(2)

    row_sum.finish()
    attend_back(
        q_heads, groups, grad_mixed, qkv, qa, ka, va, probs, cos, sin, q_gain, k_gain,
        dqkv, q_part, k_part, dq, dk, dv,
    )
    grads.to_across(0).start()
    grads.near(0)
    grads.wait_near(0)

    @pl.when(at.end)
    def _():
        dxn_step(0)

    @pl.when(jnp.logical_not(at.end))
    def _():
        take_act(2)
        down_step(2)

    take_act(3)
    load(0, gy_wide).wait()
    weight_grad(n_down, act_rows, lambda s: held[s])
    to_pair(1)
    keep(0, n_down, down_n).start()
    load(1, mixed_wide).start()

    @pl.when(jnp.logical_not(at.end))
    def _():
        dxn_step(0)

    load(1, mixed_wide).wait()
    weight_grad(n_out, lambda s, here: held[s, :, here], lambda s: da_wide[s])
    to_pair(2)
    keep(1, n_out, out_n).start()
    load(2, normed_wide).start()
    grads.take_across(0)
    grads.wait_diag(0)

    @pl.when(at.end)
    def _():
        dxn_step(1)
        dxn_step(2)

    load(2, normed_wide).wait()
    weight_grad(n_qkv, lambda s, here: held[s, :, here], lambda s: dqkv_wide[s])
    to_pair(3)
    keep(2, n_qkv, qkv_n).start()

    @pl.when(jnp.logical_not(at.end))
    def _():
        dxn_step(1)
        dxn_step(2)

    down_step(3)
    layer_out[...] = (hidden[...] + product[...]).astype(BF16)
    dxn_step(3)
    scale = scale_one[...]
    last_total.start(
        jnp.sum(product[...] * gain_one[...] * x_ref[...].astype(F32), axis=1, keepdims=True)
    )
    packet[0:1, :] = jnp.sum(product[...] * x_ref[...].astype(F32) * scale, axis=0, keepdims=True)
    packet[2:3, :HEAD_SIZE] = q_part[...]
    packet[2:3, HEAD_SIZE : 2 * HEAD_SIZE] = k_part[...]

    def to_line(step):
        return remote(
            packet, packet_got.at[step - 1], p_send.at[step - 1], p_recv.at[step - 1],
            col=lax.rem(at.col + step, 4),
        )

    def to_row(index, peer):
        return remote(by_row.at[at.row], by_row.at[at.row], r_send.at[index], r_recv.at[index], row=peer)

    def from_row(index, peer):
        return remote(by_row.at[peer], by_row.at[peer], r_send.at[index], r_recv.at[index], row=peer)

    def to_peer(step):
        return remote(
            summed, summed_got.at[step - 1], s_send.at[step - 1], s_recv.at[step - 1], dp=at.pair(pairs, step)
        )

    for step in range(1, 4):
        to_line(step).start()
    inner = last_total.finish()
    in_grad[...] = (
        dh[...]
        + scale * (product[...] * gain_one[...])
        - x_ref[...].astype(F32) * (scale * scale * scale * inner * (1.0 / model_width))
    )
    for step in range(1, 4):
        to_line(step).wait()
    by_row[at.row] = (packet[...] + packet_got[0]) + (packet_got[1] + packet_got[2])
    peers = (at.mate, at.across, at.diag)
    for index, peer in enumerate(peers):
        to_row(index, peer).start()
    for index, peer in enumerate(peers):
        from_row(index, peer).wait_recv()
        to_row(index, peer).wait_send()
    summed[...] = jnp.zeros_like(summed)
    for r in range(4):
        summed[r : r + 1, :] = by_row[r, 0:1, :]
        summed[4 + r : 5 + r, :] = by_row[r, 1:2, :]
    summed[8:9, :] = (by_row[0, 2:3, :] + by_row[1, 2:3, :]) + (by_row[2, 2:3, :] + by_row[3, 2:3, :])
    for step in range(1, pairs):
        to_peer(step).start()
    for step in range(1, pairs):
        to_peer(step).wait()
    total = summed[...]
    for step in range(1, pairs):
        total = total + summed_got[step - 1]
    one_grad[...] = total[0:4, :]
    two_grad[...] = total[4:8, :]
    q_grad[...] = total[8:9, :HEAD_SIZE]
    k_grad[...] = total[8:9, HEAD_SIZE : 2 * HEAD_SIZE]

    gather.close()
    row_sum.close()
    acts.close(4)
    grads.close(1)
    down_sum.close()
    dxn_sum.close()
    keep(0, n_down, down_n).wait()
    keep(1, n_out, out_n).wait()
    keep(2, n_qkv, qkv_n).wait()
    if pairs == 2:
        for index in range(4):
            pair_copy(narrow[index], index).wait()


def tail(pairs, q_heads, groups, number, act, weights, saved, tables, norms, wides, narrow):
    tokens, feats = norms[0].shape
    w_out, w_down = weights[:2]
    ff = w_down.shape[0]
    width = saved[0].shape[1]
    q_width, k_width = saved[1].shape[1], saved[2].shape[1]
    dma = pltpu.SemaphoreType.DMA
    any_spec, vmem = pl.BlockSpec(memory_space=pl.ANY), pl.BlockSpec(memory_space=pltpu.VMEM)
    shape = jax.ShapeDtypeStruct
    shapes = [
        shape((tokens, feats), F32),
        shape((tokens, feats), BF16),
        shape((4, feats), F32),
        shape((4, feats), F32),
        shape((1, HEAD_SIZE), F32),
        shape((1, HEAD_SIZE), F32),
    ]
    own = [shape((ff, feats), BF16), shape((q_width, feats), BF16), shape((feats, width), BF16)]
    others = [shape(n.shape, BF16) for n in narrow] + own if pairs == 2 else []
    packet = pltpu.VMEM((8, feats), F32)
    operands = (act, *weights, *saved, *tables, *norms)
    out = pl.pallas_call(
        functools.partial(tail_kernel, pairs, q_heads, groups),
        out_shape=tuple(shapes + own + others),
        in_specs=[vmem] * len(operands) + [any_spec] * 4,
        out_specs=tuple([vmem] * 6 + [any_spec] * (3 + len(others))),
        scratch_shapes=[
            pltpu.VMEM((4, tokens, feats), BF16),
            pltpu.VMEM((4, 4, tokens // 4, ff), BF16),
            pltpu.VMEM((tokens, width), BF16),
            pltpu.VMEM((4, tokens, width), BF16),
            pltpu.VMEM((4, tokens, feats), BF16),
            pltpu.VMEM((tokens, feats), F32),
            pltpu.VMEM((tokens, q_width), F32),
            pltpu.VMEM((tokens, q_width), F32),
            pltpu.VMEM((tokens, k_width), F32),
            pltpu.VMEM((tokens, k_width), F32),
            pltpu.VMEM((ff, feats), BF16),
            pltpu.VMEM((q_width, feats), BF16),
            pltpu.VMEM((feats, width), BF16),
            pltpu.VMEM((tokens, feats), F32),
            pltpu.VMEM((1, HEAD_SIZE), F32),
            pltpu.VMEM((1, HEAD_SIZE), F32),
            packet,
            pltpu.VMEM((3, 8, feats), F32),
            pltpu.VMEM((4, 8, feats), F32),
            pltpu.VMEM((16, feats), F32),
            pltpu.VMEM((max(pairs - 1, 1), 16, feats), F32),
        ]
        + row_total_scratch(tokens) * 2
        + row_sum_scratch(tokens, q_width)
        + chain_scratch(tokens, feats) * 2
        + col_gather_sems()
        + [dma((6,)), dma((4,)), dma((4,))]
        + row_sum_sems()
        + [dma((4,))] * 7
        + [dma((1,))] * 7
        + chain_sems() * 2
        + row_total_sems() * 2
        + [dma((3,))] * 4
        + [dma((max(pairs - 1, 1),))] * 2,
        compiler_params=pltpu.CompilerParams(
            collective_id=number, has_side_effects=True, vmem_limit_bytes=VMEM_LIMIT
        ),
        name="tail",
    )(*operands, *wides, *narrow)
    return out[:6], out[6:9], out[9:]


def shards(
    pairs,
    hidden_in,
    segment_ids,
    attn_gain,
    w_query,
    key_projection,
    value_projection,
    query_gain,
    key_norm_gain,
    w_out,
    ffn_gain,
    w_gate,
    w_up,
    w_down,
    out_grad,
):
    tokens, slice_width = hidden_in.shape
    model_width = attn_gain.shape[0]
    offset = lax.axis_index("row") * slice_width
    gain_one = lax.dynamic_slice_in_dim(attn_gain, offset, slice_width)
    gain_two = lax.dynamic_slice_in_dim(ffn_gain, offset, slice_width)
    q_width = w_query.shape[1]
    k_width = key_projection.shape[1]
    q_heads = q_width // HEAD_SIZE
    groups = q_width // k_width
    tables = (*turn_tables(tokens), query_gain[None, :], key_norm_gain[None, :])
    (scale_one, hidden, scale_two, ffn_in, grad_inner, qkv, q_turned, k_turned, values, probs, xn_wide, gy_wide, mixed_wide) = front(
        q_heads, groups, model_width, 0, hidden_in, out_grad,
        (w_query, key_projection, value_projection, w_out, w_down),
        (segment_ids[:, None], segment_ids[None, :]),
        tables,
        (gain_one[None, :], gain_two[None, :]),
    )
    (grad_ffn_in, inner_act, gate_n, up_n), other_gate = middle(pairs, 1, ffn_in, w_gate, w_up, grad_inner)
    (in_grad, layer_out, one_grad, two_grad, q_gain_grad, k_gain_grad), own, others = tail(
        pairs, q_heads, groups, 2, inner_act,
        (w_out, w_down, w_query, key_projection, value_projection),
        (qkv, q_turned, k_turned, values, probs),
        tables,
        (grad_ffn_in, hidden, scale_two, gain_two[None, :], out_grad, hidden_in, scale_one, gain_one[None, :]),
        (gy_wide, mixed_wide, xn_wide),
        (up_n,),
    )
    parts = (gate_n, up_n, *own)
    if pairs == 2:
        sums = [a.astype(F32) + b.astype(F32) for a, b in zip(parts, (*other_gate, *others))]
    else:
        sums = lax.psum(tuple(part.astype(F32) for part in parts), "dp")
    gate_grad, up_grad, down_grad, out_weight_grad, qkv_grad = sums
    return (
        layer_out,
        in_grad,
        one_grad.reshape(-1),
        qkv_grad[:, :q_width],
        qkv_grad[:, q_width : q_width + k_width],
        qkv_grad[:, q_width + k_width :],
        q_gain_grad.reshape(-1),
        k_gain_grad.reshape(-1),
        out_weight_grad,
        two_grad.reshape(-1),
        gate_grad,
        up_grad,
        down_grad,
    )


def solution(mesh):
    acts, grid, flip, none = P(("dp", "col"), "row"), P("row", "col"), P("col", "row"), P()
    return jax.shard_map(
        functools.partial(shards, mesh.shape["dp"]),
        mesh=mesh,
        in_specs=(
            acts, P(("dp", "row")), none, grid, grid, grid, none, none, flip, none, grid, grid, flip, acts,
        ),
        out_specs=(
            acts, acts, none, grid, grid, grid, none, none, flip, none, grid, grid, flip,
        ),
        check_vma=False,
    )
```

```python
import functools
import math

import jax
import jax.numpy as jnp
import numpy as np
from jax import lax
from jax.experimental import pallas as pl
from jax.experimental.pallas import tpu as pltpu
from jax.sharding import PartitionSpec as P

HEAD_SIZE = 128
EPSILON = 1e-06
THETA = 1000000.0
MASKED = -1e30
MESH = pl.DeviceIdType.MESH
BF16 = jnp.bfloat16
F32 = jnp.float32
VMEM_LIMIT = 60 << 20


def to(**where):
    return dict(device_id=where, device_id_type=MESH)


class Ends:
    def __init__(self):
        self.row = lax.axis_index("row")
        self.col = lax.axis_index("col")
        self.chip = lax.div(self.row, 2)
        self.core = lax.rem(self.row, 2)
        self.mate = self.chip * 2 + (1 - self.core)
        self.across = (1 - self.chip) * 2 + self.core
        self.diag = (1 - self.chip) * 2 + (1 - self.core)
        self.end = (self.col == 0) | (self.col == 3)

    def greet(self, pairs=0, line=False):
        gate = pltpu.get_barrier_semaphore()
        count = 3
        for peer in (self.mate, self.across, self.diag):
            pl.semaphore_signal(gate, inc=1, **to(row=peer))
        for step in range(1, pairs):
            pl.semaphore_signal(gate, inc=1, **to(dp=self.pair(pairs, step)))
            count += 1
        if line:
            for step in range(1, 4):
                pl.semaphore_signal(gate, inc=1, **to(col=lax.rem(self.col + step, 4)))
                count += 1
        else:

            @pl.when(self.col > 0)
            def _():
                pl.semaphore_signal(gate, inc=1, **to(col=self.col - 1))

            @pl.when(self.col < 3)
            def _():
                pl.semaphore_signal(gate, inc=1, **to(col=self.col + 1))

            count += jnp.where(self.col > 0, 1, 0) + jnp.where(self.col < 3, 1, 0)
        pl.semaphore_wait(gate, count)

    def pair(self, pairs, step):
        return lax.rem(lax.axis_index("dp") + step, pairs)


class RowTotal:
    def __init__(self, at, own, got, sends, recvs):
        self.own, self.got = own, got
        self.copies = [
            remote(own, got.at[i], sends.at[i], recvs.at[i], row=peer)
            for i, peer in enumerate((at.mate, at.across, at.diag))
        ]

    def start(self, column):
        self.own[...] = jnp.broadcast_to(column, (column.shape[0], 128)).T[:8, :]
        for copy in self.copies:
            copy.start()

    def finish(self):
        for copy in self.copies:
            copy.wait()
        total = (self.own[...] + self.got[0]) + (self.got[1] + self.got[2])
        return jnp.concatenate([total] * 16, axis=0).T[:, :1]


def row_total_scratch(tokens):
    return [pltpu.VMEM((8, tokens), F32), pltpu.VMEM((3, 8, tokens), F32)]


def row_total_sems():
    return [pltpu.SemaphoreType.DMA((3,)), pltpu.SemaphoreType.DMA((3,))]


def remote(src, dst, sends, recvs, **where):
    return pltpu.make_async_remote_copy(
        src_ref=src, dst_ref=dst, send_sem=sends, recv_sem=recvs, **to(**where)
    )


def in_rows(count, step, body, first=0):
    def one(i, _):
        body(pl.ds(pl.multiple_of(first + i * step, step), step))
        return 0

    lax.fori_loop(0, count // step, one, 0)


class ColGather:
    def __init__(self, at, wide, sends, recvs):
        self.at, self.wide, self.sends, self.recvs = at, wide, sends, recvs
        self.half = wide.shape[1] // 2

    def copy(self, s, h, side, col):
        part = self.wide.at[s, pl.ds(h * self.half, self.half)]
        return remote(part, part, self.sends.at[side, s, h], self.recvs.at[s, h], col=col)

    def up(self, s, h):
        return self.copy(s, h, 0, self.at.col + 1)

    def down(self, s, h):
        return self.copy(s, h, 1, self.at.col - 1)

    def loop(self, dist, body):
        if dist == 0:
            body(self.at.col)
            return

        def one(side, _):
            s = jnp.where(side == 0, self.at.col - dist, self.at.col + dist)
            pl.when((s >= 0) & (s <= 3))(lambda: body(s))
            return 0

        lax.fori_loop(0, 2, one, 0)

    def arrive(self, dist):
        for h in range(2):

            def take(s, h=h):
                if dist:
                    self.up(s, h).wait_recv()

                @pl.when((s <= self.at.col) & (self.at.col < 3))
                def _():
                    self.up(s, h).start()

                @pl.when((s >= self.at.col) & (self.at.col > 0))
                def _():
                    self.down(s, h).start()

            self.loop(dist, take)

    def send_up(self):
        for h in range(2):
            self.up(self.at.col, h).start()

    def send_down(self):
        for h in range(2):
            self.down(self.at.col, h).start()

    def close(self):
        def one(s, _):
            for h in range(2):

                @pl.when((s <= self.at.col) & (self.at.col < 3))
                def _():
                    self.up(s, h).wait_send()

                @pl.when((s >= self.at.col) & (self.at.col > 0))
                def _():
                    self.down(s, h).wait_send()

            return 0

        lax.fori_loop(0, 4, one, 0)


class RowSumWhole:
    def __init__(self, at, product, out, a_send, a_recv, c_recv, d_send, d_recv, m_send, m_recv, x_send, x_recv):
        self.at, self.product, self.out = at, product, out
        self.a_send, self.a_recv, self.c_recv, self.d_send, self.d_recv = a_send, a_recv, c_recv, d_send, d_recv
        self.m_send, self.m_recv, self.x_send, self.x_recv = m_send, m_recv, x_send, x_recv
        self.half = product.shape[0] // 2
        self.d = remote(d_send, d_recv, m_send.at[2], m_recv.at[2], row=at.mate)

    def a(self, i):
        return remote(self.a_send.at[i], self.a_recv.at[i], self.m_send.at[i], self.m_recv.at[i], row=self.at.mate)

    def b(self, i, s):
        core = self.at.core
        return remote(self.a_recv.at[i], self.c_recv.at[core], self.x_send.at[i], self.x_recv.at[core], row=s)

    def part(self, core, here):
        return pl.ds(pl.multiple_of(core * self.half + here.start, here.size), here.size)

    def give(self, s):
        at, product, half = self.at, self.product, self.half
        i = lax.rem(s, 2)
        ours = lax.div(s, 2) == at.chip

        @pl.when(jnp.logical_not(ours))
        def _():
            def cast(here):
                self.a_send[i, here] = product[self.part(1 - at.core, here), :].astype(BF16)

            in_rows(half, 64, cast)
            self.a(i).start()
            self.a(i).wait_recv()

            def add(here):
                total = product[self.part(at.core, here), :] + self.a_recv[i, here].astype(F32)
                self.a_recv[i, here] = total.astype(BF16)

            in_rows(half, 64, add)
            self.b(i, s).start()

        @pl.when(ours & (i != at.core))
        def _():
            def cast(here):
                self.d_send[here] = product[here, :].astype(BF16)

            in_rows(2 * half, 64, cast)
            self.d.start()

        @pl.when(s == at.row)
        def _():
            def store(here):
                self.out[here] = product[here, :]

            in_rows(2 * half, 64, store)

    def finish(self):
        self.d.wait_recv()
        for h in range(2):
            here = self.c_recv.at[h]
            remote(here, here, self.x_send.at[h], self.x_recv.at[h], row=self.at.across).wait_recv()

            def add(rows, h=h):
                spot = pl.ds(pl.multiple_of(h * self.half + rows.start, rows.size), rows.size)
                self.out[spot] += self.d_recv[spot].astype(F32) + self.c_recv[h, rows].astype(F32)

            in_rows(self.half, 64, add)

    def close(self):
        self.d.wait_send()
        for i in range(2):
            self.a(i).wait_send()
            self.b(i, self.at.across).wait_send()


def row_sum_scratch(tokens, width):
    half = pltpu.VMEM((2, tokens // 2, width), BF16)
    full = pltpu.VMEM((tokens, width), BF16)
    return [half, half, half, full, full]


def row_sum_sems():
    dma = pltpu.SemaphoreType.DMA
    return [dma((3,)), dma((3,)), dma((2,)), dma((2,))]


class RowSumQuarter:
    def __init__(self, at, chunk, keep, a_send, a_recv, c_recv, d_send, d_recv, m_send, m_recv, x_send, x_recv):
        self.at, self.chunk, self.keep = at, chunk, keep
        self.a_send, self.a_recv, self.c_recv = a_send, a_recv, c_recv
        self.d_send, self.d_recv = d_send, d_recv
        self.sems = (m_send, m_recv, x_send, x_recv)

    def a(self, s):
        m_send, m_recv, _, _ = self.sems
        return remote(self.a_send.at[s], self.a_recv.at[s], m_send.at[0, s], m_recv.at[0, s], row=self.at.mate)

    def d(self, s):
        m_send, m_recv, _, _ = self.sems
        return remote(self.d_send.at[s], self.d_recv.at[s], m_send.at[1, s], m_recv.at[1, s], row=self.at.mate)

    def b(self, s):
        _, _, x_send, x_recv = self.sems
        return remote(self.a_recv.at[s], self.c_recv.at[s], x_send.at[s], x_recv.at[s], row=self.at.across)

    def split(self, s, value, spot, own):
        at, chunk = self.at, self.chunk
        chunk[...] = value

        def quarter(q):
            return chunk[pl.ds(pl.multiple_of(q * 128, 128), 128), :]

        self.a_send[s, :, spot] = quarter(at.diag).astype(BF16)
        self.keep[:, spot] = quarter(at.across)
        self.d_send[s, :, spot] = quarter(at.mate).astype(BF16)
        own[s, :, spot] = quarter(at.row).astype(own.dtype)

    def give(self, s):
        self.a(s).start()
        self.d(s).start()
        self.a(s).wait_recv()

        def one(here):
            self.a_recv[s, here] = (self.keep[here, :] + self.a_recv[s, here].astype(F32)).astype(BF16)

        in_rows(128, 16, one)
        self.b(s).start()

    def finish(self, s):
        self.d(s).wait_recv()
        self.b(s).wait_recv()

    def close(self):
        def one(s, _):
            self.a(s).wait_send()
            self.b(s).wait_send()
            self.d(s).wait_send()
            return 0

        lax.fori_loop(0, 4, one, 0)


class RowGather:
    def __init__(self, at, own, slot, sems):
        self.at, self.own, self.slot = at, own, slot
        self.m_send, self.m_recv, self.x_send, self.x_recv, self.f_send, self.f_recv, self.local = (*sems, None)[:7]

    def to_mate(self, s):
        return remote(self.own(s), self.slot(s, self.at.row), self.m_send.at[s], self.m_recv.at[s], row=self.at.mate)

    def to_across(self, s):
        return remote(self.own(s), self.slot(s, self.at.row), self.x_send.at[s], self.x_recv.at[s], row=self.at.across)

    def pass_on(self, s):
        here = self.slot(s, self.at.across)
        return remote(here, here, self.f_send.at[s], self.f_recv.at[s], row=self.at.mate)

    def move_own(self, s):
        return pltpu.make_async_copy(self.own(s), self.slot(s, self.at.row), self.local.at[s])

    def near(self, s):
        self.to_mate(s).start()
        if self.local is not None:
            self.move_own(s).start()

    def wait_near(self, s):
        here = self.slot(s, self.at.mate)
        remote(here, here, self.m_send.at[s], self.m_recv.at[s], row=self.at.mate).wait_recv()
        if self.local is not None:
            self.move_own(s).wait()

    def take_across(self, s):
        here = self.slot(s, self.at.across)
        remote(here, here, self.x_send.at[s], self.x_recv.at[s], row=self.at.across).wait_recv()
        self.pass_on(s).start()

    def wait_diag(self, s):
        here = self.slot(s, self.at.diag)
        remote(here, here, self.f_send.at[s], self.f_recv.at[s], row=self.at.mate).wait_recv()

    def close(self, count):
        def one(s, _):
            self.to_mate(s).wait_send()
            self.to_across(s).wait_send()
            self.pass_on(s).wait_send()
            return 0

        lax.fori_loop(0, count, one, 0)


class WeightGather:
    def __init__(self, at, pairs, own, full, sems):
        self.at, self.pairs, self.own, self.full = at, pairs, own, full
        self.m_send, self.m_recv, self.x_send, self.x_recv, self.y_send, self.y_recv = sems[:6]
        self.f_send, self.f_recv, self.g_send, self.g_recv = sems[6:]
        self.step = full.shape[2] // 4
        self.mine = lax.axis_index("dp") if pairs == 2 else None

    def rows(self, j):
        return pl.ds(j * self.step, self.step)

    def piece(self, which, row, j):
        return self.full.at[which, row, self.rows(j)]

    def held(self):
        return (self.mine,) if self.pairs == 2 else (0, 1)

    def near(self, which, row):
        here = self.full.at[which, row]
        return remote(self.own[which], here, self.m_send.at[which], self.m_recv.at[which], row=self.at.mate)

    def over(self, which, row, j, src=None):
        here = self.piece(which, row, j)
        lane = 0 if self.pairs == 2 else which
        src = here if src is None else src
        return remote(src, here, self.x_send.at[lane, j], self.x_recv.at[lane, j], row=self.at.across)

    def hand(self, which, j):
        here = self.piece(which, self.at.across, j)
        return remote(here, here, self.y_send.at[j], self.y_recv.at[j], dp=self.at.pair(2, 1))

    def pass_first(self, which, row, j):
        here = self.piece(which, row, j)
        lane = 0 if self.pairs == 2 else which
        return remote(here, here, self.f_send.at[lane, j], self.f_recv.at[lane, j], row=self.at.mate)

    def pass_second(self, which, row, j):
        here = self.piece(which, row, j)
        return remote(here, here, self.g_send.at[j], self.g_recv.at[j], row=self.at.mate)

    def begin(self):
        for i in range(2):
            self.near(i, self.at.row).start()

    def send(self, j):
        for which in range(2):
            copy = self.over(which, self.at.row, j, self.own[which].at[self.rows(j)])
            if self.pairs == 2:
                pl.when(self.mine == which)(copy.start)
            else:
                copy.start()

    def forward(self, j):
        for which in self.held():
            self.over(which, self.at.across, j).wait_recv()
            if self.pairs == 2:
                self.hand(which, j).start()
            self.pass_first(which, self.at.across, j).start()

    def finish(self, j):
        if self.pairs == 2:
            self.hand(1 - self.mine, j).wait_recv()
            self.pass_second(1 - self.mine, self.at.across, j).start()

    def close(self):
        for i in range(2):
            self.near(i, self.at.mate).wait_recv()
            self.near(i, self.at.row).wait_send()
        for j in range(4):
            for which in self.held():
                self.over(which, self.at.row, j).wait_send()
                self.pass_first(which, self.at.diag, j).wait_recv()
                self.pass_first(which, self.at.across, j).wait_send()
            if self.pairs == 2:
                self.hand(self.mine, j).wait_send()
                self.pass_second(1 - self.mine, self.at.diag, j).wait_recv()
                self.pass_second(1 - self.mine, self.at.across, j).wait_send()


def weight_gather_sems(pairs):
    dma = pltpu.SemaphoreType.DMA
    lanes = 1 if pairs == 2 else 2
    return [
        dma((2,)), dma((2,)), dma((lanes, 4)), dma((lanes, 4)), dma((4,)), dma((4,)),
        dma((lanes, 4)), dma((lanes, 4)), dma((4,)), dma((4,)),
    ]


class ColSum:
    def __init__(self, at, product, sent, got, extra, sends, recvs, extra_recvs):
        self.at, self.product, self.sent, self.got, self.extra = at, product, sent, got, extra
        self.sends, self.recvs, self.extra_recvs = sends, recvs, extra_recvs
        self.half = product.shape[0] // 2

    def part(self, h):
        return pl.ds(h * self.half, self.half)

    def up(self, s, h):
        return remote(
            self.sent.at[s, self.part(h)], self.got.at[s, self.part(h)],
            self.sends.at[s, h], self.recvs.at[s, h], col=self.at.col + 1,
        )

    def down(self, s, h):
        return remote(
            self.sent.at[s, self.part(h)], self.got.at[s, self.part(h)],
            self.sends.at[s, h], self.recvs.at[s, h], col=self.at.col - 1,
        )

    def last_down(self, s, h):
        return remote(
            self.sent.at[s, self.part(h)], self.extra.at[self.part(h)],
            self.sends.at[s, h], self.extra_recvs.at[h], col=self.at.col - 1,
        )

    def step(self, s):
        col, product = self.at.col, self.product
        for h in range(2):
            @pl.when(((s >= col) & (col > 0)) | ((s < col) & (col < 3)))
            def _():
                self.up(s, h).wait_recv()

                def add(here):
                    product[here, :] += self.got[s, here].astype(F32)

                in_rows(self.half, 64, add, h * self.half)

            @pl.when((s == col) & (col < 3))
            def _():
                self.last_down(s, h).wait_recv()

                def add(here):
                    product[here, :] += self.extra[here].astype(F32)

                in_rows(self.half, 64, add, h * self.half)

            @pl.when(s != col)
            def _():
                def cast(here):
                    self.sent[s, here] = product[here, :].astype(BF16)

                in_rows(self.half, 64, cast, h * self.half)

            pl.when(s > col)(lambda: self.up(s, h).start())
            pl.when(s < col - 1)(lambda: self.down(s, h).start())
            pl.when(s == col - 1)(lambda: self.last_down(s, h).start())

    def close(self):
        def one(s, _):
            for h in range(2):
                pl.when(s != self.at.col)(lambda: self.up(s, h).wait_send())
            return 0

        lax.fori_loop(0, 4, one, 0)


def far_first(col, j):
    first = jnp.where(col < 2, 3, 0)
    second = jnp.where(col < 2, 2, 1)
    third = jnp.where(lax.rem(col, 2) == 0, col + 1, col - 1)
    return (first, second, third, col)[j]


def near_first(at, j):
    first, second, partner, _ = [far_first(at.col, i) for i in range(4)]
    mine = lax.div(at.col, 2) == at.chip
    return (
        jnp.where(mine, partner, first),
        jnp.where(mine, first, second),
        jnp.where(mine, second, partner),
        at.col,
    )[j]


def turn_tables(length):
    rates = THETA ** (-np.arange(HEAD_SIZE // 2) * 2.0 / HEAD_SIZE)
    angles = np.arange(length)[:, None] * rates[None, :]
    cos, sin = np.cos(angles), np.sin(angles)
    return (
        np.concatenate([cos, cos], axis=1).astype(np.float32),
        np.concatenate([-sin, sin], axis=1).astype(np.float32),
    )


def swap_halves(value):
    return pltpu.roll(value, HEAD_SIZE // 2, 1)


def head(ref, index):
    return ref[:, index * HEAD_SIZE : (index + 1) * HEAD_SIZE]


def root_scale(raw):
    return lax.rsqrt(jnp.mean(raw * raw, axis=1, keepdims=True) + EPSILON)


def attend(q_heads, groups, qkv, seg_col, seg_row, cos, sin, q_gain, k_gain, o, qa, ka, va, probs):
    kv = q_heads // groups
    tokens = qkv.shape[0]
    half = tokens // 2

    def turned(index, gain):
        raw = head(qkv, index)
        normed = raw * root_scale(raw) * gain[...]
        return (normed * cos[...] + swap_halves(normed) * sin[...]).astype(BF16)

    for i in range(q_heads):
        qa[:, i * HEAD_SIZE : (i + 1) * HEAD_SIZE] = turned(i, q_gain)
    for i in range(kv):
        ka[:, i * HEAD_SIZE : (i + 1) * HEAD_SIZE] = turned(q_heads + i, k_gain)
        va[:, i * HEAD_SIZE : (i + 1) * HEAD_SIZE] = head(qkv, q_heads + kv + i).astype(BF16)
    for block in range(2):
        rows = slice(block * half, (block + 1) * half)
        keys = (block + 1) * half
        spot = lax.broadcasted_iota(jnp.int32, (half, keys), 0) + block * half
        other = lax.broadcasted_iota(jnp.int32, (half, keys), 1)
        allowed = (other <= spot) & (seg_col[rows, :] == seg_row[:, :keys])
        for i in range(q_heads):
            j = i // groups
            dots = lax.dot_general(
                head(qa, i)[rows], head(ka, j)[:keys], (((1,), (1,)), ((), ())), preferred_element_type=F32
            ) * (1.0 / math.sqrt(HEAD_SIZE))
            scores = jnp.where(allowed, dots, MASKED)
            expo = jnp.exp(scores - jnp.max(scores, axis=1, keepdims=True))
            p = expo / jnp.sum(expo, axis=1, keepdims=True)
            probs[i, rows, :keys] = p.astype(BF16)
            mixed = jnp.dot(p.astype(BF16), head(va, j)[:keys], preferred_element_type=F32)
            o[rows, i * HEAD_SIZE : (i + 1) * HEAD_SIZE] = mixed.astype(BF16)


def front_kernel(pairs, q_heads, groups, model_width, *refs):
    refs = list(refs)

    def take(count):
        found = refs[:count]
        del refs[:count]
        return found

    (x_ref, gy, w_query, w_key, w_value, w_out, w_down, seg_col, seg_row, cos, sin, q_gain, k_gain, gain_one, gain_two) = take(15)
    (w_gate, w_up) = take(2)
    (scale_one, hidden, scale_two, ffn_in, dact, qkv, qa, ka, va, probs) = take(10)
    (xn_out, gy_out, mixed_out, full) = take(4)
    (xn_wide, gy_wide, mixed_wide, mixed, product, chunk, keep) = take(7)
    total_bufs = take(2)
    second_bufs = take(2)
    moved = take(5)
    moved_q = take(5)
    chain = take(3)
    x_sems, gy_sems = take(2), take(2)
    (local,) = take(1)
    moved_sems, moved_q_sems = take(4), take(4)
    mixed_sems = take(7)
    chain_sems = take(3)
    total_sems, second_sems = take(2), take(2)
    full_sems = take(10)

    at = Ends()
    full_gather = WeightGather(at, pairs, (w_gate, w_up), full, full_sems)
    tokens, feats = x_ref.shape
    first_total = RowTotal(at, *total_bufs, *total_sems)
    second_total = RowTotal(at, *second_bufs, *second_sems)
    x_gather = ColGather(at, xn_wide, *x_sems)
    gy_gather = ColGather(at, gy_wide, *gy_sems)
    row_sum = RowSumWhole(at, product, qkv, *moved, *moved_sems)
    quarter_sum = RowSumQuarter(at, chunk, keep, *moved_q, *moved_q_sems)
    mixes = RowGather(at, lambda s: mixed, lambda s, q: mixed_wide.at[q], mixed_sems)
    out_sum = ColSum(at, hidden, *chain, *chain_sems)

    gy_wide[at.col] = gy[...]
    at.greet(pairs if pairs == 2 else 0)
    stream = x_ref[...].astype(F32)
    first_total.start(jnp.sum(stream * stream, axis=1, keepdims=True))
    full_gather.begin()
    full_gather.send(0)
    scale = lax.rsqrt(first_total.finish() / model_width + EPSILON)
    scale_one[...] = scale
    xn_wide[at.col] = (x_ref[...].astype(F32) * scale * gain_one[...]).astype(BF16)

    def project(s):
        base = 0
        for w in (w_query, w_key, w_value):
            size = w.shape[1]
            product[:, base : base + size] = jnp.dot(xn_wide[s], w[...], preferred_element_type=F32)
            base += size
        row_sum.give(s)

    def back_down(s):
        size = chunk.shape[1]

        def one(j, _):
            cols = pl.ds(pl.multiple_of(j * size, size), size)
            value = lax.dot_general(
                gy_wide[s], w_down[cols, :], (((1,), (1,)), ((), ())), preferred_element_type=F32
            )
            quarter_sum.split(s, value, cols, dact)
            return 0

        lax.fori_loop(0, w_down.shape[0] // size, one, 0)
        quarter_sum.give(s)

    def end_down(s):
        quarter_sum.finish(s)

        def add(here):
            dact[s, here] += moved_q[2][s, here].astype(F32) + moved_q[4][s, here].astype(F32)

        in_rows(128, 16, add)

    def send_gy(dist):
        @pl.when((at.col == dist) & (at.col < 3))
        def _():
            gy_gather.send_up()

        @pl.when((at.col == 3 - dist) & (at.col > 0))
        def _():
            gy_gather.send_down()

    def out_step(j):
        s = near_first(at, j)
        hidden[...] = jnp.dot(mixed_wide[s], w_out[...], preferred_element_type=F32)
        out_sum.step(s)

    mid = jnp.logical_not(at.end)
    x_gather.arrive(0)
    send_gy(0)
    x_gather.loop(0, project)
    back_down(at.col)
    full_gather.send(1)
    for dist in range(1, 4):
        x_gather.arrive(dist)
        send_gy(dist)
        x_gather.loop(dist, project)
        if dist < 3:
            full_gather.forward(dist - 1)

    @pl.when(mid)
    def _():
        gy_gather.arrive(1)

    row_sum.finish()
    full_gather.send(2)
    attend(q_heads, groups, qkv, seg_col, seg_row, cos, sin, q_gain, k_gain, mixed, qa, ka, va, probs)
    mixes.to_across(0).start()
    mixes.near(0)
    full_gather.send(3)

    @pl.when(mid)
    def _():
        gy_gather.arrive(2)

    mixes.wait_near(0)

    @pl.when(at.end)
    def _():
        out_step(0)
        gy_gather.arrive(1)

    gy_gather.loop(1, back_down)
    full_gather.forward(2)
    full_gather.finish(0)
    mixes.take_across(0)
    mixes.wait_diag(0)

    @pl.when(at.end)
    def _():
        out_step(1)
        out_step(2)
        gy_gather.arrive(2)

    @pl.when(mid)
    def _():
        out_step(0)

    gy_gather.loop(2, back_down)
    full_gather.forward(3)
    full_gather.finish(1)

    @pl.when(mid)
    def _():
        out_step(1)
        out_step(2)

    @pl.when(at.end)
    def _():
        gy_gather.arrive(3)

    gy_gather.loop(3, back_down)
    wides = [
        pltpu.make_async_copy(src, dst, local.at[i])
        for i, (src, dst) in enumerate(((xn_wide, xn_out), (gy_wide, gy_out), (mixed_wide, mixed_out)))
    ]
    for copy in wides:
        copy.start()
    full_gather.finish(2)
    for dist in range(3):
        gy_gather.loop(dist, end_down)
    full_gather.finish(3)
    out_step(3)

    def residual(here):
        hidden[here, :] += x_ref[here, :].astype(F32)

    in_rows(tokens, 64, residual)
    value = hidden[...]
    second_total.start(jnp.sum(value * value, axis=1, keepdims=True))
    gy_gather.loop(3, end_down)
    scale = lax.rsqrt(second_total.finish() / model_width + EPSILON)
    scale_two[...] = scale
    ffn_in[...] = (hidden[...] * scale * gain_two[...]).astype(BF16)

    full_gather.close()
    x_gather.close()
    gy_gather.close()
    row_sum.close()
    quarter_sum.close()
    mixes.close(1)
    out_sum.close()
    for copy in wides:
        copy.wait()


def col_gather_sems():
    return [pltpu.SemaphoreType.DMA((2, 4, 2)), pltpu.SemaphoreType.DMA((4, 2))]


def chain_scratch(tokens, feats):
    return [
        pltpu.VMEM((4, tokens, feats), BF16), pltpu.VMEM((4, tokens, feats), BF16), pltpu.VMEM((tokens, feats), BF16),
    ]


def chain_sems():
    dma = pltpu.SemaphoreType.DMA
    return [dma((4, 2)), dma((4, 2)), dma((2,))]


def front(pairs, q_heads, groups, model_width, number, x, gy, weights, segments, tables, gains, ffn_weights):
    tokens, feats = x.shape
    w_query, w_key, w_value, w_out, w_down = weights
    width = w_query.shape[1] + w_key.shape[1] + w_value.shape[1]
    q_width, k_width, ff = w_query.shape[1], w_key.shape[1], w_down.shape[0]
    dma = pltpu.SemaphoreType.DMA
    any_spec, vmem = pl.BlockSpec(memory_space=pl.ANY), pl.BlockSpec(memory_space=pltpu.VMEM)
    shape = jax.ShapeDtypeStruct
    wide = pltpu.VMEM((4, tokens, feats), BF16)
    return pl.pallas_call(
        functools.partial(front_kernel, pairs, q_heads, groups, model_width),
        out_shape=(
            shape((tokens, 1), F32),
            shape((tokens, feats), F32),
            shape((tokens, 1), F32),
            shape((tokens, feats), BF16),
            shape((4, tokens // 4, ff), F32),
            shape((tokens, width), F32),
            shape((tokens, q_width), BF16),
            shape((tokens, k_width), BF16),
            shape((tokens, k_width), BF16),
            shape((q_heads, tokens, tokens), BF16),
            shape((4, tokens, feats), BF16),
            shape((4, tokens, feats), BF16),
            shape((4, tokens, q_width), BF16),
            shape((2, 4, *ffn_weights[0].shape), BF16),
        ),
        in_specs=[vmem] * 15 + [any_spec] * 2,
        out_specs=tuple([vmem] * 10 + [any_spec] * 4),
        scratch_shapes=[
            wide,
            wide,
            pltpu.VMEM((4, tokens, q_width), BF16),
            pltpu.VMEM((tokens, q_width), BF16),
            pltpu.VMEM((tokens, width), F32),
            pltpu.VMEM((tokens, 512), F32),
            pltpu.VMEM((tokens // 4, ff), F32),
        ]
        + row_total_scratch(tokens) * 2
        + row_sum_scratch(tokens, width)
        + [pltpu.VMEM((4, tokens // 4, ff), BF16)] * 5
        + chain_scratch(tokens, feats)
        + col_gather_sems() * 2
        + [dma((3,))]
        + row_sum_sems()
        + [dma((2, 4)), dma((2, 4)), dma((4,)), dma((4,))]
        + [dma((1,))] * 7
        + chain_sems()
        + row_total_sems() * 2
        + weight_gather_sems(pairs),
        compiler_params=pltpu.CompilerParams(
            collective_id=number, has_side_effects=True, vmem_limit_bytes=VMEM_LIMIT
        ),
        name="front",
    )(x, gy, *weights, *segments, *tables, *gains, *ffn_weights)


def across_rows(left, right):
    return lax.dot_general(left, right, (((0,), (0,)), ((), ())), preferred_element_type=F32)


def attend_back(q_heads, groups, grad, qkv, qa, ka, va, probs, cos, sin, q_gain, k_gain, out, q_part, k_part, dq, dk, dv):
    kv = q_heads // groups
    tokens = qkv.shape[0]
    half = tokens // 2
    scale = 1.0 / math.sqrt(HEAD_SIZE)
    dk[...] = jnp.zeros_like(dk)
    dv[...] = jnp.zeros_like(dv)
    for block in range(2):
        rows = slice(block * half, (block + 1) * half)
        keys = (block + 1) * half
        for i in range(q_heads):
            j = i // groups
            spot = slice(j * HEAD_SIZE, (j + 1) * HEAD_SIZE)
            pb = probs[i, rows, :keys]
            p = pb.astype(F32)
            g = head(grad, i)[rows].astype(BF16)
            dv[:keys, spot] += across_rows(pb.astype(BF16), g)
            dp = lax.dot_general(
                g, head(va, j)[:keys], (((1,), (1,)), ((), ())), preferred_element_type=F32
            )
            ds = (p * (dp - jnp.sum(p * dp, axis=1, keepdims=True))).astype(BF16)
            dq[rows, i * HEAD_SIZE : (i + 1) * HEAD_SIZE] = (
                jnp.dot(ds, head(ka, j)[:keys], preferred_element_type=F32) * scale
            )
            dk[:keys, spot] += across_rows(ds, head(qa, i)[rows]) * scale

    def back(turned, index, gain):
        raw = head(qkv, index)
        scales = root_scale(raw)
        normed = turned * cos[...] - swap_halves(turned) * sin[...]
        part = jnp.sum(normed * raw * scales, axis=0, keepdims=True)
        weighted = normed * gain[...]
        inner = jnp.sum(weighted * raw, axis=1, keepdims=True)
        result = scales * weighted - raw * (scales * scales * scales) * inner * (1.0 / HEAD_SIZE)
        out[:, index * HEAD_SIZE : (index + 1) * HEAD_SIZE] = result.astype(BF16)
        return part

    q_part[...] = sum(back(head(dq, i), i, q_gain) for i in range(q_heads))
    k_part[...] = sum(back(head(dk, i), q_heads + i, k_gain) for i in range(kv))
    for i in range(kv):
        spot = (q_heads + kv + i) * HEAD_SIZE
        out[:, spot : spot + HEAD_SIZE] = head(dv, i).astype(BF16)


def weight_grad(out, left, right):
    def block(here):
        total = None
        for s in range(4):
            term = across_rows(left(s, here), right(s))
            total = term if total is None else total + term
        out[here, :] = total.astype(BF16)

    in_rows(out.shape[0], 256, block)


def middle_kernel(pairs, *refs):
    refs = list(refs)

    def take(count):
        found = refs[:count]
        del refs[:count]
        return found

    (hn, w_gate, w_up, dact, full) = take(5)
    (dhn, act, gate_n, up_n) = take(4)
    others = take(1) if pairs == 2 else []
    (hn_wide, hn_full, weights, gate_up, gate_wide, up_wide, n_gate, n_up) = take(8)
    chain = take(3)
    hn_sems = take(2)
    (full_sem, share_send, share_recv) = take(3)
    gate_sems, up_sems = take(6), take(6)
    chain_sems_ = take(3)
    (local, y_send, y_recv) = take(3)

    at = Ends()
    ff = w_gate.shape[1]
    quarter = act.shape[1]
    gather = ColGather(at, hn_wide, *hn_sems)
    loads = []
    for which, own in enumerate((w_gate, w_up)):
        for i, r in enumerate((at.mate, at.across, at.diag, at.row)):
            src = own if i == 3 else full.at[which, r]
            loads.append(pltpu.make_async_copy(src, weights.at[which, r], full_sem.at[which, i]))
    for load in loads:
        load.start()
    gates = RowGather(at, lambda s: gate_wide.at[s, at.row], lambda s, q: gate_wide.at[s, q], gate_sems)
    ups = RowGather(at, lambda s: up_wide.at[s, at.row], lambda s, q: up_wide.at[s, q], up_sems)
    back_sum = ColSum(at, dhn, *chain, *chain_sems_)

    hn_wide[at.col] = hn[...]
    at.greet(pairs if pairs == 2 else 0)

    peers = (at.mate, at.across, at.diag)

    def share(s):
        hn_full[s, at.row] = hn_wide[s, pl.ds(pl.multiple_of(at.row * quarter, quarter), quarter)]
        for i, peer in enumerate(peers):
            theirs = hn_wide.at[s, pl.ds(pl.multiple_of(peer * quarter, quarter), quarter)]
            remote(theirs, hn_full.at[s, at.row], share_send.at[s, i], share_recv.at[s, i], row=peer).start()

    def hidden_units(s):
        for i, peer in enumerate(peers):
            here = hn_full.at[s, peer]
            remote(here, here, share_send.at[s, i], share_recv.at[s, i], row=peer).wait_recv()
        size = gate_up.shape[2]

        def some(j, _):
            cols = pl.ds(pl.multiple_of(j * size, size), size)
            for which in range(2):
                total = None
                for r in range(4):
                    term = jnp.dot(hn_full[s, r], weights[which, r, :, cols], preferred_element_type=F32)
                    total = term if total is None else total + term
                gate_up[which] = total

            def one(here):
                gate, up = gate_up[0, here], gate_up[1, here]
                grad = dact[s, here, cols]
                sigmoid = jax.nn.sigmoid(gate)
                silu = gate * sigmoid
                act[s, here, cols] = (silu * up).astype(BF16)
                gate_wide[s, at.row, here, cols] = (
                    grad * up * (sigmoid * (1.0 + gate * (1.0 - sigmoid)))
                ).astype(BF16)
                up_wide[s, at.row, here, cols] = (grad * silu).astype(BF16)

            in_rows(quarter, 16, one)
            return 0

        lax.fori_loop(0, ff // size, some, 0)
        gates.to_across(s).start()
        gates.near(s)
        ups.near(s)

    def close_share(s):
        for i, peer in enumerate(peers):
            here = hn_full.at[s, peer]
            remote(here, here, share_send.at[s, i], share_recv.at[s, i], row=peer).wait_send()

    def rows_of(ref, s):
        return ref[s].reshape(4 * quarter, ff)

    def back(j):
        s = far_first(at.col, j)
        contract = (((1,), (1,)), ((), ()))
        dhn[...] = lax.dot_general(
            rows_of(gate_wide, s), w_gate[...], contract, preferred_element_type=F32
        ) + lax.dot_general(rows_of(up_wide, s), w_up[...], contract, preferred_element_type=F32)

    def arrive(some, j):
        s = far_first(at.col, j)
        some.wait_near(s)
        some.take_across(s)
        some.wait_diag(s)

    def left(s, here):
        return hn_wide[s, :, here]

    mid = jnp.logical_not(at.end)
    gather.arrive(0)
    gather.loop(0, share)
    gather.arrive(1)
    gather.loop(1, share)
    for load in loads:
        load.wait()
    gather.loop(0, hidden_units)
    gather.arrive(2)
    gather.loop(2, share)
    gather.loop(1, hidden_units)
    gather.arrive(3)
    gather.loop(3, share)
    gather.loop(2, hidden_units)
    gather.loop(3, hidden_units)
    for j in range(4):
        ups.to_across(far_first(at.col, j)).start()
    for j in range(4):
        arrive(gates, j)
    weight_grad(n_gate, left, lambda s: rows_of(gate_wide, s))
    pair = remote(n_gate, others[0], y_send.at[0], y_recv.at[0], dp=at.pair(2, 1)) if pairs == 2 else None
    if pairs == 2:
        pair.start()
    keep_gate = pltpu.make_async_copy(n_gate, gate_n, local.at[0])
    keep_gate.start()
    arrive(ups, 0)
    for j in range(3):
        back(j)
        pl.when(at.end)(lambda: back_sum.step(far_first(at.col, j)))
        arrive(ups, j + 1)
        pl.when(mid)(lambda: back_sum.step(far_first(at.col, j)))
    weight_grad(n_up, left, lambda s: rows_of(up_wide, s))
    keep_up = pltpu.make_async_copy(n_up, up_n, local.at[1])
    keep_up.start()
    back(3)
    back_sum.step(at.col)

    gather.close()
    for dist in range(4):
        gather.loop(dist, close_share)
    gates.close(4)
    ups.close(4)
    back_sum.close()
    keep_gate.wait()
    keep_up.wait()
    if pairs == 2:
        pair.wait()


def middle(pairs, number, hn, w_gate, w_up, dact, full):
    tokens, feats = hn.shape
    ff = w_gate.shape[1]
    quarter = tokens // 4
    dma = pltpu.SemaphoreType.DMA
    any_spec, vmem = pl.BlockSpec(memory_space=pl.ANY), pl.BlockSpec(memory_space=pltpu.VMEM)
    shape = jax.ShapeDtypeStruct
    narrow = shape((feats, ff), BF16)
    others = 1 if pairs == 2 else 0
    out = pl.pallas_call(
        functools.partial(middle_kernel, pairs),
        out_shape=tuple(
            [shape((tokens, feats), F32), shape((4, quarter, ff), BF16), narrow, narrow] + [narrow] * others
        ),
        in_specs=[vmem] * 4 + [any_spec],
        out_specs=tuple([vmem] * 2 + [any_spec] * (2 + others)),
        scratch_shapes=[
            pltpu.VMEM((4, tokens, feats), BF16),
            pltpu.VMEM((4, 4, quarter, feats), BF16),
            pltpu.VMEM((2, 4, feats, ff), BF16),
            pltpu.VMEM((2, quarter, 512), F32),
            pltpu.VMEM((4, 4, quarter, ff), BF16),
            pltpu.VMEM((4, 4, quarter, ff), BF16),
            pltpu.VMEM((feats, ff), BF16),
            pltpu.VMEM((feats, ff), BF16),
        ]
        + chain_scratch(tokens, feats)
        + col_gather_sems()
        + [dma((2, 4)), dma((4, 3)), dma((4, 3))]
        + [dma((4,))] * 12
        + chain_sems()
        + [dma((2,)), dma((1,)), dma((1,))],
        compiler_params=pltpu.CompilerParams(
            collective_id=number, has_side_effects=True, vmem_limit_bytes=VMEM_LIMIT
        ),
        name="middle",
    )(hn, w_gate, w_up, dact, full)
    return out[:4], out[4:]


def tail_kernel(pairs, q_heads, groups, *refs):
    refs = list(refs)

    def take(count):
        found = refs[:count]
        del refs[:count]
        return found

    (act, w_out, w_down, w_query, w_key, w_value, qkv, qa, ka, va, probs, cos, sin, q_gain, k_gain) = take(15)
    (dhn, hidden, scale_two, gain_two, gy, x_ref, scale_one, gain_one) = take(8)
    (gy_wide, mixed_wide, normed_wide, up_n) = take(4)
    (in_grad, layer_out, one_grad, two_grad, q_grad, k_grad, down_n, out_n, qkv_n) = take(9)
    others = take(4) if pairs == 2 else []
    (da_wide, act_wide, dqkv, dqkv_wide, held, product, grad_mixed, dq, dk, dv, n_down, n_out, n_qkv) = take(13)
    (dh, q_part, k_part, packet, packet_got, by_row, summed, summed_got) = take(8)
    first_bufs, last_bufs = take(2), take(2)
    moved = take(5)
    down_bufs, dxn_bufs = take(3), take(3)
    (g_send, g_recv, local, y_send, y_recv) = take(5)
    moved_sems = take(4)
    act_sems, dqkv_sems = take(7), take(7)
    down_sems, dxn_sems = take(3), take(3)
    first_sems, last_sems = take(2), take(2)
    (p_send, p_recv, r_send, r_recv, s_send, s_recv) = take(6)

    at = Ends()
    model_width = 4 * dhn.shape[1]
    first_total = RowTotal(at, *first_bufs, *first_sems)
    last_total = RowTotal(at, *last_bufs, *last_sems)
    at.greet(pairs, True)

    def pair_copy(src, index):
        return remote(src, others[index], y_send.at[index], y_recv.at[index], dp=1 - lax.axis_index("dp"))

    narrow = (up_n, n_down, n_out, n_qkv)

    def to_pair(index):
        if pairs == 2:
            pair_copy(narrow[index], index).start()

    def load(index, src):
        return pltpu.make_async_copy(src, held, local.at[index])

    def keep(index, src, dst):
        return pltpu.make_async_copy(src, dst, local.at[3 + index])

    to_pair(0)
    load(0, gy_wide).start()
    gather = ColGather(at, da_wide, g_send, g_recv)
    row_sum = RowSumWhole(at, product, grad_mixed, *moved, *moved_sems)
    acts = RowGather(at, lambda s: act.at[s], lambda s, q: act_wide.at[s, q], act_sems)
    grads = RowGather(at, lambda s: dqkv, lambda s, q: dqkv_wide.at[q], dqkv_sems)
    down_sum = ColSum(at, product, *down_bufs, *down_sems)
    dxn_sum = ColSum(at, product, *dxn_bufs, *dxn_sems)

    weighted = dhn[...] * gain_two[...]
    first_total.start(jnp.sum(weighted * hidden[...], axis=1, keepdims=True))
    for j in range(2):
        acts.to_across(far_first(at.col, j)).start()
    for j in range(4):
        acts.near(far_first(at.col, j))
    scale = scale_two[...]
    packet[...] = jnp.zeros_like(packet)
    packet[1:2, :] = jnp.sum(dhn[...] * hidden[...] * scale, axis=0, keepdims=True)
    inner = first_total.finish()
    dh[...] = (
        gy[...].astype(F32)
        + scale * (dhn[...] * gain_two[...])
        - hidden[...] * (scale * scale * scale * inner * (1.0 / model_width))
    )
    da_wide[at.col] = dh[...].astype(BF16)
    gather.arrive(0)

    def back_out(s):
        product[...] = lax.dot_general(
            da_wide[s], w_out[...], (((1,), (1,)), ((), ())), preferred_element_type=F32
        )
        row_sum.give(s)

    def take_act(j):
        s = far_first(at.col, j)
        if j < 2:
            acts.to_across(far_first(at.col, j + 2)).start()
        acts.wait_near(s)
        acts.take_across(s)
        acts.wait_diag(s)

    def act_rows(s, cols):
        return act_wide[s, :, :, cols].reshape(product.shape[0], cols.size)

    def down_step(j):
        s = far_first(at.col, j)
        product[...] = jnp.dot(
            act_rows(s, pl.ds(0, act.shape[2])), w_down[...], preferred_element_type=F32
        )
        down_sum.step(s)

    def dxn_step(j):
        s = near_first(at, j)
        total, base = None, 0
        for w in (w_query, w_key, w_value):
            size = w.shape[1]
            term = lax.dot_general(
                dqkv_wide[s, :, pl.ds(base, size)], w[...], (((1,), (1,)), ((), ())), preferred_element_type=F32
            )
            total = term if total is None else total + term
            base += size
        product[...] = total
        dxn_sum.step(s)

    gather.loop(0, back_out)
    take_act(0)
    gather.arrive(1)
    gather.loop(1, back_out)
    down_step(0)
    gather.arrive(2)
    gather.loop(2, back_out)
    take_act(1)
    down_step(1)
    gather.arrive(3)
    gather.loop(3, back_out)

    @pl.when(at.end)
    def _():
        take_act(2)
        down_step(2)

    row_sum.finish()
    attend_back(
        q_heads, groups, grad_mixed, qkv, qa, ka, va, probs, cos, sin, q_gain, k_gain,
        dqkv, q_part, k_part, dq, dk, dv,
    )
    grads.to_across(0).start()
    grads.near(0)
    grads.wait_near(0)

    @pl.when(at.end)
    def _():
        dxn_step(0)

    @pl.when(jnp.logical_not(at.end))
    def _():
        take_act(2)
        down_step(2)

    take_act(3)
    load(0, gy_wide).wait()
    weight_grad(n_down, act_rows, lambda s: held[s])
    to_pair(1)
    keep(0, n_down, down_n).start()
    load(1, mixed_wide).start()

    @pl.when(jnp.logical_not(at.end))
    def _():
        dxn_step(0)

    load(1, mixed_wide).wait()
    weight_grad(n_out, lambda s, here: held[s, :, here], lambda s: da_wide[s])
    to_pair(2)
    keep(1, n_out, out_n).start()
    load(2, normed_wide).start()
    grads.take_across(0)
    grads.wait_diag(0)

    @pl.when(at.end)
    def _():
        dxn_step(1)
        dxn_step(2)

    load(2, normed_wide).wait()
    weight_grad(n_qkv, lambda s, here: held[s, :, here], lambda s: dqkv_wide[s])
    to_pair(3)
    keep(2, n_qkv, qkv_n).start()

    @pl.when(jnp.logical_not(at.end))
    def _():
        dxn_step(1)
        dxn_step(2)

    down_step(3)
    layer_out[...] = (hidden[...] + product[...]).astype(BF16)
    dxn_step(3)
    scale = scale_one[...]
    last_total.start(
        jnp.sum(product[...] * gain_one[...] * x_ref[...].astype(F32), axis=1, keepdims=True)
    )
    packet[0:1, :] = jnp.sum(product[...] * x_ref[...].astype(F32) * scale, axis=0, keepdims=True)
    packet[2:3, :HEAD_SIZE] = q_part[...]
    packet[2:3, HEAD_SIZE : 2 * HEAD_SIZE] = k_part[...]

    def to_line(step):
        return remote(
            packet, packet_got.at[step - 1], p_send.at[step - 1], p_recv.at[step - 1],
            col=lax.rem(at.col + step, 4),
        )

    def to_row(index, peer):
        return remote(by_row.at[at.row], by_row.at[at.row], r_send.at[index], r_recv.at[index], row=peer)

    def from_row(index, peer):
        return remote(by_row.at[peer], by_row.at[peer], r_send.at[index], r_recv.at[index], row=peer)

    def to_peer(step):
        return remote(
            summed, summed_got.at[step - 1], s_send.at[step - 1], s_recv.at[step - 1], dp=at.pair(pairs, step)
        )

    for step in range(1, 4):
        to_line(step).start()
    inner = last_total.finish()
    in_grad[...] = (
        dh[...]
        + scale * (product[...] * gain_one[...])
        - x_ref[...].astype(F32) * (scale * scale * scale * inner * (1.0 / model_width))
    )
    for step in range(1, 4):
        to_line(step).wait()
    by_row[at.row] = (packet[...] + packet_got[0]) + (packet_got[1] + packet_got[2])
    peers = (at.mate, at.across, at.diag)
    for index, peer in enumerate(peers):
        to_row(index, peer).start()
    for index, peer in enumerate(peers):
        from_row(index, peer).wait_recv()
        to_row(index, peer).wait_send()
    summed[...] = jnp.zeros_like(summed)
    for r in range(4):
        summed[r : r + 1, :] = by_row[r, 0:1, :]
        summed[4 + r : 5 + r, :] = by_row[r, 1:2, :]
    summed[8:9, :] = (by_row[0, 2:3, :] + by_row[1, 2:3, :]) + (by_row[2, 2:3, :] + by_row[3, 2:3, :])
    for step in range(1, pairs):
        to_peer(step).start()
    for step in range(1, pairs):
        to_peer(step).wait()
    total = summed[...]
    for step in range(1, pairs):
        total = total + summed_got[step - 1]
    one_grad[...] = total[0:4, :]
    two_grad[...] = total[4:8, :]
    q_grad[...] = total[8:9, :HEAD_SIZE]
    k_grad[...] = total[8:9, HEAD_SIZE : 2 * HEAD_SIZE]

    gather.close()
    row_sum.close()
    acts.close(4)
    grads.close(1)
    down_sum.close()
    dxn_sum.close()
    keep(0, n_down, down_n).wait()
    keep(1, n_out, out_n).wait()
    keep(2, n_qkv, qkv_n).wait()
    if pairs == 2:
        for index in range(4):
            pair_copy(narrow[index], index).wait()


def tail(pairs, q_heads, groups, number, act, weights, saved, tables, norms, wides, narrow):
    tokens, feats = norms[0].shape
    w_out, w_down = weights[:2]
    ff = w_down.shape[0]
    width = saved[0].shape[1]
    q_width, k_width = saved[1].shape[1], saved[2].shape[1]
    dma = pltpu.SemaphoreType.DMA
    any_spec, vmem = pl.BlockSpec(memory_space=pl.ANY), pl.BlockSpec(memory_space=pltpu.VMEM)
    shape = jax.ShapeDtypeStruct
    shapes = [
        shape((tokens, feats), F32),
        shape((tokens, feats), BF16),
        shape((4, feats), F32),
        shape((4, feats), F32),
        shape((1, HEAD_SIZE), F32),
        shape((1, HEAD_SIZE), F32),
    ]
    own = [shape((ff, feats), BF16), shape((q_width, feats), BF16), shape((feats, width), BF16)]
    others = [shape(n.shape, BF16) for n in narrow] + own if pairs == 2 else []
    packet = pltpu.VMEM((8, feats), F32)
    operands = (act, *weights, *saved, *tables, *norms)
    out = pl.pallas_call(
        functools.partial(tail_kernel, pairs, q_heads, groups),
        out_shape=tuple(shapes + own + others),
        in_specs=[vmem] * len(operands) + [any_spec] * 4,
        out_specs=tuple([vmem] * 6 + [any_spec] * (3 + len(others))),
        scratch_shapes=[
            pltpu.VMEM((4, tokens, feats), BF16),
            pltpu.VMEM((4, 4, tokens // 4, ff), BF16),
            pltpu.VMEM((tokens, width), BF16),
            pltpu.VMEM((4, tokens, width), BF16),
            pltpu.VMEM((4, tokens, feats), BF16),
            pltpu.VMEM((tokens, feats), F32),
            pltpu.VMEM((tokens, q_width), F32),
            pltpu.VMEM((tokens, q_width), F32),
            pltpu.VMEM((tokens, k_width), F32),
            pltpu.VMEM((tokens, k_width), F32),
            pltpu.VMEM((ff, feats), BF16),
            pltpu.VMEM((q_width, feats), BF16),
            pltpu.VMEM((feats, width), BF16),
            pltpu.VMEM((tokens, feats), F32),
            pltpu.VMEM((1, HEAD_SIZE), F32),
            pltpu.VMEM((1, HEAD_SIZE), F32),
            packet,
            pltpu.VMEM((3, 8, feats), F32),
            pltpu.VMEM((4, 8, feats), F32),
            pltpu.VMEM((16, feats), F32),
            pltpu.VMEM((max(pairs - 1, 1), 16, feats), F32),
        ]
        + row_total_scratch(tokens) * 2
        + row_sum_scratch(tokens, q_width)
        + chain_scratch(tokens, feats) * 2
        + col_gather_sems()
        + [dma((6,)), dma((4,)), dma((4,))]
        + row_sum_sems()
        + [dma((4,))] * 7
        + [dma((1,))] * 7
        + chain_sems() * 2
        + row_total_sems() * 2
        + [dma((3,))] * 4
        + [dma((max(pairs - 1, 1),))] * 2,
        compiler_params=pltpu.CompilerParams(
            collective_id=number, has_side_effects=True, vmem_limit_bytes=VMEM_LIMIT
        ),
        name="tail",
    )(*operands, *wides, *narrow)
    return out[:6], out[6:9], out[9:]


def shards(
    pairs,
    hidden_in,
    segment_ids,
    attn_gain,
    w_query,
    key_projection,
    value_projection,
    query_gain,
    key_norm_gain,
    w_out,
    ffn_gain,
    w_gate,
    w_up,
    w_down,
    out_grad,
):
    tokens, slice_width = hidden_in.shape
    model_width = attn_gain.shape[0]
    offset = lax.axis_index("row") * slice_width
    gain_one = lax.dynamic_slice_in_dim(attn_gain, offset, slice_width)
    gain_two = lax.dynamic_slice_in_dim(ffn_gain, offset, slice_width)
    q_width = w_query.shape[1]
    k_width = key_projection.shape[1]
    q_heads = q_width // HEAD_SIZE
    groups = q_width // k_width
    tables = (*turn_tables(tokens), query_gain[None, :], key_norm_gain[None, :])
    (scale_one, hidden, scale_two, ffn_in, grad_inner, qkv, q_turned, k_turned, values, probs, xn_wide, gy_wide, mixed_wide, full) = front(
        pairs, q_heads, groups, model_width, 0, hidden_in, out_grad,
        (w_query, key_projection, value_projection, w_out, w_down),
        (segment_ids[:, None], segment_ids[None, :]),
        tables,
        (gain_one[None, :], gain_two[None, :]),
        (w_gate, w_up),
    )
    (grad_ffn_in, inner_act, gate_n, up_n), other_gate = middle(pairs, 1, ffn_in, w_gate, w_up, grad_inner, full)
    (in_grad, layer_out, one_grad, two_grad, q_gain_grad, k_gain_grad), own, others = tail(
        pairs, q_heads, groups, 2, inner_act,
        (w_out, w_down, w_query, key_projection, value_projection),
        (qkv, q_turned, k_turned, values, probs),
        tables,
        (grad_ffn_in, hidden, scale_two, gain_two[None, :], out_grad, hidden_in, scale_one, gain_one[None, :]),
        (gy_wide, mixed_wide, xn_wide),
        (up_n,),
    )
    parts = (gate_n, up_n, *own)
    if pairs == 2:
        sums = [a.astype(F32) + b.astype(F32) for a, b in zip(parts, (*other_gate, *others))]
    else:
        sums = lax.psum(tuple(part.astype(F32) for part in parts), "dp")
    gate_grad, up_grad, down_grad, out_weight_grad, qkv_grad = sums
    return (
        layer_out,
        in_grad,
        one_grad.reshape(-1),
        qkv_grad[:, :q_width],
        qkv_grad[:, q_width : q_width + k_width],
        qkv_grad[:, q_width + k_width :],
        q_gain_grad.reshape(-1),
        k_gain_grad.reshape(-1),
        out_weight_grad,
        two_grad.reshape(-1),
        gate_grad,
        up_grad,
        down_grad,
    )


def solution(mesh):
    acts, grid, flip, none = P(("dp", "col"), "row"), P("row", "col"), P("col", "row"), P()
    return jax.shard_map(
        functools.partial(shards, mesh.shape["dp"]),
        mesh=mesh,
        in_specs=(
            acts, P(("dp", "row")), none, grid, grid, grid, none, none, flip, none, grid, grid, flip, acts,
        ),
        out_specs=(
            acts, acts, none, grid, grid, grid, none, none, flip, none, grid, grid, flip,
        ),
        check_vma=False,
    )
```

```python
import functools
import math

import jax
import jax.numpy as jnp
import numpy as np
from jax import lax
from jax.experimental import pallas as pl
from jax.experimental.pallas import tpu as pltpu
from jax.sharding import PartitionSpec as P

HEAD_SIZE = 128
EPSILON = 1e-06
THETA = 1000000.0
MASKED = -1e30
MESH = pl.DeviceIdType.MESH
BF16 = jnp.bfloat16
F32 = jnp.float32
VMEM_LIMIT = 60 << 20


def to(**where):
    return dict(device_id=where, device_id_type=MESH)


class Ends:
    def __init__(self):
        self.row = lax.axis_index("row")
        self.col = lax.axis_index("col")
        self.chip = lax.div(self.row, 2)
        self.core = lax.rem(self.row, 2)
        self.mate = self.chip * 2 + (1 - self.core)
        self.across = (1 - self.chip) * 2 + self.core
        self.diag = (1 - self.chip) * 2 + (1 - self.core)
        self.end = (self.col == 0) | (self.col == 3)
        self.paired = lax.div(self.col, 2) == self.chip

    def greet(self, pairs=0, line=False):
        gate = pltpu.get_barrier_semaphore()
        count = 3
        for peer in (self.mate, self.across, self.diag):
            pl.semaphore_signal(gate, inc=1, **to(row=peer))
        for step in range(1, pairs):
            pl.semaphore_signal(gate, inc=1, **to(dp=self.pair(pairs, step)))
            count += 1
        if line:
            for step in range(1, 4):
                pl.semaphore_signal(gate, inc=1, **to(col=lax.rem(self.col + step, 4)))
                count += 1
        else:

            @pl.when(self.col > 0)
            def _():
                pl.semaphore_signal(gate, inc=1, **to(col=self.col - 1))

            @pl.when(self.col < 3)
            def _():
                pl.semaphore_signal(gate, inc=1, **to(col=self.col + 1))

            count += jnp.where(self.col > 0, 1, 0) + jnp.where(self.col < 3, 1, 0)
        pl.semaphore_wait(gate, count)

    def pair(self, pairs, step):
        return lax.rem(lax.axis_index("dp") + step, pairs)


class RowTotal:
    def __init__(self, at, own, got, sends, recvs):
        self.own, self.got = own, got
        self.copies = [
            remote(own, got.at[i], sends.at[i], recvs.at[i], row=peer)
            for i, peer in enumerate((at.mate, at.across, at.diag))
        ]

    def start(self, column):
        self.own[...] = jnp.broadcast_to(column, (column.shape[0], 128)).T[:8, :]
        for copy in self.copies:
            copy.start()

    def finish(self):
        for copy in self.copies:
            copy.wait()
        total = (self.own[...] + self.got[0]) + (self.got[1] + self.got[2])
        return jnp.concatenate([total] * 16, axis=0).T[:, :1]


def row_total_scratch(tokens):
    return [pltpu.VMEM((8, tokens), F32), pltpu.VMEM((3, 8, tokens), F32)]


def row_total_sems():
    return [pltpu.SemaphoreType.DMA((3,)), pltpu.SemaphoreType.DMA((3,))]


def remote(src, dst, sends, recvs, **where):
    return pltpu.make_async_remote_copy(
        src_ref=src, dst_ref=dst, send_sem=sends, recv_sem=recvs, **to(**where)
    )


class Fetch:
    def __init__(self, pairs, sems):
        self.copies = [
            pltpu.make_async_copy(src, dst, sems.at[i]) for i, (src, dst) in enumerate(pairs)
        ]

    def start(self):
        for copy in self.copies:
            copy.start()

    def wait(self, first=0, last=None):
        for copy in self.copies[first:last]:
            copy.wait()


def held(array):
    return pltpu.VMEM(array.shape, array.dtype)


def in_rows(count, step, body, first=0):
    def one(i, _):
        body(pl.ds(pl.multiple_of(first + i * step, step), step))
        return 0

    lax.fori_loop(0, count // step, one, 0)


class ColGather:
    def __init__(self, at, wide, sends, recvs):
        self.at, self.wide, self.sends, self.recvs = at, wide, sends, recvs
        self.half = wide.shape[1] // 2

    def copy(self, s, h, side, col):
        part = self.wide.at[s, pl.ds(h * self.half, self.half)]
        return remote(part, part, self.sends.at[side, s, h], self.recvs.at[s, h], col=col)

    def up(self, s, h):
        return self.copy(s, h, 0, self.at.col + 1)

    def down(self, s, h):
        return self.copy(s, h, 1, self.at.col - 1)

    def loop(self, dist, body):
        if dist == 0:
            body(self.at.col)
            return

        def one(side, _):
            s = jnp.where(side == 0, self.at.col - dist, self.at.col + dist)
            pl.when((s >= 0) & (s <= 3))(lambda: body(s))
            return 0

        lax.fori_loop(0, 2, one, 0)

    def arrive(self, dist):
        for h in range(2):

            def take(s, h=h):
                if dist:
                    self.up(s, h).wait_recv()

                @pl.when((s <= self.at.col) & (self.at.col < 3))
                def _():
                    self.up(s, h).start()

                @pl.when((s >= self.at.col) & (self.at.col > 0))
                def _():
                    self.down(s, h).start()

            self.loop(dist, take)

    def send_up(self):
        for h in range(2):
            self.up(self.at.col, h).start()

    def send_down(self):
        for h in range(2):
            self.down(self.at.col, h).start()

    def close(self):
        def one(s, _):
            for h in range(2):

                @pl.when((s <= self.at.col) & (self.at.col < 3))
                def _():
                    self.up(s, h).wait_send()

                @pl.when((s >= self.at.col) & (self.at.col > 0))
                def _():
                    self.down(s, h).wait_send()

            return 0

        lax.fori_loop(0, 4, one, 0)


class RowSumWhole:
    def __init__(self, at, product, out, a_send, a_recv, c_recv, d_send, d_recv, m_send, m_recv, x_send, x_recv):
        self.at, self.product, self.out = at, product, out
        self.a_send, self.a_recv, self.c_recv, self.d_send, self.d_recv = a_send, a_recv, c_recv, d_send, d_recv
        self.m_send, self.m_recv, self.x_send, self.x_recv = m_send, m_recv, x_send, x_recv
        self.half = product.shape[0] // 2
        self.d = remote(d_send, d_recv, m_send.at[2], m_recv.at[2], row=at.mate)

    def a(self, i):
        return remote(self.a_send.at[i], self.a_recv.at[i], self.m_send.at[i], self.m_recv.at[i], row=self.at.mate)

    def b(self, i, s):
        core = self.at.core
        return remote(self.a_recv.at[i], self.c_recv.at[core], self.x_send.at[i], self.x_recv.at[core], row=s)

    def part(self, core, here):
        return pl.ds(pl.multiple_of(core * self.half + here.start, here.size), here.size)

    def give(self, s):
        at, product, half = self.at, self.product, self.half
        i = lax.rem(s, 2)
        ours = lax.div(s, 2) == at.chip

        @pl.when(jnp.logical_not(ours))
        def _():
            def cast(here):
                self.a_send[i, here] = product[self.part(1 - at.core, here), :].astype(BF16)

            in_rows(half, 64, cast)
            self.a(i).start()
            self.a(i).wait_recv()

            def add(here):
                total = product[self.part(at.core, here), :] + self.a_recv[i, here].astype(F32)
                self.a_recv[i, here] = total.astype(BF16)

            in_rows(half, 64, add)
            self.b(i, s).start()

        @pl.when(ours & (i != at.core))
        def _():
            def cast(here):
                self.d_send[here] = product[here, :].astype(BF16)

            in_rows(2 * half, 64, cast)
            self.d.start()

        @pl.when(s == at.row)
        def _():
            def store(here):
                self.out[here] = product[here, :]

            in_rows(2 * half, 64, store)

    def finish(self):
        self.d.wait_recv()
        for h in range(2):
            here = self.c_recv.at[h]
            remote(here, here, self.x_send.at[h], self.x_recv.at[h], row=self.at.across).wait_recv()

            def add(rows, h=h):
                spot = pl.ds(pl.multiple_of(h * self.half + rows.start, rows.size), rows.size)
                self.out[spot] += self.d_recv[spot].astype(F32) + self.c_recv[h, rows].astype(F32)

            in_rows(self.half, 64, add)

    def close(self):
        self.d.wait_send()
        for i in range(2):
            self.a(i).wait_send()
            self.b(i, self.at.across).wait_send()


def row_sum_scratch(tokens, width):
    half = pltpu.VMEM((2, tokens // 2, width), BF16)
    full = pltpu.VMEM((tokens, width), BF16)
    return [half, half, half, full, full]


def row_sum_sems():
    dma = pltpu.SemaphoreType.DMA
    return [dma((3,)), dma((3,)), dma((2,)), dma((2,))]


class RowSumQuarter:
    def __init__(self, at, chunk, keep, a_send, a_recv, c_recv, d_send, d_recv, m_send, m_recv, x_send, x_recv):
        self.at, self.chunk, self.keep = at, chunk, keep
        self.a_send, self.a_recv, self.c_recv = a_send, a_recv, c_recv
        self.d_send, self.d_recv = d_send, d_recv
        self.sems = (m_send, m_recv, x_send, x_recv)

    def a(self, s):
        m_send, m_recv, _, _ = self.sems
        return remote(self.a_send.at[s], self.a_recv.at[s], m_send.at[0, s], m_recv.at[0, s], row=self.at.mate)

    def d(self, s):
        m_send, m_recv, _, _ = self.sems
        return remote(self.d_send.at[s], self.d_recv.at[s], m_send.at[1, s], m_recv.at[1, s], row=self.at.mate)

    def b(self, s):
        _, _, x_send, x_recv = self.sems
        return remote(self.a_recv.at[s], self.c_recv.at[s], x_send.at[s], x_recv.at[s], row=self.at.across)

    def split(self, s, value, spot, own):
        at, chunk = self.at, self.chunk
        chunk[...] = value

        def quarter(q):
            return chunk[pl.ds(pl.multiple_of(q * 128, 128), 128), :]

        self.a_send[s, :, spot] = quarter(at.diag).astype(BF16)
        self.keep[:, spot] = quarter(at.across)
        self.d_send[s, :, spot] = quarter(at.mate).astype(BF16)
        own[s, :, spot] = quarter(at.row).astype(own.dtype)

    def give(self, s):
        self.a(s).start()
        self.d(s).start()
        self.a(s).wait_recv()

        def one(here):
            self.a_recv[s, here] = (self.keep[here, :] + self.a_recv[s, here].astype(F32)).astype(BF16)

        in_rows(128, 16, one)
        self.b(s).start()

    def finish(self, s):
        self.d(s).wait_recv()
        self.b(s).wait_recv()

    def close(self):
        def one(s, _):
            self.a(s).wait_send()
            self.b(s).wait_send()
            self.d(s).wait_send()
            return 0

        lax.fori_loop(0, 4, one, 0)


class RowGather:
    def __init__(self, at, own, slot, sems):
        self.at, self.own, self.slot = at, own, slot
        self.m_send, self.m_recv, self.x_send, self.x_recv, self.f_send, self.f_recv, self.local = (*sems, None)[:7]

    def to_mate(self, s):
        return remote(self.own(s), self.slot(s, self.at.row), self.m_send.at[s], self.m_recv.at[s], row=self.at.mate)

    def to_across(self, s):
        return remote(self.own(s), self.slot(s, self.at.row), self.x_send.at[s], self.x_recv.at[s], row=self.at.across)

    def pass_on(self, s):
        here = self.slot(s, self.at.across)
        return remote(here, here, self.f_send.at[s], self.f_recv.at[s], row=self.at.mate)

    def move_own(self, s):
        return pltpu.make_async_copy(self.own(s), self.slot(s, self.at.row), self.local.at[s])

    def near(self, s):
        self.to_mate(s).start()
        if self.local is not None:
            self.move_own(s).start()

    def wait_near(self, s):
        here = self.slot(s, self.at.mate)
        remote(here, here, self.m_send.at[s], self.m_recv.at[s], row=self.at.mate).wait_recv()
        if self.local is not None:
            self.move_own(s).wait()

    def take_across(self, s):
        here = self.slot(s, self.at.across)
        remote(here, here, self.x_send.at[s], self.x_recv.at[s], row=self.at.across).wait_recv()
        self.pass_on(s).start()

    def wait_diag(self, s):
        here = self.slot(s, self.at.diag)
        remote(here, here, self.f_send.at[s], self.f_recv.at[s], row=self.at.mate).wait_recv()

    def close_one(self, s):
        self.to_mate(s).wait_send()
        self.to_across(s).wait_send()
        self.pass_on(s).wait_send()

    def close(self, count):
        def one(s, _):
            self.close_one(s)
            return 0

        lax.fori_loop(0, count, one, 0)


class WeightGather:
    def __init__(self, at, pairs, own, full, sems):
        self.at, self.pairs, self.own, self.full = at, pairs, own, full
        self.m_send, self.m_recv, self.x_send, self.x_recv, self.y_send, self.y_recv = sems[:6]
        self.f_send, self.f_recv, self.g_send, self.g_recv = sems[6:]
        self.step = full.shape[2] // 4
        self.mine = lax.axis_index("dp") if pairs == 2 else None

    def rows(self, j):
        return pl.ds(j * self.step, self.step)

    def piece(self, which, row, j):
        return self.full.at[which, row, self.rows(j)]

    def held(self):
        return (self.mine,) if self.pairs == 2 else (0, 1)

    def near(self, which, row):
        here = self.full.at[which, row]
        return remote(self.own[which], here, self.m_send.at[which], self.m_recv.at[which], row=self.at.mate)

    def over(self, which, row, j, src=None):
        here = self.piece(which, row, j)
        lane = 0 if self.pairs == 2 else which
        src = here if src is None else src
        return remote(src, here, self.x_send.at[lane, j], self.x_recv.at[lane, j], row=self.at.across)

    def hand(self, which, j):
        here = self.piece(which, self.at.across, j)
        return remote(here, here, self.y_send.at[j], self.y_recv.at[j], dp=self.at.pair(2, 1))

    def pass_first(self, which, row, j):
        here = self.piece(which, row, j)
        lane = 0 if self.pairs == 2 else which
        return remote(here, here, self.f_send.at[lane, j], self.f_recv.at[lane, j], row=self.at.mate)

    def pass_second(self, which, row, j):
        here = self.piece(which, row, j)
        return remote(here, here, self.g_send.at[j], self.g_recv.at[j], row=self.at.mate)

    def begin(self):
        for i in range(2):
            self.near(i, self.at.row).start()

    def send(self, j):
        for which in range(2):
            copy = self.over(which, self.at.row, j, self.own[which].at[self.rows(j)])
            if self.pairs == 2:
                pl.when(self.mine == which)(copy.start)
            else:
                copy.start()

    def forward(self, j):
        for which in self.held():
            self.over(which, self.at.across, j).wait_recv()
            if self.pairs == 2:
                self.hand(which, j).start()
            self.pass_first(which, self.at.across, j).start()

    def finish(self, j):
        if self.pairs == 2:
            self.hand(1 - self.mine, j).wait_recv()
            self.pass_second(1 - self.mine, self.at.across, j).start()

    def close(self):
        for i in range(2):
            self.near(i, self.at.mate).wait_recv()
            self.near(i, self.at.row).wait_send()
        for j in range(4):
            for which in self.held():
                self.over(which, self.at.row, j).wait_send()
                self.pass_first(which, self.at.diag, j).wait_recv()
                self.pass_first(which, self.at.across, j).wait_send()
            if self.pairs == 2:
                self.hand(self.mine, j).wait_send()
                self.pass_second(1 - self.mine, self.at.diag, j).wait_recv()
                self.pass_second(1 - self.mine, self.at.across, j).wait_send()


def weight_gather_sems(pairs):
    dma = pltpu.SemaphoreType.DMA
    lanes = 1 if pairs == 2 else 2
    return [
        dma((2,)), dma((2,)), dma((lanes, 4)), dma((lanes, 4)), dma((4,)), dma((4,)),
        dma((lanes, 4)), dma((lanes, 4)), dma((4,)), dma((4,)),
    ]


class ColSum:
    def __init__(self, at, product, sent, got, extra, sends, recvs, extra_recvs):
        self.at, self.product, self.sent, self.got, self.extra = at, product, sent, got, extra
        self.sends, self.recvs, self.extra_recvs = sends, recvs, extra_recvs
        self.half = product.shape[0] // 2

    def part(self, h):
        return pl.ds(h * self.half, self.half)

    def up(self, s, h):
        return remote(
            self.sent.at[s, self.part(h)], self.got.at[s, self.part(h)],
            self.sends.at[s, h], self.recvs.at[s, h], col=self.at.col + 1,
        )

    def down(self, s, h):
        return remote(
            self.sent.at[s, self.part(h)], self.got.at[s, self.part(h)],
            self.sends.at[s, h], self.recvs.at[s, h], col=self.at.col - 1,
        )

    def last_down(self, s, h):
        return remote(
            self.sent.at[s, self.part(h)], self.extra.at[self.part(h)],
            self.sends.at[s, h], self.extra_recvs.at[h], col=self.at.col - 1,
        )

    def step(self, s, halves=(0, 1)):
        col, product = self.at.col, self.product
        for h in halves:
            @pl.when(((s >= col) & (col > 0)) | ((s < col) & (col < 3)))
            def _():
                self.up(s, h).wait_recv()

                def add(here):
                    product[here, :] += self.got[s, here].astype(F32)

                in_rows(self.half, 64, add, h * self.half)

            @pl.when((s == col) & (col < 3))
            def _():
                self.last_down(s, h).wait_recv()

                def add(here):
                    product[here, :] += self.extra[here].astype(F32)

                in_rows(self.half, 64, add, h * self.half)

            @pl.when(s != col)
            def _():
                def cast(here):
                    self.sent[s, here] = product[here, :].astype(BF16)

                in_rows(self.half, 64, cast, h * self.half)

            pl.when(s > col)(lambda: self.up(s, h).start())
            pl.when(s < col - 1)(lambda: self.down(s, h).start())
            pl.when(s == col - 1)(lambda: self.last_down(s, h).start())

    def close(self):
        def one(s, _):
            for h in range(2):
                pl.when(s != self.at.col)(lambda: self.up(s, h).wait_send())
            return 0

        lax.fori_loop(0, 4, one, 0)


def far_first(col, j):
    first = jnp.where(col < 2, 3, 0)
    second = jnp.where(col < 2, 2, 1)
    third = jnp.where(lax.rem(col, 2) == 0, col + 1, col - 1)
    return (first, second, third, col)[j]


def near_first(at, j):
    first, second, partner, _ = [far_first(at.col, i) for i in range(4)]
    mine = at.paired
    return (
        jnp.where(mine, partner, first),
        jnp.where(mine, first, second),
        jnp.where(mine, second, partner),
        at.col,
    )[j]


def turn_tables(length):
    rates = THETA ** (-np.arange(HEAD_SIZE // 2) * 2.0 / HEAD_SIZE)
    angles = np.arange(length)[:, None] * rates[None, :]
    cos, sin = np.cos(angles), np.sin(angles)
    return (
        np.concatenate([cos, cos], axis=1).astype(np.float32),
        np.concatenate([-sin, sin], axis=1).astype(np.float32),
    )


def swap_halves(value):
    return pltpu.roll(value, HEAD_SIZE // 2, 1)


def head(ref, index):
    return ref[:, index * HEAD_SIZE : (index + 1) * HEAD_SIZE]


def root_scale(raw):
    return lax.rsqrt(jnp.mean(raw * raw, axis=1, keepdims=True) + EPSILON)


def attend(q_heads, groups, qkv, seg_row, cos, sin, q_gain, k_gain, o, qa, ka, va, probs):
    kv = q_heads // groups
    tokens = qkv.shape[0]
    half = tokens // 2
    seg_line = seg_row[...].astype(F32)
    seg_column = jnp.broadcast_to(seg_line, (128, tokens)).T[:, :1]

    def turned(index, gain):
        raw = head(qkv, index)
        normed = raw * root_scale(raw) * gain[...]
        return (normed * cos[...] + swap_halves(normed) * sin[...]).astype(BF16)

    for i in range(q_heads):
        qa[:, i * HEAD_SIZE : (i + 1) * HEAD_SIZE] = turned(i, q_gain)
    for i in range(kv):
        ka[:, i * HEAD_SIZE : (i + 1) * HEAD_SIZE] = turned(q_heads + i, k_gain)
        va[:, i * HEAD_SIZE : (i + 1) * HEAD_SIZE] = head(qkv, q_heads + kv + i).astype(BF16)
    for block in range(2):
        rows = slice(block * half, (block + 1) * half)
        keys = (block + 1) * half
        spot = lax.broadcasted_iota(jnp.int32, (half, keys), 0) + block * half
        other = lax.broadcasted_iota(jnp.int32, (half, keys), 1)
        allowed = (other <= spot) & (seg_column[rows, :] == seg_line[:, :keys])
        for i in range(q_heads):
            j = i // groups
            dots = lax.dot_general(
                head(qa, i)[rows], head(ka, j)[:keys], (((1,), (1,)), ((), ())), preferred_element_type=F32
            ) * (1.0 / math.sqrt(HEAD_SIZE))
            scores = jnp.where(allowed, dots, MASKED)
            expo = jnp.exp(scores - jnp.max(scores, axis=1, keepdims=True))
            p = expo / jnp.sum(expo, axis=1, keepdims=True)
            probs[i, rows, :keys] = p.astype(BF16)
            mixed = jnp.dot(p.astype(BF16), head(va, j)[:keys], preferred_element_type=F32)
            o[rows, i * HEAD_SIZE : (i + 1) * HEAD_SIZE] = mixed.astype(BF16)


def front_kernel(pairs, q_heads, groups, model_width, *refs):
    refs = list(refs)

    def take(count):
        found = refs[:count]
        del refs[:count]
        return found

    (x_ref, seg_row, q_gain, k_gain, gain_one, gain_two) = take(6)
    late = take(8)
    (w_gate, w_up) = take(2)
    (scale_one, hidden, scale_two, ffn_in) = take(4)
    kept_out = take(5)
    (dact_out, xn_out, gy_out, mixed_out, full) = take(5)
    (w_query, w_key, w_value, w_out, w_down, cos, sin) = late_held = take(7)
    (qkv, qa, ka, va, probs) = kept = take(5)
    (dact,) = take(1)
    (xn_wide, gy_wide, mixed_wide, mixed, product, chunk, keep) = take(7)
    total_bufs = take(2)
    second_bufs = take(2)
    moved = take(5)
    moved_q = take(5)
    chain = take(3)
    x_sems, gy_sems = take(2), take(2)
    (local,) = take(1)
    moved_sems, moved_q_sems = take(4), take(4)
    mixed_sems = take(7)
    chain_sems = take(3)
    total_sems, second_sems = take(2), take(2)
    full_sems = take(10)
    late_sems, kept_sems, dact_sems = take(3)

    at = Ends()
    gain_spot = pl.ds(pl.multiple_of(at.row * x_ref.shape[1], x_ref.shape[1]), x_ref.shape[1])
    fetch = Fetch([*zip(late[1:], late_held), (late[0], gy_wide.at[at.col])], late_sems)
    fetch.start()
    keep_saved = Fetch(list(zip(kept, kept_out)), kept_sems)
    full_gather = WeightGather(at, pairs, (w_gate, w_up), full, full_sems)
    tokens, feats = x_ref.shape
    first_total = RowTotal(at, *total_bufs, *total_sems)
    second_total = RowTotal(at, *second_bufs, *second_sems)
    x_gather = ColGather(at, xn_wide, *x_sems)
    gy_gather = ColGather(at, gy_wide, *gy_sems)
    row_sum = RowSumWhole(at, product, qkv, *moved, *moved_sems)
    quarter_sum = RowSumQuarter(at, chunk, keep, *moved_q, *moved_q_sems)
    half = tokens // 2
    mixes = RowGather(
        at, lambda h: mixed.at[pl.ds(h * half, half)], lambda h, q: mixed_wide.at[q, pl.ds(h * half, half)], mixed_sems
    )
    out_sum = ColSum(at, hidden, *chain, *chain_sems)

    at.greet(pairs if pairs == 2 else 0)
    stream = x_ref[...].astype(F32)
    first_total.start(jnp.sum(stream * stream, axis=1, keepdims=True))
    full_gather.begin()
    full_gather.send(0)
    scale = lax.rsqrt(first_total.finish() / model_width + EPSILON)
    scale_one[...] = scale
    xn_wide[at.col] = (x_ref[...].astype(F32) * scale * gain_one[:, gain_spot]).astype(BF16)

    def project(s):
        base = 0
        for w in (w_query, w_key, w_value):
            size = w.shape[1]
            product[:, base : base + size] = jnp.dot(xn_wide[s], w[...], preferred_element_type=F32)
            base += size
        row_sum.give(s)

    def back_down(s):
        size = chunk.shape[1]

        def one(j, _):
            cols = pl.ds(pl.multiple_of(j * size, size), size)
            value = lax.dot_general(
                gy_wide[s], w_down[cols, :], (((1,), (1,)), ((), ())), preferred_element_type=F32
            )
            quarter_sum.split(s, value, cols, dact)
            return 0

        lax.fori_loop(0, w_down.shape[0] // size, one, 0)
        quarter_sum.give(s)

    def keep_dact(s):
        return pltpu.make_async_copy(dact.at[s], dact_out.at[s], dact_sems.at[s])

    def end_down(s):
        quarter_sum.finish(s)

        def add(here):
            dact[s, here] += moved_q[2][s, here].astype(F32) + moved_q[4][s, here].astype(F32)

        in_rows(128, 16, add)
        keep_dact(s).start()

    def send_gy(dist):
        @pl.when((at.col == dist) & (at.col < 3))
        def _():
            gy_gather.send_up()

        @pl.when((at.col == 3 - dist) & (at.col > 0))
        def _():
            gy_gather.send_down()

    def out_step(j, halves=(0, 1)):
        s = near_first(at, j)
        for h in halves:
            rows = pl.ds(h * half, half)
            hidden[rows, :] = jnp.dot(mixed_wide[s, rows, :], w_out[...], preferred_element_type=F32)
        out_sum.step(s, halves)

    mid = jnp.logical_not(at.end)
    x_gather.arrive(0)
    fetch.wait()
    send_gy(0)
    x_gather.loop(0, project)
    back_down(at.col)
    full_gather.send(1)
    for dist in range(1, 4):
        x_gather.arrive(dist)
        send_gy(dist)
        x_gather.loop(dist, project)
        if dist < 3:
            full_gather.forward(dist - 1)

    @pl.when(mid)
    def _():
        gy_gather.arrive(1)

    row_sum.finish()
    attend(q_heads, groups, qkv, seg_row, cos, sin, q_gain, k_gain, mixed, qa, ka, va, probs)
    for h in range(2):
        mixes.to_across(h).start()
    for h in range(2):
        mixes.near(h)
    keep_saved.start()
    full_gather.send(2)

    @pl.when(mid)
    def _():
        gy_gather.arrive(2)

    for h in range(2):
        mixes.wait_near(h)

    @pl.when(at.end)
    def _():
        out_step(0)
        pl.when(jnp.logical_not(at.paired))(lambda: out_step(1))
        gy_gather.arrive(1)

    gy_gather.loop(1, back_down)
    for h in range(2):
        mixes.take_across(h)
        mixes.wait_diag(h)

        @pl.when(at.end)
        def _():
            pl.when(at.paired)(lambda: out_step(1, (h,)))
            out_step(2, (h,))

    full_gather.send(3)
    full_gather.forward(2)
    full_gather.finish(0)

    @pl.when(at.end)
    def _():
        gy_gather.arrive(2)

    @pl.when(mid)
    def _():
        out_step(0)

    gy_gather.loop(2, back_down)
    full_gather.forward(3)
    full_gather.finish(1)

    @pl.when(mid)
    def _():
        out_step(1)
        out_step(2)

    @pl.when(at.end)
    def _():
        gy_gather.arrive(3)

    gy_gather.loop(3, back_down)
    wides = [
        pltpu.make_async_copy(src, dst, local.at[i])
        for i, (src, dst) in enumerate(((xn_wide, xn_out), (gy_wide, gy_out), (mixed_wide, mixed_out)))
    ]
    for copy in wides:
        copy.start()
    full_gather.finish(2)
    for dist in range(3):
        gy_gather.loop(dist, end_down)
    full_gather.finish(3)
    out_step(3)

    def residual(here):
        hidden[here, :] += x_ref[here, :].astype(F32)

    in_rows(tokens, 64, residual)
    value = hidden[...]
    second_total.start(jnp.sum(value * value, axis=1, keepdims=True))
    gy_gather.loop(3, end_down)
    scale = lax.rsqrt(second_total.finish() / model_width + EPSILON)
    scale_two[...] = scale
    ffn_in[...] = (hidden[...] * scale * gain_two[:, gain_spot]).astype(BF16)

    keep_saved.wait()
    for s in range(4):
        keep_dact(s).wait()
    full_gather.close()
    x_gather.close()
    gy_gather.close()
    row_sum.close()
    quarter_sum.close()
    mixes.close(2)
    out_sum.close()
    for copy in wides:
        copy.wait()


def col_gather_sems():
    return [pltpu.SemaphoreType.DMA((2, 4, 2)), pltpu.SemaphoreType.DMA((4, 2))]


def chain_scratch(tokens, feats):
    return [
        pltpu.VMEM((4, tokens, feats), BF16), pltpu.VMEM((4, tokens, feats), BF16), pltpu.VMEM((tokens, feats), BF16),
    ]


def chain_sems():
    dma = pltpu.SemaphoreType.DMA
    return [dma((4, 2)), dma((4, 2)), dma((2,))]


def front(pairs, q_heads, groups, model_width, number, x, gy, weights, segments, tables, gains, ffn_weights):
    tokens, feats = x.shape
    w_query, w_key, w_value, w_out, w_down = weights
    width = w_query.shape[1] + w_key.shape[1] + w_value.shape[1]
    q_width, k_width, ff = w_query.shape[1], w_key.shape[1], w_down.shape[0]
    dma = pltpu.SemaphoreType.DMA
    any_spec, vmem = pl.BlockSpec(memory_space=pl.ANY), pl.BlockSpec(memory_space=pltpu.VMEM)
    shape = jax.ShapeDtypeStruct
    wide = pltpu.VMEM((4, tokens, feats), BF16)
    late = (*weights, *tables[:2])
    kept = [
        shape((tokens, width), F32),
        shape((tokens, q_width), BF16),
        shape((tokens, k_width), BF16),
        shape((tokens, k_width), BF16),
        shape((q_heads, tokens, tokens), BF16),
    ]
    dact = shape((4, tokens // 4, ff), F32)
    return pl.pallas_call(
        functools.partial(front_kernel, pairs, q_heads, groups, model_width),
        out_shape=(
            shape((tokens, 1), F32),
            shape((tokens, feats), F32),
            shape((tokens, 1), F32),
            shape((tokens, feats), BF16),
            *kept,
            dact,
            shape((4, tokens, feats), BF16),
            shape((4, tokens, feats), BF16),
            shape((4, tokens, q_width), BF16),
            shape((2, 4, *ffn_weights[0].shape), BF16),
        ),
        in_specs=[vmem] * 6 + [any_spec] * 10,
        out_specs=tuple([vmem] * 4 + [any_spec] * 10),
        scratch_shapes=[held(array) for array in late]
        + [held(array) for array in kept]
        + [
            held(dact),
            wide,
            wide,
            pltpu.VMEM((4, tokens, q_width), BF16),
            pltpu.VMEM((tokens, q_width), BF16),
            pltpu.VMEM((tokens, width), F32),
            pltpu.VMEM((tokens, 512), F32),
            pltpu.VMEM((tokens // 4, ff), F32),
        ]
        + row_total_scratch(tokens) * 2
        + row_sum_scratch(tokens, width)
        + [pltpu.VMEM((4, tokens // 4, ff), BF16)] * 5
        + chain_scratch(tokens, feats)
        + col_gather_sems() * 2
        + [dma((3,))]
        + row_sum_sems()
        + [dma((2, 4)), dma((2, 4)), dma((4,)), dma((4,))]
        + [dma((2,))] * 7
        + chain_sems()
        + row_total_sems() * 2
        + weight_gather_sems(pairs)
        + [dma((8,)), dma((5,)), dma((4,))],
        compiler_params=pltpu.CompilerParams(
            collective_id=number, has_side_effects=True, vmem_limit_bytes=VMEM_LIMIT
        ),
        name="front",
    )(x, segments, *tables[2:], *gains, gy, *late, *ffn_weights)


def across_rows(left, right):
    return lax.dot_general(left, right, (((0,), (0,)), ((), ())), preferred_element_type=F32)


def attend_back(q_heads, groups, grad, qkv, qa, ka, va, probs, cos, sin, q_gain, k_gain, out, q_part, k_part, dq, dk, dv):
    kv = q_heads // groups
    tokens = qkv.shape[0]
    half = tokens // 2
    scale = 1.0 / math.sqrt(HEAD_SIZE)
    dk[...] = jnp.zeros_like(dk)
    dv[...] = jnp.zeros_like(dv)
    for block in range(2):
        rows = slice(block * half, (block + 1) * half)
        keys = (block + 1) * half
        for i in range(q_heads):
            j = i // groups
            spot = slice(j * HEAD_SIZE, (j + 1) * HEAD_SIZE)
            pb = probs[i, rows, :keys]
            p = pb.astype(F32)
            g = head(grad, i)[rows].astype(BF16)
            dv[:keys, spot] += across_rows(pb.astype(BF16), g)
            dp = lax.dot_general(
                g, head(va, j)[:keys], (((1,), (1,)), ((), ())), preferred_element_type=F32
            )
            ds = (p * (dp - jnp.sum(p * dp, axis=1, keepdims=True))).astype(BF16)
            dq[rows, i * HEAD_SIZE : (i + 1) * HEAD_SIZE] = (
                jnp.dot(ds, head(ka, j)[:keys], preferred_element_type=F32) * scale
            )
            dk[:keys, spot] += across_rows(ds, head(qa, i)[rows]) * scale

    def back(turned, index, gain):
        raw = head(qkv, index)
        scales = root_scale(raw)
        normed = turned * cos[...] - swap_halves(turned) * sin[...]
        part = jnp.sum(normed * raw * scales, axis=0, keepdims=True)
        weighted = normed * gain[...]
        inner = jnp.sum(weighted * raw, axis=1, keepdims=True)
        result = scales * weighted - raw * (scales * scales * scales) * inner * (1.0 / HEAD_SIZE)
        out[:, index * HEAD_SIZE : (index + 1) * HEAD_SIZE] = result.astype(BF16)
        return part

    q_part[...] = sum(back(head(dq, i), i, q_gain) for i in range(q_heads))
    k_part[...] = sum(back(head(dk, i), q_heads + i, k_gain) for i in range(kv))
    for i in range(kv):
        spot = (q_heads + kv + i) * HEAD_SIZE
        out[:, spot : spot + HEAD_SIZE] = head(dv, i).astype(BF16)


def act_copy(src, dst, at, j, sem):
    s = far_first(at.col, j)
    if j < 2:
        return pltpu.make_async_copy(src.at[s], dst.at[s], sem)
    return pltpu.make_async_copy(src.at[s, at.row], dst.at[s, at.row], sem)


def weight_grad(out, left, right):
    def block(here):
        total = None
        for s in range(4):
            term = across_rows(left(s, here), right(s))
            total = term if total is None else total + term
        out[here, :] = total.astype(BF16)

    in_rows(out.shape[0], 256, block)


def middle_kernel(pairs, *refs):
    refs = list(refs)

    def take(count):
        found = refs[:count]
        del refs[:count]
        return found

    (hn, w_gate, w_up, dact_in, full) = take(5)
    (dhn, act_out, gate_n, up_n) = take(4)
    others = take(1) if pairs == 2 else []
    (hn_wide, hn_full, weights, dact, gate_up, gate_wide, up_wide, act_wide, n_gate, n_up) = take(10)
    chain = take(3)
    hn_sems = take(2)
    (full_sem, share_send, share_recv) = take(3)
    gate_sems, up_sems, act_sems = take(6), take(6), take(6)
    chain_sems_ = take(3)
    (local, y_send, y_recv) = take(3)

    at = Ends()
    ff = w_gate.shape[1]
    quarter = hn.shape[0] // 4
    gather = ColGather(at, hn_wide, *hn_sems)
    loads = [pltpu.make_async_copy(dact_in, dact, full_sem.at[2, 0])]
    for which, own in enumerate((w_gate, w_up)):
        for i, r in enumerate((at.mate, at.across, at.diag, at.row)):
            src = own if i == 3 else full.at[which, r]
            loads.append(pltpu.make_async_copy(src, weights.at[which, r], full_sem.at[which, i]))
    for load in loads:
        load.start()
    gates = RowGather(at, lambda s: gate_wide.at[s, at.row], lambda s, q: gate_wide.at[s, q], gate_sems)
    ups = RowGather(at, lambda s: up_wide.at[s, at.row], lambda s, q: up_wide.at[s, q], up_sems)
    acts = RowGather(at, lambda s: act_wide.at[s, at.row], lambda s, q: act_wide.at[s, q], act_sems)
    back_sum = ColSum(at, dhn, *chain, *chain_sems_)

    hn_wide[at.col] = hn[...]
    at.greet(pairs if pairs == 2 else 0)

    peers = (at.mate, at.across, at.diag)

    def share(s):
        hn_full[s, at.row] = hn_wide[s, pl.ds(pl.multiple_of(at.row * quarter, quarter), quarter)]
        for i, peer in enumerate(peers):
            theirs = hn_wide.at[s, pl.ds(pl.multiple_of(peer * quarter, quarter), quarter)]
            remote(theirs, hn_full.at[s, at.row], share_send.at[s, i], share_recv.at[s, i], row=peer).start()

    def hidden_units(s):
        for i, peer in enumerate(peers):
            here = hn_full.at[s, peer]
            remote(here, here, share_send.at[s, i], share_recv.at[s, i], row=peer).wait_recv()
        size = gate_up.shape[2]

        def some(j, _):
            cols = pl.ds(pl.multiple_of(j * size, size), size)
            for which in range(2):
                total = None
                for r in range(4):
                    term = jnp.dot(hn_full[s, r], weights[which, r, :, cols], preferred_element_type=F32)
                    total = term if total is None else total + term
                gate_up[which] = total

            def one(here):
                gate, up = gate_up[0, here], gate_up[1, here]
                grad = dact[s, here, cols]
                sigmoid = jax.nn.sigmoid(gate)
                silu = gate * sigmoid
                act_wide[s, at.row, here, cols] = (silu * up).astype(BF16)
                gate_wide[s, at.row, here, cols] = (
                    grad * up * (sigmoid * (1.0 + gate * (1.0 - sigmoid)))
                ).astype(BF16)
                up_wide[s, at.row, here, cols] = (grad * silu).astype(BF16)

            in_rows(quarter, 16, one)
            return 0

        lax.fori_loop(0, ff // size, some, 0)
        gates.to_across(s).start()
        gates.near(s)
        ups.near(s)

    def close_share(s):
        for i, peer in enumerate(peers):
            here = hn_full.at[s, peer]
            remote(here, here, share_send.at[s, i], share_recv.at[s, i], row=peer).wait_send()

    def rows_of(ref, s):
        return ref[s].reshape(4 * quarter, ff)

    def back(j):
        s = far_first(at.col, j)
        contract = (((1,), (1,)), ((), ()))
        dhn[...] = lax.dot_general(
            rows_of(gate_wide, s), weights[0, at.row], contract, preferred_element_type=F32
        ) + lax.dot_general(rows_of(up_wide, s), weights[1, at.row], contract, preferred_element_type=F32)

    def arrive(some, j):
        s = far_first(at.col, j)
        some.wait_near(s)
        some.take_across(s)
        some.wait_diag(s)

    def left(s, here):
        return hn_wide[s, :, here]

    mid = jnp.logical_not(at.end)
    gather.arrive(0)
    gather.loop(0, share)
    for load in loads:
        load.wait()
    gather.loop(0, hidden_units)
    gather.arrive(1)
    gather.loop(1, share)
    gather.arrive(2)
    gather.loop(2, share)
    gather.loop(1, hidden_units)
    gather.arrive(3)
    gather.loop(3, share)
    gather.loop(2, hidden_units)
    gather.loop(3, hidden_units)
    for j in range(4):
        ups.to_across(far_first(at.col, j)).start()
    for j in range(2):
        acts.near(far_first(at.col, j))
        acts.to_across(far_first(at.col, j)).start()
    keep_acts = [
        act_copy(act_wide, act_out, at, j, local.at[2 + j]) for j in range(4)
    ]
    for copy in keep_acts[2:]:
        copy.start()
    for j in range(4):
        arrive(gates, j)
    weight_grad(n_gate, left, lambda s: rows_of(gate_wide, s))
    pair = remote(n_gate, others[0], y_send.at[0], y_recv.at[0], dp=at.pair(2, 1)) if pairs == 2 else None
    if pairs == 2:
        pair.start()
    keep_gate = pltpu.make_async_copy(n_gate, gate_n, local.at[0])
    keep_gate.start()
    arrive(ups, 0)
    for j in range(3):
        back(j)
        pl.when(at.end)(lambda: back_sum.step(far_first(at.col, j)))
        arrive(ups, j + 1)
        pl.when(mid)(lambda: back_sum.step(far_first(at.col, j)))
    weight_grad(n_up, left, lambda s: rows_of(up_wide, s))
    keep_up = pltpu.make_async_copy(n_up, up_n, local.at[1])
    keep_up.start()
    back(3)
    arrive(acts, 0)
    keep_acts[0].start()
    back_sum.step(at.col)
    arrive(acts, 1)
    keep_acts[1].start()

    gather.close()
    for dist in range(4):
        gather.loop(dist, close_share)
    gates.close(4)
    ups.close(4)
    for j in range(2):
        acts.close_one(far_first(at.col, j))
    back_sum.close()
    for copy in keep_acts:
        copy.wait()
    keep_gate.wait()
    keep_up.wait()
    if pairs == 2:
        pair.wait()


def middle(pairs, number, hn, w_gate, w_up, dact, full):
    tokens, feats = hn.shape
    ff = w_gate.shape[1]
    quarter = tokens // 4
    dma = pltpu.SemaphoreType.DMA
    any_spec, vmem = pl.BlockSpec(memory_space=pl.ANY), pl.BlockSpec(memory_space=pltpu.VMEM)
    shape = jax.ShapeDtypeStruct
    narrow = shape((feats, ff), BF16)
    others = 1 if pairs == 2 else 0
    out = pl.pallas_call(
        functools.partial(middle_kernel, pairs),
        out_shape=tuple(
            [shape((tokens, feats), F32), shape((4, 4, quarter, ff), BF16), narrow, narrow] + [narrow] * others
        ),
        in_specs=[vmem] + [any_spec] * 4,
        out_specs=tuple([vmem] + [any_spec] * (3 + others)),
        scratch_shapes=[
            pltpu.VMEM((4, tokens, feats), BF16),
            pltpu.VMEM((4, 4, quarter, feats), BF16),
            pltpu.VMEM((2, 4, feats, ff), BF16),
            held(dact),
            pltpu.VMEM((2, quarter, 512), F32),
            pltpu.VMEM((4, 4, quarter, ff), BF16),
            pltpu.VMEM((4, 4, quarter, ff), BF16),
            pltpu.VMEM((4, 4, quarter, ff), BF16),
            pltpu.VMEM((feats, ff), BF16),
            pltpu.VMEM((feats, ff), BF16),
        ]
        + chain_scratch(tokens, feats)
        + col_gather_sems()
        + [dma((3, 4)), dma((4, 3)), dma((4, 3))]
        + [dma((4,))] * 18
        + chain_sems()
        + [dma((6,)), dma((1,)), dma((1,))],
        compiler_params=pltpu.CompilerParams(
            collective_id=number, has_side_effects=True, vmem_limit_bytes=VMEM_LIMIT
        ),
        name="middle",
    )(hn, w_gate, w_up, dact, full)
    return out[:4], out[4:]


def tail_kernel(pairs, q_heads, groups, *refs):
    refs = list(refs)

    def take(count):
        found = refs[:count]
        del refs[:count]
        return found

    (w_out, q_gain, k_gain, dhn, hidden, scale_two, gain_two, gy, x_ref, scale_one, gain_one) = take(11)
    late = take(12)
    (gy_wide, mixed_wide, normed_wide, up_n) = take(4)
    (in_grad, layer_out, one_grad, two_grad, q_grad, k_grad) = take(6)
    kept_out = take(5)
    others = take(6) if pairs == 2 else []
    (w_down, w_query, w_key, w_value, qkv, qa, ka, va, probs, cos, sin) = late_held = take(11)
    (da_wide, act_wide, dqkv, dqkv_wide, held_wide, product, grad_mixed, dq, dk, dv, *narrow) = take(15)
    (dh, q_part, k_part, packet, packet_got, by_row, summed, summed_got) = take(8)
    first_bufs, last_bufs = take(2), take(2)
    moved = take(5)
    down_bufs, dxn_bufs = take(3), take(3)
    (g_send, g_recv, local, y_send, y_recv, late_sems) = take(6)
    moved_sems = take(4)
    act_sems, dqkv_sems = take(6), take(7)
    down_sems, dxn_sems = take(3), take(3)
    first_sems, last_sems = take(2), take(2)
    (p_send, p_recv, r_send, r_recv, s_send, s_recv) = take(6)

    at = Ends()
    feats = dhn.shape[1]
    model_width = 4 * feats
    gain_spot = pl.ds(pl.multiple_of(at.row * feats, feats), feats)
    fetch_acts = [act_copy(late[0], act_wide, at, j, local.at[8 + j]) for j in range(4)]
    for copy in reversed(fetch_acts):
        copy.start()
    fetch = Fetch(list(zip(late[1:], late_held)), late_sems)
    fetch.start()
    first_total = RowTotal(at, *first_bufs, *first_sems)
    last_total = RowTotal(at, *last_bufs, *last_sems)
    at.greet(pairs, True)

    def pair_copy(src, index):
        return remote(src, others[index], y_send.at[index], y_recv.at[index], dp=1 - lax.axis_index("dp"))

    n_down, n_out, n_query, n_key, n_value = narrow
    narrow = [up_n, *narrow]

    def to_pair(index):
        if pairs == 2:
            pair_copy(narrow[index], index).start()

    def load(index, src):
        return pltpu.make_async_copy(src, held_wide, local.at[index])

    def keep(index):
        return pltpu.make_async_copy(narrow[index], kept_out[index - 1], local.at[2 + index])

    to_pair(0)
    load(0, gy_wide).start()
    gather = ColGather(at, da_wide, g_send, g_recv)
    row_sum = RowSumWhole(at, product, grad_mixed, *moved, *moved_sems)
    acts = RowGather(at, lambda s: act_wide.at[s, at.row], lambda s, q: act_wide.at[s, q], act_sems)
    half = dqkv.shape[0] // 2
    grads = RowGather(
        at, lambda h: dqkv.at[pl.ds(h * half, half)], lambda h, q: dqkv_wide.at[q, pl.ds(h * half, half)], dqkv_sems
    )
    down_sum = ColSum(at, product, *down_bufs, *down_sems)
    dxn_sum = ColSum(at, product, *dxn_bufs, *dxn_sems)

    weighted = dhn[...] * gain_two[:, gain_spot]
    first_total.start(jnp.sum(weighted * hidden[...], axis=1, keepdims=True))
    for copy in reversed(fetch_acts):
        copy.wait()
    for j in range(2, 4):
        acts.to_across(far_first(at.col, j)).start()
        acts.near(far_first(at.col, j))
    scale = scale_two[...]
    packet[...] = jnp.zeros_like(packet)
    packet[1:2, :] = jnp.sum(dhn[...] * hidden[...] * scale, axis=0, keepdims=True)
    inner = first_total.finish()
    dh[...] = (
        gy[...].astype(F32)
        + scale * (dhn[...] * gain_two[:, gain_spot])
        - hidden[...] * (scale * scale * scale * inner * (1.0 / model_width))
    )
    da_wide[at.col] = dh[...].astype(BF16)
    gather.arrive(0)

    def back_out(s):
        product[...] = lax.dot_general(
            da_wide[s], w_out[...], (((1,), (1,)), ((), ())), preferred_element_type=F32
        )
        row_sum.give(s)

    def take_act(j):
        s = far_first(at.col, j)
        acts.wait_near(s)
        acts.take_across(s)
        acts.wait_diag(s)

    def act_rows(s, cols):
        return act_wide[s, :, :, cols].reshape(product.shape[0], cols.size)

    def down_step(j):
        s = far_first(at.col, j)
        product[...] = jnp.dot(
            act_rows(s, pl.ds(0, act_wide.shape[3])), w_down[...], preferred_element_type=F32
        )
        down_sum.step(s)

    def dxn_step(j, halves=(0, 1)):
        s = near_first(at, j)
        for h in halves:
            rows = pl.ds(h * half, half)
            total, base = None, 0
            for w in (w_query, w_key, w_value):
                size = w.shape[1]
                term = lax.dot_general(
                    dqkv_wide[s, rows, pl.ds(base, size)], w[...], (((1,), (1,)), ((), ())),
                    preferred_element_type=F32,
                )
                total = term if total is None else total + term
                base += size
            product[rows, :] = total
        dxn_sum.step(s, halves)

    def down_weight():
        load(0, gy_wide).wait()
        weight_grad(n_down, act_rows, lambda s: held_wide[s])
        to_pair(1)
        keep(1).start()
        load(1, mixed_wide).start()

    mid = jnp.logical_not(at.end)
    fetch.wait()
    gather.loop(0, back_out)
    gather.arrive(1)
    gather.loop(1, back_out)
    down_step(0)
    gather.arrive(2)
    gather.loop(2, back_out)
    take_act(2)
    down_step(1)
    take_act(3)

    @pl.when(at.end)
    def _():
        down_step(2)

    down_weight()
    gather.arrive(3)
    gather.loop(3, back_out)
    row_sum.finish()
    attend_back(
        q_heads, groups, grad_mixed, qkv, qa, ka, va, probs, cos, sin, q_gain, k_gain,
        dqkv, q_part, k_part, dq, dk, dv,
    )
    for h in range(2):
        grads.to_across(h).start()
    for h in range(2):
        grads.near(h)
    for h in range(2):
        grads.wait_near(h)

    @pl.when(at.end)
    def _():
        dxn_step(0)
        pl.when(jnp.logical_not(at.paired))(lambda: dxn_step(1))

    @pl.when(mid)
    def _():
        down_step(2)

    load(1, mixed_wide).wait()
    weight_grad(n_out, lambda s, here: held_wide[s, :, here], lambda s: da_wide[s])
    to_pair(2)
    keep(2).start()
    load(2, normed_wide).start()
    for h in range(2):
        grads.take_across(h)
        grads.wait_diag(h)

        @pl.when(at.end)
        def _():
            pl.when(at.paired)(lambda: dxn_step(1, (h,)))
            dxn_step(2, (h,))

        if h == 0:
            pl.when(mid)(lambda: dxn_step(0))

    load(2, normed_wide).wait()
    base = 0
    for index, some in ((3, n_query), (4, n_key), (5, n_value)):
        spot = pl.ds(base, some.shape[1])
        weight_grad(some, lambda s, here: held_wide[s, :, here], lambda s, spot=spot: dqkv_wide[s, :, spot])
        to_pair(index)
        keep(index).start()
        base += some.shape[1]

    @pl.when(mid)
    def _():
        dxn_step(1)
        dxn_step(2)

    down_step(3)
    layer_out[...] = (hidden[...] + product[...]).astype(BF16)
    dxn_step(3)
    scale = scale_one[...]
    last_total.start(
        jnp.sum(product[...] * gain_one[:, gain_spot] * x_ref[...].astype(F32), axis=1, keepdims=True)
    )
    packet[0:1, :] = jnp.sum(product[...] * x_ref[...].astype(F32) * scale, axis=0, keepdims=True)
    packet[2:3, :HEAD_SIZE] = q_part[...]
    packet[2:3, HEAD_SIZE : 2 * HEAD_SIZE] = k_part[...]

    def to_line(step):
        return remote(
            packet, packet_got.at[step - 1], p_send.at[step - 1], p_recv.at[step - 1],
            col=lax.rem(at.col + step, 4),
        )

    def to_row(index, peer):
        return remote(by_row.at[at.row], by_row.at[at.row], r_send.at[index], r_recv.at[index], row=peer)

    def from_row(index, peer):
        return remote(by_row.at[peer], by_row.at[peer], r_send.at[index], r_recv.at[index], row=peer)

    def to_peer(step):
        return remote(
            summed, summed_got.at[step - 1], s_send.at[step - 1], s_recv.at[step - 1], dp=at.pair(pairs, step)
        )

    for step in range(1, 4):
        to_line(step).start()
    inner = last_total.finish()
    in_grad[...] = (
        dh[...]
        + scale * (product[...] * gain_one[:, gain_spot])
        - x_ref[...].astype(F32) * (scale * scale * scale * inner * (1.0 / model_width))
    )
    for step in range(1, 4):
        to_line(step).wait()
    by_row[at.row] = (packet[...] + packet_got[0]) + (packet_got[1] + packet_got[2])
    peers = (at.mate, at.across, at.diag)
    for index, peer in enumerate(peers):
        to_row(index, peer).start()
    for index, peer in enumerate(peers):
        from_row(index, peer).wait_recv()
        to_row(index, peer).wait_send()
    summed[...] = jnp.zeros_like(summed)
    for r in range(4):
        summed[r : r + 1, :] = by_row[r, 0:1, :]
        summed[4 + r : 5 + r, :] = by_row[r, 1:2, :]
    summed[8:9, :] = (by_row[0, 2:3, :] + by_row[1, 2:3, :]) + (by_row[2, 2:3, :] + by_row[3, 2:3, :])
    for step in range(1, pairs):
        to_peer(step).start()
    for step in range(1, pairs):
        to_peer(step).wait()
    total = summed[...]
    for step in range(1, pairs):
        total = total + summed_got[step - 1]
    for r in range(4):
        one_grad[:, r * feats : (r + 1) * feats] = total[r : r + 1, :]
        two_grad[:, r * feats : (r + 1) * feats] = total[4 + r : 5 + r, :]
    q_grad[...] = total[8:9, :HEAD_SIZE]
    k_grad[...] = total[8:9, HEAD_SIZE : 2 * HEAD_SIZE]

    gather.close()
    row_sum.close()
    for j in range(2, 4):
        acts.close_one(far_first(at.col, j))
    grads.close(2)
    down_sum.close()
    dxn_sum.close()
    for index in range(1, 6):
        keep(index).wait()
    if pairs == 2:
        for index in range(6):
            pair_copy(narrow[index], index).wait()


def tail(pairs, q_heads, groups, number, act, weights, saved, tables, norms, wides, narrow):
    tokens, feats = norms[0].shape
    w_out, w_down, w_query, w_key, _ = weights
    ff = w_down.shape[0]
    width = saved[0].shape[1]
    q_width, k_width = saved[1].shape[1], saved[2].shape[1]
    dma = pltpu.SemaphoreType.DMA
    any_spec, vmem = pl.BlockSpec(memory_space=pl.ANY), pl.BlockSpec(memory_space=pltpu.VMEM)
    shape = jax.ShapeDtypeStruct
    shapes = [
        shape((tokens, feats), F32),
        shape((tokens, feats), BF16),
        shape((1, 4 * feats), F32),
        shape((1, 4 * feats), F32),
        shape((1, HEAD_SIZE), F32),
        shape((1, HEAD_SIZE), F32),
    ]
    own = [
        shape((ff, feats), BF16),
        shape((q_width, feats), BF16),
        shape((feats, q_width), BF16),
        shape((feats, k_width), BF16),
        shape((feats, k_width), BF16),
    ]
    others = [shape(n.shape, BF16) for n in narrow] + own if pairs == 2 else []
    packet = pltpu.VMEM((8, feats), F32)
    early = (w_out, *tables[2:], *norms)
    late = (act, *weights[1:], *saved, *tables[:2])
    out = pl.pallas_call(
        functools.partial(tail_kernel, pairs, q_heads, groups),
        out_shape=tuple(shapes + own + others),
        in_specs=[vmem] * len(early) + [any_spec] * (len(late) + 4),
        out_specs=tuple([vmem] * 6 + [any_spec] * (5 + len(others))),
        scratch_shapes=[held(array) for array in late[1:]]
        + [
            pltpu.VMEM((4, tokens, feats), BF16),
            pltpu.VMEM((4, 4, tokens // 4, ff), BF16),
            pltpu.VMEM((tokens, width), BF16),
            pltpu.VMEM((4, tokens, width), BF16),
            pltpu.VMEM((4, tokens, feats), BF16),
            pltpu.VMEM((tokens, feats), F32),
            pltpu.VMEM((tokens, q_width), F32),
            pltpu.VMEM((tokens, q_width), F32),
            pltpu.VMEM((tokens, k_width), F32),
            pltpu.VMEM((tokens, k_width), F32),
        ]
        + [held(array) for array in own]
        + [
            pltpu.VMEM((tokens, feats), F32),
            pltpu.VMEM((1, HEAD_SIZE), F32),
            pltpu.VMEM((1, HEAD_SIZE), F32),
            packet,
            pltpu.VMEM((3, 8, feats), F32),
            pltpu.VMEM((4, 8, feats), F32),
            pltpu.VMEM((16, feats), F32),
            pltpu.VMEM((max(pairs - 1, 1), 16, feats), F32),
        ]
        + row_total_scratch(tokens) * 2
        + row_sum_scratch(tokens, q_width)
        + chain_scratch(tokens, feats) * 2
        + col_gather_sems()
        + [dma((12,)), dma((6,)), dma((6,)), dma((12,))]
        + row_sum_sems()
        + [dma((4,))] * 6
        + [dma((2,))] * 7
        + chain_sems() * 2
        + row_total_sems() * 2
        + [dma((3,))] * 4
        + [dma((max(pairs - 1, 1),))] * 2,
        compiler_params=pltpu.CompilerParams(
            collective_id=number, has_side_effects=True, vmem_limit_bytes=VMEM_LIMIT
        ),
        name="tail",
    )(*early, *late, *wides, *narrow)
    return out[:6], out[6:11], out[11:]


def finish_kernel(count, *refs):
    parts, others, rest = refs[:count], refs[count : 2 * count], refs[2 * count :]
    kept = len(rest) - count
    for a, b, out in zip(parts, others, rest[kept // 2 :]):
        out[...] = a[...].astype(F32) + b[...].astype(F32)
    for src, dst in zip(rest[: kept // 2], rest[kept // 2 + count :]):
        dst[...] = src[...]


def finish(parts, others, rest, steps=8):
    def spec(array):
        block = (array.shape[0] // steps, array.shape[1]) if array.shape[0] % steps == 0 else array.shape
        index = (lambda i: (i, 0)) if block != array.shape else (lambda i: (0, 0))
        return pl.BlockSpec(block, index)

    outs = [jax.ShapeDtypeStruct(a.shape, F32) for a in parts] + [jax.ShapeDtypeStruct(a.shape, a.dtype) for a in rest]
    operands = (*parts, *others, *rest)
    out = pl.pallas_call(
        functools.partial(finish_kernel, len(parts)),
        grid=(steps,),
        out_shape=tuple(outs),
        in_specs=[spec(a) for a in operands],
        out_specs=tuple(spec(a) for a in outs),
        compiler_params=pltpu.CompilerParams(vmem_limit_bytes=VMEM_LIMIT),
        name="finish",
    )(*operands)
    return out[: len(parts)], out[len(parts) :]


def shards(
    pairs,
    hidden_in,
    segment_ids,
    attn_gain,
    w_query,
    key_projection,
    value_projection,
    query_gain,
    key_norm_gain,
    w_out,
    ffn_gain,
    w_gate,
    w_up,
    w_down,
    out_grad,
):
    tokens = hidden_in.shape[0]
    model_width = attn_gain.shape[0]
    q_width = w_query.shape[1]
    k_width = key_projection.shape[1]
    q_heads = q_width // HEAD_SIZE
    groups = q_width // k_width
    tables = (*turn_tables(tokens), query_gain[None, :], key_norm_gain[None, :])
    (scale_one, hidden, scale_two, ffn_in, qkv, q_turned, k_turned, values, probs, grad_inner, xn_wide, gy_wide, mixed_wide, full) = front(
        pairs, q_heads, groups, model_width, 0, hidden_in, out_grad,
        (w_query, key_projection, value_projection, w_out, w_down),
        segment_ids[None, :],
        tables,
        (attn_gain[None, :], ffn_gain[None, :]),
        (w_gate, w_up),
    )
    (grad_ffn_in, inner_act, gate_n, up_n), other_gate = middle(pairs, 1, ffn_in, w_gate, w_up, grad_inner, full)
    (in_grad, layer_out, one_grad, two_grad, q_gain_grad, k_gain_grad), own, others = tail(
        pairs, q_heads, groups, 2, inner_act,
        (w_out, w_down, w_query, key_projection, value_projection),
        (qkv, q_turned, k_turned, values, probs),
        tables,
        (grad_ffn_in, hidden, scale_two, ffn_gain[None, :], out_grad, hidden_in, scale_one, attn_gain[None, :]),
        (gy_wide, mixed_wide, xn_wide),
        (up_n,),
    )
    parts = (gate_n, up_n, *own)
    if pairs == 2:
        rest = (in_grad, layer_out, one_grad, two_grad, q_gain_grad, k_gain_grad)
        sums, rest = finish(parts, (*other_gate, *others), rest)
        in_grad, layer_out, one_grad, two_grad, q_gain_grad, k_gain_grad = rest
    else:
        sums = lax.psum(tuple(part.astype(F32) for part in parts), "dp")
    gate_grad, up_grad, down_grad, out_weight_grad, query_grad, key_grad, value_grad = sums
    return (
        layer_out,
        in_grad,
        one_grad.reshape(-1),
        query_grad,
        key_grad,
        value_grad,
        q_gain_grad.reshape(-1),
        k_gain_grad.reshape(-1),
        out_weight_grad,
        two_grad.reshape(-1),
        gate_grad,
        up_grad,
        down_grad,
    )


def solution(mesh):
    acts, grid, flip, none = P(("dp", "col"), "row"), P("row", "col"), P("col", "row"), P()
    return jax.shard_map(
        functools.partial(shards, mesh.shape["dp"]),
        mesh=mesh,
        in_specs=(
            acts, P(("dp", "row")), none, grid, grid, grid, none, none, flip, none, grid, grid, flip, acts,
        ),
        out_specs=(
            acts, acts, none, grid, grid, grid, none, none, flip, none, grid, grid, flip,
        ),
        check_vma=False,
    )
```

```python
import functools
import math

import jax
import jax.numpy as jnp
import numpy as np
from jax import lax
from jax.experimental import pallas as pl
from jax.experimental.pallas import tpu as pltpu
from jax.sharding import PartitionSpec as P

HEAD_SIZE = 128
EPSILON = 1e-06
THETA = 1000000.0
MASKED = -1e30
MESH = pl.DeviceIdType.MESH
BF16 = jnp.bfloat16
F32 = jnp.float32
VMEM_LIMIT = 60 << 20


def to(**where):
    return dict(device_id=where, device_id_type=MESH)


class Ends:
    def __init__(self):
        self.row = lax.axis_index("row")
        self.col = lax.axis_index("col")
        self.chip = lax.div(self.row, 2)
        self.core = lax.rem(self.row, 2)
        self.mate = self.chip * 2 + (1 - self.core)
        self.across = (1 - self.chip) * 2 + self.core
        self.diag = (1 - self.chip) * 2 + (1 - self.core)
        self.end = (self.col == 0) | (self.col == 3)
        self.paired = lax.div(self.col, 2) == self.chip

    def greet(self, pairs=0, line=False, rows=False):
        gate = pltpu.get_barrier_semaphore()
        count = 3
        for peer in (self.mate, self.across, self.diag):
            pl.semaphore_signal(gate, inc=1, **to(row=peer))
        for step in range(1, pairs):
            dp = self.pair(pairs, step)
            for row in range(4) if rows else (self.row,):
                pl.semaphore_signal(gate, inc=1, **to(dp=dp, row=row))
                count += 1
        if line:
            for step in range(1, 4):
                pl.semaphore_signal(gate, inc=1, **to(col=lax.rem(self.col + step, 4)))
                count += 1
        else:

            @pl.when(self.col > 0)
            def _():
                pl.semaphore_signal(gate, inc=1, **to(col=self.col - 1))

            @pl.when(self.col < 3)
            def _():
                pl.semaphore_signal(gate, inc=1, **to(col=self.col + 1))

            count += jnp.where(self.col > 0, 1, 0) + jnp.where(self.col < 3, 1, 0)
        pl.semaphore_wait(gate, count)

    def pair(self, pairs, step):
        return lax.rem(lax.axis_index("dp") + step, pairs)


class RowTotal:
    def __init__(self, at, own, got, sends, recvs):
        self.own, self.got = own, got
        self.copies = [
            remote(own, got.at[i], sends.at[i], recvs.at[i], row=peer)
            for i, peer in enumerate((at.mate, at.across, at.diag))
        ]

    def start(self, column):
        self.own[...] = jnp.broadcast_to(column, (column.shape[0], 128)).T[:8, :]
        for copy in self.copies:
            copy.start()

    def finish(self):
        for copy in self.copies:
            copy.wait()
        total = (self.own[...] + self.got[0]) + (self.got[1] + self.got[2])
        return jnp.concatenate([total] * 16, axis=0).T[:, :1]


def row_total_scratch(tokens):
    return [pltpu.VMEM((8, tokens), F32), pltpu.VMEM((3, 8, tokens), F32)]


def row_total_sems():
    return [pltpu.SemaphoreType.DMA((3,)), pltpu.SemaphoreType.DMA((3,))]


def remote(src, dst, sends, recvs, **where):
    return pltpu.make_async_remote_copy(
        src_ref=src, dst_ref=dst, send_sem=sends, recv_sem=recvs, **to(**where)
    )


class Fetch:
    def __init__(self, pairs, sems):
        self.copies = [
            pltpu.make_async_copy(src, dst, sems.at[i]) for i, (src, dst) in enumerate(pairs)
        ]

    def start(self):
        for copy in self.copies:
            copy.start()

    def wait(self, first=0, last=None):
        for copy in self.copies[first:last]:
            copy.wait()


def held(array):
    return pltpu.VMEM(array.shape, array.dtype)


def in_rows(count, step, body, first=0):
    def one(i, _):
        body(pl.ds(pl.multiple_of(first + i * step, step), step))
        return 0

    lax.fori_loop(0, count // step, one, 0)


class ColGather:
    def __init__(self, at, wide, sends, recvs):
        self.at, self.wide, self.sends, self.recvs = at, wide, sends, recvs
        self.half = wide.shape[1] // 2

    def copy(self, s, h, side, col):
        part = self.wide.at[s, pl.ds(h * self.half, self.half)]
        return remote(part, part, self.sends.at[side, s, h], self.recvs.at[s, h], col=col)

    def up(self, s, h):
        return self.copy(s, h, 0, self.at.col + 1)

    def down(self, s, h):
        return self.copy(s, h, 1, self.at.col - 1)

    def loop(self, dist, body):
        if dist == 0:
            body(self.at.col)
            return

        def one(side, _):
            s = jnp.where(side == 0, self.at.col - dist, self.at.col + dist)
            pl.when((s >= 0) & (s <= 3))(lambda: body(s))
            return 0

        lax.fori_loop(0, 2, one, 0)

    def arrive(self, dist):
        for h in range(2):

            def take(s, h=h):
                if dist:
                    self.up(s, h).wait_recv()

                @pl.when((s <= self.at.col) & (self.at.col < 3))
                def _():
                    self.up(s, h).start()

                @pl.when((s >= self.at.col) & (self.at.col > 0))
                def _():
                    self.down(s, h).start()

            self.loop(dist, take)

    def send_up(self):
        for h in range(2):
            self.up(self.at.col, h).start()

    def send_down(self):
        for h in range(2):
            self.down(self.at.col, h).start()

    def close(self):
        def one(s, _):
            for h in range(2):

                @pl.when((s <= self.at.col) & (self.at.col < 3))
                def _():
                    self.up(s, h).wait_send()

                @pl.when((s >= self.at.col) & (self.at.col > 0))
                def _():
                    self.down(s, h).wait_send()

            return 0

        lax.fori_loop(0, 4, one, 0)


class RowSumWhole:
    def __init__(self, at, product, out, a_send, a_recv, c_recv, d_send, d_recv, m_send, m_recv, x_send, x_recv):
        self.at, self.product, self.out = at, product, out
        self.a_send, self.a_recv, self.c_recv, self.d_send, self.d_recv = a_send, a_recv, c_recv, d_send, d_recv
        self.m_send, self.m_recv, self.x_send, self.x_recv = m_send, m_recv, x_send, x_recv
        self.half = product.shape[0] // 2
        self.d = remote(d_send, d_recv, m_send.at[2], m_recv.at[2], row=at.mate)

    def a(self, i):
        return remote(self.a_send.at[i], self.a_recv.at[i], self.m_send.at[i], self.m_recv.at[i], row=self.at.mate)

    def b(self, i, s):
        core = self.at.core
        return remote(self.a_recv.at[i], self.c_recv.at[core], self.x_send.at[i], self.x_recv.at[core], row=s)

    def part(self, core, here):
        return pl.ds(pl.multiple_of(core * self.half + here.start, here.size), here.size)

    def give(self, s):
        at, product, half = self.at, self.product, self.half
        i = lax.rem(s, 2)
        ours = lax.div(s, 2) == at.chip

        @pl.when(jnp.logical_not(ours))
        def _():
            def cast(here):
                self.a_send[i, here] = product[self.part(1 - at.core, here), :].astype(BF16)

            in_rows(half, 64, cast)
            self.a(i).start()
            self.a(i).wait_recv()

            def add(here):
                total = product[self.part(at.core, here), :] + self.a_recv[i, here].astype(F32)
                self.a_recv[i, here] = total.astype(BF16)

            in_rows(half, 64, add)
            self.b(i, s).start()

        @pl.when(ours & (i != at.core))
        def _():
            def cast(here):
                self.d_send[here] = product[here, :].astype(BF16)

            in_rows(2 * half, 64, cast)
            self.d.start()

        @pl.when(s == at.row)
        def _():
            def store(here):
                self.out[here] = product[here, :]

            in_rows(2 * half, 64, store)

    def finish(self):
        self.d.wait_recv()
        for h in range(2):
            here = self.c_recv.at[h]
            remote(here, here, self.x_send.at[h], self.x_recv.at[h], row=self.at.across).wait_recv()

            def add(rows, h=h):
                spot = pl.ds(pl.multiple_of(h * self.half + rows.start, rows.size), rows.size)
                self.out[spot] += self.d_recv[spot].astype(F32) + self.c_recv[h, rows].astype(F32)

            in_rows(self.half, 64, add)

    def close(self):
        self.d.wait_send()
        for i in range(2):
            self.a(i).wait_send()
            self.b(i, self.at.across).wait_send()


def row_sum_scratch(tokens, width):
    half = pltpu.VMEM((2, tokens // 2, width), BF16)
    full = pltpu.VMEM((tokens, width), BF16)
    return [half, half, half, full, full]


def row_sum_sems():
    dma = pltpu.SemaphoreType.DMA
    return [dma((3,)), dma((3,)), dma((2,)), dma((2,))]


class RowSumQuarter:
    def __init__(self, at, chunk, keep, a_send, a_recv, c_recv, d_send, d_recv, m_send, m_recv, x_send, x_recv):
        self.at, self.chunk, self.keep = at, chunk, keep
        self.a_send, self.a_recv, self.c_recv = a_send, a_recv, c_recv
        self.d_send, self.d_recv = d_send, d_recv
        self.sems = (m_send, m_recv, x_send, x_recv)

    def a(self, s):
        m_send, m_recv, _, _ = self.sems
        return remote(self.a_send.at[s], self.a_recv.at[s], m_send.at[0, s], m_recv.at[0, s], row=self.at.mate)

    def d(self, s):
        m_send, m_recv, _, _ = self.sems
        return remote(self.d_send.at[s], self.d_recv.at[s], m_send.at[1, s], m_recv.at[1, s], row=self.at.mate)

    def b(self, s):
        _, _, x_send, x_recv = self.sems
        return remote(self.a_recv.at[s], self.c_recv.at[s], x_send.at[s], x_recv.at[s], row=self.at.across)

    def split(self, s, value, spot, own):
        at, chunk = self.at, self.chunk
        chunk[...] = value

        def quarter(q):
            return chunk[pl.ds(pl.multiple_of(q * 128, 128), 128), :]

        self.a_send[s, :, spot] = quarter(at.diag).astype(BF16)
        self.keep[:, spot] = quarter(at.across)
        self.d_send[s, :, spot] = quarter(at.mate).astype(BF16)
        own[s, :, spot] = quarter(at.row).astype(own.dtype)

    def give(self, s):
        self.a(s).start()
        self.d(s).start()
        self.a(s).wait_recv()

        def one(here):
            self.a_recv[s, here] = (self.keep[here, :] + self.a_recv[s, here].astype(F32)).astype(BF16)

        in_rows(128, 16, one)
        self.b(s).start()

    def finish(self, s):
        self.d(s).wait_recv()
        self.b(s).wait_recv()

    def close(self):
        def one(s, _):
            self.a(s).wait_send()
            self.b(s).wait_send()
            self.d(s).wait_send()
            return 0

        lax.fori_loop(0, 4, one, 0)


class RowGather:
    def __init__(self, at, own, slot, sems):
        self.at, self.own, self.slot = at, own, slot
        self.m_send, self.m_recv, self.x_send, self.x_recv, self.f_send, self.f_recv, self.local = (*sems, None)[:7]

    def to_mate(self, s):
        return remote(self.own(s), self.slot(s, self.at.row), self.m_send.at[s], self.m_recv.at[s], row=self.at.mate)

    def to_across(self, s):
        return remote(self.own(s), self.slot(s, self.at.row), self.x_send.at[s], self.x_recv.at[s], row=self.at.across)

    def pass_on(self, s):
        here = self.slot(s, self.at.across)
        return remote(here, here, self.f_send.at[s], self.f_recv.at[s], row=self.at.mate)

    def move_own(self, s):
        return pltpu.make_async_copy(self.own(s), self.slot(s, self.at.row), self.local.at[s])

    def near(self, s):
        self.to_mate(s).start()
        if self.local is not None:
            self.move_own(s).start()

    def wait_near(self, s):
        here = self.slot(s, self.at.mate)
        remote(here, here, self.m_send.at[s], self.m_recv.at[s], row=self.at.mate).wait_recv()
        if self.local is not None:
            self.move_own(s).wait()

    def take_across(self, s):
        here = self.slot(s, self.at.across)
        remote(here, here, self.x_send.at[s], self.x_recv.at[s], row=self.at.across).wait_recv()
        self.pass_on(s).start()

    def wait_diag(self, s):
        here = self.slot(s, self.at.diag)
        remote(here, here, self.f_send.at[s], self.f_recv.at[s], row=self.at.mate).wait_recv()

    def close_one(self, s):
        self.to_mate(s).wait_send()
        self.to_across(s).wait_send()
        self.pass_on(s).wait_send()

    def close(self, count):
        def one(s, _):
            self.close_one(s)
            return 0

        lax.fori_loop(0, count, one, 0)


class WeightGather:
    def __init__(self, at, pairs, own, full, sems):
        self.at, self.pairs, self.own, self.full = at, pairs, own, full
        self.m_send, self.m_recv, self.x_send, self.x_recv, self.y_send, self.y_recv = sems[:6]
        self.f_send, self.f_recv, self.g_send, self.g_recv = sems[6:]
        self.step = full.shape[2] // 4
        self.mine = lax.axis_index("dp") if pairs == 2 else None

    def rows(self, j):
        return pl.ds(j * self.step, self.step)

    def piece(self, which, row, j):
        return self.full.at[which, row, self.rows(j)]

    def held(self):
        return (self.mine,) if self.pairs == 2 else (0, 1)

    def near(self, which, row):
        here = self.full.at[which, row]
        return remote(self.own[which], here, self.m_send.at[which], self.m_recv.at[which], row=self.at.mate)

    def over(self, which, row, j, src=None):
        here = self.piece(which, row, j)
        lane = 0 if self.pairs == 2 else which
        src = here if src is None else src
        return remote(src, here, self.x_send.at[lane, j], self.x_recv.at[lane, j], row=self.at.across)

    def hand(self, which, j):
        here = self.piece(which, self.at.across, j)
        return remote(here, here, self.y_send.at[j], self.y_recv.at[j], dp=self.at.pair(2, 1))

    def pass_first(self, which, row, j):
        here = self.piece(which, row, j)
        lane = 0 if self.pairs == 2 else which
        return remote(here, here, self.f_send.at[lane, j], self.f_recv.at[lane, j], row=self.at.mate)

    def pass_second(self, which, row, j):
        here = self.piece(which, row, j)
        return remote(here, here, self.g_send.at[j], self.g_recv.at[j], row=self.at.mate)

    def begin(self):
        for i in range(2):
            self.near(i, self.at.row).start()

    def send(self, j):
        for which in range(2):
            copy = self.over(which, self.at.row, j, self.own[which].at[self.rows(j)])
            if self.pairs == 2:
                pl.when(self.mine == which)(copy.start)
            else:
                copy.start()

    def forward(self, j):
        for which in self.held():
            self.over(which, self.at.across, j).wait_recv()
            if self.pairs == 2:
                self.hand(which, j).start()
            self.pass_first(which, self.at.across, j).start()

    def finish(self, j):
        if self.pairs == 2:
            self.hand(1 - self.mine, j).wait_recv()
            self.pass_second(1 - self.mine, self.at.across, j).start()

    def close(self):
        for i in range(2):
            self.near(i, self.at.mate).wait_recv()
            self.near(i, self.at.row).wait_send()
        for j in range(4):
            for which in self.held():
                self.over(which, self.at.row, j).wait_send()
                self.pass_first(which, self.at.diag, j).wait_recv()
                self.pass_first(which, self.at.across, j).wait_send()
            if self.pairs == 2:
                self.hand(self.mine, j).wait_send()
                self.pass_second(1 - self.mine, self.at.diag, j).wait_recv()
                self.pass_second(1 - self.mine, self.at.across, j).wait_send()


def weight_gather_sems(pairs):
    dma = pltpu.SemaphoreType.DMA
    lanes = 1 if pairs == 2 else 2
    return [
        dma((2,)), dma((2,)), dma((lanes, 4)), dma((lanes, 4)), dma((4,)), dma((4,)),
        dma((lanes, 4)), dma((lanes, 4)), dma((4,)), dma((4,)),
    ]


class ColSum:
    def __init__(self, at, product, sent, got, extra, sends, recvs, extra_recvs):
        self.at, self.product, self.sent, self.got, self.extra = at, product, sent, got, extra
        self.sends, self.recvs, self.extra_recvs = sends, recvs, extra_recvs
        self.half = product.shape[0] // 2

    def part(self, h):
        return pl.ds(h * self.half, self.half)

    def up(self, s, h):
        return remote(
            self.sent.at[s, self.part(h)], self.got.at[s, self.part(h)],
            self.sends.at[s, h], self.recvs.at[s, h], col=self.at.col + 1,
        )

    def down(self, s, h):
        return remote(
            self.sent.at[s, self.part(h)], self.got.at[s, self.part(h)],
            self.sends.at[s, h], self.recvs.at[s, h], col=self.at.col - 1,
        )

    def last_down(self, s, h):
        return remote(
            self.sent.at[s, self.part(h)], self.extra.at[self.part(h)],
            self.sends.at[s, h], self.extra_recvs.at[h], col=self.at.col - 1,
        )

    def step(self, s, halves=(0, 1)):
        col, product = self.at.col, self.product
        for h in halves:
            @pl.when(((s >= col) & (col > 0)) | ((s < col) & (col < 3)))
            def _():
                self.up(s, h).wait_recv()

                def add(here):
                    product[here, :] += self.got[s, here].astype(F32)

                in_rows(self.half, 64, add, h * self.half)

            @pl.when((s == col) & (col < 3))
            def _():
                self.last_down(s, h).wait_recv()

                def add(here):
                    product[here, :] += self.extra[here].astype(F32)

                in_rows(self.half, 64, add, h * self.half)

            @pl.when(s != col)
            def _():
                def cast(here):
                    self.sent[s, here] = product[here, :].astype(BF16)

                in_rows(self.half, 64, cast, h * self.half)

            pl.when(s > col)(lambda: self.up(s, h).start())
            pl.when(s < col - 1)(lambda: self.down(s, h).start())
            pl.when(s == col - 1)(lambda: self.last_down(s, h).start())

    def close(self):
        def one(s, _):
            for h in range(2):
                pl.when(s != self.at.col)(lambda: self.up(s, h).wait_send())
            return 0

        lax.fori_loop(0, 4, one, 0)


def far_first(col, j):
    first = jnp.where(col < 2, 3, 0)
    near = jnp.where(col < 2, 2, 1)
    partner = jnp.where(lax.rem(col, 2) == 0, col + 1, col - 1)
    end = (col == 0) | (col == 3)
    return (first, jnp.where(end, near, partner), jnp.where(end, partner, near), col)[j]


def near_first(at, j):
    first = jnp.where(at.col < 2, 3, 0)
    near = jnp.where(at.col < 2, 2, 1)
    partner = jnp.where(lax.rem(at.col, 2) == 0, at.col + 1, at.col - 1)
    mine = at.paired
    return (
        jnp.where(mine, partner, first),
        jnp.where(mine, first, near),
        jnp.where(mine, near, partner),
        at.col,
    )[j]


def turn_tables(length):
    rates = THETA ** (-np.arange(HEAD_SIZE // 2) * 2.0 / HEAD_SIZE)
    angles = np.arange(length)[:, None] * rates[None, :]
    cos, sin = np.cos(angles), np.sin(angles)
    return (
        np.concatenate([cos, cos], axis=1).astype(np.float32),
        np.concatenate([-sin, sin], axis=1).astype(np.float32),
    )


def swap_halves(value):
    return pltpu.roll(value, HEAD_SIZE // 2, 1)


def head(ref, index):
    return ref[:, index * HEAD_SIZE : (index + 1) * HEAD_SIZE]


def root_scale(raw):
    return lax.rsqrt(jnp.mean(raw * raw, axis=1, keepdims=True) + EPSILON)


def attend(q_heads, groups, qkv, seg_row, cos, sin, q_gain, k_gain, o, qa, ka, va, probs):
    kv = q_heads // groups
    tokens = qkv.shape[0]
    half = tokens // 2
    seg_line = seg_row[...].astype(F32)
    seg_column = jnp.broadcast_to(seg_line, (128, tokens)).T[:, :1]

    def turned(index, gain):
        raw = head(qkv, index)
        normed = raw * root_scale(raw) * gain[...]
        return (normed * cos[...] + swap_halves(normed) * sin[...]).astype(BF16)

    for i in range(q_heads):
        qa[:, i * HEAD_SIZE : (i + 1) * HEAD_SIZE] = turned(i, q_gain)
    for i in range(kv):
        ka[:, i * HEAD_SIZE : (i + 1) * HEAD_SIZE] = turned(q_heads + i, k_gain)
        va[:, i * HEAD_SIZE : (i + 1) * HEAD_SIZE] = head(qkv, q_heads + kv + i).astype(BF16)
    for block in range(2):
        rows = slice(block * half, (block + 1) * half)
        keys = (block + 1) * half
        spot = lax.broadcasted_iota(jnp.int32, (half, keys), 0) + block * half
        other = lax.broadcasted_iota(jnp.int32, (half, keys), 1)
        allowed = (other <= spot) & (seg_column[rows, :] == seg_line[:, :keys])
        for i in range(q_heads):
            j = i // groups
            dots = lax.dot_general(
                head(qa, i)[rows], head(ka, j)[:keys], (((1,), (1,)), ((), ())), preferred_element_type=F32
            ) * (1.0 / math.sqrt(HEAD_SIZE))
            scores = jnp.where(allowed, dots, MASKED)
            expo = jnp.exp(scores - jnp.max(scores, axis=1, keepdims=True))
            p = expo / jnp.sum(expo, axis=1, keepdims=True)
            probs[i, rows, :keys] = p.astype(BF16)
            mixed = jnp.dot(p.astype(BF16), head(va, j)[:keys], preferred_element_type=F32)
            o[rows, i * HEAD_SIZE : (i + 1) * HEAD_SIZE] = mixed.astype(BF16)


def front_kernel(pairs, q_heads, groups, model_width, *refs):
    refs = list(refs)

    def take(count):
        found = refs[:count]
        del refs[:count]
        return found

    (x_ref, seg_row, q_gain, k_gain, gain_one, gain_two) = take(6)
    late = take(8)
    (w_gate, w_up) = take(2)
    (scale_one, hidden, scale_two, ffn_in) = take(4)
    kept_out = take(5)
    (dact_out, xn_out, gy_out, mixed_out, full) = take(5)
    (w_query, w_key, w_value, w_out, w_down, cos, sin) = late_held = take(7)
    (qkv, qa, ka, va, probs) = kept = take(5)
    (dact,) = take(1)
    (xn_wide, gy_wide, mixed_wide, mixed, product, chunk, keep) = take(7)
    total_bufs = take(2)
    second_bufs = take(2)
    moved = take(5)
    moved_q = take(5)
    chain = take(3)
    x_sems, gy_sems = take(2), take(2)
    (local,) = take(1)
    moved_sems, moved_q_sems = take(4), take(4)
    mixed_sems = take(7)
    chain_sems = take(3)
    total_sems, second_sems = take(2), take(2)
    full_sems = take(10)
    late_sems, kept_sems, dact_sems = take(3)

    at = Ends()
    gain_spot = pl.ds(pl.multiple_of(at.row * x_ref.shape[1], x_ref.shape[1]), x_ref.shape[1])
    fetch = Fetch([*zip(late[1:], late_held), (late[0], gy_wide.at[at.col])], late_sems)
    fetch.start()
    keep_saved = Fetch(list(zip(kept, kept_out)), kept_sems)
    full_gather = WeightGather(at, pairs, (w_gate, w_up), full, full_sems)
    tokens, feats = x_ref.shape
    first_total = RowTotal(at, *total_bufs, *total_sems)
    second_total = RowTotal(at, *second_bufs, *second_sems)
    x_gather = ColGather(at, xn_wide, *x_sems)
    gy_gather = ColGather(at, gy_wide, *gy_sems)
    row_sum = RowSumWhole(at, product, qkv, *moved, *moved_sems)
    quarter_sum = RowSumQuarter(at, chunk, keep, *moved_q, *moved_q_sems)
    half = tokens // 2
    mixes = RowGather(
        at, lambda h: mixed.at[pl.ds(h * half, half)], lambda h, q: mixed_wide.at[q, pl.ds(h * half, half)], mixed_sems
    )
    out_sum = ColSum(at, hidden, *chain, *chain_sems)

    at.greet(pairs if pairs == 2 else 0)
    stream = x_ref[...].astype(F32)
    first_total.start(jnp.sum(stream * stream, axis=1, keepdims=True))
    full_gather.begin()
    full_gather.send(0)
    scale = lax.rsqrt(first_total.finish() / model_width + EPSILON)
    scale_one[...] = scale
    xn_wide[at.col] = (x_ref[...].astype(F32) * scale * gain_one[:, gain_spot]).astype(BF16)

    def project(s):
        base = 0
        for w in (w_query, w_key, w_value):
            size = w.shape[1]
            product[:, base : base + size] = jnp.dot(xn_wide[s], w[...], preferred_element_type=F32)
            base += size
        row_sum.give(s)

    def back_down(s):
        size = chunk.shape[1]

        def one(j, _):
            cols = pl.ds(pl.multiple_of(j * size, size), size)
            value = lax.dot_general(
                gy_wide[s], w_down[cols, :], (((1,), (1,)), ((), ())), preferred_element_type=F32
            )
            quarter_sum.split(s, value, cols, dact)
            return 0

        lax.fori_loop(0, w_down.shape[0] // size, one, 0)
        quarter_sum.give(s)

    def keep_dact(s):
        return pltpu.make_async_copy(dact.at[s], dact_out.at[s], dact_sems.at[s])

    def end_down(s):
        quarter_sum.finish(s)

        def add(here):
            dact[s, here] += moved_q[2][s, here].astype(F32) + moved_q[4][s, here].astype(F32)

        in_rows(128, 16, add)
        keep_dact(s).start()

    def send_gy(dist):
        @pl.when((at.col == dist) & (at.col < 3))
        def _():
            gy_gather.send_up()

        @pl.when((at.col == 3 - dist) & (at.col > 0))
        def _():
            gy_gather.send_down()

    def out_step(j, halves=(0, 1)):
        s = near_first(at, j)
        for h in halves:
            rows = pl.ds(h * half, half)
            hidden[rows, :] = jnp.dot(mixed_wide[s, rows, :], w_out[...], preferred_element_type=F32)
        out_sum.step(s, halves)

    mid = jnp.logical_not(at.end)
    x_gather.arrive(0)
    fetch.wait()
    send_gy(0)
    x_gather.loop(0, project)
    back_down(at.col)
    full_gather.send(1)
    for dist in range(1, 4):
        x_gather.arrive(dist)
        send_gy(dist)
        x_gather.loop(dist, project)
        if dist < 3:
            full_gather.forward(dist - 1)

    @pl.when(mid)
    def _():
        gy_gather.arrive(1)

    row_sum.finish()
    attend(q_heads, groups, qkv, seg_row, cos, sin, q_gain, k_gain, mixed, qa, ka, va, probs)
    for h in range(2):
        mixes.to_across(h).start()
    for h in range(2):
        mixes.near(h)
    keep_saved.start()
    full_gather.send(2)

    @pl.when(mid)
    def _():
        gy_gather.arrive(2)

    for h in range(2):
        mixes.wait_near(h)

    @pl.when(at.end)
    def _():
        out_step(0)
        pl.when(jnp.logical_not(at.paired))(lambda: out_step(1))
        gy_gather.arrive(1)

    gy_gather.loop(1, back_down)
    for h in range(2):
        mixes.take_across(h)
        mixes.wait_diag(h)

        @pl.when(at.end)
        def _():
            pl.when(at.paired)(lambda: out_step(1, (h,)))
            out_step(2, (h,))

    full_gather.send(3)

    @pl.when(at.end)
    def _():
        gy_gather.arrive(2)

    paired = mid & at.paired
    unpaired = mid & jnp.logical_not(at.paired)

    @pl.when(paired)
    def _():
        for h in range(2):
            out_step(1, (h,))
            out_step(0, (h,))

    pl.when(unpaired)(lambda: out_step(0))
    gy_gather.loop(2, back_down)
    full_gather.forward(2)
    pl.when(unpaired)(lambda: out_step(1))
    pl.when(mid)(lambda: out_step(2))

    @pl.when(at.end)
    def _():
        gy_gather.arrive(3)

    gy_gather.loop(3, back_down)
    full_gather.finish(0)
    full_gather.finish(1)
    full_gather.forward(3)
    wides = [
        pltpu.make_async_copy(src, dst, local.at[i])
        for i, (src, dst) in enumerate(((xn_wide, xn_out), (gy_wide, gy_out), (mixed_wide, mixed_out)))
    ]
    for copy in wides:
        copy.start()
    full_gather.finish(2)
    for dist in range(3):
        gy_gather.loop(dist, end_down)
    full_gather.finish(3)
    out_step(3)

    def residual(here):
        hidden[here, :] += x_ref[here, :].astype(F32)

    in_rows(tokens, 64, residual)
    value = hidden[...]
    second_total.start(jnp.sum(value * value, axis=1, keepdims=True))
    gy_gather.loop(3, end_down)
    scale = lax.rsqrt(second_total.finish() / model_width + EPSILON)
    scale_two[...] = scale
    ffn_in[...] = (hidden[...] * scale * gain_two[:, gain_spot]).astype(BF16)

    keep_saved.wait()
    for s in range(4):
        keep_dact(s).wait()
    full_gather.close()
    x_gather.close()
    gy_gather.close()
    row_sum.close()
    quarter_sum.close()
    mixes.close(2)
    out_sum.close()
    for copy in wides:
        copy.wait()


def col_gather_sems():
    return [pltpu.SemaphoreType.DMA((2, 4, 2)), pltpu.SemaphoreType.DMA((4, 2))]


def chain_scratch(tokens, feats):
    return [
        pltpu.VMEM((4, tokens, feats), BF16), pltpu.VMEM((4, tokens, feats), BF16), pltpu.VMEM((tokens, feats), BF16),
    ]


def chain_sems():
    dma = pltpu.SemaphoreType.DMA
    return [dma((4, 2)), dma((4, 2)), dma((2,))]


def front(pairs, q_heads, groups, model_width, number, x, gy, weights, segments, tables, gains, ffn_weights):
    tokens, feats = x.shape
    w_query, w_key, w_value, w_out, w_down = weights
    width = w_query.shape[1] + w_key.shape[1] + w_value.shape[1]
    q_width, k_width, ff = w_query.shape[1], w_key.shape[1], w_down.shape[0]
    dma = pltpu.SemaphoreType.DMA
    any_spec, vmem = pl.BlockSpec(memory_space=pl.ANY), pl.BlockSpec(memory_space=pltpu.VMEM)
    shape = jax.ShapeDtypeStruct
    wide = pltpu.VMEM((4, tokens, feats), BF16)
    late = (*weights, *tables[:2])
    kept = [
        shape((tokens, width), F32),
        shape((tokens, q_width), BF16),
        shape((tokens, k_width), BF16),
        shape((tokens, k_width), BF16),
        shape((q_heads, tokens, tokens), BF16),
    ]
    dact = shape((4, tokens // 4, ff), F32)
    return pl.pallas_call(
        functools.partial(front_kernel, pairs, q_heads, groups, model_width),
        out_shape=(
            shape((tokens, 1), F32),
            shape((tokens, feats), F32),
            shape((tokens, 1), F32),
            shape((tokens, feats), BF16),
            *kept,
            dact,
            shape((4, tokens, feats), BF16),
            shape((4, tokens, feats), BF16),
            shape((4, tokens, q_width), BF16),
            shape((2, 4, *ffn_weights[0].shape), BF16),
        ),
        in_specs=[vmem] * 6 + [any_spec] * 10,
        out_specs=tuple([vmem] * 4 + [any_spec] * 10),
        scratch_shapes=[held(array) for array in late]
        + [held(array) for array in kept]
        + [
            held(dact),
            wide,
            wide,
            pltpu.VMEM((4, tokens, q_width), BF16),
            pltpu.VMEM((tokens, q_width), BF16),
            pltpu.VMEM((tokens, width), F32),
            pltpu.VMEM((tokens, 512), F32),
            pltpu.VMEM((tokens // 4, ff), F32),
        ]
        + row_total_scratch(tokens) * 2
        + row_sum_scratch(tokens, width)
        + [pltpu.VMEM((4, tokens // 4, ff), BF16)] * 5
        + chain_scratch(tokens, feats)
        + col_gather_sems() * 2
        + [dma((3,))]
        + row_sum_sems()
        + [dma((2, 4)), dma((2, 4)), dma((4,)), dma((4,))]
        + [dma((2,))] * 7
        + chain_sems()
        + row_total_sems() * 2
        + weight_gather_sems(pairs)
        + [dma((8,)), dma((5,)), dma((4,))],
        compiler_params=pltpu.CompilerParams(
            collective_id=number, has_side_effects=True, vmem_limit_bytes=VMEM_LIMIT
        ),
        name="front",
    )(x, segments, *tables[2:], *gains, gy, *late, *ffn_weights)


def across_rows(left, right):
    return lax.dot_general(left, right, (((0,), (0,)), ((), ())), preferred_element_type=F32)


def attend_back(q_heads, groups, grad, qkv, qa, ka, va, probs, cos, sin, q_gain, k_gain, out, q_part, k_part, dq, dk, dv):
    kv = q_heads // groups
    tokens = qkv.shape[0]
    half = tokens // 2
    scale = 1.0 / math.sqrt(HEAD_SIZE)
    dk[...] = jnp.zeros_like(dk)
    dv[...] = jnp.zeros_like(dv)
    for block in range(2):
        rows = slice(block * half, (block + 1) * half)
        keys = (block + 1) * half
        for i in range(q_heads):
            j = i // groups
            spot = slice(j * HEAD_SIZE, (j + 1) * HEAD_SIZE)
            pb = probs[i, rows, :keys]
            p = pb.astype(F32)
            g = head(grad, i)[rows].astype(BF16)
            dv[:keys, spot] += across_rows(pb.astype(BF16), g)
            dp = lax.dot_general(
                g, head(va, j)[:keys], (((1,), (1,)), ((), ())), preferred_element_type=F32
            )
            ds = (p * (dp - jnp.sum(p * dp, axis=1, keepdims=True))).astype(BF16)
            dq[rows, i * HEAD_SIZE : (i + 1) * HEAD_SIZE] = (
                jnp.dot(ds, head(ka, j)[:keys], preferred_element_type=F32) * scale
            )
            dk[:keys, spot] += across_rows(ds, head(qa, i)[rows]) * scale

    def back(turned, index, gain):
        raw = head(qkv, index)
        scales = root_scale(raw)
        normed = turned * cos[...] - swap_halves(turned) * sin[...]
        part = jnp.sum(normed * raw * scales, axis=0, keepdims=True)
        weighted = normed * gain[...]
        inner = jnp.sum(weighted * raw, axis=1, keepdims=True)
        result = scales * weighted - raw * (scales * scales * scales) * inner * (1.0 / HEAD_SIZE)
        out[:, index * HEAD_SIZE : (index + 1) * HEAD_SIZE] = result.astype(BF16)
        return part

    q_part[...] = sum(back(head(dq, i), i, q_gain) for i in range(q_heads))
    k_part[...] = sum(back(head(dk, i), q_heads + i, k_gain) for i in range(kv))
    for i in range(kv):
        spot = (q_heads + kv + i) * HEAD_SIZE
        out[:, spot : spot + HEAD_SIZE] = head(dv, i).astype(BF16)


def act_copy(src, dst, at, j, sem):
    s = far_first(at.col, j)
    if j < 2:
        return pltpu.make_async_copy(src.at[s], dst.at[s], sem)
    return pltpu.make_async_copy(src.at[s, at.row], dst.at[s, at.row], sem)


def weight_grad(out, left, right):
    def block(here):
        total = None
        for s in range(4):
            term = across_rows(left(s, here), right(s))
            total = term if total is None else total + term
        out[here, :] = total.astype(BF16)

    in_rows(out.shape[0], 256, block)


def middle_kernel(pairs, *refs):
    refs = list(refs)

    def take(count):
        found = refs[:count]
        del refs[:count]
        return found

    (hn, w_gate, w_up, dact_in, full) = take(5)
    (dhn, act_out, gate_n, up_n) = take(4)
    others = take(1) if pairs == 2 else []
    (hn_wide, hn_full, weights, dact, gate_up, gate_wide, up_wide, act_wide, n_gate, n_up) = take(10)
    chain = take(3)
    hn_sems = take(2)
    (full_sem, share_send, share_recv) = take(3)
    gate_sems, up_sems, act_sems = take(6), take(6), take(6)
    chain_sems_ = take(3)
    (local, y_send, y_recv) = take(3)

    at = Ends()
    ff = w_gate.shape[1]
    quarter = hn.shape[0] // 4
    gather = ColGather(at, hn_wide, *hn_sems)
    loads = [pltpu.make_async_copy(dact_in, dact, full_sem.at[2, 0])]
    for which, own in enumerate((w_gate, w_up)):
        for i, r in enumerate((at.mate, at.across, at.diag, at.row)):
            src = own if i == 3 else full.at[which, r]
            loads.append(pltpu.make_async_copy(src, weights.at[which, r], full_sem.at[which, i]))
    for load in loads:
        load.start()
    gates = RowGather(at, lambda s: gate_wide.at[s, at.row], lambda s, q: gate_wide.at[s, q], gate_sems)
    ups = RowGather(at, lambda s: up_wide.at[s, at.row], lambda s, q: up_wide.at[s, q], up_sems)
    acts = RowGather(at, lambda s: act_wide.at[s, at.row], lambda s, q: act_wide.at[s, q], act_sems)
    back_sum = ColSum(at, dhn, *chain, *chain_sems_)

    hn_wide[at.col] = hn[...]
    at.greet(pairs if pairs == 2 else 0)

    peers = (at.mate, at.across, at.diag)

    def share(s):
        hn_full[s, at.row] = hn_wide[s, pl.ds(pl.multiple_of(at.row * quarter, quarter), quarter)]
        for i, peer in enumerate(peers):
            theirs = hn_wide.at[s, pl.ds(pl.multiple_of(peer * quarter, quarter), quarter)]
            remote(theirs, hn_full.at[s, at.row], share_send.at[s, i], share_recv.at[s, i], row=peer).start()

    def hidden_units(s):
        for i, peer in enumerate(peers):
            here = hn_full.at[s, peer]
            remote(here, here, share_send.at[s, i], share_recv.at[s, i], row=peer).wait_recv()
        size = gate_up.shape[2]

        def some(j, _):
            cols = pl.ds(pl.multiple_of(j * size, size), size)
            for which in range(2):
                total = None
                for r in range(4):
                    term = jnp.dot(hn_full[s, r], weights[which, r, :, cols], preferred_element_type=F32)
                    total = term if total is None else total + term
                gate_up[which] = total

            def one(here):
                gate, up = gate_up[0, here], gate_up[1, here]
                grad = dact[s, here, cols]
                sigmoid = jax.nn.sigmoid(gate)
                silu = gate * sigmoid
                act_wide[s, at.row, here, cols] = (silu * up).astype(BF16)
                gate_wide[s, at.row, here, cols] = (
                    grad * up * (sigmoid * (1.0 + gate * (1.0 - sigmoid)))
                ).astype(BF16)
                up_wide[s, at.row, here, cols] = (grad * silu).astype(BF16)

            in_rows(quarter, 16, one)
            return 0

        lax.fori_loop(0, ff // size, some, 0)
        gates.to_across(s).start()
        gates.near(s)
        ups.near(s)

    def close_share(s):
        for i, peer in enumerate(peers):
            here = hn_full.at[s, peer]
            remote(here, here, share_send.at[s, i], share_recv.at[s, i], row=peer).wait_send()

    def rows_of(ref, s):
        return ref[s].reshape(4 * quarter, ff)

    def back(j):
        s = far_first(at.col, j)
        contract = (((1,), (1,)), ((), ()))
        dhn[...] = lax.dot_general(
            rows_of(gate_wide, s), weights[0, at.row], contract, preferred_element_type=F32
        ) + lax.dot_general(rows_of(up_wide, s), weights[1, at.row], contract, preferred_element_type=F32)

    def arrive(some, j):
        s = far_first(at.col, j)
        some.wait_near(s)
        some.take_across(s)
        some.wait_diag(s)

    def left(s, here):
        return hn_wide[s, :, here]

    mid = jnp.logical_not(at.end)
    gather.arrive(0)
    gather.loop(0, share)
    for load in loads:
        load.wait()
    gather.loop(0, hidden_units)
    gather.arrive(1)
    gather.loop(1, share)
    gather.arrive(2)
    gather.loop(2, share)
    gather.loop(1, hidden_units)
    gather.arrive(3)
    gather.loop(3, share)
    gather.loop(2, hidden_units)
    gather.loop(3, hidden_units)
    for j in range(4):
        ups.to_across(far_first(at.col, j)).start()
    for j in range(2):
        acts.near(far_first(at.col, j))
        acts.to_across(far_first(at.col, j)).start()
    keep_acts = [
        act_copy(act_wide, act_out, at, j, local.at[2 + j]) for j in range(4)
    ]
    for copy in keep_acts[2:]:
        copy.start()
    for j in range(4):
        arrive(gates, j)
    weight_grad(n_gate, left, lambda s: rows_of(gate_wide, s))
    pair = remote(n_gate, others[0], y_send.at[0], y_recv.at[0], dp=at.pair(2, 1)) if pairs == 2 else None
    if pairs == 2:
        pair.start()
    keep_gate = pltpu.make_async_copy(n_gate, gate_n, local.at[0])
    keep_gate.start()
    arrive(ups, 0)
    for j in range(3):
        back(j)
        pl.when(at.end)(lambda: back_sum.step(far_first(at.col, j)))
        arrive(ups, j + 1)
        pl.when(mid)(lambda: back_sum.step(far_first(at.col, j)))
    weight_grad(n_up, left, lambda s: rows_of(up_wide, s))
    keep_up = pltpu.make_async_copy(n_up, up_n, local.at[1])
    keep_up.start()
    back(3)
    arrive(acts, 0)
    keep_acts[0].start()
    back_sum.step(at.col)
    arrive(acts, 1)
    keep_acts[1].start()

    gather.close()
    for dist in range(4):
        gather.loop(dist, close_share)
    gates.close(4)
    ups.close(4)
    for j in range(2):
        acts.close_one(far_first(at.col, j))
    back_sum.close()
    for copy in keep_acts:
        copy.wait()
    keep_gate.wait()
    keep_up.wait()
    if pairs == 2:
        pair.wait()


def middle(pairs, number, hn, w_gate, w_up, dact, full):
    tokens, feats = hn.shape
    ff = w_gate.shape[1]
    quarter = tokens // 4
    dma = pltpu.SemaphoreType.DMA
    any_spec, vmem = pl.BlockSpec(memory_space=pl.ANY), pl.BlockSpec(memory_space=pltpu.VMEM)
    shape = jax.ShapeDtypeStruct
    narrow = shape((feats, ff), BF16)
    others = 1 if pairs == 2 else 0
    out = pl.pallas_call(
        functools.partial(middle_kernel, pairs),
        out_shape=tuple(
            [shape((tokens, feats), F32), shape((4, 4, quarter, ff), BF16), narrow, narrow] + [narrow] * others
        ),
        in_specs=[vmem] + [any_spec] * 4,
        out_specs=tuple([vmem] + [any_spec] * (3 + others)),
        scratch_shapes=[
            pltpu.VMEM((4, tokens, feats), BF16),
            pltpu.VMEM((4, 4, quarter, feats), BF16),
            pltpu.VMEM((2, 4, feats, ff), BF16),
            held(dact),
            pltpu.VMEM((2, quarter, 512), F32),
            pltpu.VMEM((4, 4, quarter, ff), BF16),
            pltpu.VMEM((4, 4, quarter, ff), BF16),
            pltpu.VMEM((4, 4, quarter, ff), BF16),
            pltpu.VMEM((feats, ff), BF16),
            pltpu.VMEM((feats, ff), BF16),
        ]
        + chain_scratch(tokens, feats)
        + col_gather_sems()
        + [dma((3, 4)), dma((4, 3)), dma((4, 3))]
        + [dma((4,))] * 18
        + chain_sems()
        + [dma((6,)), dma((1,)), dma((1,))],
        compiler_params=pltpu.CompilerParams(
            collective_id=number, has_side_effects=True, vmem_limit_bytes=VMEM_LIMIT
        ),
        name="middle",
    )(hn, w_gate, w_up, dact, full)
    return out[:4], out[4:]


def tail_kernel(pairs, q_heads, groups, *refs):
    refs = list(refs)

    def take(count):
        found = refs[:count]
        del refs[:count]
        return found

    (w_out, q_gain, k_gain, dhn, hidden, scale_two, gain_two, gy, x_ref, scale_one, gain_one) = take(11)
    late = take(12)
    (gy_wide, mixed_wide, normed_wide, up_n) = take(4)
    (in_grad, layer_out, one_grad, two_grad, q_grad, k_grad) = take(6)
    kept_out = take(5)
    others = take(6) if pairs == 2 else []
    (w_down, w_query, w_key, w_value, qkv, qa, ka, va, probs, cos, sin) = late_held = take(11)
    (da_wide, act_wide, dqkv, dqkv_wide, held_wide, product, grad_mixed, dq, dk, dv, *narrow) = take(15)
    (dh, q_part, k_part, packet, packet_got, by_row, summed) = take(7)
    first_bufs, last_bufs = take(2), take(2)
    moved = take(5)
    down_bufs, dxn_bufs = take(3), take(3)
    (g_send, g_recv, local, y_send, y_recv, late_sems) = take(6)
    moved_sems = take(4)
    act_sems, dqkv_sems = take(6), take(7)
    down_sems, dxn_sems = take(3), take(3)
    first_sems, last_sems = take(2), take(2)
    (p_send, p_recv, r_send, r_recv) = take(4)

    at = Ends()
    feats = dhn.shape[1]
    model_width = 4 * feats
    gain_spot = pl.ds(pl.multiple_of(at.row * feats, feats), feats)
    fetch_acts = [act_copy(late[0], act_wide, at, j, local.at[8 + j]) for j in range(4)]
    for copy in reversed(fetch_acts):
        copy.start()
    fetch = Fetch(list(zip(late[1:], late_held)), late_sems)
    fetch.start()
    first_total = RowTotal(at, *first_bufs, *first_sems)
    last_total = RowTotal(at, *last_bufs, *last_sems)
    at.greet(pairs, True, True)

    def pair_copy(src, index):
        return remote(src, others[index], y_send.at[index], y_recv.at[index], dp=1 - lax.axis_index("dp"))

    n_down, n_out, n_query, n_key, n_value = narrow
    narrow = [up_n, *narrow]

    def to_pair(index):
        if pairs == 2:
            pair_copy(narrow[index], index).start()

    def load(index, src):
        return pltpu.make_async_copy(src, held_wide, local.at[index])

    def keep(index):
        return pltpu.make_async_copy(narrow[index], kept_out[index - 1], local.at[2 + index])

    to_pair(0)
    load(0, gy_wide).start()
    gather = ColGather(at, da_wide, g_send, g_recv)
    row_sum = RowSumWhole(at, product, grad_mixed, *moved, *moved_sems)
    acts = RowGather(at, lambda s: act_wide.at[s, at.row], lambda s, q: act_wide.at[s, q], act_sems)
    half = dqkv.shape[0] // 2
    grads = RowGather(
        at, lambda h: dqkv.at[pl.ds(h * half, half)], lambda h, q: dqkv_wide.at[q, pl.ds(h * half, half)], dqkv_sems
    )
    down_sum = ColSum(at, product, *down_bufs, *down_sems)
    dxn_sum = ColSum(at, product, *dxn_bufs, *dxn_sems)

    weighted = dhn[...] * gain_two[:, gain_spot]
    first_total.start(jnp.sum(weighted * hidden[...], axis=1, keepdims=True))
    scale = scale_two[...]
    packet[...] = jnp.zeros_like(packet)
    packet[1:2, :] = jnp.sum(dhn[...] * hidden[...] * scale, axis=0, keepdims=True)
    inner = first_total.finish()
    dh[...] = (
        gy[...].astype(F32)
        + scale * (dhn[...] * gain_two[:, gain_spot])
        - hidden[...] * (scale * scale * scale * inner * (1.0 / model_width))
    )
    da_wide[at.col] = dh[...].astype(BF16)
    gather.arrive(0)
    for copy in reversed(fetch_acts):
        copy.wait()
    for j in range(2, 4):
        acts.to_across(far_first(at.col, j)).start()
        acts.near(far_first(at.col, j))

    def back_out(s):
        product[...] = lax.dot_general(
            da_wide[s], w_out[...], (((1,), (1,)), ((), ())), preferred_element_type=F32
        )
        row_sum.give(s)

    def take_act(j):
        s = far_first(at.col, j)
        acts.wait_near(s)
        acts.take_across(s)
        acts.wait_diag(s)

    def act_rows(s, cols):
        return act_wide[s, :, :, cols].reshape(product.shape[0], cols.size)

    def down_step(j):
        s = far_first(at.col, j)
        product[...] = jnp.dot(
            act_rows(s, pl.ds(0, act_wide.shape[3])), w_down[...], preferred_element_type=F32
        )
        down_sum.step(s)

    def dxn_step(j, halves=(0, 1)):
        s = near_first(at, j)
        for h in halves:
            rows = pl.ds(h * half, half)
            total, base = None, 0
            for w in (w_query, w_key, w_value):
                size = w.shape[1]
                term = lax.dot_general(
                    dqkv_wide[s, rows, pl.ds(base, size)], w[...], (((1,), (1,)), ((), ())),
                    preferred_element_type=F32,
                )
                total = term if total is None else total + term
                base += size
            product[rows, :] = total
        dxn_sum.step(s, halves)

    def down_weight():
        load(0, gy_wide).wait()
        weight_grad(n_down, act_rows, lambda s: held_wide[s])
        to_pair(1)
        keep(1).start()
        load(1, mixed_wide).start()

    mid = jnp.logical_not(at.end)
    fetch.wait()
    gather.loop(0, back_out)
    gather.arrive(1)
    gather.loop(1, back_out)
    down_step(0)
    gather.arrive(2)
    gather.loop(2, back_out)
    take_act(2)
    pl.when(at.end)(lambda: down_step(1))
    take_act(3)
    pl.when(at.end)(lambda: down_step(2))
    down_weight()
    pl.when(mid)(lambda: down_step(1))
    gather.arrive(3)
    gather.loop(3, back_out)
    row_sum.finish()
    attend_back(
        q_heads, groups, grad_mixed, qkv, qa, ka, va, probs, cos, sin, q_gain, k_gain,
        dqkv, q_part, k_part, dq, dk, dv,
    )
    for h in range(2):
        grads.to_across(h).start()
    for h in range(2):
        grads.near(h)
    for h in range(2):
        grads.wait_near(h)

    @pl.when(at.end)
    def _():
        dxn_step(0)
        pl.when(jnp.logical_not(at.paired))(lambda: dxn_step(1))

    @pl.when(mid)
    def _():
        down_step(2)

    load(1, mixed_wide).wait()
    weight_grad(n_out, lambda s, here: held_wide[s, :, here], lambda s: da_wide[s])
    to_pair(2)
    keep(2).start()
    load(2, normed_wide).start()
    paired = mid & at.paired
    unpaired = mid & jnp.logical_not(at.paired)
    pl.when(unpaired)(lambda: dxn_step(0))
    grads.take_across(0)
    grads.wait_diag(0)

    @pl.when(at.end)
    def _():
        pl.when(at.paired)(lambda: dxn_step(1, (0,)))
        dxn_step(2, (0,))

    @pl.when(paired)
    def _():
        dxn_step(1, (0,))
        dxn_step(0, (0,))

    pl.when(unpaired)(lambda: dxn_step(1, (0,)))
    grads.take_across(1)
    grads.wait_diag(1)

    @pl.when(at.end)
    def _():
        pl.when(at.paired)(lambda: dxn_step(1, (1,)))
        dxn_step(2, (1,))

    @pl.when(paired)
    def _():
        dxn_step(2, (0,))
        dxn_step(0, (1,))

    pl.when(unpaired)(lambda: dxn_step(1, (1,)))
    load(2, normed_wide).wait()
    base = 0
    for index, some in ((3, n_query), (4, n_key), (5, n_value)):
        spot = pl.ds(base, some.shape[1])
        weight_grad(some, lambda s, here: held_wide[s, :, here], lambda s, spot=spot: dqkv_wide[s, :, spot])
        to_pair(index)
        keep(index).start()
        base += some.shape[1]

    @pl.when(paired)
    def _():
        dxn_step(1, (1,))
        dxn_step(2, (1,))

    pl.when(unpaired)(lambda: dxn_step(2))
    down_step(3)
    layer_out[...] = (hidden[...] + product[...]).astype(BF16)
    dxn_step(3)
    scale = scale_one[...]
    last_total.start(
        jnp.sum(product[...] * gain_one[:, gain_spot] * x_ref[...].astype(F32), axis=1, keepdims=True)
    )
    packet[0:1, :] = jnp.sum(product[...] * x_ref[...].astype(F32) * scale, axis=0, keepdims=True)
    packet[2:3, :HEAD_SIZE] = q_part[...]
    packet[2:3, HEAD_SIZE : 2 * HEAD_SIZE] = k_part[...]

    def to_line(step):
        return remote(
            packet, packet_got.at[step - 1], p_send.at[step - 1], p_recv.at[step - 1],
            col=lax.rem(at.col + step, 4),
        )

    def to_group(index, row, step):
        where = dict(row=row) if step == 0 else dict(row=row, dp=at.pair(pairs, step))
        return remote(summed, by_row.at[step, at.row], r_send.at[index], r_recv.at[step, at.row], **where)

    def from_group(index, row, step):
        here = by_row.at[step, row]
        return remote(summed, here, r_send.at[index], r_recv.at[step, row], row=at.mate)

    group = [(row, 0) for row in (at.mate, at.across, at.diag)]
    group += [(row, step) for step in range(1, pairs) for row in range(4)]
    for step in range(1, 4):
        to_line(step).start()
    inner = last_total.finish()
    in_grad[...] = (
        dh[...]
        + scale * (product[...] * gain_one[:, gain_spot])
        - x_ref[...].astype(F32) * (scale * scale * scale * inner * (1.0 / model_width))
    )
    for step in range(1, 4):
        to_line(step).wait()
    summed[...] = (packet[...] + packet_got[0]) + (packet_got[1] + packet_got[2])
    by_row[0, at.row] = summed[...]
    for index, (row, step) in enumerate(group):
        to_group(index, row, step).start()
    for index, (row, step) in enumerate(group):
        from_group(index, row, step).wait_recv()
        to_group(index, row, step).wait_send()
    total = by_row[0]
    for step in range(1, pairs):
        total = total + by_row[step]
    for r in range(4):
        one_grad[:, r * feats : (r + 1) * feats] = total[r, 0:1, :]
        two_grad[:, r * feats : (r + 1) * feats] = total[r, 1:2, :]
    heads = (total[0, 2:3, :] + total[1, 2:3, :]) + (total[2, 2:3, :] + total[3, 2:3, :])
    q_grad[...] = heads[:, :HEAD_SIZE]
    k_grad[...] = heads[:, HEAD_SIZE : 2 * HEAD_SIZE]

    gather.close()
    row_sum.close()
    for j in range(2, 4):
        acts.close_one(far_first(at.col, j))
    grads.close(2)
    down_sum.close()
    dxn_sum.close()
    for index in range(1, 6):
        keep(index).wait()
    if pairs == 2:
        for index in range(6):
            pair_copy(narrow[index], index).wait()


def tail(pairs, q_heads, groups, number, act, weights, saved, tables, norms, wides, narrow):
    tokens, feats = norms[0].shape
    w_out, w_down, w_query, w_key, _ = weights
    ff = w_down.shape[0]
    width = saved[0].shape[1]
    q_width, k_width = saved[1].shape[1], saved[2].shape[1]
    dma = pltpu.SemaphoreType.DMA
    any_spec, vmem = pl.BlockSpec(memory_space=pl.ANY), pl.BlockSpec(memory_space=pltpu.VMEM)
    shape = jax.ShapeDtypeStruct
    shapes = [
        shape((tokens, feats), F32),
        shape((tokens, feats), BF16),
        shape((1, 4 * feats), F32),
        shape((1, 4 * feats), F32),
        shape((1, HEAD_SIZE), F32),
        shape((1, HEAD_SIZE), F32),
    ]
    own = [
        shape((ff, feats), BF16),
        shape((q_width, feats), BF16),
        shape((feats, q_width), BF16),
        shape((feats, k_width), BF16),
        shape((feats, k_width), BF16),
    ]
    others = [shape(n.shape, BF16) for n in narrow] + own if pairs == 2 else []
    packet = pltpu.VMEM((8, feats), F32)
    early = (w_out, *tables[2:], *norms)
    late = (act, *weights[1:], *saved, *tables[:2])
    out = pl.pallas_call(
        functools.partial(tail_kernel, pairs, q_heads, groups),
        out_shape=tuple(shapes + own + others),
        in_specs=[vmem] * len(early) + [any_spec] * (len(late) + 4),
        out_specs=tuple([vmem] * 6 + [any_spec] * (5 + len(others))),
        scratch_shapes=[held(array) for array in late[1:]]
        + [
            pltpu.VMEM((4, tokens, feats), BF16),
            pltpu.VMEM((4, 4, tokens // 4, ff), BF16),
            pltpu.VMEM((tokens, width), BF16),
            pltpu.VMEM((4, tokens, width), BF16),
            pltpu.VMEM((4, tokens, feats), BF16),
            pltpu.VMEM((tokens, feats), F32),
            pltpu.VMEM((tokens, q_width), F32),
            pltpu.VMEM((tokens, q_width), F32),
            pltpu.VMEM((tokens, k_width), F32),
            pltpu.VMEM((tokens, k_width), F32),
        ]
        + [held(array) for array in own]
        + [
            pltpu.VMEM((tokens, feats), F32),
            pltpu.VMEM((1, HEAD_SIZE), F32),
            pltpu.VMEM((1, HEAD_SIZE), F32),
            packet,
            pltpu.VMEM((3, 8, feats), F32),
            pltpu.VMEM((pairs, 4, 8, feats), F32),
            packet,
        ]
        + row_total_scratch(tokens) * 2
        + row_sum_scratch(tokens, q_width)
        + chain_scratch(tokens, feats) * 2
        + col_gather_sems()
        + [dma((12,)), dma((6,)), dma((6,)), dma((12,))]
        + row_sum_sems()
        + [dma((4,))] * 6
        + [dma((2,))] * 7
        + chain_sems() * 2
        + row_total_sems() * 2
        + [dma((3,)), dma((3,)), dma((4 * pairs - 1,)), dma((pairs, 4))],
        compiler_params=pltpu.CompilerParams(
            collective_id=number, has_side_effects=True, vmem_limit_bytes=VMEM_LIMIT
        ),
        name="tail",
    )(*early, *late, *wides, *narrow)
    return out[:6], out[6:11], out[11:]


def finish_kernel(count, *refs):
    parts, others, rest = refs[:count], refs[count : 2 * count], refs[2 * count :]
    kept = len(rest) - count
    for a, b, out in zip(parts, others, rest[kept // 2 :]):
        out[...] = a[...].astype(F32) + b[...].astype(F32)
    for src, dst in zip(rest[: kept // 2], rest[kept // 2 + count :]):
        dst[...] = src[...]


def finish(parts, others, rest, steps=8):
    def spec(array):
        block = (array.shape[0] // steps, array.shape[1]) if array.shape[0] % steps == 0 else array.shape
        index = (lambda i: (i, 0)) if block != array.shape else (lambda i: (0, 0))
        return pl.BlockSpec(block, index)

    outs = [jax.ShapeDtypeStruct(a.shape, F32) for a in parts] + [jax.ShapeDtypeStruct(a.shape, a.dtype) for a in rest]
    operands = (*parts, *others, *rest)
    out = pl.pallas_call(
        functools.partial(finish_kernel, len(parts)),
        grid=(steps,),
        out_shape=tuple(outs),
        in_specs=[spec(a) for a in operands],
        out_specs=tuple(spec(a) for a in outs),
        compiler_params=pltpu.CompilerParams(vmem_limit_bytes=VMEM_LIMIT),
        name="finish",
    )(*operands)
    return out[: len(parts)], out[len(parts) :]


def shards(
    pairs,
    hidden_in,
    segment_ids,
    attn_gain,
    w_query,
    key_projection,
    value_projection,
    query_gain,
    key_norm_gain,
    w_out,
    ffn_gain,
    w_gate,
    w_up,
    w_down,
    out_grad,
):
    tokens = hidden_in.shape[0]
    model_width = attn_gain.shape[0]
    q_width = w_query.shape[1]
    k_width = key_projection.shape[1]
    q_heads = q_width // HEAD_SIZE
    groups = q_width // k_width
    tables = (*turn_tables(tokens), query_gain[None, :], key_norm_gain[None, :])
    (scale_one, hidden, scale_two, ffn_in, qkv, q_turned, k_turned, values, probs, grad_inner, xn_wide, gy_wide, mixed_wide, full) = front(
        pairs, q_heads, groups, model_width, 0, hidden_in, out_grad,
        (w_query, key_projection, value_projection, w_out, w_down),
        segment_ids[None, :],
        tables,
        (attn_gain[None, :], ffn_gain[None, :]),
        (w_gate, w_up),
    )
    (grad_ffn_in, inner_act, gate_n, up_n), other_gate = middle(pairs, 1, ffn_in, w_gate, w_up, grad_inner, full)
    (in_grad, layer_out, one_grad, two_grad, q_gain_grad, k_gain_grad), own, others = tail(
        pairs, q_heads, groups, 2, inner_act,
        (w_out, w_down, w_query, key_projection, value_projection),
        (qkv, q_turned, k_turned, values, probs),
        tables,
        (grad_ffn_in, hidden, scale_two, ffn_gain[None, :], out_grad, hidden_in, scale_one, attn_gain[None, :]),
        (gy_wide, mixed_wide, xn_wide),
        (up_n,),
    )
    parts = (gate_n, up_n, *own)
    if pairs == 2:
        rest = (in_grad, layer_out, one_grad, two_grad, q_gain_grad, k_gain_grad)
        sums, rest = finish(parts, (*other_gate, *others), rest)
        in_grad, layer_out, one_grad, two_grad, q_gain_grad, k_gain_grad = rest
    else:
        sums = lax.psum(tuple(part.astype(F32) for part in parts), "dp")
    gate_grad, up_grad, down_grad, out_weight_grad, query_grad, key_grad, value_grad = sums
    return (
        layer_out,
        in_grad,
        one_grad.reshape(-1),
        query_grad,
        key_grad,
        value_grad,
        q_gain_grad.reshape(-1),
        k_gain_grad.reshape(-1),
        out_weight_grad,
        two_grad.reshape(-1),
        gate_grad,
        up_grad,
        down_grad,
    )


def solution(mesh):
    acts, grid, flip, none = P(("dp", "col"), "row"), P("row", "col"), P("col", "row"), P()
    return jax.shard_map(
        functools.partial(shards, mesh.shape["dp"]),
        mesh=mesh,
        in_specs=(
            acts, P(("dp", "row")), none, grid, grid, grid, none, none, flip, none, grid, grid, flip, acts,
        ),
        out_specs=(
            acts, acts, none, grid, grid, grid, none, none, flip, none, grid, grid, flip,
        ),
        check_vma=False,
    )
```

```python
import functools
import math

import jax
import jax.numpy as jnp
import numpy as np
from jax import lax
from jax.experimental import pallas as pl
from jax.experimental.pallas import tpu as pltpu
from jax.sharding import PartitionSpec as P

HEAD_SIZE = 128
EPSILON = 1e-06
THETA = 1000000.0
MASKED = -1e30
MESH = pl.DeviceIdType.MESH
BF16 = jnp.bfloat16
F32 = jnp.float32
VMEM_LIMIT = 60 << 20


def to(**where):
    return dict(device_id=where, device_id_type=MESH)


class Ends:
    def __init__(self):
        self.row = lax.axis_index("row")
        self.col = lax.axis_index("col")
        self.chip = lax.div(self.row, 2)
        self.core = lax.rem(self.row, 2)
        self.mate = self.chip * 2 + (1 - self.core)
        self.across = (1 - self.chip) * 2 + self.core
        self.diag = (1 - self.chip) * 2 + (1 - self.core)
        self.end = (self.col == 0) | (self.col == 3)
        self.paired = lax.div(self.col, 2) == self.chip

    def greet(self, pairs=0, line=False, rows=False):
        gate = pltpu.get_barrier_semaphore()
        count = 3
        for peer in (self.mate, self.across, self.diag):
            pl.semaphore_signal(gate, inc=1, **to(row=peer))
        for step in range(1, pairs):
            dp = self.pair(pairs, step)
            for row in range(4) if rows else (self.row,):
                pl.semaphore_signal(gate, inc=1, **to(dp=dp, row=row))
                count += 1
        if line:
            for step in range(1, 4):
                pl.semaphore_signal(gate, inc=1, **to(col=lax.rem(self.col + step, 4)))
                count += 1
        else:

            @pl.when(self.col > 0)
            def _():
                pl.semaphore_signal(gate, inc=1, **to(col=self.col - 1))

            @pl.when(self.col < 3)
            def _():
                pl.semaphore_signal(gate, inc=1, **to(col=self.col + 1))

            count += jnp.where(self.col > 0, 1, 0) + jnp.where(self.col < 3, 1, 0)
        pl.semaphore_wait(gate, count)

    def pair(self, pairs, step):
        return lax.rem(lax.axis_index("dp") + step, pairs)


class RowTotal:
    def __init__(self, at, own, got, sends, recvs):
        self.own, self.got = own, got
        self.copies = [
            remote(own, got.at[i], sends.at[i], recvs.at[i], row=peer)
            for i, peer in enumerate((at.mate, at.across, at.diag))
        ]

    def start(self, column):
        self.own[...] = jnp.broadcast_to(column, (column.shape[0], 128)).T[:8, :]
        for copy in self.copies:
            copy.start()

    def total(self):
        for copy in self.copies:
            copy.wait()
        return (self.own[...] + self.got[0]) + (self.got[1] + self.got[2])

    def finish(self):
        return as_column(self.total())


def as_column(lines):
    return jnp.concatenate([lines] * 16, axis=0).T[:, :1]


class LineShare:
    def __init__(self, at, blocks, sends, recvs):
        self.at, self.blocks, self.sends, self.recvs = at, blocks, sends, recvs

    def copy(self, s, step):
        here = self.blocks.at[s]
        col = lax.rem(self.at.col + step, 4)
        return remote(here, here, self.sends.at[step - 1], self.recvs.at[s], col=col)

    def start(self):
        for step in range(1, 4):
            self.copy(self.at.col, step).start()

    def wait(self, s):
        pl.when(s != self.at.col)(lambda: self.copy(s, 1).wait_recv())

    def close(self):
        for step in range(1, 4):
            self.copy(self.at.col, step).wait_send()


def row_total_scratch(tokens):
    return [pltpu.VMEM((8, tokens), F32), pltpu.VMEM((3, 8, tokens), F32)]


def row_total_sems():
    return [pltpu.SemaphoreType.DMA((3,)), pltpu.SemaphoreType.DMA((3,))]


def remote(src, dst, sends, recvs, **where):
    return pltpu.make_async_remote_copy(
        src_ref=src, dst_ref=dst, send_sem=sends, recv_sem=recvs, **to(**where)
    )


class Fetch:
    def __init__(self, pairs, sems):
        self.copies = [
            pltpu.make_async_copy(src, dst, sems.at[i]) for i, (src, dst) in enumerate(pairs)
        ]

    def start(self):
        for copy in self.copies:
            copy.start()

    def wait(self, first=0, last=None):
        for copy in self.copies[first:last]:
            copy.wait()


def held(array):
    return pltpu.VMEM(array.shape, array.dtype)


def in_rows(count, step, body, first=0):
    def one(i, _):
        body(pl.ds(pl.multiple_of(first + i * step, step), step))
        return 0

    lax.fori_loop(0, count // step, one, 0)


class ColGather:
    def __init__(self, at, wide, sends, recvs):
        self.at, self.wide, self.sends, self.recvs = at, wide, sends, recvs
        self.half = wide.shape[1] // 2

    def copy(self, s, h, side, col):
        part = self.wide.at[s, pl.ds(h * self.half, self.half)]
        return remote(part, part, self.sends.at[side, s, h], self.recvs.at[s, h], col=col)

    def up(self, s, h):
        return self.copy(s, h, 0, self.at.col + 1)

    def down(self, s, h):
        return self.copy(s, h, 1, self.at.col - 1)

    def loop(self, dist, body):
        if dist == 0:
            body(self.at.col)
            return

        def one(side, _):
            s = jnp.where(side == 0, self.at.col - dist, self.at.col + dist)
            pl.when((s >= 0) & (s <= 3))(lambda: body(s))
            return 0

        lax.fori_loop(0, 2, one, 0)

    def arrive(self, dist):
        for h in range(2):

            def take(s, h=h):
                if dist:
                    self.up(s, h).wait_recv()

                @pl.when((s <= self.at.col) & (self.at.col < 3))
                def _():
                    self.up(s, h).start()

                @pl.when((s >= self.at.col) & (self.at.col > 0))
                def _():
                    self.down(s, h).start()

            self.loop(dist, take)

    def send_up(self):
        for h in range(2):
            self.up(self.at.col, h).start()

    def send_down(self):
        for h in range(2):
            self.down(self.at.col, h).start()

    def close(self):
        def one(s, _):
            for h in range(2):

                @pl.when((s <= self.at.col) & (self.at.col < 3))
                def _():
                    self.up(s, h).wait_send()

                @pl.when((s >= self.at.col) & (self.at.col > 0))
                def _():
                    self.down(s, h).wait_send()

            return 0

        lax.fori_loop(0, 4, one, 0)


class RowSumWhole:
    def __init__(self, at, product, out, a_send, a_recv, c_recv, d_send, d_recv, m_send, m_recv, x_send, x_recv):
        self.at, self.product, self.out = at, product, out
        self.a_send, self.a_recv, self.c_recv, self.d_send, self.d_recv = a_send, a_recv, c_recv, d_send, d_recv
        self.m_send, self.m_recv, self.x_send, self.x_recv = m_send, m_recv, x_send, x_recv
        self.half = product.shape[0] // 2
        self.d = remote(d_send, d_recv, m_send.at[2], m_recv.at[2], row=at.mate)

    def a(self, i):
        return remote(self.a_send.at[i], self.a_recv.at[i], self.m_send.at[i], self.m_recv.at[i], row=self.at.mate)

    def b(self, i, s):
        core = self.at.core
        return remote(self.a_recv.at[i], self.c_recv.at[core], self.x_send.at[i], self.x_recv.at[core], row=s)

    def part(self, core, here):
        return pl.ds(pl.multiple_of(core * self.half + here.start, here.size), here.size)

    def give(self, s):
        at, product, half = self.at, self.product, self.half
        i = lax.rem(s, 2)
        ours = lax.div(s, 2) == at.chip

        @pl.when(jnp.logical_not(ours))
        def _():
            def cast(here):
                self.a_send[i, here] = product[self.part(1 - at.core, here), :].astype(BF16)

            in_rows(half, 64, cast)
            self.a(i).start()
            self.a(i).wait_recv()

            def add(here):
                total = product[self.part(at.core, here), :] + self.a_recv[i, here].astype(F32)
                self.a_recv[i, here] = total.astype(BF16)

            in_rows(half, 64, add)
            self.b(i, s).start()

        @pl.when(ours & (i != at.core))
        def _():
            def cast(here):
                self.d_send[here] = product[here, :].astype(BF16)

            in_rows(2 * half, 64, cast)
            self.d.start()

        @pl.when(s == at.row)
        def _():
            def store(here):
                self.out[here] = product[here, :]

            in_rows(2 * half, 64, store)

    def finish(self):
        self.d.wait_recv()
        for h in range(2):
            here = self.c_recv.at[h]
            remote(here, here, self.x_send.at[h], self.x_recv.at[h], row=self.at.across).wait_recv()

            def add(rows, h=h):
                spot = pl.ds(pl.multiple_of(h * self.half + rows.start, rows.size), rows.size)
                self.out[spot] += self.d_recv[spot].astype(F32) + self.c_recv[h, rows].astype(F32)

            in_rows(self.half, 64, add)

    def close(self):
        self.d.wait_send()
        for i in range(2):
            self.a(i).wait_send()
            self.b(i, self.at.across).wait_send()


def row_sum_scratch(tokens, width):
    half = pltpu.VMEM((2, tokens // 2, width), BF16)
    full = pltpu.VMEM((tokens, width), BF16)
    return [half, half, half, full, full]


def row_sum_sems():
    dma = pltpu.SemaphoreType.DMA
    return [dma((3,)), dma((3,)), dma((2,)), dma((2,))]


class RowSumQuarter:
    def __init__(self, at, chunk, keep, a_send, a_recv, c_recv, d_send, d_recv, m_send, m_recv, x_send, x_recv):
        self.at, self.chunk, self.keep = at, chunk, keep
        self.a_send, self.a_recv, self.c_recv = a_send, a_recv, c_recv
        self.d_send, self.d_recv = d_send, d_recv
        self.sems = (m_send, m_recv, x_send, x_recv)

    def a(self, s):
        m_send, m_recv, _, _ = self.sems
        return remote(self.a_send.at[s], self.a_recv.at[s], m_send.at[0, s], m_recv.at[0, s], row=self.at.mate)

    def d(self, s):
        m_send, m_recv, _, _ = self.sems
        return remote(self.d_send.at[s], self.d_recv.at[s], m_send.at[1, s], m_recv.at[1, s], row=self.at.mate)

    def b(self, s):
        _, _, x_send, x_recv = self.sems
        return remote(self.a_recv.at[s], self.c_recv.at[s], x_send.at[s], x_recv.at[s], row=self.at.across)

    def split(self, s, value, spot, own):
        at, chunk = self.at, self.chunk
        chunk[...] = value

        def quarter(q):
            return chunk[pl.ds(pl.multiple_of(q * 128, 128), 128), :]

        self.a_send[s, :, spot] = quarter(at.diag).astype(BF16)
        self.keep[:, spot] = quarter(at.across)
        self.d_send[s, :, spot] = quarter(at.mate).astype(BF16)
        own[s, :, spot] = quarter(at.row).astype(own.dtype)

    def give(self, s):
        self.a(s).start()
        self.d(s).start()
        self.a(s).wait_recv()

        def one(here):
            self.a_recv[s, here] = (self.keep[here, :] + self.a_recv[s, here].astype(F32)).astype(BF16)

        in_rows(128, 16, one)
        self.b(s).start()

    def finish(self, s):
        self.d(s).wait_recv()
        self.b(s).wait_recv()

    def close(self):
        def one(s, _):
            self.a(s).wait_send()
            self.b(s).wait_send()
            self.d(s).wait_send()
            return 0

        lax.fori_loop(0, 4, one, 0)


class RowGather:
    def __init__(self, at, own, slot, sems):
        self.at, self.own, self.slot = at, own, slot
        self.m_send, self.m_recv, self.x_send, self.x_recv, self.f_send, self.f_recv, self.local = (*sems, None)[:7]

    def to_mate(self, s):
        return remote(self.own(s), self.slot(s, self.at.row), self.m_send.at[s], self.m_recv.at[s], row=self.at.mate)

    def to_across(self, s):
        return remote(self.own(s), self.slot(s, self.at.row), self.x_send.at[s], self.x_recv.at[s], row=self.at.across)

    def pass_on(self, s):
        here = self.slot(s, self.at.across)
        return remote(here, here, self.f_send.at[s], self.f_recv.at[s], row=self.at.mate)

    def move_own(self, s):
        return pltpu.make_async_copy(self.own(s), self.slot(s, self.at.row), self.local.at[s])

    def near(self, s):
        self.to_mate(s).start()
        if self.local is not None:
            self.move_own(s).start()

    def wait_near(self, s):
        here = self.slot(s, self.at.mate)
        remote(here, here, self.m_send.at[s], self.m_recv.at[s], row=self.at.mate).wait_recv()
        if self.local is not None:
            self.move_own(s).wait()

    def take_across(self, s):
        here = self.slot(s, self.at.across)
        remote(here, here, self.x_send.at[s], self.x_recv.at[s], row=self.at.across).wait_recv()
        self.pass_on(s).start()

    def wait_diag(self, s):
        here = self.slot(s, self.at.diag)
        remote(here, here, self.f_send.at[s], self.f_recv.at[s], row=self.at.mate).wait_recv()

    def close_one(self, s):
        self.to_mate(s).wait_send()
        self.to_across(s).wait_send()
        self.pass_on(s).wait_send()

    def close(self, count):
        def one(s, _):
            self.close_one(s)
            return 0

        lax.fori_loop(0, count, one, 0)


class WeightGather:
    def __init__(self, at, pairs, own, full, sems):
        self.at, self.pairs, self.own, self.full = at, pairs, own, full
        self.m_send, self.m_recv, self.x_send, self.x_recv, self.y_send, self.y_recv = sems[:6]
        self.f_send, self.f_recv, self.g_send, self.g_recv = sems[6:]
        self.step = full.shape[2] // 4
        self.mine = lax.axis_index("dp") if pairs == 2 else None

    def rows(self, j):
        return pl.ds(j * self.step, self.step)

    def piece(self, which, row, j):
        return self.full.at[which, row, self.rows(j)]

    def held(self):
        return (self.mine,) if self.pairs == 2 else (0, 1)

    def near(self, which, row):
        here = self.full.at[which, row]
        return remote(self.own[which], here, self.m_send.at[which], self.m_recv.at[which], row=self.at.mate)

    def over(self, which, row, j, src=None):
        here = self.piece(which, row, j)
        lane = 0 if self.pairs == 2 else which
        src = here if src is None else src
        return remote(src, here, self.x_send.at[lane, j], self.x_recv.at[lane, j], row=self.at.across)

    def hand(self, which, j):
        here = self.piece(which, self.at.across, j)
        return remote(here, here, self.y_send.at[j], self.y_recv.at[j], dp=self.at.pair(2, 1))

    def pass_first(self, which, row, j):
        here = self.piece(which, row, j)
        lane = 0 if self.pairs == 2 else which
        return remote(here, here, self.f_send.at[lane, j], self.f_recv.at[lane, j], row=self.at.mate)

    def pass_second(self, which, row, j):
        here = self.piece(which, row, j)
        return remote(here, here, self.g_send.at[j], self.g_recv.at[j], row=self.at.mate)

    def begin(self):
        for i in range(2):
            self.near(i, self.at.row).start()

    def send(self, j):
        for which in range(2):
            copy = self.over(which, self.at.row, j, self.own[which].at[self.rows(j)])
            if self.pairs == 2:
                pl.when(self.mine == which)(copy.start)
            else:
                copy.start()

    def forward(self, j):
        for which in self.held():
            self.over(which, self.at.across, j).wait_recv()
            if self.pairs == 2:
                self.hand(which, j).start()
            self.pass_first(which, self.at.across, j).start()

    def finish(self, j):
        if self.pairs == 2:
            self.hand(1 - self.mine, j).wait_recv()
            self.pass_second(1 - self.mine, self.at.across, j).start()

    def close(self):
        for i in range(2):
            self.near(i, self.at.mate).wait_recv()
            self.near(i, self.at.row).wait_send()
        for j in range(4):
            for which in self.held():
                self.over(which, self.at.row, j).wait_send()
                self.pass_first(which, self.at.diag, j).wait_recv()
                self.pass_first(which, self.at.across, j).wait_send()
            if self.pairs == 2:
                self.hand(self.mine, j).wait_send()
                self.pass_second(1 - self.mine, self.at.diag, j).wait_recv()
                self.pass_second(1 - self.mine, self.at.across, j).wait_send()


def weight_gather_sems(pairs):
    dma = pltpu.SemaphoreType.DMA
    lanes = 1 if pairs == 2 else 2
    return [
        dma((2,)), dma((2,)), dma((lanes, 4)), dma((lanes, 4)), dma((4,)), dma((4,)),
        dma((lanes, 4)), dma((lanes, 4)), dma((4,)), dma((4,)),
    ]


class ColSum:
    def __init__(self, at, product, sent, got, extra, sends, recvs, extra_recvs):
        self.at, self.product, self.sent, self.got, self.extra = at, product, sent, got, extra
        self.sends, self.recvs, self.extra_recvs = sends, recvs, extra_recvs
        self.half = product.shape[0] // 2

    def part(self, h):
        return pl.ds(h * self.half, self.half)

    def up(self, s, h):
        return remote(
            self.sent.at[s, self.part(h)], self.got.at[s, self.part(h)],
            self.sends.at[s, h], self.recvs.at[s, h], col=self.at.col + 1,
        )

    def down(self, s, h):
        return remote(
            self.sent.at[s, self.part(h)], self.got.at[s, self.part(h)],
            self.sends.at[s, h], self.recvs.at[s, h], col=self.at.col - 1,
        )

    def last_down(self, s, h):
        return remote(
            self.sent.at[s, self.part(h)], self.extra.at[self.part(h)],
            self.sends.at[s, h], self.extra_recvs.at[h], col=self.at.col - 1,
        )

    def step(self, s, halves=(0, 1)):
        col, product = self.at.col, self.product
        for h in halves:
            @pl.when(((s >= col) & (col > 0)) | ((s < col) & (col < 3)))
            def _():
                self.up(s, h).wait_recv()

                def add(here):
                    product[here, :] += self.got[s, here].astype(F32)

                in_rows(self.half, 64, add, h * self.half)

            @pl.when((s == col) & (col < 3))
            def _():
                self.last_down(s, h).wait_recv()

                def add(here):
                    product[here, :] += self.extra[here].astype(F32)

                in_rows(self.half, 64, add, h * self.half)

            @pl.when(s != col)
            def _():
                def cast(here):
                    self.sent[s, here] = product[here, :].astype(BF16)

                in_rows(self.half, 64, cast, h * self.half)

            pl.when(s > col)(lambda: self.up(s, h).start())
            pl.when(s < col - 1)(lambda: self.down(s, h).start())
            pl.when(s == col - 1)(lambda: self.last_down(s, h).start())

    def close(self):
        def one(s, _):
            for h in range(2):
                pl.when(s != self.at.col)(lambda: self.up(s, h).wait_send())
            return 0

        lax.fori_loop(0, 4, one, 0)


def far_first(col, j):
    first = jnp.where(col < 2, 3, 0)
    near = jnp.where(col < 2, 2, 1)
    partner = jnp.where(lax.rem(col, 2) == 0, col + 1, col - 1)
    end = (col == 0) | (col == 3)
    return (first, jnp.where(end, near, partner), jnp.where(end, partner, near), col)[j]


def near_first(at, j):
    first = jnp.where(at.col < 2, 3, 0)
    near = jnp.where(at.col < 2, 2, 1)
    partner = jnp.where(lax.rem(at.col, 2) == 0, at.col + 1, at.col - 1)
    mine = at.paired
    return (
        jnp.where(mine, partner, first),
        jnp.where(mine, first, near),
        jnp.where(mine, near, partner),
        at.col,
    )[j]


def turn_tables(length):
    rates = THETA ** (-np.arange(HEAD_SIZE // 2) * 2.0 / HEAD_SIZE)
    angles = np.arange(length)[:, None] * rates[None, :]
    cos, sin = np.cos(angles), np.sin(angles)
    return (
        np.concatenate([cos, cos], axis=1).astype(np.float32),
        np.concatenate([-sin, sin], axis=1).astype(np.float32),
    )


def swap_halves(value):
    return pltpu.roll(value, HEAD_SIZE // 2, 1)


def head(ref, index):
    return ref[:, index * HEAD_SIZE : (index + 1) * HEAD_SIZE]


def root_scale(raw):
    return lax.rsqrt(jnp.mean(raw * raw, axis=1, keepdims=True) + EPSILON)


def attend(q_heads, groups, qkv, seg_row, cos, sin, q_gain, k_gain, o, qa, ka, va, probs):
    kv = q_heads // groups
    tokens = qkv.shape[0]
    half = tokens // 2
    seg_line = seg_row[...].astype(F32)
    seg_column = jnp.broadcast_to(seg_line, (128, tokens)).T[:, :1]

    def turned(index, gain):
        raw = head(qkv, index)
        normed = raw * root_scale(raw) * gain[...]
        return (normed * cos[...] + swap_halves(normed) * sin[...]).astype(BF16)

    for i in range(q_heads):
        qa[:, i * HEAD_SIZE : (i + 1) * HEAD_SIZE] = turned(i, q_gain)
    for i in range(kv):
        ka[:, i * HEAD_SIZE : (i + 1) * HEAD_SIZE] = turned(q_heads + i, k_gain)
        va[:, i * HEAD_SIZE : (i + 1) * HEAD_SIZE] = head(qkv, q_heads + kv + i).astype(BF16)
    for block in range(2):
        rows = slice(block * half, (block + 1) * half)
        keys = (block + 1) * half
        spot = lax.broadcasted_iota(jnp.int32, (half, keys), 0) + block * half
        other = lax.broadcasted_iota(jnp.int32, (half, keys), 1)
        allowed = (other <= spot) & (seg_column[rows, :] == seg_line[:, :keys])
        for i in range(q_heads):
            j = i // groups
            dots = lax.dot_general(
                head(qa, i)[rows], head(ka, j)[:keys], (((1,), (1,)), ((), ())), preferred_element_type=F32
            ) * (1.0 / math.sqrt(HEAD_SIZE))
            scores = jnp.where(allowed, dots, MASKED)
            expo = jnp.exp(scores - jnp.max(scores, axis=1, keepdims=True))
            p = expo / jnp.sum(expo, axis=1, keepdims=True)
            probs[i, rows, :keys] = p.astype(BF16)
            mixed = jnp.dot(p.astype(BF16), head(va, j)[:keys], preferred_element_type=F32)
            o[rows, i * HEAD_SIZE : (i + 1) * HEAD_SIZE] = mixed.astype(BF16)


def front_kernel(pairs, q_heads, groups, model_width, *refs):
    refs = list(refs)

    def take(count):
        found = refs[:count]
        del refs[:count]
        return found

    (x_ref, seg_row, q_gain, k_gain, gain_one, gain_two) = take(6)
    late = take(8)
    (w_gate, w_up) = take(2)
    (scale_one, hidden, scale_two, ffn_in) = take(4)
    kept_out = take(5)
    (dact_out, xn_out, gy_out, mixed_out, full) = take(5)
    (w_query, w_key, w_value, w_out, w_down, cos, sin) = late_held = take(7)
    (qkv, qa, ka, va, probs) = kept = take(5)
    (dact,) = take(1)
    (x_wide, scales, xn_wide, gy_wide, mixed_wide, mixed, product, chunk, keep) = take(9)
    total_bufs = take(2)
    second_bufs = take(2)
    moved = take(5)
    moved_q = take(5)
    chain = take(3)
    x_sems, gy_sems = take(2), take(2)
    (local,) = take(1)
    moved_sems, moved_q_sems = take(4), take(4)
    mixed_sems = take(7)
    chain_sems = take(3)
    total_sems, second_sems = take(2), take(2)
    full_sems = take(10)
    late_sems, kept_sems, dact_sems = take(3)
    scale_sems = take(2)

    at = Ends()
    gain_spot = pl.ds(pl.multiple_of(at.row * x_ref.shape[1], x_ref.shape[1]), x_ref.shape[1])
    fetch = Fetch([*zip(late[1:], late_held), (late[0], gy_wide.at[at.col])], late_sems)
    fetch.start()
    keep_saved = Fetch(list(zip(kept, kept_out)), kept_sems)
    full_gather = WeightGather(at, pairs, (w_gate, w_up), full, full_sems)
    tokens, feats = x_ref.shape
    first_total = RowTotal(at, *total_bufs, *total_sems)
    second_total = RowTotal(at, *second_bufs, *second_sems)
    x_gather = ColGather(at, x_wide, *x_sems)
    scale_share = LineShare(at, scales, *scale_sems)
    gy_gather = ColGather(at, gy_wide, *gy_sems)
    row_sum = RowSumWhole(at, product, qkv, *moved, *moved_sems)
    quarter_sum = RowSumQuarter(at, chunk, keep, *moved_q, *moved_q_sems)
    half = tokens // 2
    mixes = RowGather(
        at, lambda h: mixed.at[pl.ds(h * half, half)], lambda h, q: mixed_wide.at[q, pl.ds(h * half, half)], mixed_sems
    )
    out_sum = ColSum(at, hidden, *chain, *chain_sems)

    x_wide[at.col] = x_ref[...]
    at.greet(pairs if pairs == 2 else 0, True)
    x_gather.arrive(0)
    stream = x_ref[...].astype(F32)
    first_total.start(jnp.sum(stream * stream, axis=1, keepdims=True))
    full_gather.begin()
    full_gather.send(0)
    scales[at.col] = lax.rsqrt(first_total.total() / model_width + EPSILON)
    scale_share.start()
    scale_one[...] = as_column(scales[at.col])

    def project(s):
        scale_share.wait(s)
        scale = as_column(scales[s])
        xn_wide[s] = (x_wide[s].astype(F32) * scale * gain_one[:, gain_spot]).astype(BF16)
        base = 0
        for w in (w_query, w_key, w_value):
            size = w.shape[1]
            product[:, base : base + size] = jnp.dot(xn_wide[s], w[...], preferred_element_type=F32)
            base += size
        row_sum.give(s)

    def back_down(s):
        size = chunk.shape[1]

        def one(j, _):
            cols = pl.ds(pl.multiple_of(j * size, size), size)
            value = lax.dot_general(
                gy_wide[s], w_down[cols, :], (((1,), (1,)), ((), ())), preferred_element_type=F32
            )
            quarter_sum.split(s, value, cols, dact)
            return 0

        lax.fori_loop(0, w_down.shape[0] // size, one, 0)
        quarter_sum.give(s)

    def keep_dact(s):
        return pltpu.make_async_copy(dact.at[s], dact_out.at[s], dact_sems.at[s])

    def end_down(s):
        quarter_sum.finish(s)

        def add(here):
            dact[s, here] += moved_q[2][s, here].astype(F32) + moved_q[4][s, here].astype(F32)

        in_rows(128, 16, add)
        keep_dact(s).start()

    def send_gy(dist):
        @pl.when((at.col == dist) & (at.col < 3))
        def _():
            gy_gather.send_up()

        @pl.when((at.col == 3 - dist) & (at.col > 0))
        def _():
            gy_gather.send_down()

    def out_step(j, halves=(0, 1)):
        s = near_first(at, j)
        for h in halves:
            rows = pl.ds(h * half, half)
            hidden[rows, :] = jnp.dot(mixed_wide[s, rows, :], w_out[...], preferred_element_type=F32)
        out_sum.step(s, halves)

    mid = jnp.logical_not(at.end)
    fetch.wait()
    send_gy(0)
    x_gather.loop(0, project)
    back_down(at.col)
    full_gather.send(1)
    for dist in range(1, 4):
        x_gather.arrive(dist)
        send_gy(dist)
        x_gather.loop(dist, project)
        if dist == 1:
            full_gather.forward(0)

    @pl.when(mid)
    def _():
        gy_gather.arrive(1)

    row_sum.finish()
    attend(q_heads, groups, qkv, seg_row, cos, sin, q_gain, k_gain, mixed, qa, ka, va, probs)
    for h in range(2):
        mixes.to_across(h).start()
    for h in range(2):
        mixes.near(h)
    keep_saved.start()
    full_gather.send(2)
    full_gather.forward(1)

    @pl.when(mid)
    def _():
        gy_gather.arrive(2)

    for h in range(2):
        mixes.wait_near(h)

    @pl.when(at.end)
    def _():
        out_step(0)
        pl.when(jnp.logical_not(at.paired))(lambda: out_step(1))
        gy_gather.arrive(1)

    full_gather.send(3)
    gy_gather.loop(1, back_down)
    for h in range(2):
        mixes.take_across(h)
        mixes.wait_diag(h)

        @pl.when(at.end)
        def _():
            pl.when(at.paired)(lambda: out_step(1, (h,)))
            out_step(2, (h,))

    @pl.when(at.end)
    def _():
        gy_gather.arrive(2)

    paired = mid & at.paired
    unpaired = mid & jnp.logical_not(at.paired)

    @pl.when(paired)
    def _():
        out_step(1, (0,))
        out_step(0, (0,))

    pl.when(unpaired)(lambda: out_step(0))
    gy_gather.loop(2, back_down)
    full_gather.forward(2)

    @pl.when(paired)
    def _():
        out_step(1, (1,))
        out_step(0, (1,))

    pl.when(unpaired)(lambda: out_step(1))
    pl.when(mid)(lambda: out_step(2))

    @pl.when(at.end)
    def _():
        gy_gather.arrive(3)

    gy_gather.loop(3, back_down)
    full_gather.finish(0)
    full_gather.finish(1)
    full_gather.forward(3)
    wides = [
        pltpu.make_async_copy(src, dst, local.at[i])
        for i, (src, dst) in enumerate(((xn_wide, xn_out), (gy_wide, gy_out), (mixed_wide, mixed_out)))
    ]
    for copy in wides:
        copy.start()
    full_gather.finish(2)
    for dist in range(3):
        gy_gather.loop(dist, end_down)
    full_gather.finish(3)
    out_step(3)

    def residual(here):
        hidden[here, :] += x_ref[here, :].astype(F32)

    in_rows(tokens, 64, residual)
    value = hidden[...]
    second_total.start(jnp.sum(value * value, axis=1, keepdims=True))
    gy_gather.loop(3, end_down)
    scale = lax.rsqrt(second_total.finish() / model_width + EPSILON)
    scale_two[...] = scale
    ffn_in[...] = (hidden[...] * scale * gain_two[:, gain_spot]).astype(BF16)

    keep_saved.wait()
    for s in range(4):
        keep_dact(s).wait()
    full_gather.close()
    scale_share.close()
    x_gather.close()
    gy_gather.close()
    row_sum.close()
    quarter_sum.close()
    mixes.close(2)
    out_sum.close()
    for copy in wides:
        copy.wait()


def col_gather_sems():
    return [pltpu.SemaphoreType.DMA((2, 4, 2)), pltpu.SemaphoreType.DMA((4, 2))]


def chain_scratch(tokens, feats):
    return [
        pltpu.VMEM((4, tokens, feats), BF16), pltpu.VMEM((4, tokens, feats), BF16), pltpu.VMEM((tokens, feats), BF16),
    ]


def chain_sems():
    dma = pltpu.SemaphoreType.DMA
    return [dma((4, 2)), dma((4, 2)), dma((2,))]


def front(pairs, q_heads, groups, model_width, number, x, gy, weights, segments, tables, gains, ffn_weights):
    tokens, feats = x.shape
    w_query, w_key, w_value, w_out, w_down = weights
    width = w_query.shape[1] + w_key.shape[1] + w_value.shape[1]
    q_width, k_width, ff = w_query.shape[1], w_key.shape[1], w_down.shape[0]
    dma = pltpu.SemaphoreType.DMA
    any_spec, vmem = pl.BlockSpec(memory_space=pl.ANY), pl.BlockSpec(memory_space=pltpu.VMEM)
    shape = jax.ShapeDtypeStruct
    wide = pltpu.VMEM((4, tokens, feats), BF16)
    late = (*weights, *tables[:2])
    kept = [
        shape((tokens, width), F32),
        shape((tokens, q_width), BF16),
        shape((tokens, k_width), BF16),
        shape((tokens, k_width), BF16),
        shape((q_heads, tokens, tokens), BF16),
    ]
    dact = shape((4, tokens // 4, ff), F32)
    return pl.pallas_call(
        functools.partial(front_kernel, pairs, q_heads, groups, model_width),
        out_shape=(
            shape((tokens, 1), F32),
            shape((tokens, feats), F32),
            shape((tokens, 1), F32),
            shape((tokens, feats), BF16),
            *kept,
            dact,
            shape((4, tokens, feats), BF16),
            shape((4, tokens, feats), BF16),
            shape((4, tokens, q_width), BF16),
            shape((2, 4, *ffn_weights[0].shape), BF16),
        ),
        in_specs=[vmem] * 6 + [any_spec] * 10,
        out_specs=tuple([vmem] * 4 + [any_spec] * 10),
        scratch_shapes=[held(array) for array in late]
        + [held(array) for array in kept]
        + [
            held(dact),
            wide,
            pltpu.VMEM((4, 8, tokens), F32),
            wide,
            wide,
            pltpu.VMEM((4, tokens, q_width), BF16),
            pltpu.VMEM((tokens, q_width), BF16),
            pltpu.VMEM((tokens, width), F32),
            pltpu.VMEM((tokens, 512), F32),
            pltpu.VMEM((tokens // 4, ff), F32),
        ]
        + row_total_scratch(tokens) * 2
        + row_sum_scratch(tokens, width)
        + [pltpu.VMEM((4, tokens // 4, ff), BF16)] * 5
        + chain_scratch(tokens, feats)
        + col_gather_sems() * 2
        + [dma((3,))]
        + row_sum_sems()
        + [dma((2, 4)), dma((2, 4)), dma((4,)), dma((4,))]
        + [dma((2,))] * 7
        + chain_sems()
        + row_total_sems() * 2
        + weight_gather_sems(pairs)
        + [dma((8,)), dma((5,)), dma((4,)), dma((3,)), dma((4,))],
        compiler_params=pltpu.CompilerParams(
            collective_id=number, has_side_effects=True, vmem_limit_bytes=VMEM_LIMIT
        ),
        name="front",
    )(x, segments, *tables[2:], *gains, gy, *late, *ffn_weights)


def across_rows(left, right):
    return lax.dot_general(left, right, (((0,), (0,)), ((), ())), preferred_element_type=F32)


def attend_back(q_heads, groups, grad, qkv, qa, ka, va, probs, cos, sin, q_gain, k_gain, out, q_part, k_part, dq, dk, dv):
    kv = q_heads // groups
    tokens = qkv.shape[0]
    half = tokens // 2
    scale = 1.0 / math.sqrt(HEAD_SIZE)
    dk[...] = jnp.zeros_like(dk)
    dv[...] = jnp.zeros_like(dv)
    for block in range(2):
        rows = slice(block * half, (block + 1) * half)
        keys = (block + 1) * half
        for i in range(q_heads):
            j = i // groups
            spot = slice(j * HEAD_SIZE, (j + 1) * HEAD_SIZE)
            pb = probs[i, rows, :keys]
            p = pb.astype(F32)
            g = head(grad, i)[rows].astype(BF16)
            dv[:keys, spot] += across_rows(pb.astype(BF16), g)
            dp = lax.dot_general(
                g, head(va, j)[:keys], (((1,), (1,)), ((), ())), preferred_element_type=F32
            )
            ds = (p * (dp - jnp.sum(p * dp, axis=1, keepdims=True))).astype(BF16)
            dq[rows, i * HEAD_SIZE : (i + 1) * HEAD_SIZE] = (
                jnp.dot(ds, head(ka, j)[:keys], preferred_element_type=F32) * scale
            )
            dk[:keys, spot] += across_rows(ds, head(qa, i)[rows]) * scale

    def back(turned, index, gain):
        raw = head(qkv, index)
        scales = root_scale(raw)
        normed = turned * cos[...] - swap_halves(turned) * sin[...]
        part = jnp.sum(normed * raw * scales, axis=0, keepdims=True)
        weighted = normed * gain[...]
        inner = jnp.sum(weighted * raw, axis=1, keepdims=True)
        result = scales * weighted - raw * (scales * scales * scales) * inner * (1.0 / HEAD_SIZE)
        out[:, index * HEAD_SIZE : (index + 1) * HEAD_SIZE] = result.astype(BF16)
        return part

    q_part[...] = sum(back(head(dq, i), i, q_gain) for i in range(q_heads))
    k_part[...] = sum(back(head(dk, i), q_heads + i, k_gain) for i in range(kv))
    for i in range(kv):
        spot = (q_heads + kv + i) * HEAD_SIZE
        out[:, spot : spot + HEAD_SIZE] = head(dv, i).astype(BF16)


def act_copy(src, dst, at, j, sem):
    s = far_first(at.col, j)
    if j < 2:
        return pltpu.make_async_copy(src.at[s], dst.at[s], sem)
    return pltpu.make_async_copy(src.at[s, at.row], dst.at[s, at.row], sem)


def weight_grad(out, left, right):
    def block(here):
        total = None
        for s in range(4):
            term = across_rows(left(s, here), right(s))
            total = term if total is None else total + term
        out[here, :] = total.astype(BF16)

    in_rows(out.shape[0], 256, block)


def middle_kernel(pairs, *refs):
    refs = list(refs)

    def take(count):
        found = refs[:count]
        del refs[:count]
        return found

    (hn, w_gate, w_up, dact_in, full) = take(5)
    (dhn, act_out, gate_n, up_n) = take(4)
    others = take(1) if pairs == 2 else []
    (hn_wide, hn_full, weights, dact, gate_up, gate_wide, up_wide, act_wide, n_gate, n_up) = take(10)
    chain = take(3)
    hn_sems = take(2)
    (full_sem, share_send, share_recv) = take(3)
    gate_sems, up_sems, act_sems = take(6), take(6), take(6)
    chain_sems_ = take(3)
    (local, y_send, y_recv) = take(3)

    at = Ends()
    ff = w_gate.shape[1]
    quarter = hn.shape[0] // 4
    gather = ColGather(at, hn_wide, *hn_sems)
    loads = [pltpu.make_async_copy(dact_in, dact, full_sem.at[2, 0])]
    for which, own in enumerate((w_gate, w_up)):
        for i, r in enumerate((at.mate, at.across, at.diag, at.row)):
            src = own if i == 3 else full.at[which, r]
            loads.append(pltpu.make_async_copy(src, weights.at[which, r], full_sem.at[which, i]))
    for load in loads:
        load.start()
    gates = RowGather(at, lambda s: gate_wide.at[s, at.row], lambda s, q: gate_wide.at[s, q], gate_sems)
    ups = RowGather(at, lambda s: up_wide.at[s, at.row], lambda s, q: up_wide.at[s, q], up_sems)
    acts = RowGather(at, lambda s: act_wide.at[s, at.row], lambda s, q: act_wide.at[s, q], act_sems)
    back_sum = ColSum(at, dhn, *chain, *chain_sems_)

    hn_wide[at.col] = hn[...]
    at.greet(pairs if pairs == 2 else 0)

    peers = (at.mate, at.across, at.diag)

    def share(s):
        hn_full[s, at.row] = hn_wide[s, pl.ds(pl.multiple_of(at.row * quarter, quarter), quarter)]
        for i, peer in enumerate(peers):
            theirs = hn_wide.at[s, pl.ds(pl.multiple_of(peer * quarter, quarter), quarter)]
            remote(theirs, hn_full.at[s, at.row], share_send.at[s, i], share_recv.at[s, i], row=peer).start()

    def hidden_units(s):
        for i, peer in enumerate(peers):
            here = hn_full.at[s, peer]
            remote(here, here, share_send.at[s, i], share_recv.at[s, i], row=peer).wait_recv()
        size = gate_up.shape[2]

        def some(j, _):
            cols = pl.ds(pl.multiple_of(j * size, size), size)
            for which in range(2):
                total = None
                for r in range(4):
                    term = jnp.dot(hn_full[s, r], weights[which, r, :, cols], preferred_element_type=F32)
                    total = term if total is None else total + term
                gate_up[which] = total

            def one(here):
                gate, up = gate_up[0, here], gate_up[1, here]
                grad = dact[s, here, cols]
                sigmoid = jax.nn.sigmoid(gate)
                silu = gate * sigmoid
                act_wide[s, at.row, here, cols] = (silu * up).astype(BF16)
                gate_wide[s, at.row, here, cols] = (
                    grad * up * (sigmoid * (1.0 + gate * (1.0 - sigmoid)))
                ).astype(BF16)
                up_wide[s, at.row, here, cols] = (grad * silu).astype(BF16)

            in_rows(quarter, 16, one)
            return 0

        lax.fori_loop(0, ff // size, some, 0)
        gates.to_across(s).start()
        gates.near(s)
        ups.near(s)

    def close_share(s):
        for i, peer in enumerate(peers):
            here = hn_full.at[s, peer]
            remote(here, here, share_send.at[s, i], share_recv.at[s, i], row=peer).wait_send()

    def rows_of(ref, s):
        return ref[s].reshape(4 * quarter, ff)

    def back(j):
        s = far_first(at.col, j)
        contract = (((1,), (1,)), ((), ()))
        dhn[...] = lax.dot_general(
            rows_of(gate_wide, s), weights[0, at.row], contract, preferred_element_type=F32
        ) + lax.dot_general(rows_of(up_wide, s), weights[1, at.row], contract, preferred_element_type=F32)

    def arrive(some, j):
        s = far_first(at.col, j)
        some.wait_near(s)
        some.take_across(s)
        some.wait_diag(s)

    def left(s, here):
        return hn_wide[s, :, here]

    mid = jnp.logical_not(at.end)
    gather.arrive(0)
    gather.loop(0, share)
    for load in loads:
        load.wait()
    gather.loop(0, hidden_units)
    gather.arrive(1)
    gather.loop(1, share)
    gather.arrive(2)
    gather.loop(2, share)
    gather.loop(1, hidden_units)
    gather.arrive(3)
    gather.loop(3, share)
    gather.loop(2, hidden_units)
    gather.loop(3, hidden_units)
    for j in range(4):
        ups.to_across(far_first(at.col, j)).start()
    for j in range(2):
        acts.near(far_first(at.col, j))
        acts.to_across(far_first(at.col, j)).start()
    keep_acts = [
        act_copy(act_wide, act_out, at, j, local.at[2 + j]) for j in range(4)
    ]
    for copy in keep_acts[2:]:
        copy.start()
    for j in range(4):
        arrive(gates, j)
    weight_grad(n_gate, left, lambda s: rows_of(gate_wide, s))
    pair = remote(n_gate, others[0], y_send.at[0], y_recv.at[0], dp=at.pair(2, 1)) if pairs == 2 else None
    if pairs == 2:
        pair.start()
    keep_gate = pltpu.make_async_copy(n_gate, gate_n, local.at[0])
    keep_gate.start()
    arrive(ups, 0)
    for j in range(3):
        back(j)
        pl.when(at.end)(lambda: back_sum.step(far_first(at.col, j)))
        arrive(ups, j + 1)
        pl.when(mid)(lambda: back_sum.step(far_first(at.col, j)))
    weight_grad(n_up, left, lambda s: rows_of(up_wide, s))
    keep_up = pltpu.make_async_copy(n_up, up_n, local.at[1])
    keep_up.start()
    back(3)
    arrive(acts, 0)
    keep_acts[0].start()
    back_sum.step(at.col)
    arrive(acts, 1)
    keep_acts[1].start()

    gather.close()
    for dist in range(4):
        gather.loop(dist, close_share)
    gates.close(4)
    ups.close(4)
    for j in range(2):
        acts.close_one(far_first(at.col, j))
    back_sum.close()
    for copy in keep_acts:
        copy.wait()
    keep_gate.wait()
    keep_up.wait()
    if pairs == 2:
        pair.wait()


def middle(pairs, number, hn, w_gate, w_up, dact, full):
    tokens, feats = hn.shape
    ff = w_gate.shape[1]
    quarter = tokens // 4
    dma = pltpu.SemaphoreType.DMA
    any_spec, vmem = pl.BlockSpec(memory_space=pl.ANY), pl.BlockSpec(memory_space=pltpu.VMEM)
    shape = jax.ShapeDtypeStruct
    narrow = shape((feats, ff), BF16)
    others = 1 if pairs == 2 else 0
    out = pl.pallas_call(
        functools.partial(middle_kernel, pairs),
        out_shape=tuple(
            [shape((tokens, feats), F32), shape((4, 4, quarter, ff), BF16), narrow, narrow] + [narrow] * others
        ),
        in_specs=[vmem] + [any_spec] * 4,
        out_specs=tuple([vmem] + [any_spec] * (3 + others)),
        scratch_shapes=[
            pltpu.VMEM((4, tokens, feats), BF16),
            pltpu.VMEM((4, 4, quarter, feats), BF16),
            pltpu.VMEM((2, 4, feats, ff), BF16),
            held(dact),
            pltpu.VMEM((2, quarter, 512), F32),
            pltpu.VMEM((4, 4, quarter, ff), BF16),
            pltpu.VMEM((4, 4, quarter, ff), BF16),
            pltpu.VMEM((4, 4, quarter, ff), BF16),
            pltpu.VMEM((feats, ff), BF16),
            pltpu.VMEM((feats, ff), BF16),
        ]
        + chain_scratch(tokens, feats)
        + col_gather_sems()
        + [dma((3, 4)), dma((4, 3)), dma((4, 3))]
        + [dma((4,))] * 18
        + chain_sems()
        + [dma((6,)), dma((1,)), dma((1,))],
        compiler_params=pltpu.CompilerParams(
            collective_id=number, has_side_effects=True, vmem_limit_bytes=VMEM_LIMIT
        ),
        name="middle",
    )(hn, w_gate, w_up, dact, full)
    return out[:4], out[4:]


def tail_kernel(pairs, q_heads, groups, *refs):
    refs = list(refs)

    def take(count):
        found = refs[:count]
        del refs[:count]
        return found

    (w_out, q_gain, k_gain, dhn, hidden, scale_two, gain_two, gy, x_ref, scale_one, gain_one) = take(11)
    late = take(12)
    (gy_wide, mixed_wide, normed_wide, up_n) = take(4)
    (in_grad, layer_out, one_grad, two_grad, q_grad, k_grad) = take(6)
    kept_out = take(5)
    others = take(6) if pairs == 2 else []
    (w_down, w_query, w_key, w_value, qkv, qa, ka, va, probs, cos, sin) = late_held = take(11)
    (da_wide, act_wide, dqkv, dqkv_wide, held_wide, product, grad_mixed, dq, dk, dv, *narrow) = take(15)
    (dh, q_part, k_part, packet, packet_got, by_row, summed) = take(7)
    first_bufs, last_bufs = take(2), take(2)
    moved = take(5)
    down_bufs, dxn_bufs = take(3), take(3)
    (g_send, g_recv, local, y_send, y_recv, late_sems) = take(6)
    moved_sems = take(4)
    act_sems, dqkv_sems = take(6), take(7)
    down_sems, dxn_sems = take(3), take(3)
    first_sems, last_sems = take(2), take(2)
    (p_send, p_recv, r_send, r_recv) = take(4)

    at = Ends()
    feats = dhn.shape[1]
    model_width = 4 * feats
    gain_spot = pl.ds(pl.multiple_of(at.row * feats, feats), feats)
    fetch_acts = [act_copy(late[0], act_wide, at, j, local.at[8 + j]) for j in range(4)]
    for copy in reversed(fetch_acts):
        copy.start()
    fetch = Fetch(list(zip(late[1:], late_held)), late_sems)
    fetch.start()
    first_total = RowTotal(at, *first_bufs, *first_sems)
    last_total = RowTotal(at, *last_bufs, *last_sems)
    at.greet(pairs, True, True)

    def pair_copy(src, index):
        return remote(src, others[index], y_send.at[index], y_recv.at[index], dp=1 - lax.axis_index("dp"))

    n_down, n_out, n_query, n_key, n_value = narrow
    narrow = [up_n, *narrow]

    def to_pair(index):
        if pairs == 2:
            pair_copy(narrow[index], index).start()

    def load(index, src):
        return pltpu.make_async_copy(src, held_wide, local.at[index])

    def keep(index):
        return pltpu.make_async_copy(narrow[index], kept_out[index - 1], local.at[2 + index])

    to_pair(0)
    load(0, gy_wide).start()
    gather = ColGather(at, da_wide, g_send, g_recv)
    row_sum = RowSumWhole(at, product, grad_mixed, *moved, *moved_sems)
    acts = RowGather(at, lambda s: act_wide.at[s, at.row], lambda s, q: act_wide.at[s, q], act_sems)
    half = dqkv.shape[0] // 2
    grads = RowGather(
        at, lambda h: dqkv.at[pl.ds(h * half, half)], lambda h, q: dqkv_wide.at[q, pl.ds(h * half, half)], dqkv_sems
    )
    down_sum = ColSum(at, product, *down_bufs, *down_sems)
    dxn_sum = ColSum(at, product, *dxn_bufs, *dxn_sems)

    weighted = dhn[...] * gain_two[:, gain_spot]
    first_total.start(jnp.sum(weighted * hidden[...], axis=1, keepdims=True))
    scale = scale_two[...]
    packet[...] = jnp.zeros_like(packet)
    packet[1:2, :] = jnp.sum(dhn[...] * hidden[...] * scale, axis=0, keepdims=True)
    inner = first_total.finish()
    dh[...] = (
        gy[...].astype(F32)
        + scale * (dhn[...] * gain_two[:, gain_spot])
        - hidden[...] * (scale * scale * scale * inner * (1.0 / model_width))
    )
    da_wide[at.col] = dh[...].astype(BF16)
    gather.arrive(0)
    for copy in reversed(fetch_acts):
        copy.wait()
    for j in range(2, 4):
        acts.to_across(far_first(at.col, j)).start()
        acts.near(far_first(at.col, j))

    def back_out(s):
        product[...] = lax.dot_general(
            da_wide[s], w_out[...], (((1,), (1,)), ((), ())), preferred_element_type=F32
        )
        row_sum.give(s)

    def take_act(j):
        s = far_first(at.col, j)
        acts.wait_near(s)
        acts.take_across(s)
        acts.wait_diag(s)

    def act_rows(s, cols):
        return act_wide[s, :, :, cols].reshape(product.shape[0], cols.size)

    def down_step(j):
        s = far_first(at.col, j)
        product[...] = jnp.dot(
            act_rows(s, pl.ds(0, act_wide.shape[3])), w_down[...], preferred_element_type=F32
        )
        down_sum.step(s)

    def dxn_step(j, halves=(0, 1)):
        s = near_first(at, j)
        for h in halves:
            rows = pl.ds(h * half, half)
            total, base = None, 0
            for w in (w_query, w_key, w_value):
                size = w.shape[1]
                term = lax.dot_general(
                    dqkv_wide[s, rows, pl.ds(base, size)], w[...], (((1,), (1,)), ((), ())),
                    preferred_element_type=F32,
                )
                total = term if total is None else total + term
                base += size
            product[rows, :] = total
        dxn_sum.step(s, halves)

    def down_weight():
        load(0, gy_wide).wait()
        weight_grad(n_down, act_rows, lambda s: held_wide[s])
        to_pair(1)
        keep(1).start()
        load(1, mixed_wide).start()

    mid = jnp.logical_not(at.end)
    fetch.wait()
    gather.loop(0, back_out)
    gather.arrive(1)
    gather.loop(1, back_out)
    pl.when(at.end)(lambda: down_step(0))
    gather.arrive(2)
    gather.loop(2, back_out)
    pl.when(mid)(lambda: down_step(0))
    take_act(2)
    pl.when(at.end)(lambda: down_step(1))
    take_act(3)
    pl.when(at.end)(lambda: down_step(2))
    down_weight()
    pl.when(mid)(lambda: down_step(1))
    gather.arrive(3)
    gather.loop(3, back_out)
    row_sum.finish()
    attend_back(
        q_heads, groups, grad_mixed, qkv, qa, ka, va, probs, cos, sin, q_gain, k_gain,
        dqkv, q_part, k_part, dq, dk, dv,
    )
    for h in range(2):
        grads.to_across(h).start()
    for h in range(2):
        grads.near(h)
    for h in range(2):
        grads.wait_near(h)

    @pl.when(at.end)
    def _():
        dxn_step(0)
        pl.when(jnp.logical_not(at.paired))(lambda: dxn_step(1))

    @pl.when(mid)
    def _():
        down_step(2)

    load(1, mixed_wide).wait()
    weight_grad(n_out, lambda s, here: held_wide[s, :, here], lambda s: da_wide[s])
    to_pair(2)
    keep(2).start()
    load(2, normed_wide).start()
    paired = mid & at.paired
    unpaired = mid & jnp.logical_not(at.paired)
    pl.when(unpaired)(lambda: dxn_step(0))
    grads.take_across(0)
    grads.wait_diag(0)

    @pl.when(at.end)
    def _():
        pl.when(at.paired)(lambda: dxn_step(1, (0,)))
        dxn_step(2, (0,))

    @pl.when(paired)
    def _():
        dxn_step(1, (0,))
        dxn_step(0, (0,))

    pl.when(unpaired)(lambda: dxn_step(1, (0,)))
    grads.take_across(1)
    grads.wait_diag(1)

    @pl.when(at.end)
    def _():
        pl.when(at.paired)(lambda: dxn_step(1, (1,)))
        dxn_step(2, (1,))

    @pl.when(paired)
    def _():
        dxn_step(2, (0,))
        dxn_step(0, (1,))

    pl.when(unpaired)(lambda: dxn_step(1, (1,)))
    load(2, normed_wide).wait()
    base = 0
    for index, some in ((3, n_query), (4, n_key), (5, n_value)):
        spot = pl.ds(base, some.shape[1])
        weight_grad(some, lambda s, here: held_wide[s, :, here], lambda s, spot=spot: dqkv_wide[s, :, spot])
        to_pair(index)
        keep(index).start()
        base += some.shape[1]

    @pl.when(paired)
    def _():
        dxn_step(1, (1,))
        dxn_step(2, (1,))

    pl.when(unpaired)(lambda: dxn_step(2))
    down_step(3)
    layer_out[...] = (hidden[...] + product[...]).astype(BF16)
    dxn_step(3)
    scale = scale_one[...]
    last_total.start(
        jnp.sum(product[...] * gain_one[:, gain_spot] * x_ref[...].astype(F32), axis=1, keepdims=True)
    )
    packet[0:1, :] = jnp.sum(product[...] * x_ref[...].astype(F32) * scale, axis=0, keepdims=True)
    packet[2:3, :HEAD_SIZE] = q_part[...]
    packet[2:3, HEAD_SIZE : 2 * HEAD_SIZE] = k_part[...]

    def to_line(step):
        return remote(
            packet, packet_got.at[step - 1], p_send.at[step - 1], p_recv.at[step - 1],
            col=lax.rem(at.col + step, 4),
        )

    def to_group(index, row, step):
        where = dict(row=row) if step == 0 else dict(row=row, dp=at.pair(pairs, step))
        return remote(summed, by_row.at[step, at.row], r_send.at[index], r_recv.at[step, at.row], **where)

    def from_group(index, row, step):
        here = by_row.at[step, row]
        return remote(summed, here, r_send.at[index], r_recv.at[step, row], row=at.mate)

    group = [(row, 0) for row in (at.mate, at.across, at.diag)]
    group += [(row, step) for step in range(1, pairs) for row in range(4)]
    for step in range(1, 4):
        to_line(step).start()
    inner = last_total.finish()
    in_grad[...] = (
        dh[...]
        + scale * (product[...] * gain_one[:, gain_spot])
        - x_ref[...].astype(F32) * (scale * scale * scale * inner * (1.0 / model_width))
    )
    for step in range(1, 4):
        to_line(step).wait()
    summed[...] = (packet[...] + packet_got[0]) + (packet_got[1] + packet_got[2])
    by_row[0, at.row] = summed[...]
    for index, (row, step) in enumerate(group):
        to_group(index, row, step).start()
    for index, (row, step) in enumerate(group):
        from_group(index, row, step).wait_recv()
        to_group(index, row, step).wait_send()
    total = by_row[0]
    for step in range(1, pairs):
        total = total + by_row[step]
    for r in range(4):
        one_grad[:, r * feats : (r + 1) * feats] = total[r, 0:1, :]
        two_grad[:, r * feats : (r + 1) * feats] = total[r, 1:2, :]
    heads = (total[0, 2:3, :] + total[1, 2:3, :]) + (total[2, 2:3, :] + total[3, 2:3, :])
    q_grad[...] = heads[:, :HEAD_SIZE]
    k_grad[...] = heads[:, HEAD_SIZE : 2 * HEAD_SIZE]

    gather.close()
    row_sum.close()
    for j in range(2, 4):
        acts.close_one(far_first(at.col, j))
    grads.close(2)
    down_sum.close()
    dxn_sum.close()
    for index in range(1, 6):
        keep(index).wait()
    if pairs == 2:
        for index in range(6):
            pair_copy(narrow[index], index).wait()


def tail(pairs, q_heads, groups, number, act, weights, saved, tables, norms, wides, narrow):
    tokens, feats = norms[0].shape
    w_out, w_down, w_query, w_key, _ = weights
    ff = w_down.shape[0]
    width = saved[0].shape[1]
    q_width, k_width = saved[1].shape[1], saved[2].shape[1]
    dma = pltpu.SemaphoreType.DMA
    any_spec, vmem = pl.BlockSpec(memory_space=pl.ANY), pl.BlockSpec(memory_space=pltpu.VMEM)
    shape = jax.ShapeDtypeStruct
    shapes = [
        shape((tokens, feats), F32),
        shape((tokens, feats), BF16),
        shape((1, 4 * feats), F32),
        shape((1, 4 * feats), F32),
        shape((1, HEAD_SIZE), F32),
        shape((1, HEAD_SIZE), F32),
    ]
    own = [
        shape((ff, feats), BF16),
        shape((q_width, feats), BF16),
        shape((feats, q_width), BF16),
        shape((feats, k_width), BF16),
        shape((feats, k_width), BF16),
    ]
    others = [shape(n.shape, BF16) for n in narrow] + own if pairs == 2 else []
    packet = pltpu.VMEM((8, feats), F32)
    early = (w_out, *tables[2:], *norms)
    late = (act, *weights[1:], *saved, *tables[:2])
    out = pl.pallas_call(
        functools.partial(tail_kernel, pairs, q_heads, groups),
        out_shape=tuple(shapes + own + others),
        in_specs=[vmem] * len(early) + [any_spec] * (len(late) + 4),
        out_specs=tuple([vmem] * 6 + [any_spec] * (5 + len(others))),
        scratch_shapes=[held(array) for array in late[1:]]
        + [
            pltpu.VMEM((4, tokens, feats), BF16),
            pltpu.VMEM((4, 4, tokens // 4, ff), BF16),
            pltpu.VMEM((tokens, width), BF16),
            pltpu.VMEM((4, tokens, width), BF16),
            pltpu.VMEM((4, tokens, feats), BF16),
            pltpu.VMEM((tokens, feats), F32),
            pltpu.VMEM((tokens, q_width), F32),
            pltpu.VMEM((tokens, q_width), F32),
            pltpu.VMEM((tokens, k_width), F32),
            pltpu.VMEM((tokens, k_width), F32),
        ]
        + [held(array) for array in own]
        + [
            pltpu.VMEM((tokens, feats), F32),
            pltpu.VMEM((1, HEAD_SIZE), F32),
            pltpu.VMEM((1, HEAD_SIZE), F32),
            packet,
            pltpu.VMEM((3, 8, feats), F32),
            pltpu.VMEM((pairs, 4, 8, feats), F32),
            packet,
        ]
        + row_total_scratch(tokens) * 2
        + row_sum_scratch(tokens, q_width)
        + chain_scratch(tokens, feats) * 2
        + col_gather_sems()
        + [dma((12,)), dma((6,)), dma((6,)), dma((12,))]
        + row_sum_sems()
        + [dma((4,))] * 6
        + [dma((2,))] * 7
        + chain_sems() * 2
        + row_total_sems() * 2
        + [dma((3,)), dma((3,)), dma((4 * pairs - 1,)), dma((pairs, 4))],
        compiler_params=pltpu.CompilerParams(
            collective_id=number, has_side_effects=True, vmem_limit_bytes=VMEM_LIMIT
        ),
        name="tail",
    )(*early, *late, *wides, *narrow)
    return out[:6], out[6:11], out[11:]


def finish_kernel(count, *refs):
    parts, others, rest = refs[:count], refs[count : 2 * count], refs[2 * count :]
    kept = len(rest) - count
    for a, b, out in zip(parts, others, rest[kept // 2 :]):
        out[...] = a[...].astype(F32) + b[...].astype(F32)
    for src, dst in zip(rest[: kept // 2], rest[kept // 2 + count :]):
        dst[...] = src[...]


def finish(parts, others, rest, steps=4):
    def spec(array):
        block = (array.shape[0] // steps, array.shape[1]) if array.shape[0] % steps == 0 else array.shape
        index = (lambda i: (i, 0)) if block != array.shape else (lambda i: (0, 0))
        return pl.BlockSpec(block, index)

    outs = [jax.ShapeDtypeStruct(a.shape, F32) for a in parts] + [jax.ShapeDtypeStruct(a.shape, a.dtype) for a in rest]
    operands = (*parts, *others, *rest)
    out = pl.pallas_call(
        functools.partial(finish_kernel, len(parts)),
        grid=(steps,),
        out_shape=tuple(outs),
        in_specs=[spec(a) for a in operands],
        out_specs=tuple(spec(a) for a in outs),
        compiler_params=pltpu.CompilerParams(vmem_limit_bytes=VMEM_LIMIT),
        name="finish",
    )(*operands)
    return out[: len(parts)], out[len(parts) :]


def shards(
    pairs,
    hidden_in,
    segment_ids,
    attn_gain,
    w_query,
    key_projection,
    value_projection,
    query_gain,
    key_norm_gain,
    w_out,
    ffn_gain,
    w_gate,
    w_up,
    w_down,
    out_grad,
):
    tokens = hidden_in.shape[0]
    model_width = attn_gain.shape[0]
    q_width = w_query.shape[1]
    k_width = key_projection.shape[1]
    q_heads = q_width // HEAD_SIZE
    groups = q_width // k_width
    tables = (*turn_tables(tokens), query_gain[None, :], key_norm_gain[None, :])
    (scale_one, hidden, scale_two, ffn_in, qkv, q_turned, k_turned, values, probs, grad_inner, xn_wide, gy_wide, mixed_wide, full) = front(
        pairs, q_heads, groups, model_width, 0, hidden_in, out_grad,
        (w_query, key_projection, value_projection, w_out, w_down),
        segment_ids[None, :],
        tables,
        (attn_gain[None, :], ffn_gain[None, :]),
        (w_gate, w_up),
    )
    (grad_ffn_in, inner_act, gate_n, up_n), other_gate = middle(pairs, 1, ffn_in, w_gate, w_up, grad_inner, full)
    (in_grad, layer_out, one_grad, two_grad, q_gain_grad, k_gain_grad), own, others = tail(
        pairs, q_heads, groups, 2, inner_act,
        (w_out, w_down, w_query, key_projection, value_projection),
        (qkv, q_turned, k_turned, values, probs),
        tables,
        (grad_ffn_in, hidden, scale_two, ffn_gain[None, :], out_grad, hidden_in, scale_one, attn_gain[None, :]),
        (gy_wide, mixed_wide, xn_wide),
        (up_n,),
    )
    parts = (gate_n, up_n, *own)
    if pairs == 2:
        rest = (in_grad, layer_out, one_grad, two_grad, q_gain_grad, k_gain_grad)
        sums, rest = finish(parts, (*other_gate, *others), rest)
        in_grad, layer_out, one_grad, two_grad, q_gain_grad, k_gain_grad = rest
    else:
        sums = lax.psum(tuple(part.astype(F32) for part in parts), "dp")
    gate_grad, up_grad, down_grad, out_weight_grad, query_grad, key_grad, value_grad = sums
    return (
        layer_out,
        in_grad,
        one_grad.reshape(-1),
        query_grad,
        key_grad,
        value_grad,
        q_gain_grad.reshape(-1),
        k_gain_grad.reshape(-1),
        out_weight_grad,
        two_grad.reshape(-1),
        gate_grad,
        up_grad,
        down_grad,
    )


def solution(mesh):
    acts, grid, flip, none = P(("dp", "col"), "row"), P("row", "col"), P("col", "row"), P()
    return jax.shard_map(
        functools.partial(shards, mesh.shape["dp"]),
        mesh=mesh,
        in_specs=(
            acts, P(("dp", "row")), none, grid, grid, grid, none, none, flip, none, grid, grid, flip, acts,
        ),
        out_specs=(
            acts, acts, none, grid, grid, grid, none, none, flip, none, grid, grid, flip,
        ),
        check_vma=False,
    )
```

```python
import functools
import math

import jax
import jax.numpy as jnp
import numpy as np
from jax import lax
from jax.experimental import pallas as pl
from jax.experimental.pallas import tpu as pltpu
from jax.sharding import PartitionSpec as P

HEAD_SIZE = 128
EPSILON = 1e-06
THETA = 1000000.0
MASKED = -1e30
MESH = pl.DeviceIdType.MESH
BF16 = jnp.bfloat16
F32 = jnp.float32
VMEM_LIMIT = 60 << 20


def to(**where):
    return dict(device_id=where, device_id_type=MESH)


class Ends:
    def __init__(self):
        self.row = lax.axis_index("row")
        self.col = lax.axis_index("col")
        self.chip = lax.div(self.row, 2)
        self.core = lax.rem(self.row, 2)
        self.mate = self.chip * 2 + (1 - self.core)
        self.across = (1 - self.chip) * 2 + self.core
        self.diag = (1 - self.chip) * 2 + (1 - self.core)
        self.end = (self.col == 0) | (self.col == 3)
        self.paired = lax.div(self.col, 2) == self.chip

    def greet(self, pairs=0, line=False, rows=False):
        gate = pltpu.get_barrier_semaphore()
        count = 3
        for peer in (self.mate, self.across, self.diag):
            pl.semaphore_signal(gate, inc=1, **to(row=peer))
        for step in range(1, pairs):
            dp = self.pair(pairs, step)
            for row in range(4) if rows else (self.row,):
                pl.semaphore_signal(gate, inc=1, **to(dp=dp, row=row))
                count += 1
        if line:
            for step in range(1, 4):
                pl.semaphore_signal(gate, inc=1, **to(col=lax.rem(self.col + step, 4)))
                count += 1
        else:

            @pl.when(self.col > 0)
            def _():
                pl.semaphore_signal(gate, inc=1, **to(col=self.col - 1))

            @pl.when(self.col < 3)
            def _():
                pl.semaphore_signal(gate, inc=1, **to(col=self.col + 1))

            count += jnp.where(self.col > 0, 1, 0) + jnp.where(self.col < 3, 1, 0)
        pl.semaphore_wait(gate, count)

    def pair(self, pairs, step):
        return lax.rem(lax.axis_index("dp") + step, pairs)


class RowTotal:
    def __init__(self, at, own, got, sends, recvs):
        self.own, self.got = own, got
        self.copies = [
            remote(own, got.at[i], sends.at[i], recvs.at[i], row=peer)
            for i, peer in enumerate((at.mate, at.across, at.diag))
        ]

    def start(self, column):
        self.own[...] = jnp.broadcast_to(column, (column.shape[0], 128)).T[:8, :]
        for copy in self.copies:
            copy.start()

    def total(self):
        for copy in self.copies:
            copy.wait()
        return (self.own[...] + self.got[0]) + (self.got[1] + self.got[2])

    def finish(self):
        return as_column(self.total())


def as_column(lines):
    return jnp.concatenate([lines] * 16, axis=0).T[:, :1]


class LineShare:
    def __init__(self, at, blocks, sends, recvs):
        self.at, self.blocks, self.sends, self.recvs = at, blocks, sends, recvs

    def copy(self, s, step):
        here = self.blocks.at[s]
        col = lax.rem(self.at.col + step, 4)
        return remote(here, here, self.sends.at[step - 1], self.recvs.at[s], col=col)

    def start(self):
        for step in range(1, 4):
            self.copy(self.at.col, step).start()

    def wait(self, s):
        pl.when(s != self.at.col)(lambda: self.copy(s, 1).wait_recv())

    def close(self):
        for step in range(1, 4):
            self.copy(self.at.col, step).wait_send()


def row_total_scratch(tokens):
    return [pltpu.VMEM((8, tokens), F32), pltpu.VMEM((3, 8, tokens), F32)]


def row_total_sems():
    return [pltpu.SemaphoreType.DMA((3,)), pltpu.SemaphoreType.DMA((3,))]


def remote(src, dst, sends, recvs, **where):
    return pltpu.make_async_remote_copy(
        src_ref=src, dst_ref=dst, send_sem=sends, recv_sem=recvs, **to(**where)
    )


class Fetch:
    def __init__(self, pairs, sems):
        self.copies = [
            pltpu.make_async_copy(src, dst, sems.at[i]) for i, (src, dst) in enumerate(pairs)
        ]

    def start(self):
        for copy in self.copies:
            copy.start()

    def wait(self, first=0, last=None):
        for copy in self.copies[first:last]:
            copy.wait()


def held(array):
    return pltpu.VMEM(array.shape, array.dtype)


def in_rows(count, step, body, first=0):
    def one(i, _):
        body(pl.ds(pl.multiple_of(first + i * step, step), step))
        return 0

    lax.fori_loop(0, count // step, one, 0)


class ColGather:
    def __init__(self, at, wide, sends, recvs):
        self.at, self.wide, self.sends, self.recvs = at, wide, sends, recvs
        self.half = wide.shape[1] // 2

    def copy(self, s, h, side, col):
        part = self.wide.at[s, pl.ds(h * self.half, self.half)]
        return remote(part, part, self.sends.at[side, s, h], self.recvs.at[s, h], col=col)

    def up(self, s, h):
        return self.copy(s, h, 0, self.at.col + 1)

    def down(self, s, h):
        return self.copy(s, h, 1, self.at.col - 1)

    def loop(self, dist, body):
        if dist == 0:
            body(self.at.col)
            return

        def one(side, _):
            s = jnp.where(side == 0, self.at.col - dist, self.at.col + dist)
            pl.when((s >= 0) & (s <= 3))(lambda: body(s))
            return 0

        lax.fori_loop(0, 2, one, 0)

    def arrive(self, dist):
        for h in range(2):

            def take(s, h=h):
                if dist:
                    self.up(s, h).wait_recv()

                @pl.when((s <= self.at.col) & (self.at.col < 3))
                def _():
                    self.up(s, h).start()

                @pl.when((s >= self.at.col) & (self.at.col > 0))
                def _():
                    self.down(s, h).start()

            self.loop(dist, take)

    def send_up(self):
        for h in range(2):
            self.up(self.at.col, h).start()

    def send_down(self):
        for h in range(2):
            self.down(self.at.col, h).start()

    def close(self):
        def one(s, _):
            for h in range(2):

                @pl.when((s <= self.at.col) & (self.at.col < 3))
                def _():
                    self.up(s, h).wait_send()

                @pl.when((s >= self.at.col) & (self.at.col > 0))
                def _():
                    self.down(s, h).wait_send()

            return 0

        lax.fori_loop(0, 4, one, 0)


class RowSumWhole:
    def __init__(self, at, product, out, a_send, a_recv, c_recv, d_send, d_recv, m_send, m_recv, x_send, x_recv):
        self.at, self.product, self.out = at, product, out
        self.a_send, self.a_recv, self.c_recv, self.d_send, self.d_recv = a_send, a_recv, c_recv, d_send, d_recv
        self.m_send, self.m_recv, self.x_send, self.x_recv = m_send, m_recv, x_send, x_recv
        self.half = product.shape[0] // 2
        self.d = remote(d_send, d_recv, m_send.at[2], m_recv.at[2], row=at.mate)

    def a(self, i):
        return remote(self.a_send.at[i], self.a_recv.at[i], self.m_send.at[i], self.m_recv.at[i], row=self.at.mate)

    def b(self, i, s):
        core = self.at.core
        return remote(self.a_recv.at[i], self.c_recv.at[core], self.x_send.at[i], self.x_recv.at[core], row=s)

    def part(self, core, here):
        return pl.ds(pl.multiple_of(core * self.half + here.start, here.size), here.size)

    def give(self, s):
        at, product, half = self.at, self.product, self.half
        i = lax.rem(s, 2)
        ours = lax.div(s, 2) == at.chip

        @pl.when(jnp.logical_not(ours))
        def _():
            def cast(here):
                self.a_send[i, here] = product[self.part(1 - at.core, here), :].astype(BF16)

            in_rows(half, 64, cast)
            self.a(i).start()
            self.a(i).wait_recv()

            def add(here):
                total = product[self.part(at.core, here), :] + self.a_recv[i, here].astype(F32)
                self.a_recv[i, here] = total.astype(BF16)

            in_rows(half, 64, add)
            self.b(i, s).start()

        @pl.when(ours & (i != at.core))
        def _():
            def cast(here):
                self.d_send[here] = product[here, :].astype(BF16)

            in_rows(2 * half, 64, cast)
            self.d.start()

        @pl.when(s == at.row)
        def _():
            def store(here):
                self.out[here] = product[here, :]

            in_rows(2 * half, 64, store)

    def finish(self):
        self.d.wait_recv()
        for h in range(2):
            here = self.c_recv.at[h]
            remote(here, here, self.x_send.at[h], self.x_recv.at[h], row=self.at.across).wait_recv()

            def add(rows, h=h):
                spot = pl.ds(pl.multiple_of(h * self.half + rows.start, rows.size), rows.size)
                self.out[spot] += self.d_recv[spot].astype(F32) + self.c_recv[h, rows].astype(F32)

            in_rows(self.half, 64, add)

    def close(self):
        self.d.wait_send()
        for i in range(2):
            self.a(i).wait_send()
            self.b(i, self.at.across).wait_send()


def row_sum_scratch(tokens, width):
    half = pltpu.VMEM((2, tokens // 2, width), BF16)
    full = pltpu.VMEM((tokens, width), BF16)
    return [half, half, half, full, full]


def row_sum_sems():
    dma = pltpu.SemaphoreType.DMA
    return [dma((3,)), dma((3,)), dma((2,)), dma((2,))]


class RowSumQuarter:
    def __init__(self, at, chunk, keep, a_send, a_recv, c_recv, d_send, d_recv, m_send, m_recv, x_send, x_recv):
        self.at, self.chunk, self.keep = at, chunk, keep
        self.a_send, self.a_recv, self.c_recv = a_send, a_recv, c_recv
        self.d_send, self.d_recv = d_send, d_recv
        self.sems = (m_send, m_recv, x_send, x_recv)

    def a(self, s):
        m_send, m_recv, _, _ = self.sems
        return remote(self.a_send.at[s], self.a_recv.at[s], m_send.at[0, s], m_recv.at[0, s], row=self.at.mate)

    def d(self, s):
        m_send, m_recv, _, _ = self.sems
        return remote(self.d_send.at[s], self.d_recv.at[s], m_send.at[1, s], m_recv.at[1, s], row=self.at.mate)

    def b(self, s):
        _, _, x_send, x_recv = self.sems
        return remote(self.a_recv.at[s], self.c_recv.at[s], x_send.at[s], x_recv.at[s], row=self.at.across)

    def split(self, s, value, spot, own):
        at, chunk = self.at, self.chunk
        chunk[...] = value

        def quarter(q):
            return chunk[pl.ds(pl.multiple_of(q * 128, 128), 128), :]

        self.a_send[s, :, spot] = quarter(at.diag).astype(BF16)
        self.keep[:, spot] = quarter(at.across)
        self.d_send[s, :, spot] = quarter(at.mate).astype(BF16)
        own[s, :, spot] = quarter(at.row).astype(own.dtype)

    def give(self, s):
        self.a(s).start()
        self.d(s).start()
        self.a(s).wait_recv()

        def one(here):
            self.a_recv[s, here] = (self.keep[here, :] + self.a_recv[s, here].astype(F32)).astype(BF16)

        in_rows(128, 16, one)
        self.b(s).start()

    def finish(self, s):
        self.d(s).wait_recv()
        self.b(s).wait_recv()

    def close(self):
        def one(s, _):
            self.a(s).wait_send()
            self.b(s).wait_send()
            self.d(s).wait_send()
            return 0

        lax.fori_loop(0, 4, one, 0)


class RowGather:
    def __init__(self, at, own, slot, sems):
        self.at, self.own, self.slot = at, own, slot
        self.m_send, self.m_recv, self.x_send, self.x_recv, self.f_send, self.f_recv, self.local = (*sems, None)[:7]

    def to_mate(self, s):
        return remote(self.own(s), self.slot(s, self.at.row), self.m_send.at[s], self.m_recv.at[s], row=self.at.mate)

    def to_across(self, s):
        return remote(self.own(s), self.slot(s, self.at.row), self.x_send.at[s], self.x_recv.at[s], row=self.at.across)

    def pass_on(self, s):
        here = self.slot(s, self.at.across)
        return remote(here, here, self.f_send.at[s], self.f_recv.at[s], row=self.at.mate)

    def move_own(self, s):
        return pltpu.make_async_copy(self.own(s), self.slot(s, self.at.row), self.local.at[s])

    def near(self, s):
        self.to_mate(s).start()
        if self.local is not None:
            self.move_own(s).start()

    def wait_near(self, s):
        here = self.slot(s, self.at.mate)
        remote(here, here, self.m_send.at[s], self.m_recv.at[s], row=self.at.mate).wait_recv()
        if self.local is not None:
            self.move_own(s).wait()

    def take_across(self, s):
        here = self.slot(s, self.at.across)
        remote(here, here, self.x_send.at[s], self.x_recv.at[s], row=self.at.across).wait_recv()
        self.pass_on(s).start()

    def wait_diag(self, s):
        here = self.slot(s, self.at.diag)
        remote(here, here, self.f_send.at[s], self.f_recv.at[s], row=self.at.mate).wait_recv()

    def close_one(self, s):
        self.to_mate(s).wait_send()
        self.to_across(s).wait_send()
        self.pass_on(s).wait_send()

    def close(self, count):
        def one(s, _):
            self.close_one(s)
            return 0

        lax.fori_loop(0, count, one, 0)


class WeightGather:
    def __init__(self, at, pairs, own, full, sems):
        self.at, self.pairs, self.own, self.full = at, pairs, own, full
        self.m_send, self.m_recv, self.x_send, self.x_recv, self.y_send, self.y_recv = sems[:6]
        self.f_send, self.f_recv, self.g_send, self.g_recv = sems[6:]
        self.step = full.shape[2] // 4
        self.mine = lax.axis_index("dp") if pairs == 2 else None

    def rows(self, j):
        return pl.ds(j * self.step, self.step)

    def piece(self, which, row, j):
        return self.full.at[which, row, self.rows(j)]

    def held(self):
        return (self.mine,) if self.pairs == 2 else (0, 1)

    def near(self, which, row):
        here = self.full.at[which, row]
        return remote(self.own[which], here, self.m_send.at[which], self.m_recv.at[which], row=self.at.mate)

    def over(self, which, row, j, src=None):
        here = self.piece(which, row, j)
        lane = 0 if self.pairs == 2 else which
        src = here if src is None else src
        return remote(src, here, self.x_send.at[lane, j], self.x_recv.at[lane, j], row=self.at.across)

    def hand(self, which, j):
        here = self.piece(which, self.at.across, j)
        return remote(here, here, self.y_send.at[j], self.y_recv.at[j], dp=self.at.pair(2, 1))

    def pass_first(self, which, row, j):
        here = self.piece(which, row, j)
        lane = 0 if self.pairs == 2 else which
        return remote(here, here, self.f_send.at[lane, j], self.f_recv.at[lane, j], row=self.at.mate)

    def pass_second(self, which, row, j):
        here = self.piece(which, row, j)
        return remote(here, here, self.g_send.at[j], self.g_recv.at[j], row=self.at.mate)

    def begin(self):
        for i in range(2):
            self.near(i, self.at.row).start()

    def send(self, j):
        for which in range(2):
            copy = self.over(which, self.at.row, j, self.own[which].at[self.rows(j)])
            if self.pairs == 2:
                pl.when(self.mine == which)(copy.start)
            else:
                copy.start()

    def forward(self, j):
        for which in self.held():
            self.over(which, self.at.across, j).wait_recv()
            if self.pairs == 2:
                self.hand(which, j).start()
            self.pass_first(which, self.at.across, j).start()

    def finish(self, j):
        if self.pairs == 2:
            self.hand(1 - self.mine, j).wait_recv()
            self.pass_second(1 - self.mine, self.at.across, j).start()

    def close(self):
        for i in range(2):
            self.near(i, self.at.mate).wait_recv()
            self.near(i, self.at.row).wait_send()
        for j in range(4):
            for which in self.held():
                self.over(which, self.at.row, j).wait_send()
                self.pass_first(which, self.at.diag, j).wait_recv()
                self.pass_first(which, self.at.across, j).wait_send()
            if self.pairs == 2:
                self.hand(self.mine, j).wait_send()
                self.pass_second(1 - self.mine, self.at.diag, j).wait_recv()
                self.pass_second(1 - self.mine, self.at.across, j).wait_send()


def weight_gather_sems(pairs):
    dma = pltpu.SemaphoreType.DMA
    lanes = 1 if pairs == 2 else 2
    return [
        dma((2,)), dma((2,)), dma((lanes, 4)), dma((lanes, 4)), dma((4,)), dma((4,)),
        dma((lanes, 4)), dma((lanes, 4)), dma((4,)), dma((4,)),
    ]


class ColSum:
    def __init__(self, at, product, sent, got, extra, sends, recvs, extra_recvs):
        self.at, self.product, self.sent, self.got, self.extra = at, product, sent, got, extra
        self.sends, self.recvs, self.extra_recvs = sends, recvs, extra_recvs
        self.half = product.shape[0] // 2

    def part(self, h):
        return pl.ds(h * self.half, self.half)

    def up(self, s, h):
        return remote(
            self.sent.at[s, self.part(h)], self.got.at[s, self.part(h)],
            self.sends.at[s, h], self.recvs.at[s, h], col=self.at.col + 1,
        )

    def down(self, s, h):
        return remote(
            self.sent.at[s, self.part(h)], self.got.at[s, self.part(h)],
            self.sends.at[s, h], self.recvs.at[s, h], col=self.at.col - 1,
        )

    def last_down(self, s, h):
        return remote(
            self.sent.at[s, self.part(h)], self.extra.at[self.part(h)],
            self.sends.at[s, h], self.extra_recvs.at[h], col=self.at.col - 1,
        )

    def step(self, s, halves=(0, 1)):
        col, product = self.at.col, self.product
        for h in halves:
            @pl.when(((s >= col) & (col > 0)) | ((s < col) & (col < 3)))
            def _():
                self.up(s, h).wait_recv()

                def add(here):
                    product[here, :] += self.got[s, here].astype(F32)

                in_rows(self.half, 64, add, h * self.half)

            @pl.when((s == col) & (col < 3))
            def _():
                self.last_down(s, h).wait_recv()

                def add(here):
                    product[here, :] += self.extra[here].astype(F32)

                in_rows(self.half, 64, add, h * self.half)

            @pl.when(s != col)
            def _():
                def cast(here):
                    self.sent[s, here] = product[here, :].astype(BF16)

                in_rows(self.half, 64, cast, h * self.half)

            pl.when(s > col)(lambda: self.up(s, h).start())
            pl.when(s < col - 1)(lambda: self.down(s, h).start())
            pl.when(s == col - 1)(lambda: self.last_down(s, h).start())

    def close(self):
        def one(s, _):
            for h in range(2):
                pl.when(s != self.at.col)(lambda: self.up(s, h).wait_send())
            return 0

        lax.fori_loop(0, 4, one, 0)


def far_first(col, j):
    first = jnp.where(col < 2, 3, 0)
    near = jnp.where(col < 2, 2, 1)
    partner = jnp.where(lax.rem(col, 2) == 0, col + 1, col - 1)
    end = (col == 0) | (col == 3)
    return (first, jnp.where(end, near, partner), jnp.where(end, partner, near), col)[j]


def near_first(at, j):
    first = jnp.where(at.col < 2, 3, 0)
    near = jnp.where(at.col < 2, 2, 1)
    partner = jnp.where(lax.rem(at.col, 2) == 0, at.col + 1, at.col - 1)
    mine = at.paired
    return (
        jnp.where(mine, partner, first),
        jnp.where(mine, first, near),
        jnp.where(mine, near, partner),
        at.col,
    )[j]


def turn_tables(length):
    rates = THETA ** (-np.arange(HEAD_SIZE // 2) * 2.0 / HEAD_SIZE)
    angles = np.arange(length)[:, None] * rates[None, :]
    cos, sin = np.cos(angles), np.sin(angles)
    return (
        np.concatenate([cos, cos], axis=1).astype(np.float32),
        np.concatenate([-sin, sin], axis=1).astype(np.float32),
    )


def swap_halves(value):
    return pltpu.roll(value, HEAD_SIZE // 2, 1)


def head(ref, index):
    return ref[:, index * HEAD_SIZE : (index + 1) * HEAD_SIZE]


def root_scale(raw):
    return lax.rsqrt(jnp.mean(raw * raw, axis=1, keepdims=True) + EPSILON)


def attend(q_heads, groups, qkv, seg_row, cos, sin, q_gain, k_gain, o, qa, ka, va, probs):
    kv = q_heads // groups
    tokens = qkv.shape[0]
    half = tokens // 2
    seg_line = seg_row[...].astype(F32)
    seg_column = jnp.broadcast_to(seg_line, (128, tokens)).T[:, :1]

    def turned(index, gain):
        raw = head(qkv, index)
        normed = raw * root_scale(raw) * gain[...]
        return (normed * cos[...] + swap_halves(normed) * sin[...]).astype(BF16)

    for i in range(q_heads):
        qa[:, i * HEAD_SIZE : (i + 1) * HEAD_SIZE] = turned(i, q_gain)
    for i in range(kv):
        ka[:, i * HEAD_SIZE : (i + 1) * HEAD_SIZE] = turned(q_heads + i, k_gain)
        va[:, i * HEAD_SIZE : (i + 1) * HEAD_SIZE] = head(qkv, q_heads + kv + i).astype(BF16)
    for block in range(2):
        rows = slice(block * half, (block + 1) * half)
        keys = (block + 1) * half
        spot = lax.broadcasted_iota(jnp.int32, (half, keys), 0) + block * half
        other = lax.broadcasted_iota(jnp.int32, (half, keys), 1)
        allowed = (other <= spot) & (seg_column[rows, :] == seg_line[:, :keys])
        for i in range(q_heads):
            j = i // groups
            dots = lax.dot_general(
                head(qa, i)[rows], head(ka, j)[:keys], (((1,), (1,)), ((), ())), preferred_element_type=F32
            ) * (1.0 / math.sqrt(HEAD_SIZE))
            scores = jnp.where(allowed, dots, MASKED)
            expo = jnp.exp(scores - jnp.max(scores, axis=1, keepdims=True))
            p = expo / jnp.sum(expo, axis=1, keepdims=True)
            probs[i, rows, :keys] = p.astype(BF16)
            mixed = jnp.dot(p.astype(BF16), head(va, j)[:keys], preferred_element_type=F32)
            o[rows, i * HEAD_SIZE : (i + 1) * HEAD_SIZE] = mixed.astype(BF16)


def front_kernel(pairs, q_heads, groups, model_width, *refs):
    refs = list(refs)

    def take(count):
        found = refs[:count]
        del refs[:count]
        return found

    (x_ref, seg_row, q_gain, k_gain, gain_one, gain_two) = take(6)
    late = take(8)
    (w_gate, w_up) = take(2)
    (scale_one, hidden, scale_two, ffn_in) = take(4)
    kept_out = take(5)
    (dact_out, xn_out, gy_out, mixed_out, full) = take(5)
    (w_query, w_key, w_value, w_out, w_down, cos, sin) = late_held = take(7)
    (qkv, qa, ka, va, probs) = kept = take(5)
    (dact,) = take(1)
    (x_wide, scales, xn_wide, gy_wide, mixed_wide, mixed, product, chunk, keep) = take(9)
    total_bufs = take(2)
    second_bufs = take(2)
    moved = take(5)
    moved_q = take(5)
    chain = take(3)
    x_sems, gy_sems = take(2), take(2)
    (local,) = take(1)
    moved_sems, moved_q_sems = take(4), take(4)
    mixed_sems = take(7)
    chain_sems = take(3)
    total_sems, second_sems = take(2), take(2)
    full_sems = take(10)
    late_sems, kept_sems, dact_sems = take(3)
    scale_sems = take(2)

    at = Ends()
    gain_spot = pl.ds(pl.multiple_of(at.row * x_ref.shape[1], x_ref.shape[1]), x_ref.shape[1])
    fetch = Fetch([*zip(late[1:], late_held), (late[0], gy_wide.at[at.col])], late_sems)
    fetch.start()
    keep_saved = Fetch(list(zip(kept, kept_out)), kept_sems)
    full_gather = WeightGather(at, pairs, (w_gate, w_up), full, full_sems)
    tokens, feats = x_ref.shape
    first_total = RowTotal(at, *total_bufs, *total_sems)
    second_total = RowTotal(at, *second_bufs, *second_sems)
    x_gather = ColGather(at, x_wide, *x_sems)
    scale_share = LineShare(at, scales, *scale_sems)
    gy_gather = ColGather(at, gy_wide, *gy_sems)
    row_sum = RowSumWhole(at, product, qkv, *moved, *moved_sems)
    quarter_sum = RowSumQuarter(at, chunk, keep, *moved_q, *moved_q_sems)
    half = tokens // 2
    mixes = RowGather(
        at, lambda h: mixed.at[pl.ds(h * half, half)], lambda h, q: mixed_wide.at[q, pl.ds(h * half, half)], mixed_sems
    )
    out_sum = ColSum(at, hidden, *chain, *chain_sems)

    x_wide[at.col] = x_ref[...]
    at.greet(pairs if pairs == 2 else 0, True)
    x_gather.arrive(0)
    stream = x_ref[...].astype(F32)
    first_total.start(jnp.sum(stream * stream, axis=1, keepdims=True))
    full_gather.begin()
    full_gather.send(0)
    scales[at.col] = lax.rsqrt(first_total.total() / model_width + EPSILON)
    scale_share.start()
    scale_one[...] = as_column(scales[at.col])

    def project(s):
        scale_share.wait(s)
        scale = as_column(scales[s])
        xn_wide[s] = (x_wide[s].astype(F32) * scale * gain_one[:, gain_spot]).astype(BF16)
        base = 0
        for w in (w_query, w_key, w_value):
            size = w.shape[1]
            product[:, base : base + size] = jnp.dot(xn_wide[s], w[...], preferred_element_type=F32)
            base += size
        row_sum.give(s)

    def back_down(s):
        size = chunk.shape[1]

        def one(j, _):
            cols = pl.ds(pl.multiple_of(j * size, size), size)
            value = lax.dot_general(
                gy_wide[s], w_down[cols, :], (((1,), (1,)), ((), ())), preferred_element_type=F32
            )
            quarter_sum.split(s, value, cols, dact)
            return 0

        lax.fori_loop(0, w_down.shape[0] // size, one, 0)
        quarter_sum.give(s)

    def keep_dact(s):
        return pltpu.make_async_copy(dact.at[s], dact_out.at[s], dact_sems.at[s])

    def end_down(s):
        quarter_sum.finish(s)

        def add(here):
            dact[s, here] += moved_q[2][s, here].astype(F32) + moved_q[4][s, here].astype(F32)

        in_rows(128, 16, add)
        keep_dact(s).start()

    def send_gy(dist):
        @pl.when((at.col == dist) & (at.col < 3))
        def _():
            gy_gather.send_up()

        @pl.when((at.col == 3 - dist) & (at.col > 0))
        def _():
            gy_gather.send_down()

    def out_step(j, halves=(0, 1)):
        s = near_first(at, j)
        for h in halves:
            rows = pl.ds(h * half, half)
            hidden[rows, :] = jnp.dot(mixed_wide[s, rows, :], w_out[...], preferred_element_type=F32)
        out_sum.step(s, halves)

    mid = jnp.logical_not(at.end)
    fetch.wait()
    send_gy(0)
    x_gather.loop(0, project)
    back_down(at.col)
    full_gather.send(1)
    for dist in range(1, 4):
        x_gather.arrive(dist)
        send_gy(dist)
        x_gather.loop(dist, project)
        if dist == 1:
            full_gather.forward(0)

    @pl.when(mid)
    def _():
        gy_gather.arrive(1)

    row_sum.finish()
    attend(q_heads, groups, qkv, seg_row, cos, sin, q_gain, k_gain, mixed, qa, ka, va, probs)
    for h in range(2):
        mixes.to_across(h).start()
    for h in range(2):
        mixes.near(h)
    keep_saved.start()
    full_gather.send(2)
    full_gather.forward(1)

    @pl.when(mid)
    def _():
        gy_gather.arrive(2)

    for h in range(2):
        mixes.wait_near(h)

    @pl.when(at.end)
    def _():
        out_step(0)
        pl.when(jnp.logical_not(at.paired))(lambda: out_step(1))
        gy_gather.arrive(1)

    full_gather.send(3)
    gy_gather.loop(1, back_down)
    for h in range(2):
        mixes.take_across(h)
        mixes.wait_diag(h)

        @pl.when(at.end)
        def _():
            pl.when(at.paired)(lambda: out_step(1, (h,)))
            out_step(2, (h,))

    @pl.when(at.end)
    def _():
        gy_gather.arrive(2)

    paired = mid & at.paired
    unpaired = mid & jnp.logical_not(at.paired)

    @pl.when(paired)
    def _():
        out_step(1, (0,))
        out_step(0, (0,))

    pl.when(unpaired)(lambda: out_step(0))
    gy_gather.loop(2, back_down)
    full_gather.forward(2)

    @pl.when(paired)
    def _():
        out_step(1, (1,))
        out_step(0, (1,))

    pl.when(unpaired)(lambda: out_step(1))

    @pl.when(mid)
    def _():
        full_gather.forward(3)
        out_step(2)

    @pl.when(at.end)
    def _():
        gy_gather.arrive(3)

    gy_gather.loop(3, back_down)
    full_gather.finish(0)
    full_gather.finish(1)
    pl.when(at.end)(lambda: full_gather.forward(3))
    wides = [
        pltpu.make_async_copy(src, dst, local.at[i])
        for i, (src, dst) in enumerate(((xn_wide, xn_out), (gy_wide, gy_out), (mixed_wide, mixed_out)))
    ]
    for copy in wides:
        copy.start()
    full_gather.finish(2)
    for dist in range(3):
        gy_gather.loop(dist, end_down)
    full_gather.finish(3)
    out_step(3)

    def residual(here):
        hidden[here, :] += x_ref[here, :].astype(F32)

    in_rows(tokens, 64, residual)
    value = hidden[...]
    second_total.start(jnp.sum(value * value, axis=1, keepdims=True))
    gy_gather.loop(3, end_down)
    scale = lax.rsqrt(second_total.finish() / model_width + EPSILON)
    scale_two[...] = scale
    ffn_in[...] = (hidden[...] * scale * gain_two[:, gain_spot]).astype(BF16)

    keep_saved.wait()
    for s in range(4):
        keep_dact(s).wait()
    full_gather.close()
    scale_share.close()
    x_gather.close()
    gy_gather.close()
    row_sum.close()
    quarter_sum.close()
    mixes.close(2)
    out_sum.close()
    for copy in wides:
        copy.wait()


def col_gather_sems():
    return [pltpu.SemaphoreType.DMA((2, 4, 2)), pltpu.SemaphoreType.DMA((4, 2))]


def chain_scratch(tokens, feats):
    return [
        pltpu.VMEM((4, tokens, feats), BF16), pltpu.VMEM((4, tokens, feats), BF16), pltpu.VMEM((tokens, feats), BF16),
    ]


def chain_sems():
    dma = pltpu.SemaphoreType.DMA
    return [dma((4, 2)), dma((4, 2)), dma((2,))]


def front(pairs, q_heads, groups, model_width, number, x, gy, weights, segments, tables, gains, ffn_weights):
    tokens, feats = x.shape
    w_query, w_key, w_value, w_out, w_down = weights
    width = w_query.shape[1] + w_key.shape[1] + w_value.shape[1]
    q_width, k_width, ff = w_query.shape[1], w_key.shape[1], w_down.shape[0]
    dma = pltpu.SemaphoreType.DMA
    any_spec, vmem = pl.BlockSpec(memory_space=pl.ANY), pl.BlockSpec(memory_space=pltpu.VMEM)
    shape = jax.ShapeDtypeStruct
    wide = pltpu.VMEM((4, tokens, feats), BF16)
    late = (*weights, *tables[:2])
    kept = [
        shape((tokens, width), F32),
        shape((tokens, q_width), BF16),
        shape((tokens, k_width), BF16),
        shape((tokens, k_width), BF16),
        shape((q_heads, tokens, tokens), BF16),
    ]
    dact = shape((4, tokens // 4, ff), F32)
    return pl.pallas_call(
        functools.partial(front_kernel, pairs, q_heads, groups, model_width),
        out_shape=(
            shape((tokens, 1), F32),
            shape((tokens, feats), F32),
            shape((tokens, 1), F32),
            shape((tokens, feats), BF16),
            *kept,
            dact,
            shape((4, tokens, feats), BF16),
            shape((4, tokens, feats), BF16),
            shape((4, tokens, q_width), BF16),
            shape((2, 4, *ffn_weights[0].shape), BF16),
        ),
        in_specs=[vmem] * 6 + [any_spec] * 10,
        out_specs=tuple([vmem] * 4 + [any_spec] * 10),
        scratch_shapes=[held(array) for array in late]
        + [held(array) for array in kept]
        + [
            held(dact),
            wide,
            pltpu.VMEM((4, 8, tokens), F32),
            wide,
            wide,
            pltpu.VMEM((4, tokens, q_width), BF16),
            pltpu.VMEM((tokens, q_width), BF16),
            pltpu.VMEM((tokens, width), F32),
            pltpu.VMEM((tokens, 512), F32),
            pltpu.VMEM((tokens // 4, ff), F32),
        ]
        + row_total_scratch(tokens) * 2
        + row_sum_scratch(tokens, width)
        + [pltpu.VMEM((4, tokens // 4, ff), BF16)] * 5
        + chain_scratch(tokens, feats)
        + col_gather_sems() * 2
        + [dma((3,))]
        + row_sum_sems()
        + [dma((2, 4)), dma((2, 4)), dma((4,)), dma((4,))]
        + [dma((2,))] * 7
        + chain_sems()
        + row_total_sems() * 2
        + weight_gather_sems(pairs)
        + [dma((8,)), dma((5,)), dma((4,)), dma((3,)), dma((4,))],
        compiler_params=pltpu.CompilerParams(
            collective_id=number, has_side_effects=True, vmem_limit_bytes=VMEM_LIMIT
        ),
        name="front",
    )(x, segments, *tables[2:], *gains, gy, *late, *ffn_weights)


def across_rows(left, right):
    return lax.dot_general(left, right, (((0,), (0,)), ((), ())), preferred_element_type=F32)


def attend_back(q_heads, groups, grad, qkv, qa, ka, va, probs, cos, sin, q_gain, k_gain, out, q_part, k_part, dq, dk, dv):
    kv = q_heads // groups
    tokens = qkv.shape[0]
    half = tokens // 2
    scale = 1.0 / math.sqrt(HEAD_SIZE)
    dk[...] = jnp.zeros_like(dk)
    dv[...] = jnp.zeros_like(dv)
    for block in range(2):
        rows = slice(block * half, (block + 1) * half)
        keys = (block + 1) * half
        for i in range(q_heads):
            j = i // groups
            spot = slice(j * HEAD_SIZE, (j + 1) * HEAD_SIZE)
            pb = probs[i, rows, :keys]
            p = pb.astype(F32)
            g = head(grad, i)[rows].astype(BF16)
            dv[:keys, spot] += across_rows(pb.astype(BF16), g)
            dp = lax.dot_general(
                g, head(va, j)[:keys], (((1,), (1,)), ((), ())), preferred_element_type=F32
            )
            ds = (p * (dp - jnp.sum(p * dp, axis=1, keepdims=True))).astype(BF16)
            dq[rows, i * HEAD_SIZE : (i + 1) * HEAD_SIZE] = (
                jnp.dot(ds, head(ka, j)[:keys], preferred_element_type=F32) * scale
            )
            dk[:keys, spot] += across_rows(ds, head(qa, i)[rows]) * scale

    def back(turned, index, gain):
        raw = head(qkv, index)
        scales = root_scale(raw)
        normed = turned * cos[...] - swap_halves(turned) * sin[...]
        part = jnp.sum(normed * raw * scales, axis=0, keepdims=True)
        weighted = normed * gain[...]
        inner = jnp.sum(weighted * raw, axis=1, keepdims=True)
        result = scales * weighted - raw * (scales * scales * scales) * inner * (1.0 / HEAD_SIZE)
        out[:, index * HEAD_SIZE : (index + 1) * HEAD_SIZE] = result.astype(BF16)
        return part

    q_part[...] = sum(back(head(dq, i), i, q_gain) for i in range(q_heads))
    k_part[...] = sum(back(head(dk, i), q_heads + i, k_gain) for i in range(kv))
    for i in range(kv):
        spot = (q_heads + kv + i) * HEAD_SIZE
        out[:, spot : spot + HEAD_SIZE] = head(dv, i).astype(BF16)


def act_copy(src, dst, at, j, sem):
    s = far_first(at.col, j)
    if j < 1:
        return pltpu.make_async_copy(src.at[s], dst.at[s], sem)
    return pltpu.make_async_copy(src.at[s, at.row], dst.at[s, at.row], sem)


def weight_grad(out, left, right, send=None):
    def block(here):
        total = None
        for s in range(4):
            term = across_rows(left(s, here), right(s))
            total = term if total is None else total + term
        out[here, :] = total.astype(BF16)
        if send is not None:
            send(here).start()

    in_rows(out.shape[0], 256, block)


def middle_kernel(pairs, *refs):
    refs = list(refs)

    def take(count):
        found = refs[:count]
        del refs[:count]
        return found

    (hn, w_gate, w_up, dact_in, full) = take(5)
    (dhn, act_out, gate_n, up_n) = take(4)
    others = take(1) if pairs == 2 else []
    (hn_wide, hn_full, weights, dact, gate_up, gate_wide, up_wide, act_wide, n_gate, n_up) = take(10)
    chain = take(3)
    hn_sems = take(2)
    (full_sem, share_send, share_recv) = take(3)
    gate_sems, up_sems, act_sems = take(6), take(6), take(6)
    chain_sems_ = take(3)
    (local, y_send, y_recv) = take(3)

    at = Ends()
    ff = w_gate.shape[1]
    quarter = hn.shape[0] // 4
    gather = ColGather(at, hn_wide, *hn_sems)
    loads = [pltpu.make_async_copy(dact_in, dact, full_sem.at[2, 0])]
    for which, own in enumerate((w_gate, w_up)):
        for i, r in enumerate((at.mate, at.across, at.diag, at.row)):
            src = own if i == 3 else full.at[which, r]
            loads.append(pltpu.make_async_copy(src, weights.at[which, r], full_sem.at[which, i]))
    for load in loads:
        load.start()
    gates = RowGather(at, lambda s: gate_wide.at[s, at.row], lambda s, q: gate_wide.at[s, q], gate_sems)
    ups = RowGather(at, lambda s: up_wide.at[s, at.row], lambda s, q: up_wide.at[s, q], up_sems)
    acts = RowGather(at, lambda s: act_wide.at[s, at.row], lambda s, q: act_wide.at[s, q], act_sems)
    back_sum = ColSum(at, dhn, *chain, *chain_sems_)

    hn_wide[at.col] = hn[...]
    at.greet(pairs if pairs == 2 else 0)

    peers = (at.mate, at.across, at.diag)

    def share(s):
        hn_full[s, at.row] = hn_wide[s, pl.ds(pl.multiple_of(at.row * quarter, quarter), quarter)]
        for i, peer in enumerate(peers):
            theirs = hn_wide.at[s, pl.ds(pl.multiple_of(peer * quarter, quarter), quarter)]
            remote(theirs, hn_full.at[s, at.row], share_send.at[s, i], share_recv.at[s, i], row=peer).start()

    def hidden_units(s):
        for i, peer in enumerate(peers):
            here = hn_full.at[s, peer]
            remote(here, here, share_send.at[s, i], share_recv.at[s, i], row=peer).wait_recv()
        size = gate_up.shape[2]

        def some(j, _):
            cols = pl.ds(pl.multiple_of(j * size, size), size)
            for which in range(2):
                total = None
                for r in range(4):
                    term = jnp.dot(hn_full[s, r], weights[which, r, :, cols], preferred_element_type=F32)
                    total = term if total is None else total + term
                gate_up[which] = total

            def one(here):
                gate, up = gate_up[0, here], gate_up[1, here]
                grad = dact[s, here, cols]
                sigmoid = jax.nn.sigmoid(gate)
                silu = gate * sigmoid
                act_wide[s, at.row, here, cols] = (silu * up).astype(BF16)
                gate_wide[s, at.row, here, cols] = (
                    grad * up * (sigmoid * (1.0 + gate * (1.0 - sigmoid)))
                ).astype(BF16)
                up_wide[s, at.row, here, cols] = (grad * silu).astype(BF16)

            in_rows(quarter, 16, one)
            return 0

        lax.fori_loop(0, ff // size, some, 0)
        gates.to_across(s).start()
        gates.near(s)
        ups.near(s)

    def close_share(s):
        for i, peer in enumerate(peers):
            here = hn_full.at[s, peer]
            remote(here, here, share_send.at[s, i], share_recv.at[s, i], row=peer).wait_send()

    def rows_of(ref, s):
        return ref[s].reshape(4 * quarter, ff)

    def back(j):
        s = far_first(at.col, j)
        contract = (((1,), (1,)), ((), ()))
        dhn[...] = lax.dot_general(
            rows_of(gate_wide, s), weights[0, at.row], contract, preferred_element_type=F32
        ) + lax.dot_general(rows_of(up_wide, s), weights[1, at.row], contract, preferred_element_type=F32)

    def arrive(some, j):
        s = far_first(at.col, j)
        some.wait_near(s)
        some.take_across(s)
        some.wait_diag(s)

    def left(s, here):
        return hn_wide[s, :, here]

    mid = jnp.logical_not(at.end)
    gather.arrive(0)
    gather.loop(0, share)
    for load in loads:
        load.wait()
    gather.loop(0, hidden_units)
    gather.arrive(1)
    gather.loop(1, share)
    gather.arrive(2)
    gather.loop(2, share)
    gather.loop(1, hidden_units)
    gather.arrive(3)
    gather.loop(3, share)
    gather.loop(2, hidden_units)
    gather.loop(3, hidden_units)
    for j in range(4):
        ups.to_across(far_first(at.col, j)).start()
    acts.near(far_first(at.col, 0))
    acts.to_across(far_first(at.col, 0)).start()
    keep_acts = [
        act_copy(act_wide, act_out, at, j, local.at[2 + j]) for j in range(4)
    ]
    for copy in keep_acts[1:]:
        copy.start()
    for j in range(4):
        arrive(gates, j)

    def to_other(here=slice(None)):
        return remote(n_gate.at[here], others[0].at[here], y_send.at[0], y_recv.at[0], dp=at.pair(2, 1))

    weight_grad(n_gate, left, lambda s: rows_of(gate_wide, s), to_other if pairs == 2 else None)
    keep_gate = pltpu.make_async_copy(n_gate, gate_n, local.at[0])
    keep_gate.start()
    arrive(ups, 0)
    for j in range(3):
        back(j)
        pl.when(at.end)(lambda: back_sum.step(far_first(at.col, j)))
        arrive(ups, j + 1)
        pl.when(mid)(lambda: back_sum.step(far_first(at.col, j)))
    weight_grad(n_up, left, lambda s: rows_of(up_wide, s))
    keep_up = pltpu.make_async_copy(n_up, up_n, local.at[1])
    keep_up.start()
    back(3)
    arrive(acts, 0)
    keep_acts[0].start()
    back_sum.step(at.col)

    gather.close()
    for dist in range(4):
        gather.loop(dist, close_share)
    gates.close(4)
    ups.close(4)
    acts.close_one(far_first(at.col, 0))
    back_sum.close()
    for copy in keep_acts:
        copy.wait()
    keep_gate.wait()
    keep_up.wait()
    if pairs == 2:
        to_other().wait()


def middle(pairs, number, hn, w_gate, w_up, dact, full):
    tokens, feats = hn.shape
    ff = w_gate.shape[1]
    quarter = tokens // 4
    dma = pltpu.SemaphoreType.DMA
    any_spec, vmem = pl.BlockSpec(memory_space=pl.ANY), pl.BlockSpec(memory_space=pltpu.VMEM)
    shape = jax.ShapeDtypeStruct
    narrow = shape((feats, ff), BF16)
    others = 1 if pairs == 2 else 0
    out = pl.pallas_call(
        functools.partial(middle_kernel, pairs),
        out_shape=tuple(
            [shape((tokens, feats), F32), shape((4, 4, quarter, ff), BF16), narrow, narrow] + [narrow] * others
        ),
        in_specs=[vmem] + [any_spec] * 4,
        out_specs=tuple([vmem] + [any_spec] * (3 + others)),
        scratch_shapes=[
            pltpu.VMEM((4, tokens, feats), BF16),
            pltpu.VMEM((4, 4, quarter, feats), BF16),
            pltpu.VMEM((2, 4, feats, ff), BF16),
            held(dact),
            pltpu.VMEM((2, quarter, 512), F32),
            pltpu.VMEM((4, 4, quarter, ff), BF16),
            pltpu.VMEM((4, 4, quarter, ff), BF16),
            pltpu.VMEM((4, 4, quarter, ff), BF16),
            pltpu.VMEM((feats, ff), BF16),
            pltpu.VMEM((feats, ff), BF16),
        ]
        + chain_scratch(tokens, feats)
        + col_gather_sems()
        + [dma((3, 4)), dma((4, 3)), dma((4, 3))]
        + [dma((4,))] * 18
        + chain_sems()
        + [dma((6,)), dma((1,)), dma((1,))],
        compiler_params=pltpu.CompilerParams(
            collective_id=number, has_side_effects=True, vmem_limit_bytes=VMEM_LIMIT
        ),
        name="middle",
    )(hn, w_gate, w_up, dact, full)
    return out[:4], out[4:]


def tail_kernel(pairs, q_heads, groups, *refs):
    refs = list(refs)

    def take(count):
        found = refs[:count]
        del refs[:count]
        return found

    (w_out, q_gain, k_gain, dhn, hidden, scale_two, gain_two, gy, x_ref, scale_one, gain_one) = take(11)
    late = take(12)
    (gy_wide, mixed_wide, normed_wide, up_n) = take(4)
    (in_grad, layer_out, one_grad, two_grad, q_grad, k_grad) = take(6)
    kept_out = take(5)
    others = take(6) if pairs == 2 else []
    (w_down, w_query, w_key, w_value, qkv, qa, ka, va, probs, cos, sin) = late_held = take(11)
    (da_wide, act_wide, dqkv, dqkv_wide, held_wide, product, grad_mixed, dq, dk, dv, *narrow) = take(15)
    (dh, q_part, k_part, packet, packet_got, by_row, summed) = take(7)
    first_bufs, last_bufs = take(2), take(2)
    moved = take(5)
    down_bufs, dxn_bufs = take(3), take(3)
    (g_send, g_recv, local, y_send, y_recv, late_sems) = take(6)
    moved_sems = take(4)
    act_sems, dqkv_sems = take(6), take(7)
    down_sems, dxn_sems = take(3), take(3)
    first_sems, last_sems = take(2), take(2)
    (p_send, p_recv, r_send, r_recv) = take(4)

    at = Ends()
    feats = dhn.shape[1]
    model_width = 4 * feats
    gain_spot = pl.ds(pl.multiple_of(at.row * feats, feats), feats)
    fetch_acts = [act_copy(late[0], act_wide, at, j, local.at[8 + j]) for j in range(4)]
    for copy in reversed(fetch_acts):
        copy.start()
    fetch = Fetch(list(zip(late[1:], late_held)), late_sems)
    fetch.start()
    first_total = RowTotal(at, *first_bufs, *first_sems)
    last_total = RowTotal(at, *last_bufs, *last_sems)
    at.greet(pairs, True, True)

    def pair_copy(index, here=slice(None)):
        return remote(
            narrow[index].at[here], others[index].at[here], y_send.at[index], y_recv.at[index],
            dp=1 - lax.axis_index("dp"),
        )

    n_down, n_out, n_query, n_key, n_value = narrow
    narrow = [up_n, *narrow]

    def to_pair(index):
        return functools.partial(pair_copy, index) if pairs == 2 else None

    def load(index, src):
        return pltpu.make_async_copy(src, held_wide, local.at[index])

    def keep(index):
        return pltpu.make_async_copy(narrow[index], kept_out[index - 1], local.at[2 + index])

    if pairs == 2:
        pair_copy(0).start()
    load(0, gy_wide).start()
    gather = ColGather(at, da_wide, g_send, g_recv)
    row_sum = RowSumWhole(at, product, grad_mixed, *moved, *moved_sems)
    acts = RowGather(at, lambda s: act_wide.at[s, at.row], lambda s, q: act_wide.at[s, q], act_sems)
    half = dqkv.shape[0] // 2
    grads = RowGather(
        at, lambda h: dqkv.at[pl.ds(h * half, half)], lambda h, q: dqkv_wide.at[q, pl.ds(h * half, half)], dqkv_sems
    )
    down_sum = ColSum(at, product, *down_bufs, *down_sems)
    dxn_sum = ColSum(at, product, *dxn_bufs, *dxn_sems)

    weighted = dhn[...] * gain_two[:, gain_spot]
    first_total.start(jnp.sum(weighted * hidden[...], axis=1, keepdims=True))
    scale = scale_two[...]
    packet[...] = jnp.zeros_like(packet)
    packet[1:2, :] = jnp.sum(dhn[...] * hidden[...] * scale, axis=0, keepdims=True)
    inner = first_total.finish()
    dh[...] = (
        gy[...].astype(F32)
        + scale * (dhn[...] * gain_two[:, gain_spot])
        - hidden[...] * (scale * scale * scale * inner * (1.0 / model_width))
    )
    da_wide[at.col] = dh[...].astype(BF16)
    gather.arrive(0)
    for copy in reversed(fetch_acts):
        copy.wait()
    for j in range(1, 4):
        acts.to_across(far_first(at.col, j)).start()
        acts.near(far_first(at.col, j))

    def back_out(s):
        product[...] = lax.dot_general(
            da_wide[s], w_out[...], (((1,), (1,)), ((), ())), preferred_element_type=F32
        )
        row_sum.give(s)

    def take_act(j):
        s = far_first(at.col, j)
        acts.wait_near(s)
        acts.take_across(s)
        acts.wait_diag(s)

    def act_rows(s, cols):
        return act_wide[s, :, :, cols].reshape(product.shape[0], cols.size)

    def down_step(j):
        s = far_first(at.col, j)
        product[...] = jnp.dot(
            act_rows(s, pl.ds(0, act_wide.shape[3])), w_down[...], preferred_element_type=F32
        )
        down_sum.step(s)

    def dxn_step(j, halves=(0, 1)):
        s = near_first(at, j)
        for h in halves:
            rows = pl.ds(h * half, half)
            total, base = None, 0
            for w in (w_query, w_key, w_value):
                size = w.shape[1]
                term = lax.dot_general(
                    dqkv_wide[s, rows, pl.ds(base, size)], w[...], (((1,), (1,)), ((), ())),
                    preferred_element_type=F32,
                )
                total = term if total is None else total + term
                base += size
            product[rows, :] = total
        dxn_sum.step(s, halves)

    def down_weight():
        load(0, gy_wide).wait()
        weight_grad(n_down, act_rows, lambda s: held_wide[s], to_pair(1))
        keep(1).start()
        load(1, mixed_wide).start()

    mid = jnp.logical_not(at.end)
    fetch.wait()
    gather.loop(0, back_out)
    gather.arrive(1)
    gather.loop(1, back_out)
    pl.when(at.end)(lambda: down_step(0))
    gather.arrive(2)
    gather.loop(2, back_out)
    pl.when(mid)(lambda: down_step(0))
    take_act(1)
    pl.when(at.end)(lambda: down_step(1))
    take_act(2)
    take_act(3)
    pl.when(at.end)(lambda: down_step(2))
    down_weight()
    pl.when(mid)(lambda: down_step(1))
    gather.arrive(3)
    gather.loop(3, back_out)
    row_sum.finish()
    attend_back(
        q_heads, groups, grad_mixed, qkv, qa, ka, va, probs, cos, sin, q_gain, k_gain,
        dqkv, q_part, k_part, dq, dk, dv,
    )
    for h in range(2):
        grads.to_across(h).start()
    for h in range(2):
        grads.near(h)
    for h in range(2):
        grads.wait_near(h)

    @pl.when(at.end)
    def _():
        dxn_step(0)
        pl.when(jnp.logical_not(at.paired))(lambda: dxn_step(1))

    @pl.when(mid)
    def _():
        down_step(2)

    load(1, mixed_wide).wait()
    weight_grad(n_out, lambda s, here: held_wide[s, :, here], lambda s: da_wide[s], to_pair(2))
    keep(2).start()
    load(2, normed_wide).start()
    paired = mid & at.paired
    unpaired = mid & jnp.logical_not(at.paired)
    pl.when(unpaired)(lambda: dxn_step(0))
    grads.take_across(0)
    grads.wait_diag(0)

    @pl.when(at.end)
    def _():
        pl.when(at.paired)(lambda: dxn_step(1, (0,)))
        dxn_step(2, (0,))

    @pl.when(paired)
    def _():
        dxn_step(1, (0,))
        dxn_step(0, (0,))

    pl.when(unpaired)(lambda: dxn_step(1, (0,)))
    grads.take_across(1)
    grads.wait_diag(1)

    @pl.when(at.end)
    def _():
        pl.when(at.paired)(lambda: dxn_step(1, (1,)))
        dxn_step(2, (1,))

    pl.when(unpaired)(lambda: dxn_step(1, (1,)))
    load(2, normed_wide).wait()
    base = 0
    for index, some in ((3, n_query), (4, n_key), (5, n_value)):
        spot = pl.ds(base, some.shape[1])
        weight_grad(
            some, lambda s, here: held_wide[s, :, here], lambda s, spot=spot: dqkv_wide[s, :, spot], to_pair(index)
        )
        keep(index).start()
        base += some.shape[1]

    @pl.when(paired)
    def _():
        dxn_step(2, (0,))
        dxn_step(0, (1,))

    @pl.when(paired)
    def _():
        dxn_step(1, (1,))
        dxn_step(2, (1,))

    pl.when(unpaired)(lambda: dxn_step(2))
    down_step(3)
    layer_out[...] = (hidden[...] + product[...]).astype(BF16)
    dxn_step(3)
    scale = scale_one[...]
    last_total.start(
        jnp.sum(product[...] * gain_one[:, gain_spot] * x_ref[...].astype(F32), axis=1, keepdims=True)
    )
    packet[0:1, :] = jnp.sum(product[...] * x_ref[...].astype(F32) * scale, axis=0, keepdims=True)
    packet[2:3, :HEAD_SIZE] = q_part[...]
    packet[2:3, HEAD_SIZE : 2 * HEAD_SIZE] = k_part[...]

    def to_line(step):
        return remote(
            packet, packet_got.at[step - 1], p_send.at[step - 1], p_recv.at[step - 1],
            col=lax.rem(at.col + step, 4),
        )

    def to_group(index, row, step):
        where = dict(row=row) if step == 0 else dict(row=row, dp=at.pair(pairs, step))
        return remote(summed, by_row.at[step, at.row], r_send.at[index], r_recv.at[step, at.row], **where)

    def from_group(index, row, step):
        here = by_row.at[step, row]
        return remote(summed, here, r_send.at[index], r_recv.at[step, row], row=at.mate)

    group = [(row, 0) for row in (at.mate, at.across, at.diag)]
    group += [(row, step) for step in range(1, pairs) for row in range(4)]
    for step in range(1, 4):
        to_line(step).start()
    inner = last_total.finish()
    in_grad[...] = (
        dh[...]
        + scale * (product[...] * gain_one[:, gain_spot])
        - x_ref[...].astype(F32) * (scale * scale * scale * inner * (1.0 / model_width))
    )
    for step in range(1, 4):
        to_line(step).wait()
    summed[...] = (packet[...] + packet_got[0]) + (packet_got[1] + packet_got[2])
    by_row[0, at.row] = summed[...]
    for index, (row, step) in enumerate(group):
        to_group(index, row, step).start()
    for index, (row, step) in enumerate(group):
        from_group(index, row, step).wait_recv()
        to_group(index, row, step).wait_send()
    total = by_row[0]
    for step in range(1, pairs):
        total = total + by_row[step]
    for r in range(4):
        one_grad[:, r * feats : (r + 1) * feats] = total[r, 0:1, :]
        two_grad[:, r * feats : (r + 1) * feats] = total[r, 1:2, :]
    heads = (total[0, 2:3, :] + total[1, 2:3, :]) + (total[2, 2:3, :] + total[3, 2:3, :])
    q_grad[...] = heads[:, :HEAD_SIZE]
    k_grad[...] = heads[:, HEAD_SIZE : 2 * HEAD_SIZE]

    gather.close()
    row_sum.close()
    for j in range(1, 4):
        acts.close_one(far_first(at.col, j))
    grads.close(2)
    down_sum.close()
    dxn_sum.close()
    for index in range(1, 6):
        keep(index).wait()
    if pairs == 2:
        for index in range(6):
            pair_copy(index).wait()


def tail(pairs, q_heads, groups, number, act, weights, saved, tables, norms, wides, narrow):
    tokens, feats = norms[0].shape
    w_out, w_down, w_query, w_key, _ = weights
    ff = w_down.shape[0]
    width = saved[0].shape[1]
    q_width, k_width = saved[1].shape[1], saved[2].shape[1]
    dma = pltpu.SemaphoreType.DMA
    any_spec, vmem = pl.BlockSpec(memory_space=pl.ANY), pl.BlockSpec(memory_space=pltpu.VMEM)
    shape = jax.ShapeDtypeStruct
    shapes = [
        shape((tokens, feats), F32),
        shape((tokens, feats), BF16),
        shape((1, 4 * feats), F32),
        shape((1, 4 * feats), F32),
        shape((1, HEAD_SIZE), F32),
        shape((1, HEAD_SIZE), F32),
    ]
    own = [
        shape((ff, feats), BF16),
        shape((q_width, feats), BF16),
        shape((feats, q_width), BF16),
        shape((feats, k_width), BF16),
        shape((feats, k_width), BF16),
    ]
    others = [shape(n.shape, BF16) for n in narrow] + own if pairs == 2 else []
    packet = pltpu.VMEM((8, feats), F32)
    early = (w_out, *tables[2:], *norms)
    late = (act, *weights[1:], *saved, *tables[:2])
    out = pl.pallas_call(
        functools.partial(tail_kernel, pairs, q_heads, groups),
        out_shape=tuple(shapes + own + others),
        in_specs=[vmem] * len(early) + [any_spec] * (len(late) + 4),
        out_specs=tuple([vmem] * 6 + [any_spec] * (5 + len(others))),
        scratch_shapes=[held(array) for array in late[1:]]
        + [
            pltpu.VMEM((4, tokens, feats), BF16),
            pltpu.VMEM((4, 4, tokens // 4, ff), BF16),
            pltpu.VMEM((tokens, width), BF16),
            pltpu.VMEM((4, tokens, width), BF16),
            pltpu.VMEM((4, tokens, feats), BF16),
            pltpu.VMEM((tokens, feats), F32),
            pltpu.VMEM((tokens, q_width), F32),
            pltpu.VMEM((tokens, q_width), F32),
            pltpu.VMEM((tokens, k_width), F32),
            pltpu.VMEM((tokens, k_width), F32),
        ]
        + [held(array) for array in own]
        + [
            pltpu.VMEM((tokens, feats), F32),
            pltpu.VMEM((1, HEAD_SIZE), F32),
            pltpu.VMEM((1, HEAD_SIZE), F32),
            packet,
            pltpu.VMEM((3, 8, feats), F32),
            pltpu.VMEM((pairs, 4, 8, feats), F32),
            packet,
        ]
        + row_total_scratch(tokens) * 2
        + row_sum_scratch(tokens, q_width)
        + chain_scratch(tokens, feats) * 2
        + col_gather_sems()
        + [dma((12,)), dma((6,)), dma((6,)), dma((12,))]
        + row_sum_sems()
        + [dma((4,))] * 6
        + [dma((2,))] * 7
        + chain_sems() * 2
        + row_total_sems() * 2
        + [dma((3,)), dma((3,)), dma((4 * pairs - 1,)), dma((pairs, 4))],
        compiler_params=pltpu.CompilerParams(
            collective_id=number, has_side_effects=True, vmem_limit_bytes=VMEM_LIMIT
        ),
        name="tail",
    )(*early, *late, *wides, *narrow)
    return out[:6], out[6:11], out[11:]


def finish_kernel(count, *refs):
    parts, others, rest = refs[:count], refs[count : 2 * count], refs[2 * count :]
    kept = len(rest) - count
    for a, b, out in zip(parts, others, rest[kept // 2 :]):
        out[...] = a[...].astype(F32) + b[...].astype(F32)
    for src, dst in zip(rest[: kept // 2], rest[kept // 2 + count :]):
        dst[...] = src[...]


def finish(parts, others, rest, steps=4):
    def spec(array):
        block = (array.shape[0] // steps, array.shape[1]) if array.shape[0] % steps == 0 else array.shape
        index = (lambda i: (i, 0)) if block != array.shape else (lambda i: (0, 0))
        return pl.BlockSpec(block, index)

    outs = [jax.ShapeDtypeStruct(a.shape, F32) for a in parts] + [jax.ShapeDtypeStruct(a.shape, a.dtype) for a in rest]
    operands = (*parts, *others, *rest)
    out = pl.pallas_call(
        functools.partial(finish_kernel, len(parts)),
        grid=(steps,),
        out_shape=tuple(outs),
        in_specs=[spec(a) for a in operands],
        out_specs=tuple(spec(a) for a in outs),
        compiler_params=pltpu.CompilerParams(vmem_limit_bytes=VMEM_LIMIT),
        name="finish",
    )(*operands)
    return out[: len(parts)], out[len(parts) :]


def shards(
    pairs,
    hidden_in,
    segment_ids,
    attn_gain,
    w_query,
    key_projection,
    value_projection,
    query_gain,
    key_norm_gain,
    w_out,
    ffn_gain,
    w_gate,
    w_up,
    w_down,
    out_grad,
):
    tokens = hidden_in.shape[0]
    model_width = attn_gain.shape[0]
    q_width = w_query.shape[1]
    k_width = key_projection.shape[1]
    q_heads = q_width // HEAD_SIZE
    groups = q_width // k_width
    tables = (*turn_tables(tokens), query_gain[None, :], key_norm_gain[None, :])
    (scale_one, hidden, scale_two, ffn_in, qkv, q_turned, k_turned, values, probs, grad_inner, xn_wide, gy_wide, mixed_wide, full) = front(
        pairs, q_heads, groups, model_width, 0, hidden_in, out_grad,
        (w_query, key_projection, value_projection, w_out, w_down),
        segment_ids[None, :],
        tables,
        (attn_gain[None, :], ffn_gain[None, :]),
        (w_gate, w_up),
    )
    (grad_ffn_in, inner_act, gate_n, up_n), other_gate = middle(pairs, 1, ffn_in, w_gate, w_up, grad_inner, full)
    (in_grad, layer_out, one_grad, two_grad, q_gain_grad, k_gain_grad), own, others = tail(
        pairs, q_heads, groups, 2, inner_act,
        (w_out, w_down, w_query, key_projection, value_projection),
        (qkv, q_turned, k_turned, values, probs),
        tables,
        (grad_ffn_in, hidden, scale_two, ffn_gain[None, :], out_grad, hidden_in, scale_one, attn_gain[None, :]),
        (gy_wide, mixed_wide, xn_wide),
        (up_n,),
    )
    parts = (gate_n, up_n, *own)
    if pairs == 2:
        rest = (in_grad, layer_out, one_grad, two_grad, q_gain_grad, k_gain_grad)
        sums, rest = finish(parts, (*other_gate, *others), rest)
        in_grad, layer_out, one_grad, two_grad, q_gain_grad, k_gain_grad = rest
    else:
        sums = lax.psum(tuple(part.astype(F32) for part in parts), "dp")
    gate_grad, up_grad, down_grad, out_weight_grad, query_grad, key_grad, value_grad = sums
    return (
        layer_out,
        in_grad,
        one_grad.reshape(-1),
        query_grad,
        key_grad,
        value_grad,
        q_gain_grad.reshape(-1),
        k_gain_grad.reshape(-1),
        out_weight_grad,
        two_grad.reshape(-1),
        gate_grad,
        up_grad,
        down_grad,
    )


def solution(mesh):
    acts, grid, flip, none = P(("dp", "col"), "row"), P("row", "col"), P("col", "row"), P()
    return jax.shard_map(
        functools.partial(shards, mesh.shape["dp"]),
        mesh=mesh,
        in_specs=(
            acts, P(("dp", "row")), none, grid, grid, grid, none, none, flip, none, grid, grid, flip, acts,
        ),
        out_specs=(
            acts, acts, none, grid, grid, grid, none, none, flip, none, grid, grid, flip,
        ),
        check_vma=False,
    )
```

```python
import functools
import math

import jax
import jax.numpy as jnp
import numpy as np
from jax import lax
from jax.experimental import pallas as pl
from jax.experimental.pallas import tpu as pltpu
from jax.sharding import PartitionSpec as P

HEAD_SIZE = 128
EPSILON = 1e-06
THETA = 1000000.0
MASKED = -1e30
MESH = pl.DeviceIdType.MESH
BF16 = jnp.bfloat16
F32 = jnp.float32
VMEM_LIMIT = 60 << 20


def to(**where):
    return dict(device_id=where, device_id_type=MESH)


class Ends:
    def __init__(self):
        self.row = lax.axis_index("row")
        self.col = lax.axis_index("col")
        self.chip = lax.div(self.row, 2)
        self.core = lax.rem(self.row, 2)
        self.mate = self.chip * 2 + (1 - self.core)
        self.across = (1 - self.chip) * 2 + self.core
        self.diag = (1 - self.chip) * 2 + (1 - self.core)
        self.end = (self.col == 0) | (self.col == 3)
        self.paired = lax.div(self.col, 2) == self.chip
        self.above = jnp.minimum(self.col + 1, 3)
        self.below = jnp.maximum(self.col - 1, 0)

    def greet(self, pairs=0, line=False, rows=False):
        gate = pltpu.get_barrier_semaphore()
        count = 3
        for peer in (self.mate, self.across, self.diag):
            pl.semaphore_signal(gate, inc=1, **to(row=peer))
        for step in range(1, pairs):
            dp = self.pair(pairs, step)
            for row in range(4) if rows else (self.row,):
                pl.semaphore_signal(gate, inc=1, **to(dp=dp, row=row))
                count += 1
        if line:
            for step in range(1, 4):
                pl.semaphore_signal(gate, inc=1, **to(col=lax.rem(self.col + step, 4)))
                count += 1
        else:

            @pl.when(self.col > 0)
            def _():
                pl.semaphore_signal(gate, inc=1, **to(col=self.col - 1))

            @pl.when(self.col < 3)
            def _():
                pl.semaphore_signal(gate, inc=1, **to(col=self.col + 1))

            count += jnp.where(self.col > 0, 1, 0) + jnp.where(self.col < 3, 1, 0)
        pl.semaphore_wait(gate, count)

    def pair(self, pairs, step):
        return lax.rem(lax.axis_index("dp") + step, pairs)


class RowTotal:
    def __init__(self, at, own, got, sends, recvs):
        self.own, self.got = own, got
        self.copies = [
            remote(own, got.at[i], sends.at[i], recvs.at[i], row=peer)
            for i, peer in enumerate((at.mate, at.across, at.diag))
        ]

    def start(self, column):
        self.own[...] = jnp.broadcast_to(column, (column.shape[0], 128)).T[:8, :]
        for copy in self.copies:
            copy.start()

    def total(self):
        for copy in self.copies:
            copy.wait()
        return (self.own[...] + self.got[0]) + (self.got[1] + self.got[2])

    def finish(self):
        return as_column(self.total())


def as_column(lines):
    return jnp.concatenate([lines] * 16, axis=0).T[:, :1]


class LineShare:
    def __init__(self, at, blocks, sends, recvs):
        self.at, self.blocks, self.sends, self.recvs = at, blocks, sends, recvs

    def copy(self, s, step):
        here = self.blocks.at[s]
        col = lax.rem(self.at.col + step, 4)
        return remote(here, here, self.sends.at[step - 1], self.recvs.at[s], col=col)

    def start(self):
        for step in range(1, 4):
            self.copy(self.at.col, step).start()

    def wait(self, s):
        pl.when(s != self.at.col)(lambda: self.copy(s, 1).wait_recv())

    def close(self):
        for step in range(1, 4):
            self.copy(self.at.col, step).wait_send()


def row_total_scratch(tokens):
    return [pltpu.VMEM((8, tokens), F32), pltpu.VMEM((3, 8, tokens), F32)]


def row_total_sems():
    return [pltpu.SemaphoreType.DMA((3,)), pltpu.SemaphoreType.DMA((3,))]


def remote(src, dst, sends, recvs, **where):
    return pltpu.make_async_remote_copy(
        src_ref=src, dst_ref=dst, send_sem=sends, recv_sem=recvs, **to(**where)
    )


class Fetch:
    def __init__(self, pairs, sems):
        self.copies = [
            pltpu.make_async_copy(src, dst, sems.at[i]) for i, (src, dst) in enumerate(pairs)
        ]

    def start(self):
        for copy in self.copies:
            copy.start()

    def wait(self, first=0, last=None):
        for copy in self.copies[first:last]:
            copy.wait()


def held(array):
    return pltpu.VMEM(array.shape, array.dtype)


def in_rows(count, step, body, first=0):
    def one(i, _):
        body(pl.ds(pl.multiple_of(first + i * step, step), step))
        return 0

    lax.fori_loop(0, count // step, one, 0)


class ColGather:
    def __init__(self, at, wide, sends, recvs):
        self.at, self.wide, self.sends, self.recvs = at, wide, sends, recvs
        self.half = wide.shape[1] // 2

    def copy(self, s, h, side, col):
        part = self.wide.at[s, pl.ds(h * self.half, self.half)]
        return remote(part, part, self.sends.at[side, s, h], self.recvs.at[s, h], col=col)

    def up(self, s, h):
        return self.copy(s, h, 0, self.at.above)

    def down(self, s, h):
        return self.copy(s, h, 1, self.at.below)

    def loop(self, dist, body):
        if dist == 0:
            body(self.at.col)
            return

        def one(side, _):
            s = jnp.where(side == 0, self.at.col - dist, self.at.col + dist)
            pl.when((s >= 0) & (s <= 3))(lambda: body(s))
            return 0

        lax.fori_loop(0, 2, one, 0)

    def arrive(self, dist):
        for h in range(2):

            def take(s, h=h):
                if dist:
                    self.up(s, h).wait_recv()

                @pl.when((s <= self.at.col) & (self.at.col < 3))
                def _():
                    self.up(s, h).start()

                @pl.when((s >= self.at.col) & (self.at.col > 0))
                def _():
                    self.down(s, h).start()

            self.loop(dist, take)

    def send_up(self):
        for h in range(2):
            self.up(self.at.col, h).start()

    def send_down(self):
        for h in range(2):
            self.down(self.at.col, h).start()

    def close(self):
        def one(s, _):
            for h in range(2):

                @pl.when((s <= self.at.col) & (self.at.col < 3))
                def _():
                    self.up(s, h).wait_send()

                @pl.when((s >= self.at.col) & (self.at.col > 0))
                def _():
                    self.down(s, h).wait_send()

            return 0

        lax.fori_loop(0, 4, one, 0)


class RowSumWhole:
    def __init__(self, at, product, out, a_send, a_recv, c_recv, d_send, d_recv, m_send, m_recv, x_send, x_recv):
        self.at, self.product, self.out = at, product, out
        self.a_send, self.a_recv, self.c_recv, self.d_send, self.d_recv = a_send, a_recv, c_recv, d_send, d_recv
        self.m_send, self.m_recv, self.x_send, self.x_recv = m_send, m_recv, x_send, x_recv
        self.half = product.shape[0] // 2
        self.d = remote(d_send, d_recv, m_send.at[2], m_recv.at[2], row=at.mate)

    def a(self, i):
        return remote(self.a_send.at[i], self.a_recv.at[i], self.m_send.at[i], self.m_recv.at[i], row=self.at.mate)

    def b(self, i, s):
        core = self.at.core
        return remote(self.a_recv.at[i], self.c_recv.at[core], self.x_send.at[i], self.x_recv.at[core], row=s)

    def part(self, core, here):
        return pl.ds(pl.multiple_of(core * self.half + here.start, here.size), here.size)

    def give(self, s):
        at, product, half = self.at, self.product, self.half
        i = lax.rem(s, 2)
        ours = lax.div(s, 2) == at.chip

        @pl.when(jnp.logical_not(ours))
        def _():
            def cast(here):
                self.a_send[i, here] = product[self.part(1 - at.core, here), :].astype(BF16)

            in_rows(half, 64, cast)
            self.a(i).start()
            self.a(i).wait_recv()

            def add(here):
                total = product[self.part(at.core, here), :] + self.a_recv[i, here].astype(F32)
                self.a_recv[i, here] = total.astype(BF16)

            in_rows(half, 64, add)
            self.b(i, s).start()

        @pl.when(ours & (i != at.core))
        def _():
            def cast(here):
                self.d_send[here] = product[here, :].astype(BF16)

            in_rows(2 * half, 64, cast)
            self.d.start()

        @pl.when(s == at.row)
        def _():
            def store(here):
                self.out[here] = product[here, :]

            in_rows(2 * half, 64, store)

    def finish(self):
        self.d.wait_recv()
        for h in range(2):
            here = self.c_recv.at[h]
            remote(here, here, self.x_send.at[h], self.x_recv.at[h], row=self.at.across).wait_recv()

            def add(rows, h=h):
                spot = pl.ds(pl.multiple_of(h * self.half + rows.start, rows.size), rows.size)
                self.out[spot] += self.d_recv[spot].astype(F32) + self.c_recv[h, rows].astype(F32)

            in_rows(self.half, 64, add)

    def close(self):
        self.d.wait_send()
        for i in range(2):
            self.a(i).wait_send()
            self.b(i, self.at.across).wait_send()


def row_sum_scratch(tokens, width):
    half = pltpu.VMEM((2, tokens // 2, width), BF16)
    full = pltpu.VMEM((tokens, width), BF16)
    return [half, half, half, full, full]


def row_sum_sems():
    dma = pltpu.SemaphoreType.DMA
    return [dma((3,)), dma((3,)), dma((2,)), dma((2,))]


class RowSumQuarter:
    def __init__(self, at, chunk, keep, a_send, a_recv, c_recv, d_send, d_recv, m_send, m_recv, x_send, x_recv):
        self.at, self.chunk, self.keep = at, chunk, keep
        self.a_send, self.a_recv, self.c_recv = a_send, a_recv, c_recv
        self.d_send, self.d_recv = d_send, d_recv
        self.sems = (m_send, m_recv, x_send, x_recv)

    def a(self, s):
        m_send, m_recv, _, _ = self.sems
        return remote(self.a_send.at[s], self.a_recv.at[s], m_send.at[0, s], m_recv.at[0, s], row=self.at.mate)

    def d(self, s):
        m_send, m_recv, _, _ = self.sems
        return remote(self.d_send.at[s], self.d_recv.at[s], m_send.at[1, s], m_recv.at[1, s], row=self.at.mate)

    def b(self, s):
        _, _, x_send, x_recv = self.sems
        return remote(self.a_recv.at[s], self.c_recv.at[s], x_send.at[s], x_recv.at[s], row=self.at.across)

    def split(self, s, value, spot, own):
        at, chunk = self.at, self.chunk
        chunk[...] = value

        def quarter(q):
            return chunk[pl.ds(pl.multiple_of(q * 128, 128), 128), :]

        self.a_send[s, :, spot] = quarter(at.diag).astype(BF16)
        self.keep[:, spot] = quarter(at.across)
        self.d_send[s, :, spot] = quarter(at.mate).astype(BF16)
        own[s, :, spot] = quarter(at.row).astype(own.dtype)

    def give(self, s):
        self.a(s).start()
        self.d(s).start()
        self.a(s).wait_recv()

        def one(here):
            self.a_recv[s, here] = (self.keep[here, :] + self.a_recv[s, here].astype(F32)).astype(BF16)

        in_rows(128, 16, one)
        self.b(s).start()

    def finish(self, s):
        self.d(s).wait_recv()
        self.b(s).wait_recv()

    def close(self):
        def one(s, _):
            self.a(s).wait_send()
            self.b(s).wait_send()
            self.d(s).wait_send()
            return 0

        lax.fori_loop(0, 4, one, 0)


class RowGather:
    def __init__(self, at, own, slot, sems):
        self.at, self.own, self.slot = at, own, slot
        self.m_send, self.m_recv, self.x_send, self.x_recv, self.f_send, self.f_recv, self.local = (*sems, None)[:7]

    def to_mate(self, s):
        return remote(self.own(s), self.slot(s, self.at.row), self.m_send.at[s], self.m_recv.at[s], row=self.at.mate)

    def to_across(self, s):
        return remote(self.own(s), self.slot(s, self.at.row), self.x_send.at[s], self.x_recv.at[s], row=self.at.across)

    def pass_on(self, s):
        here = self.slot(s, self.at.across)
        return remote(here, here, self.f_send.at[s], self.f_recv.at[s], row=self.at.mate)

    def move_own(self, s):
        return pltpu.make_async_copy(self.own(s), self.slot(s, self.at.row), self.local.at[s])

    def near(self, s):
        self.to_mate(s).start()
        if self.local is not None:
            self.move_own(s).start()

    def wait_near(self, s):
        here = self.slot(s, self.at.mate)
        remote(here, here, self.m_send.at[s], self.m_recv.at[s], row=self.at.mate).wait_recv()
        if self.local is not None:
            self.move_own(s).wait()

    def take_across(self, s):
        here = self.slot(s, self.at.across)
        remote(here, here, self.x_send.at[s], self.x_recv.at[s], row=self.at.across).wait_recv()
        self.pass_on(s).start()

    def wait_diag(self, s):
        here = self.slot(s, self.at.diag)
        remote(here, here, self.f_send.at[s], self.f_recv.at[s], row=self.at.mate).wait_recv()

    def close_one(self, s):
        self.to_mate(s).wait_send()
        self.to_across(s).wait_send()
        self.pass_on(s).wait_send()

    def close(self, count):
        def one(s, _):
            self.close_one(s)
            return 0

        lax.fori_loop(0, count, one, 0)


class WeightGather:
    def __init__(self, at, pairs, own, full, sems):
        self.at, self.pairs, self.own, self.full = at, pairs, own, full
        self.m_send, self.m_recv, self.x_send, self.x_recv, self.y_send, self.y_recv = sems[:6]
        self.f_send, self.f_recv, self.g_send, self.g_recv = sems[6:]
        self.step = full.shape[2] // 4
        self.mine = lax.axis_index("dp") if pairs == 2 else None

    def rows(self, j):
        return pl.ds(j * self.step, self.step)

    def piece(self, which, row, j):
        return self.full.at[which, row, self.rows(j)]

    def held(self):
        return (self.mine,) if self.pairs == 2 else (0, 1)

    def near(self, which, row):
        here = self.full.at[which, row]
        return remote(self.own[which], here, self.m_send.at[which], self.m_recv.at[which], row=self.at.mate)

    def over(self, which, row, j, src=None):
        here = self.piece(which, row, j)
        lane = 0 if self.pairs == 2 else which
        src = here if src is None else src
        return remote(src, here, self.x_send.at[lane, j], self.x_recv.at[lane, j], row=self.at.across)

    def hand(self, which, j):
        here = self.piece(which, self.at.across, j)
        return remote(here, here, self.y_send.at[j], self.y_recv.at[j], dp=self.at.pair(2, 1))

    def pass_first(self, which, row, j):
        here = self.piece(which, row, j)
        lane = 0 if self.pairs == 2 else which
        return remote(here, here, self.f_send.at[lane, j], self.f_recv.at[lane, j], row=self.at.mate)

    def pass_second(self, which, row, j):
        here = self.piece(which, row, j)
        return remote(here, here, self.g_send.at[j], self.g_recv.at[j], row=self.at.mate)

    def begin(self):
        for i in range(2):
            self.near(i, self.at.row).start()

    def send(self, j):
        for which in range(2):
            copy = self.over(which, self.at.row, j, self.own[which].at[self.rows(j)])
            if self.pairs == 2:
                pl.when(self.mine == which)(copy.start)
            else:
                copy.start()

    def forward(self, j):
        for which in self.held():
            self.over(which, self.at.across, j).wait_recv()
            if self.pairs == 2:
                self.hand(which, j).start()
            self.pass_first(which, self.at.across, j).start()

    def finish(self, j):
        if self.pairs == 2:
            self.hand(1 - self.mine, j).wait_recv()
            self.pass_second(1 - self.mine, self.at.across, j).start()

    def close(self):
        for i in range(2):
            self.near(i, self.at.mate).wait_recv()
            self.near(i, self.at.row).wait_send()
        for j in range(4):
            for which in self.held():
                self.over(which, self.at.row, j).wait_send()
                self.pass_first(which, self.at.diag, j).wait_recv()
                self.pass_first(which, self.at.across, j).wait_send()
            if self.pairs == 2:
                self.hand(self.mine, j).wait_send()
                self.pass_second(1 - self.mine, self.at.diag, j).wait_recv()
                self.pass_second(1 - self.mine, self.at.across, j).wait_send()


def weight_gather_sems(pairs):
    dma = pltpu.SemaphoreType.DMA
    lanes = 1 if pairs == 2 else 2
    return [
        dma((2,)), dma((2,)), dma((lanes, 4)), dma((lanes, 4)), dma((4,)), dma((4,)),
        dma((lanes, 4)), dma((lanes, 4)), dma((4,)), dma((4,)),
    ]


class ColSum:
    def __init__(self, at, product, sent, got, extra, sends, recvs, extra_recvs):
        self.at, self.product, self.sent, self.got, self.extra = at, product, sent, got, extra
        self.sends, self.recvs, self.extra_recvs = sends, recvs, extra_recvs
        self.half = product.shape[0] // 2

    def part(self, h):
        return pl.ds(h * self.half, self.half)

    def up(self, s, h):
        return remote(
            self.sent.at[s, self.part(h)], self.got.at[s, self.part(h)],
            self.sends.at[s, h], self.recvs.at[s, h], col=self.at.above,
        )

    def down(self, s, h):
        return remote(
            self.sent.at[s, self.part(h)], self.got.at[s, self.part(h)],
            self.sends.at[s, h], self.recvs.at[s, h], col=self.at.below,
        )

    def last_down(self, s, h):
        return remote(
            self.sent.at[s, self.part(h)], self.extra.at[self.part(h)],
            self.sends.at[s, h], self.extra_recvs.at[h], col=self.at.below,
        )

    def step(self, s, halves=(0, 1)):
        col, product = self.at.col, self.product
        for h in halves:
            @pl.when(((s >= col) & (col > 0)) | ((s < col) & (col < 3)))
            def _():
                self.up(s, h).wait_recv()

                def add(here):
                    product[here, :] += self.got[s, here].astype(F32)

                in_rows(self.half, 64, add, h * self.half)

            @pl.when((s == col) & (col < 3))
            def _():
                self.last_down(s, h).wait_recv()

                def add(here):
                    product[here, :] += self.extra[here].astype(F32)

                in_rows(self.half, 64, add, h * self.half)

            @pl.when(s != col)
            def _():
                def cast(here):
                    self.sent[s, here] = product[here, :].astype(BF16)

                in_rows(self.half, 64, cast, h * self.half)

            pl.when(s > col)(lambda: self.up(s, h).start())
            pl.when(s < col - 1)(lambda: self.down(s, h).start())
            pl.when(s == col - 1)(lambda: self.last_down(s, h).start())

    def close(self):
        def one(s, _):
            for h in range(2):
                pl.when(s != self.at.col)(lambda: self.up(s, h).wait_send())
            return 0

        lax.fori_loop(0, 4, one, 0)


def far_first(col, j):
    first = jnp.where(col < 2, 3, 0)
    near = jnp.where(col < 2, 2, 1)
    partner = jnp.where(lax.rem(col, 2) == 0, col + 1, col - 1)
    end = (col == 0) | (col == 3)
    return (first, jnp.where(end, near, partner), jnp.where(end, partner, near), col)[j]


def near_first(at, j):
    first = jnp.where(at.col < 2, 3, 0)
    near = jnp.where(at.col < 2, 2, 1)
    partner = jnp.where(lax.rem(at.col, 2) == 0, at.col + 1, at.col - 1)
    mine = at.paired
    return (
        jnp.where(mine, partner, first),
        jnp.where(mine, first, near),
        jnp.where(mine, near, partner),
        at.col,
    )[j]


def turn_tables(length):
    rates = THETA ** (-np.arange(HEAD_SIZE // 2) * 2.0 / HEAD_SIZE)
    angles = np.arange(length)[:, None] * rates[None, :]
    cos, sin = np.cos(angles), np.sin(angles)
    return (
        np.concatenate([cos, cos], axis=1).astype(np.float32),
        np.concatenate([-sin, sin], axis=1).astype(np.float32),
    )


def swap_halves(value):
    return pltpu.roll(value, HEAD_SIZE // 2, 1)


def head(ref, index):
    return ref[:, index * HEAD_SIZE : (index + 1) * HEAD_SIZE]


def root_scale(raw):
    return lax.rsqrt(jnp.mean(raw * raw, axis=1, keepdims=True) + EPSILON)


def attend(q_heads, groups, qkv, seg_row, cos, sin, q_gain, k_gain, o, qa, ka, va, probs, done):
    kv = q_heads // groups
    tokens = qkv.shape[0]
    half = tokens // 2
    seg_line = seg_row[...].astype(F32)
    seg_column = jnp.broadcast_to(seg_line, (128, tokens)).T[:, :1]

    def turned(index, gain):
        raw = head(qkv, index)
        normed = raw * root_scale(raw) * gain[...]
        return (normed * cos[...] + swap_halves(normed) * sin[...]).astype(BF16)

    for i in range(q_heads):
        qa[:, i * HEAD_SIZE : (i + 1) * HEAD_SIZE] = turned(i, q_gain)
    for i in range(kv):
        ka[:, i * HEAD_SIZE : (i + 1) * HEAD_SIZE] = turned(q_heads + i, k_gain)
        va[:, i * HEAD_SIZE : (i + 1) * HEAD_SIZE] = head(qkv, q_heads + kv + i).astype(BF16)
    for block in range(2):
        rows = slice(block * half, (block + 1) * half)
        keys = (block + 1) * half
        spot = lax.broadcasted_iota(jnp.int32, (half, keys), 0) + block * half
        other = lax.broadcasted_iota(jnp.int32, (half, keys), 1)
        allowed = (other <= spot) & (seg_column[rows, :] == seg_line[:, :keys])
        for i in range(q_heads):
            j = i // groups
            dots = lax.dot_general(
                head(qa, i)[rows], head(ka, j)[:keys], (((1,), (1,)), ((), ())), preferred_element_type=F32
            ) * (1.0 / math.sqrt(HEAD_SIZE))
            scores = jnp.where(allowed, dots, MASKED)
            expo = jnp.exp(scores - jnp.max(scores, axis=1, keepdims=True))
            p = expo / jnp.sum(expo, axis=1, keepdims=True)
            probs[i, rows, :keys] = p.astype(BF16)
            mixed = jnp.dot(p.astype(BF16), head(va, j)[:keys], preferred_element_type=F32)
            o[rows, i * HEAD_SIZE : (i + 1) * HEAD_SIZE] = mixed.astype(BF16)
        done(block)


def front_kernel(pairs, q_heads, groups, model_width, *refs):
    refs = list(refs)

    def take(count):
        found = refs[:count]
        del refs[:count]
        return found

    (x_ref, seg_row, q_gain, k_gain, gain_one, gain_two) = take(6)
    late = take(8)
    (w_gate, w_up) = take(2)
    (scale_one, hidden, scale_two, ffn_in) = take(4)
    kept_out = take(5)
    (dact_out, xn_out, gy_out, mixed_out, full) = take(5)
    (w_query, w_key, w_value, w_out, w_down, cos, sin) = late_held = take(7)
    (qkv, qa, ka, va, probs) = kept = take(5)
    (dact,) = take(1)
    (x_wide, scales, xn_wide, gy_wide, mixed_wide, mixed, product, chunk, keep) = take(9)
    total_bufs = take(2)
    second_bufs = take(2)
    moved = take(5)
    moved_q = take(5)
    chain = take(3)
    x_sems, gy_sems = take(2), take(2)
    (local,) = take(1)
    moved_sems, moved_q_sems = take(4), take(4)
    mixed_sems = take(7)
    chain_sems = take(3)
    total_sems, second_sems = take(2), take(2)
    full_sems = take(10)
    late_sems, kept_sems, dact_sems = take(3)
    scale_sems = take(2)

    at = Ends()
    gain_spot = pl.ds(pl.multiple_of(at.row * x_ref.shape[1], x_ref.shape[1]), x_ref.shape[1])
    fetch = Fetch([*zip(late[1:], late_held), (late[0], gy_wide.at[at.col])], late_sems)
    fetch.start()
    keep_saved = Fetch(list(zip(kept, kept_out)), kept_sems)
    full_gather = WeightGather(at, pairs, (w_gate, w_up), full, full_sems)
    tokens, feats = x_ref.shape
    first_total = RowTotal(at, *total_bufs, *total_sems)
    second_total = RowTotal(at, *second_bufs, *second_sems)
    x_gather = ColGather(at, x_wide, *x_sems)
    scale_share = LineShare(at, scales, *scale_sems)
    gy_gather = ColGather(at, gy_wide, *gy_sems)
    row_sum = RowSumWhole(at, product, qkv, *moved, *moved_sems)
    quarter_sum = RowSumQuarter(at, chunk, keep, *moved_q, *moved_q_sems)
    half = tokens // 2
    mixes = RowGather(
        at, lambda h: mixed.at[pl.ds(h * half, half)], lambda h, q: mixed_wide.at[q, pl.ds(h * half, half)], mixed_sems
    )
    out_sum = ColSum(at, hidden, *chain, *chain_sems)

    x_wide[at.col] = x_ref[...]
    at.greet(pairs if pairs == 2 else 0, True)
    x_gather.arrive(0)
    stream = x_ref[...].astype(F32)
    first_total.start(jnp.sum(stream * stream, axis=1, keepdims=True))
    full_gather.begin()
    full_gather.send(0)
    scales[at.col] = lax.rsqrt(first_total.total() / model_width + EPSILON)
    scale_share.start()
    scale_one[...] = as_column(scales[at.col])

    def project(s):
        scale_share.wait(s)
        scale = as_column(scales[s])
        xn_wide[s] = (x_wide[s].astype(F32) * scale * gain_one[:, gain_spot]).astype(BF16)
        base = 0
        for w in (w_query, w_key, w_value):
            size = w.shape[1]
            product[:, base : base + size] = jnp.dot(xn_wide[s], w[...], preferred_element_type=F32)
            base += size
        row_sum.give(s)

    def back_down(s):
        size = chunk.shape[1]

        def one(j, _):
            cols = pl.ds(pl.multiple_of(j * size, size), size)
            value = lax.dot_general(
                gy_wide[s], w_down[cols, :], (((1,), (1,)), ((), ())), preferred_element_type=F32
            )
            quarter_sum.split(s, value, cols, dact)
            return 0

        lax.fori_loop(0, w_down.shape[0] // size, one, 0)
        quarter_sum.give(s)

    def keep_dact(s):
        return pltpu.make_async_copy(dact.at[s], dact_out.at[s], dact_sems.at[s])

    def end_down(s):
        quarter_sum.finish(s)

        def add(here):
            dact[s, here] += moved_q[2][s, here].astype(F32) + moved_q[4][s, here].astype(F32)

        in_rows(128, 16, add)
        keep_dact(s).start()

    def send_gy(dist):
        @pl.when((at.col == dist) & (at.col < 3))
        def _():
            gy_gather.send_up()

        @pl.when((at.col == 3 - dist) & (at.col > 0))
        def _():
            gy_gather.send_down()

    def out_step(j, halves=(0, 1)):
        s = near_first(at, j)
        for h in halves:
            rows = pl.ds(h * half, half)
            hidden[rows, :] = jnp.dot(mixed_wide[s, rows, :], w_out[...], preferred_element_type=F32)
        out_sum.step(s, halves)

    mid = jnp.logical_not(at.end)
    fetch.wait()
    send_gy(0)
    x_gather.loop(0, project)
    back_down(at.col)
    full_gather.send(1)
    for dist in range(1, 4):
        x_gather.arrive(dist)
        send_gy(dist)
        x_gather.loop(dist, project)
        if dist == 1:
            full_gather.forward(0)

    @pl.when(mid)
    def _():
        gy_gather.arrive(1)

    row_sum.finish()

    def send_mixed(h):
        mixes.to_across(h).start()
        mixes.near(h)

    attend(q_heads, groups, qkv, seg_row, cos, sin, q_gain, k_gain, mixed, qa, ka, va, probs, send_mixed)
    keep_saved.start()
    full_gather.send(2)
    full_gather.forward(1)

    @pl.when(mid)
    def _():
        gy_gather.arrive(2)

    for h in range(2):
        mixes.wait_near(h)

    @pl.when(at.end)
    def _():
        out_step(0)
        pl.when(jnp.logical_not(at.paired))(lambda: out_step(1))
        gy_gather.arrive(1)

    full_gather.send(3)
    gy_gather.loop(1, back_down)
    for h in range(2):
        mixes.take_across(h)
        mixes.wait_diag(h)

        @pl.when(at.end)
        def _():
            pl.when(at.paired)(lambda: out_step(1, (h,)))
            out_step(2, (h,))

    @pl.when(at.end)
    def _():
        gy_gather.arrive(2)

    paired = mid & at.paired
    unpaired = mid & jnp.logical_not(at.paired)

    @pl.when(paired)
    def _():
        out_step(1, (0,))
        out_step(0, (0,))

    pl.when(unpaired)(lambda: out_step(0))
    gy_gather.loop(2, back_down)
    full_gather.forward(2)

    @pl.when(paired)
    def _():
        out_step(1, (1,))
        out_step(0, (1,))

    pl.when(unpaired)(lambda: out_step(1))

    @pl.when(mid)
    def _():
        full_gather.forward(3)
        out_step(2)

    @pl.when(at.end)
    def _():
        gy_gather.arrive(3)

    gy_gather.loop(3, back_down)
    full_gather.finish(0)
    full_gather.finish(1)
    pl.when(at.end)(lambda: full_gather.forward(3))
    wides = [
        pltpu.make_async_copy(src, dst, local.at[i])
        for i, (src, dst) in enumerate(((xn_wide, xn_out), (gy_wide, gy_out), (mixed_wide, mixed_out)))
    ]
    for copy in wides:
        copy.start()
    full_gather.finish(2)
    for dist in range(3):
        gy_gather.loop(dist, end_down)
    full_gather.finish(3)
    out_step(3)

    def residual(here):
        hidden[here, :] += x_ref[here, :].astype(F32)

    in_rows(tokens, 64, residual)
    value = hidden[...]
    second_total.start(jnp.sum(value * value, axis=1, keepdims=True))
    gy_gather.loop(3, end_down)
    scale = lax.rsqrt(second_total.finish() / model_width + EPSILON)
    scale_two[...] = scale
    ffn_in[...] = (hidden[...] * scale * gain_two[:, gain_spot]).astype(BF16)

    keep_saved.wait()
    for s in range(4):
        keep_dact(s).wait()
    full_gather.close()
    scale_share.close()
    x_gather.close()
    gy_gather.close()
    row_sum.close()
    quarter_sum.close()
    mixes.close(2)
    out_sum.close()
    for copy in wides:
        copy.wait()


def col_gather_sems():
    return [pltpu.SemaphoreType.DMA((2, 4, 2)), pltpu.SemaphoreType.DMA((4, 2))]


def chain_scratch(tokens, feats):
    return [
        pltpu.VMEM((4, tokens, feats), BF16), pltpu.VMEM((4, tokens, feats), BF16), pltpu.VMEM((tokens, feats), BF16),
    ]


def chain_sems():
    dma = pltpu.SemaphoreType.DMA
    return [dma((4, 2)), dma((4, 2)), dma((2,))]


def front(pairs, q_heads, groups, model_width, number, x, gy, weights, segments, tables, gains, ffn_weights):
    tokens, feats = x.shape
    w_query, w_key, w_value, w_out, w_down = weights
    width = w_query.shape[1] + w_key.shape[1] + w_value.shape[1]
    q_width, k_width, ff = w_query.shape[1], w_key.shape[1], w_down.shape[0]
    dma = pltpu.SemaphoreType.DMA
    any_spec, vmem = pl.BlockSpec(memory_space=pl.ANY), pl.BlockSpec(memory_space=pltpu.VMEM)
    shape = jax.ShapeDtypeStruct
    wide = pltpu.VMEM((4, tokens, feats), BF16)
    late = (*weights, *tables[:2])
    kept = [
        shape((tokens, width), F32),
        shape((tokens, q_width), BF16),
        shape((tokens, k_width), BF16),
        shape((tokens, k_width), BF16),
        shape((q_heads, tokens, tokens), BF16),
    ]
    dact = shape((4, tokens // 4, ff), F32)
    return pl.pallas_call(
        functools.partial(front_kernel, pairs, q_heads, groups, model_width),
        out_shape=(
            shape((tokens, 1), F32),
            shape((tokens, feats), F32),
            shape((tokens, 1), F32),
            shape((tokens, feats), BF16),
            *kept,
            dact,
            shape((4, tokens, feats), BF16),
            shape((4, tokens, feats), BF16),
            shape((4, tokens, q_width), BF16),
            shape((2, 4, *ffn_weights[0].shape), BF16),
        ),
        in_specs=[vmem] * 6 + [any_spec] * 10,
        out_specs=tuple([vmem] * 4 + [any_spec] * 10),
        scratch_shapes=[held(array) for array in late]
        + [held(array) for array in kept]
        + [
            held(dact),
            wide,
            pltpu.VMEM((4, 8, tokens), F32),
            wide,
            wide,
            pltpu.VMEM((4, tokens, q_width), BF16),
            pltpu.VMEM((tokens, q_width), BF16),
            pltpu.VMEM((tokens, width), F32),
            pltpu.VMEM((tokens, 512), F32),
            pltpu.VMEM((tokens // 4, ff), F32),
        ]
        + row_total_scratch(tokens) * 2
        + row_sum_scratch(tokens, width)
        + [pltpu.VMEM((4, tokens // 4, ff), BF16)] * 5
        + chain_scratch(tokens, feats)
        + col_gather_sems() * 2
        + [dma((3,))]
        + row_sum_sems()
        + [dma((2, 4)), dma((2, 4)), dma((4,)), dma((4,))]
        + [dma((2,))] * 7
        + chain_sems()
        + row_total_sems() * 2
        + weight_gather_sems(pairs)
        + [dma((8,)), dma((5,)), dma((4,)), dma((3,)), dma((4,))],
        compiler_params=pltpu.CompilerParams(
            collective_id=number, has_side_effects=True, vmem_limit_bytes=VMEM_LIMIT
        ),
        name="front",
    )(x, segments, *tables[2:], *gains, gy, *late, *ffn_weights)


def across_rows(left, right):
    return lax.dot_general(left, right, (((0,), (0,)), ((), ())), preferred_element_type=F32)


def attend_back(
    q_heads, groups, grad, qkv, qa, ka, va, probs, cos, sin, q_gain, k_gain, out, q_part, k_part, dq, dk, dv, done
):
    kv = q_heads // groups
    tokens = qkv.shape[0]
    half = tokens // 2
    scale = 1.0 / math.sqrt(HEAD_SIZE)
    dk[...] = jnp.zeros_like(dk)
    dv[...] = jnp.zeros_like(dv)
    q_part[...] = jnp.zeros_like(q_part)
    k_part[...] = jnp.zeros_like(k_part)

    def back(turned, index, gain, rows):
        raw = head(qkv, index)[rows]
        scales = root_scale(raw)
        normed = turned * cos[rows, :] - swap_halves(turned) * sin[rows, :]
        part = jnp.sum(normed * raw * scales, axis=0, keepdims=True)
        weighted = normed * gain[...]
        inner = jnp.sum(weighted * raw, axis=1, keepdims=True)
        result = scales * weighted - raw * (scales * scales * scales) * inner * (1.0 / HEAD_SIZE)
        out[rows, index * HEAD_SIZE : (index + 1) * HEAD_SIZE] = result.astype(BF16)
        return part

    for block in (1, 0):
        rows = slice(block * half, (block + 1) * half)
        keys = (block + 1) * half
        for i in range(q_heads):
            j = i // groups
            spot = slice(j * HEAD_SIZE, (j + 1) * HEAD_SIZE)
            pb = probs[i, rows, :keys]
            p = pb.astype(F32)
            g = head(grad, i)[rows].astype(BF16)
            dv[:keys, spot] += across_rows(pb, g)
            dp = lax.dot_general(
                g, head(va, j)[:keys], (((1,), (1,)), ((), ())), preferred_element_type=F32
            )
            ds = (p * (dp - jnp.sum(p * dp, axis=1, keepdims=True))).astype(BF16)
            dq[rows, i * HEAD_SIZE : (i + 1) * HEAD_SIZE] = (
                jnp.dot(ds, head(ka, j)[:keys], preferred_element_type=F32) * scale
            )
            dk[:keys, spot] += across_rows(ds, head(qa, i)[rows]) * scale
        q_part[...] += sum(back(head(dq, i)[rows], i, q_gain, rows) for i in range(q_heads))
        k_part[...] += sum(back(head(dk, i)[rows], q_heads + i, k_gain, rows) for i in range(kv))
        for i in range(kv):
            spot = (q_heads + kv + i) * HEAD_SIZE
            out[rows, spot : spot + HEAD_SIZE] = head(dv, i)[rows].astype(BF16)
        done(block)


def act_copy(src, dst, at, j, sem):
    s = far_first(at.col, j)
    if j < 1:
        return pltpu.make_async_copy(src.at[s], dst.at[s], sem)
    return pltpu.make_async_copy(src.at[s, at.row], dst.at[s, at.row], sem)


def weight_grad(out, left, right, send=None):
    def block(here):
        total = None
        for s in range(4):
            term = across_rows(left(s, here), right(s))
            total = term if total is None else total + term
        out[here, :] = total.astype(BF16)
        if send is not None:
            send(here).start()

    in_rows(out.shape[0], 256, block)


def middle_kernel(pairs, *refs):
    refs = list(refs)

    def take(count):
        found = refs[:count]
        del refs[:count]
        return found

    (hn, w_gate, w_up, dact_in, full) = take(5)
    (dhn, act_out, gate_n, up_n) = take(4)
    others = take(1) if pairs == 2 else []
    (hn_wide, hn_full, weights, dact, gate_up, gate_wide, up_wide, act_wide, n_gate, n_up) = take(10)
    chain = take(3)
    hn_sems = take(2)
    (full_sem, share_send, share_recv) = take(3)
    gate_sems, up_sems, act_sems = take(6), take(6), take(6)
    chain_sems_ = take(3)
    (local, y_send, y_recv) = take(3)

    at = Ends()
    ff = w_gate.shape[1]
    quarter = hn.shape[0] // 4
    gather = ColGather(at, hn_wide, *hn_sems)
    loads = [pltpu.make_async_copy(dact_in, dact, full_sem.at[2, 0])]
    for which, own in enumerate((w_gate, w_up)):
        for i, r in enumerate((at.mate, at.across, at.diag, at.row)):
            src = own if i == 3 else full.at[which, r]
            loads.append(pltpu.make_async_copy(src, weights.at[which, r], full_sem.at[which, i]))
    for load in loads:
        load.start()
    gates = RowGather(at, lambda s: gate_wide.at[s, at.row], lambda s, q: gate_wide.at[s, q], gate_sems)
    ups = RowGather(at, lambda s: up_wide.at[s, at.row], lambda s, q: up_wide.at[s, q], up_sems)
    acts = RowGather(at, lambda s: act_wide.at[s, at.row], lambda s, q: act_wide.at[s, q], act_sems)
    back_sum = ColSum(at, dhn, *chain, *chain_sems_)

    hn_wide[at.col] = hn[...]
    at.greet(pairs if pairs == 2 else 0)

    peers = (at.mate, at.across, at.diag)

    def share(s):
        hn_full[s, at.row] = hn_wide[s, pl.ds(pl.multiple_of(at.row * quarter, quarter), quarter)]
        for i, peer in enumerate(peers):
            theirs = hn_wide.at[s, pl.ds(pl.multiple_of(peer * quarter, quarter), quarter)]
            remote(theirs, hn_full.at[s, at.row], share_send.at[s, i], share_recv.at[s, i], row=peer).start()

    def hidden_units(s):
        for i, peer in enumerate(peers):
            here = hn_full.at[s, peer]
            remote(here, here, share_send.at[s, i], share_recv.at[s, i], row=peer).wait_recv()
        size = gate_up.shape[2]

        def some(j, _):
            cols = pl.ds(pl.multiple_of(j * size, size), size)
            for which in range(2):
                total = None
                for r in range(4):
                    term = jnp.dot(hn_full[s, r], weights[which, r, :, cols], preferred_element_type=F32)
                    total = term if total is None else total + term
                gate_up[which] = total

            def one(here):
                gate, up = gate_up[0, here], gate_up[1, here]
                grad = dact[s, here, cols]
                sigmoid = jax.nn.sigmoid(gate)
                silu = gate * sigmoid
                act_wide[s, at.row, here, cols] = (silu * up).astype(BF16)
                gate_wide[s, at.row, here, cols] = (
                    grad * up * (sigmoid * (1.0 + gate * (1.0 - sigmoid)))
                ).astype(BF16)
                up_wide[s, at.row, here, cols] = (grad * silu).astype(BF16)

            in_rows(quarter, 16, one)
            return 0

        lax.fori_loop(0, ff // size, some, 0)
        gates.to_across(s).start()
        gates.near(s)
        ups.near(s)

    def close_share(s):
        for i, peer in enumerate(peers):
            here = hn_full.at[s, peer]
            remote(here, here, share_send.at[s, i], share_recv.at[s, i], row=peer).wait_send()

    def rows_of(ref, s):
        return ref[s].reshape(4 * quarter, ff)

    def back(j):
        s = far_first(at.col, j)
        contract = (((1,), (1,)), ((), ()))
        dhn[...] = lax.dot_general(
            rows_of(gate_wide, s), weights[0, at.row], contract, preferred_element_type=F32
        ) + lax.dot_general(rows_of(up_wide, s), weights[1, at.row], contract, preferred_element_type=F32)

    def arrive(some, j):
        s = far_first(at.col, j)
        some.wait_near(s)
        some.take_across(s)
        some.wait_diag(s)

    def left(s, here):
        return hn_wide[s, :, here]

    mid = jnp.logical_not(at.end)
    gather.arrive(0)
    gather.loop(0, share)
    for load in loads:
        load.wait()
    gather.loop(0, hidden_units)
    gather.arrive(1)
    gather.loop(1, share)
    gather.arrive(2)
    gather.loop(2, share)
    gather.loop(1, hidden_units)
    gather.arrive(3)
    gather.loop(3, share)
    gather.loop(2, hidden_units)
    gather.loop(3, hidden_units)
    for j in range(4):
        ups.to_across(far_first(at.col, j)).start()
    acts.near(far_first(at.col, 0))
    acts.to_across(far_first(at.col, 0)).start()
    keep_acts = [
        act_copy(act_wide, act_out, at, j, local.at[2 + j]) for j in range(4)
    ]
    for copy in keep_acts[1:]:
        copy.start()
    for j in range(4):
        arrive(gates, j)

    def to_other(here=slice(None)):
        return remote(n_gate.at[here], others[0].at[here], y_send.at[0], y_recv.at[0], dp=at.pair(2, 1))

    weight_grad(n_gate, left, lambda s: rows_of(gate_wide, s), to_other if pairs == 2 else None)
    keep_gate = pltpu.make_async_copy(n_gate, gate_n, local.at[0])
    keep_gate.start()
    arrive(ups, 0)
    for j in range(3):
        back(j)
        pl.when(at.end)(lambda: back_sum.step(far_first(at.col, j)))
        arrive(ups, j + 1)
        pl.when(mid)(lambda: back_sum.step(far_first(at.col, j)))
    weight_grad(n_up, left, lambda s: rows_of(up_wide, s))
    keep_up = pltpu.make_async_copy(n_up, up_n, local.at[1])
    keep_up.start()
    back(3)
    arrive(acts, 0)
    keep_acts[0].start()
    back_sum.step(at.col)

    gather.close()
    for dist in range(4):
        gather.loop(dist, close_share)
    gates.close(4)
    ups.close(4)
    acts.close_one(far_first(at.col, 0))
    back_sum.close()
    for copy in keep_acts:
        copy.wait()
    keep_gate.wait()
    keep_up.wait()
    if pairs == 2:
        to_other().wait()


def middle(pairs, number, hn, w_gate, w_up, dact, full):
    tokens, feats = hn.shape
    ff = w_gate.shape[1]
    quarter = tokens // 4
    dma = pltpu.SemaphoreType.DMA
    any_spec, vmem = pl.BlockSpec(memory_space=pl.ANY), pl.BlockSpec(memory_space=pltpu.VMEM)
    shape = jax.ShapeDtypeStruct
    narrow = shape((feats, ff), BF16)
    others = 1 if pairs == 2 else 0
    out = pl.pallas_call(
        functools.partial(middle_kernel, pairs),
        out_shape=tuple(
            [shape((tokens, feats), F32), shape((4, 4, quarter, ff), BF16), narrow, narrow] + [narrow] * others
        ),
        in_specs=[vmem] + [any_spec] * 4,
        out_specs=tuple([vmem] + [any_spec] * (3 + others)),
        scratch_shapes=[
            pltpu.VMEM((4, tokens, feats), BF16),
            pltpu.VMEM((4, 4, quarter, feats), BF16),
            pltpu.VMEM((2, 4, feats, ff), BF16),
            held(dact),
            pltpu.VMEM((2, quarter, 512), F32),
            pltpu.VMEM((4, 4, quarter, ff), BF16),
            pltpu.VMEM((4, 4, quarter, ff), BF16),
            pltpu.VMEM((4, 4, quarter, ff), BF16),
            pltpu.VMEM((feats, ff), BF16),
            pltpu.VMEM((feats, ff), BF16),
        ]
        + chain_scratch(tokens, feats)
        + col_gather_sems()
        + [dma((3, 4)), dma((4, 3)), dma((4, 3))]
        + [dma((4,))] * 18
        + chain_sems()
        + [dma((6,)), dma((1,)), dma((1,))],
        compiler_params=pltpu.CompilerParams(
            collective_id=number, has_side_effects=True, vmem_limit_bytes=VMEM_LIMIT
        ),
        name="middle",
    )(hn, w_gate, w_up, dact, full)
    return out[:4], out[4:]


def tail_kernel(pairs, q_heads, groups, *refs):
    refs = list(refs)

    def take(count):
        found = refs[:count]
        del refs[:count]
        return found

    (w_out, q_gain, k_gain, dhn, hidden, scale_two, gain_two, gy, x_ref, scale_one, gain_one) = take(11)
    late = take(12)
    (gy_wide, mixed_wide, normed_wide, up_n) = take(4)
    (in_grad, layer_out, one_grad, two_grad, q_grad, k_grad) = take(6)
    kept_out = take(5)
    others = take(6) if pairs == 2 else []
    (w_down, w_query, w_key, w_value, qkv, qa, ka, va, probs, cos, sin) = late_held = take(11)
    (da_wide, act_wide, dqkv, dqkv_wide, held_wide, product, grad_mixed, dq, dk, dv, *narrow) = take(15)
    (dh, q_part, k_part, packet, packet_got, by_row, summed) = take(7)
    first_bufs, last_bufs = take(2), take(2)
    moved = take(5)
    down_bufs, dxn_bufs = take(3), take(3)
    (g_send, g_recv, local, y_send, y_recv, late_sems) = take(6)
    moved_sems = take(4)
    act_sems, dqkv_sems = take(6), take(7)
    down_sems, dxn_sems = take(3), take(3)
    first_sems, last_sems = take(2), take(2)
    (p_send, p_recv, r_send, r_recv) = take(4)

    at = Ends()
    feats = dhn.shape[1]
    model_width = 4 * feats
    gain_spot = pl.ds(pl.multiple_of(at.row * feats, feats), feats)
    fetch_acts = [act_copy(late[0], act_wide, at, j, local.at[8 + j]) for j in range(4)]
    for copy in reversed(fetch_acts):
        copy.start()
    fetch = Fetch(list(zip(late[1:], late_held)), late_sems)
    fetch.start()
    first_total = RowTotal(at, *first_bufs, *first_sems)
    last_total = RowTotal(at, *last_bufs, *last_sems)
    at.greet(pairs, True, True)

    def pair_copy(index, here=slice(None)):
        return remote(
            narrow[index].at[here], others[index].at[here], y_send.at[index], y_recv.at[index],
            dp=1 - lax.axis_index("dp"),
        )

    n_down, n_out, n_query, n_key, n_value = narrow
    narrow = [up_n, *narrow]

    def to_pair(index):
        return functools.partial(pair_copy, index) if pairs == 2 else None

    def load(index, src):
        return pltpu.make_async_copy(src, held_wide, local.at[index])

    def keep(index):
        return pltpu.make_async_copy(narrow[index], kept_out[index - 1], local.at[2 + index])

    if pairs == 2:
        pair_copy(0).start()
    load(0, gy_wide).start()
    gather = ColGather(at, da_wide, g_send, g_recv)
    row_sum = RowSumWhole(at, product, grad_mixed, *moved, *moved_sems)
    acts = RowGather(at, lambda s: late[0].at[s, at.row], lambda s, q: act_wide.at[s, q], act_sems)
    half = dqkv.shape[0] // 2
    grads = RowGather(
        at, lambda h: dqkv.at[pl.ds(h * half, half)], lambda h, q: dqkv_wide.at[q, pl.ds(h * half, half)], dqkv_sems
    )
    down_sum = ColSum(at, product, *down_bufs, *down_sems)
    dxn_sum = ColSum(at, product, *dxn_bufs, *dxn_sems)

    weighted = dhn[...] * gain_two[:, gain_spot]
    first_total.start(jnp.sum(weighted * hidden[...], axis=1, keepdims=True))
    for j in range(1, 4):
        acts.to_across(far_first(at.col, j)).start()
        acts.near(far_first(at.col, j))
    scale = scale_two[...]
    packet[...] = jnp.zeros_like(packet)
    packet[1:2, :] = jnp.sum(dhn[...] * hidden[...] * scale, axis=0, keepdims=True)
    inner = first_total.finish()
    dh[...] = (
        gy[...].astype(F32)
        + scale * (dhn[...] * gain_two[:, gain_spot])
        - hidden[...] * (scale * scale * scale * inner * (1.0 / model_width))
    )
    da_wide[at.col] = dh[...].astype(BF16)
    gather.arrive(0)
    for copy in reversed(fetch_acts):
        copy.wait()

    def back_out(s):
        product[...] = lax.dot_general(
            da_wide[s], w_out[...], (((1,), (1,)), ((), ())), preferred_element_type=F32
        )
        row_sum.give(s)

    def take_act(j):
        s = far_first(at.col, j)
        acts.wait_near(s)
        acts.take_across(s)
        acts.wait_diag(s)

    def act_rows(s, cols):
        return act_wide[s, :, :, cols].reshape(product.shape[0], cols.size)

    def down_step(j):
        s = far_first(at.col, j)
        product[...] = jnp.dot(
            act_rows(s, pl.ds(0, act_wide.shape[3])), w_down[...], preferred_element_type=F32
        )
        down_sum.step(s)

    def dxn_step(j, halves=(1, 0)):
        s = near_first(at, j)
        for h in halves:
            rows = pl.ds(h * half, half)
            total, base = None, 0
            for w in (w_query, w_key, w_value):
                size = w.shape[1]
                term = lax.dot_general(
                    dqkv_wide[s, rows, pl.ds(base, size)], w[...], (((1,), (1,)), ((), ())),
                    preferred_element_type=F32,
                )
                total = term if total is None else total + term
                base += size
            product[rows, :] = total
        dxn_sum.step(s, halves)

    def down_weight():
        load(0, gy_wide).wait()
        weight_grad(n_down, act_rows, lambda s: held_wide[s], to_pair(1))
        keep(1).start()
        load(1, mixed_wide).start()

    mid = jnp.logical_not(at.end)
    fetch.wait()
    gather.loop(0, back_out)
    gather.arrive(1)
    gather.loop(1, back_out)
    pl.when(at.end)(lambda: down_step(0))
    gather.arrive(2)
    gather.loop(2, back_out)
    pl.when(mid)(lambda: down_step(0))
    take_act(1)
    pl.when(at.end)(lambda: down_step(1))
    take_act(2)
    take_act(3)
    pl.when(at.end)(lambda: down_step(2))
    down_weight()
    pl.when(mid)(lambda: down_step(1))
    gather.arrive(3)
    gather.loop(3, back_out)
    row_sum.finish()

    def send_grads(h):
        grads.to_across(h).start()
        grads.near(h)

    attend_back(
        q_heads, groups, grad_mixed, qkv, qa, ka, va, probs, cos, sin, q_gain, k_gain,
        dqkv, q_part, k_part, dq, dk, dv, send_grads,
    )
    for h in range(2):
        grads.wait_near(h)

    @pl.when(at.end)
    def _():
        dxn_step(0)
        pl.when(jnp.logical_not(at.paired))(lambda: dxn_step(1))

    @pl.when(mid)
    def _():
        down_step(2)

    load(1, mixed_wide).wait()
    weight_grad(n_out, lambda s, here: held_wide[s, :, here], lambda s: da_wide[s], to_pair(2))
    keep(2).start()
    load(2, normed_wide).start()
    paired = mid & at.paired
    unpaired = mid & jnp.logical_not(at.paired)
    pl.when(unpaired)(lambda: dxn_step(0))
    grads.take_across(1)
    grads.wait_diag(1)

    @pl.when(at.end)
    def _():
        pl.when(at.paired)(lambda: dxn_step(1, (1,)))
        dxn_step(2, (1,))

    @pl.when(paired)
    def _():
        dxn_step(1, (1,))
        dxn_step(0, (1,))

    pl.when(unpaired)(lambda: dxn_step(1, (1,)))
    grads.take_across(0)
    grads.wait_diag(0)

    @pl.when(at.end)
    def _():
        pl.when(at.paired)(lambda: dxn_step(1, (0,)))
        dxn_step(2, (0,))

    pl.when(unpaired)(lambda: dxn_step(1, (0,)))
    load(2, normed_wide).wait()
    base = 0
    for index, some in ((3, n_query), (4, n_key), (5, n_value)):
        spot = pl.ds(base, some.shape[1])
        weight_grad(
            some, lambda s, here: held_wide[s, :, here], lambda s, spot=spot: dqkv_wide[s, :, spot], to_pair(index)
        )
        keep(index).start()
        base += some.shape[1]

    @pl.when(paired)
    def _():
        dxn_step(2, (1,))
        dxn_step(0, (0,))

    @pl.when(paired)
    def _():
        dxn_step(1, (0,))
        dxn_step(2, (0,))

    pl.when(unpaired)(lambda: dxn_step(2))
    down_step(3)
    layer_out[...] = (hidden[...] + product[...]).astype(BF16)
    dxn_step(3)
    scale = scale_one[...]
    last_total.start(
        jnp.sum(product[...] * gain_one[:, gain_spot] * x_ref[...].astype(F32), axis=1, keepdims=True)
    )
    packet[0:1, :] = jnp.sum(product[...] * x_ref[...].astype(F32) * scale, axis=0, keepdims=True)
    packet[2:3, :HEAD_SIZE] = q_part[...]
    packet[2:3, HEAD_SIZE : 2 * HEAD_SIZE] = k_part[...]

    def to_line(step):
        return remote(
            packet, packet_got.at[step - 1], p_send.at[step - 1], p_recv.at[step - 1],
            col=lax.rem(at.col + step, 4),
        )

    def to_group(index, row, step):
        where = dict(row=row) if step == 0 else dict(row=row, dp=at.pair(pairs, step))
        return remote(summed, by_row.at[step, at.row], r_send.at[index], r_recv.at[step, at.row], **where)

    def from_group(index, row, step):
        here = by_row.at[step, row]
        return remote(summed, here, r_send.at[index], r_recv.at[step, row], row=at.mate)

    group = [(row, 0) for row in (at.mate, at.across, at.diag)]
    group += [(row, step) for step in range(1, pairs) for row in range(4)]
    for step in range(1, 4):
        to_line(step).start()
    for step in range(1, 4):
        to_line(step).wait()
    summed[...] = (packet[...] + packet_got[0]) + (packet_got[1] + packet_got[2])
    by_row[0, at.row] = summed[...]
    for index, (row, step) in enumerate(group):
        to_group(index, row, step).start()
    inner = last_total.finish()
    in_grad[...] = (
        dh[...]
        + scale * (product[...] * gain_one[:, gain_spot])
        - x_ref[...].astype(F32) * (scale * scale * scale * inner * (1.0 / model_width))
    )
    for index, (row, step) in enumerate(group):
        from_group(index, row, step).wait_recv()
        to_group(index, row, step).wait_send()
    total = by_row[0]
    for step in range(1, pairs):
        total = total + by_row[step]
    for r in range(4):
        one_grad[:, r * feats : (r + 1) * feats] = total[r, 0:1, :]
        two_grad[:, r * feats : (r + 1) * feats] = total[r, 1:2, :]
    heads = (total[0, 2:3, :] + total[1, 2:3, :]) + (total[2, 2:3, :] + total[3, 2:3, :])
    q_grad[...] = heads[:, :HEAD_SIZE]
    k_grad[...] = heads[:, HEAD_SIZE : 2 * HEAD_SIZE]

    gather.close()
    row_sum.close()
    for j in range(1, 4):
        acts.close_one(far_first(at.col, j))
    grads.close(2)
    down_sum.close()
    dxn_sum.close()
    for index in range(1, 6):
        keep(index).wait()
    if pairs == 2:
        for index in range(6):
            pair_copy(index).wait()


def tail(pairs, q_heads, groups, number, act, weights, saved, tables, norms, wides, narrow):
    tokens, feats = norms[0].shape
    w_out, w_down, w_query, w_key, _ = weights
    ff = w_down.shape[0]
    width = saved[0].shape[1]
    q_width, k_width = saved[1].shape[1], saved[2].shape[1]
    dma = pltpu.SemaphoreType.DMA
    any_spec, vmem = pl.BlockSpec(memory_space=pl.ANY), pl.BlockSpec(memory_space=pltpu.VMEM)
    shape = jax.ShapeDtypeStruct
    shapes = [
        shape((tokens, feats), F32),
        shape((tokens, feats), BF16),
        shape((1, 4 * feats), F32),
        shape((1, 4 * feats), F32),
        shape((1, HEAD_SIZE), F32),
        shape((1, HEAD_SIZE), F32),
    ]
    own = [
        shape((ff, feats), BF16),
        shape((q_width, feats), BF16),
        shape((feats, q_width), BF16),
        shape((feats, k_width), BF16),
        shape((feats, k_width), BF16),
    ]
    others = [shape(n.shape, BF16) for n in narrow] + own if pairs == 2 else []
    packet = pltpu.VMEM((8, feats), F32)
    early = (w_out, *tables[2:], *norms)
    late = (act, *weights[1:], *saved, *tables[:2])
    out = pl.pallas_call(
        functools.partial(tail_kernel, pairs, q_heads, groups),
        out_shape=tuple(shapes + own + others),
        in_specs=[vmem] * len(early) + [any_spec] * (len(late) + 4),
        out_specs=tuple([vmem] * 6 + [any_spec] * (5 + len(others))),
        scratch_shapes=[held(array) for array in late[1:]]
        + [
            pltpu.VMEM((4, tokens, feats), BF16),
            pltpu.VMEM((4, 4, tokens // 4, ff), BF16),
            pltpu.VMEM((tokens, width), BF16),
            pltpu.VMEM((4, tokens, width), BF16),
            pltpu.VMEM((4, tokens, feats), BF16),
            pltpu.VMEM((tokens, feats), F32),
            pltpu.VMEM((tokens, q_width), F32),
            pltpu.VMEM((tokens, q_width), F32),
            pltpu.VMEM((tokens, k_width), F32),
            pltpu.VMEM((tokens, k_width), F32),
        ]
        + [held(array) for array in own]
        + [
            pltpu.VMEM((tokens, feats), F32),
            pltpu.VMEM((1, HEAD_SIZE), F32),
            pltpu.VMEM((1, HEAD_SIZE), F32),
            packet,
            pltpu.VMEM((3, 8, feats), F32),
            pltpu.VMEM((pairs, 4, 8, feats), F32),
            packet,
        ]
        + row_total_scratch(tokens) * 2
        + row_sum_scratch(tokens, q_width)
        + chain_scratch(tokens, feats) * 2
        + col_gather_sems()
        + [dma((12,)), dma((6,)), dma((6,)), dma((12,))]
        + row_sum_sems()
        + [dma((4,))] * 6
        + [dma((2,))] * 7
        + chain_sems() * 2
        + row_total_sems() * 2
        + [dma((3,)), dma((3,)), dma((4 * pairs - 1,)), dma((pairs, 4))],
        compiler_params=pltpu.CompilerParams(
            collective_id=number, has_side_effects=True, vmem_limit_bytes=VMEM_LIMIT
        ),
        name="tail",
    )(*early, *late, *wides, *narrow)
    return out[:6], out[6:11], out[11:]


def finish_kernel(count, *refs):
    parts, others, rest = refs[:count], refs[count : 2 * count], refs[2 * count :]
    kept = len(rest) - count
    for a, b, out in zip(parts, others, rest[kept // 2 :]):
        out[...] = a[...].astype(F32) + b[...].astype(F32)
    for src, dst in zip(rest[: kept // 2], rest[kept // 2 + count :]):
        dst[...] = src[...]


def finish(parts, others, rest, steps=4):
    def spec(array):
        block = (array.shape[0] // steps, array.shape[1]) if array.shape[0] % steps == 0 else array.shape
        index = (lambda i: (i, 0)) if block != array.shape else (lambda i: (0, 0))
        return pl.BlockSpec(block, index)

    outs = [jax.ShapeDtypeStruct(a.shape, F32) for a in parts] + [jax.ShapeDtypeStruct(a.shape, a.dtype) for a in rest]
    operands = (*parts, *others, *rest)
    out = pl.pallas_call(
        functools.partial(finish_kernel, len(parts)),
        grid=(steps,),
        out_shape=tuple(outs),
        in_specs=[spec(a) for a in operands],
        out_specs=tuple(spec(a) for a in outs),
        compiler_params=pltpu.CompilerParams(vmem_limit_bytes=VMEM_LIMIT),
        name="finish",
    )(*operands)
    return out[: len(parts)], out[len(parts) :]


def shards(
    pairs,
    hidden_in,
    segment_ids,
    attn_gain,
    w_query,
    key_projection,
    value_projection,
    query_gain,
    key_norm_gain,
    w_out,
    ffn_gain,
    w_gate,
    w_up,
    w_down,
    out_grad,
):
    tokens = hidden_in.shape[0]
    model_width = attn_gain.shape[0]
    q_width = w_query.shape[1]
    k_width = key_projection.shape[1]
    q_heads = q_width // HEAD_SIZE
    groups = q_width // k_width
    tables = (*turn_tables(tokens), query_gain[None, :], key_norm_gain[None, :])
    (scale_one, hidden, scale_two, ffn_in, qkv, q_turned, k_turned, values, probs, grad_inner, xn_wide, gy_wide, mixed_wide, full) = front(
        pairs, q_heads, groups, model_width, 0, hidden_in, out_grad,
        (w_query, key_projection, value_projection, w_out, w_down),
        segment_ids[None, :],
        tables,
        (attn_gain[None, :], ffn_gain[None, :]),
        (w_gate, w_up),
    )
    (grad_ffn_in, inner_act, gate_n, up_n), other_gate = middle(pairs, 1, ffn_in, w_gate, w_up, grad_inner, full)
    (in_grad, layer_out, one_grad, two_grad, q_gain_grad, k_gain_grad), own, others = tail(
        pairs, q_heads, groups, 2, inner_act,
        (w_out, w_down, w_query, key_projection, value_projection),
        (qkv, q_turned, k_turned, values, probs),
        tables,
        (grad_ffn_in, hidden, scale_two, ffn_gain[None, :], out_grad, hidden_in, scale_one, attn_gain[None, :]),
        (gy_wide, mixed_wide, xn_wide),
        (up_n,),
    )
    parts = (gate_n, up_n, *own)
    if pairs == 2:
        rest = (in_grad, layer_out, one_grad, two_grad, q_gain_grad, k_gain_grad)
        sums, rest = finish(parts, (*other_gate, *others), rest)
        in_grad, layer_out, one_grad, two_grad, q_gain_grad, k_gain_grad = rest
    else:
        sums = lax.psum(tuple(part.astype(F32) for part in parts), "dp")
    gate_grad, up_grad, down_grad, out_weight_grad, query_grad, key_grad, value_grad = sums
    return (
        layer_out,
        in_grad,
        one_grad.reshape(-1),
        query_grad,
        key_grad,
        value_grad,
        q_gain_grad.reshape(-1),
        k_gain_grad.reshape(-1),
        out_weight_grad,
        two_grad.reshape(-1),
        gate_grad,
        up_grad,
        down_grad,
    )


def solution(mesh):
    acts, grid, flip, none = P(("dp", "col"), "row"), P("row", "col"), P("col", "row"), P()
    return jax.shard_map(
        functools.partial(shards, mesh.shape["dp"]),
        mesh=mesh,
        in_specs=(
            acts, P(("dp", "row")), none, grid, grid, grid, none, none, flip, none, grid, grid, flip, acts,
        ),
        out_specs=(
            acts, acts, none, grid, grid, grid, none, none, flip, none, grid, grid, flip,
        ),
        check_vma=False,
    )
```

```python
import functools
import math

import jax
import jax.numpy as jnp
import numpy as np
from jax import lax
from jax.experimental import pallas as pl
from jax.experimental.pallas import tpu as pltpu
from jax.sharding import PartitionSpec as P

HEAD_SIZE = 128
EPSILON = 1e-06
THETA = 1000000.0
MASKED = -1e30
MESH = pl.DeviceIdType.MESH
BF16 = jnp.bfloat16
F32 = jnp.float32
VMEM_LIMIT = 60 << 20


def to(**where):
    return dict(device_id=where, device_id_type=MESH)


class Ends:
    def __init__(self):
        self.row = lax.axis_index("row")
        self.col = lax.axis_index("col")
        self.chip = lax.div(self.row, 2)
        self.core = lax.rem(self.row, 2)
        self.mate = self.chip * 2 + (1 - self.core)
        self.across = (1 - self.chip) * 2 + self.core
        self.diag = (1 - self.chip) * 2 + (1 - self.core)
        self.end = (self.col == 0) | (self.col == 3)
        self.paired = lax.div(self.col, 2) == self.chip
        self.above = jnp.minimum(self.col + 1, 3)
        self.below = jnp.maximum(self.col - 1, 0)

    def greet(self, pairs=0, line=False, rows=False):
        gate = pltpu.get_barrier_semaphore()
        count = 3
        for peer in (self.mate, self.across, self.diag):
            pl.semaphore_signal(gate, inc=1, **to(row=peer))
        for step in range(1, pairs):
            dp = self.pair(pairs, step)
            for row in range(4) if rows else (self.row,):
                pl.semaphore_signal(gate, inc=1, **to(dp=dp, row=row))
                count += 1
        if line:
            for step in range(1, 4):
                pl.semaphore_signal(gate, inc=1, **to(col=lax.rem(self.col + step, 4)))
                count += 1
        else:

            @pl.when(self.col > 0)
            def _():
                pl.semaphore_signal(gate, inc=1, **to(col=self.col - 1))

            @pl.when(self.col < 3)
            def _():
                pl.semaphore_signal(gate, inc=1, **to(col=self.col + 1))

            count += jnp.where(self.col > 0, 1, 0) + jnp.where(self.col < 3, 1, 0)
        pl.semaphore_wait(gate, count)

    def pair(self, pairs, step):
        return lax.rem(lax.axis_index("dp") + step, pairs)


class RowTotal:
    def __init__(self, at, own, got, sends, recvs):
        self.own, self.got = own, got
        self.copies = [
            remote(own, got.at[i], sends.at[i], recvs.at[i], row=peer)
            for i, peer in enumerate((at.mate, at.across, at.diag))
        ]

    def start(self, column):
        self.own[...] = jnp.broadcast_to(column, (column.shape[0], 128)).T[:8, :]
        for copy in self.copies:
            copy.start()

    def total(self):
        for copy in self.copies:
            copy.wait()
        return (self.own[...] + self.got[0]) + (self.got[1] + self.got[2])

    def finish(self):
        return as_column(self.total())


def as_column(lines):
    return jnp.concatenate([lines] * 16, axis=0).T[:, :1]


class LineShare:
    def __init__(self, at, blocks, sends, recvs):
        self.at, self.blocks, self.sends, self.recvs = at, blocks, sends, recvs

    def copy(self, s, step):
        here = self.blocks.at[s]
        col = lax.rem(self.at.col + step, 4)
        return remote(here, here, self.sends.at[step - 1], self.recvs.at[s], col=col)

    def start(self):
        for step in range(1, 4):
            self.copy(self.at.col, step).start()

    def wait(self, s):
        pl.when(s != self.at.col)(lambda: self.copy(s, 1).wait_recv())

    def close(self):
        for step in range(1, 4):
            self.copy(self.at.col, step).wait_send()


def row_total_scratch(tokens):
    return [pltpu.VMEM((8, tokens), F32), pltpu.VMEM((3, 8, tokens), F32)]


def row_total_sems():
    return [pltpu.SemaphoreType.DMA((3,)), pltpu.SemaphoreType.DMA((3,))]


def remote(src, dst, sends, recvs, **where):
    return pltpu.make_async_remote_copy(
        src_ref=src, dst_ref=dst, send_sem=sends, recv_sem=recvs, **to(**where)
    )


class Fetch:
    def __init__(self, pairs, sems):
        self.copies = [
            pltpu.make_async_copy(src, dst, sems.at[i]) for i, (src, dst) in enumerate(pairs)
        ]

    def start(self):
        for copy in self.copies:
            copy.start()

    def wait(self, first=0, last=None):
        for copy in self.copies[first:last]:
            copy.wait()


def held(array):
    return pltpu.VMEM(array.shape, array.dtype)


def in_rows(count, step, body, first=0):
    def one(i, _):
        body(pl.ds(pl.multiple_of(first + i * step, step), step))
        return 0

    lax.fori_loop(0, count // step, one, 0)


class ColGather:
    def __init__(self, at, wide, sends, recvs):
        self.at, self.wide, self.sends, self.recvs = at, wide, sends, recvs
        self.half = wide.shape[1] // 2

    def copy(self, s, h, side, col):
        part = self.wide.at[s, pl.ds(h * self.half, self.half)]
        return remote(part, part, self.sends.at[side, s, h], self.recvs.at[s, h], col=col)

    def up(self, s, h):
        return self.copy(s, h, 0, self.at.above)

    def down(self, s, h):
        return self.copy(s, h, 1, self.at.below)

    def loop(self, dist, body):
        if dist == 0:
            body(self.at.col)
            return

        def one(side, _):
            s = jnp.where(side == 0, self.at.col - dist, self.at.col + dist)
            pl.when((s >= 0) & (s <= 3))(lambda: body(s))
            return 0

        lax.fori_loop(0, 2, one, 0)

    def arrive(self, dist):
        for h in range(2):

            def take(s, h=h):
                if dist:
                    self.up(s, h).wait_recv()

                @pl.when((s <= self.at.col) & (self.at.col < 3))
                def _():
                    self.up(s, h).start()

                @pl.when((s >= self.at.col) & (self.at.col > 0))
                def _():
                    self.down(s, h).start()

            self.loop(dist, take)

    def send_up(self):
        for h in range(2):
            self.up(self.at.col, h).start()

    def send_down(self):
        for h in range(2):
            self.down(self.at.col, h).start()

    def close(self):
        def one(s, _):
            for h in range(2):

                @pl.when((s <= self.at.col) & (self.at.col < 3))
                def _():
                    self.up(s, h).wait_send()

                @pl.when((s >= self.at.col) & (self.at.col > 0))
                def _():
                    self.down(s, h).wait_send()

            return 0

        lax.fori_loop(0, 4, one, 0)


class RowSumWhole:
    def __init__(self, at, product, out, a_send, a_recv, c_recv, d_send, d_recv, m_send, m_recv, x_send, x_recv):
        self.at, self.product, self.out = at, product, out
        self.a_send, self.a_recv, self.c_recv, self.d_send, self.d_recv = a_send, a_recv, c_recv, d_send, d_recv
        self.m_send, self.m_recv, self.x_send, self.x_recv = m_send, m_recv, x_send, x_recv
        self.half = product.shape[0] // 2
        self.d = remote(d_send, d_recv, m_send.at[2], m_recv.at[2], row=at.mate)

    def a(self, i):
        return remote(self.a_send.at[i], self.a_recv.at[i], self.m_send.at[i], self.m_recv.at[i], row=self.at.mate)

    def b(self, i, s):
        core = self.at.core
        return remote(self.a_recv.at[i], self.c_recv.at[core], self.x_send.at[i], self.x_recv.at[core], row=s)

    def part(self, core, here):
        return pl.ds(pl.multiple_of(core * self.half + here.start, here.size), here.size)

    def give(self, s):
        at, product, half = self.at, self.product, self.half
        i = lax.rem(s, 2)
        ours = lax.div(s, 2) == at.chip

        @pl.when(jnp.logical_not(ours))
        def _():
            def cast(here):
                self.a_send[i, here] = product[self.part(1 - at.core, here), :].astype(BF16)

            in_rows(half, 64, cast)
            self.a(i).start()
            self.a(i).wait_recv()

            def add(here):
                total = product[self.part(at.core, here), :] + self.a_recv[i, here].astype(F32)
                self.a_recv[i, here] = total.astype(BF16)

            in_rows(half, 64, add)
            self.b(i, s).start()

        @pl.when(ours & (i != at.core))
        def _():
            def cast(here):
                self.d_send[here] = product[here, :].astype(BF16)

            in_rows(2 * half, 64, cast)
            self.d.start()

        @pl.when(s == at.row)
        def _():
            def store(here):
                self.out[here] = product[here, :]

            in_rows(2 * half, 64, store)

    def finish(self):
        self.d.wait_recv()
        for h in range(2):
            here = self.c_recv.at[h]
            remote(here, here, self.x_send.at[h], self.x_recv.at[h], row=self.at.across).wait_recv()

            def add(rows, h=h):
                spot = pl.ds(pl.multiple_of(h * self.half + rows.start, rows.size), rows.size)
                self.out[spot] += self.d_recv[spot].astype(F32) + self.c_recv[h, rows].astype(F32)

            in_rows(self.half, 64, add)

    def close(self):
        self.d.wait_send()
        for i in range(2):
            self.a(i).wait_send()
            self.b(i, self.at.across).wait_send()


def row_sum_scratch(tokens, width):
    half = pltpu.VMEM((2, tokens // 2, width), BF16)
    full = pltpu.VMEM((tokens, width), BF16)
    return [half, half, half, full, full]


def row_sum_sems():
    dma = pltpu.SemaphoreType.DMA
    return [dma((3,)), dma((3,)), dma((2,)), dma((2,))]


class RowSumQuarter:
    def __init__(self, at, chunk, keep, a_send, a_recv, c_recv, d_send, d_recv, m_send, m_recv, x_send, x_recv):
        self.at, self.chunk, self.keep = at, chunk, keep
        self.a_send, self.a_recv, self.c_recv = a_send, a_recv, c_recv
        self.d_send, self.d_recv = d_send, d_recv
        self.sems = (m_send, m_recv, x_send, x_recv)

    def a(self, s):
        m_send, m_recv, _, _ = self.sems
        return remote(self.a_send.at[s], self.a_recv.at[s], m_send.at[0, s], m_recv.at[0, s], row=self.at.mate)

    def d(self, s):
        m_send, m_recv, _, _ = self.sems
        return remote(self.d_send.at[s], self.d_recv.at[s], m_send.at[1, s], m_recv.at[1, s], row=self.at.mate)

    def b(self, s):
        _, _, x_send, x_recv = self.sems
        return remote(self.a_recv.at[s], self.c_recv.at[s], x_send.at[s], x_recv.at[s], row=self.at.across)

    def split(self, s, value, spot, own):
        at, chunk = self.at, self.chunk
        chunk[...] = value

        def quarter(q):
            return chunk[pl.ds(pl.multiple_of(q * 128, 128), 128), :]

        self.a_send[s, :, spot] = quarter(at.diag).astype(BF16)
        self.keep[:, spot] = quarter(at.across)
        self.d_send[s, :, spot] = quarter(at.mate).astype(BF16)
        own[s, :, spot] = quarter(at.row).astype(own.dtype)

    def give(self, s):
        self.a(s).start()
        self.d(s).start()
        self.a(s).wait_recv()

        def one(here):
            self.a_recv[s, here] = (self.keep[here, :] + self.a_recv[s, here].astype(F32)).astype(BF16)

        in_rows(128, 16, one)
        self.b(s).start()

    def finish(self, s):
        self.d(s).wait_recv()
        self.b(s).wait_recv()

    def close(self):
        def one(s, _):
            self.a(s).wait_send()
            self.b(s).wait_send()
            self.d(s).wait_send()
            return 0

        lax.fori_loop(0, 4, one, 0)


class RowGather:
    def __init__(self, at, own, slot, sems):
        self.at, self.own, self.slot = at, own, slot
        self.m_send, self.m_recv, self.x_send, self.x_recv, self.f_send, self.f_recv, self.local = (*sems, None)[:7]

    def to_mate(self, s):
        return remote(self.own(s), self.slot(s, self.at.row), self.m_send.at[s], self.m_recv.at[s], row=self.at.mate)

    def to_across(self, s):
        return remote(self.own(s), self.slot(s, self.at.row), self.x_send.at[s], self.x_recv.at[s], row=self.at.across)

    def pass_on(self, s):
        here = self.slot(s, self.at.across)
        return remote(here, here, self.f_send.at[s], self.f_recv.at[s], row=self.at.mate)

    def move_own(self, s):
        return pltpu.make_async_copy(self.own(s), self.slot(s, self.at.row), self.local.at[s])

    def near(self, s):
        self.to_mate(s).start()
        if self.local is not None:
            self.move_own(s).start()

    def wait_near(self, s):
        here = self.slot(s, self.at.mate)
        remote(here, here, self.m_send.at[s], self.m_recv.at[s], row=self.at.mate).wait_recv()
        if self.local is not None:
            self.move_own(s).wait()

    def take_across(self, s):
        here = self.slot(s, self.at.across)
        remote(here, here, self.x_send.at[s], self.x_recv.at[s], row=self.at.across).wait_recv()
        self.pass_on(s).start()

    def wait_diag(self, s):
        here = self.slot(s, self.at.diag)
        remote(here, here, self.f_send.at[s], self.f_recv.at[s], row=self.at.mate).wait_recv()

    def close_one(self, s):
        self.to_mate(s).wait_send()
        self.to_across(s).wait_send()
        self.pass_on(s).wait_send()

    def close(self, count):
        def one(s, _):
            self.close_one(s)
            return 0

        lax.fori_loop(0, count, one, 0)


class WeightGather:
    def __init__(self, at, pairs, own, full, sems):
        self.at, self.pairs, self.own, self.full = at, pairs, own, full
        self.m_send, self.m_recv, self.x_send, self.x_recv, self.y_send, self.y_recv = sems[:6]
        self.f_send, self.f_recv, self.g_send, self.g_recv = sems[6:]
        self.step = full.shape[2] // 4
        self.mine = lax.axis_index("dp") if pairs == 2 else None

    def rows(self, j):
        return pl.ds(j * self.step, self.step)

    def piece(self, which, row, j):
        return self.full.at[which, row, self.rows(j)]

    def held(self):
        return (self.mine,) if self.pairs == 2 else (0, 1)

    def near(self, which, row):
        here = self.full.at[which, row]
        return remote(self.own[which], here, self.m_send.at[which], self.m_recv.at[which], row=self.at.mate)

    def over(self, which, row, j, src=None):
        here = self.piece(which, row, j)
        lane = 0 if self.pairs == 2 else which
        src = here if src is None else src
        return remote(src, here, self.x_send.at[lane, j], self.x_recv.at[lane, j], row=self.at.across)

    def hand(self, which, j):
        here = self.piece(which, self.at.across, j)
        return remote(here, here, self.y_send.at[j], self.y_recv.at[j], dp=self.at.pair(2, 1))

    def pass_first(self, which, row, j):
        here = self.piece(which, row, j)
        lane = 0 if self.pairs == 2 else which
        return remote(here, here, self.f_send.at[lane, j], self.f_recv.at[lane, j], row=self.at.mate)

    def pass_second(self, which, row, j):
        here = self.piece(which, row, j)
        return remote(here, here, self.g_send.at[j], self.g_recv.at[j], row=self.at.mate)

    def begin(self):
        for i in range(2):
            self.near(i, self.at.row).start()

    def send(self, j):
        for which in range(2):
            copy = self.over(which, self.at.row, j, self.own[which].at[self.rows(j)])
            if self.pairs == 2:
                pl.when(self.mine == which)(copy.start)
            else:
                copy.start()

    def forward(self, j):
        for which in self.held():
            self.over(which, self.at.across, j).wait_recv()
            if self.pairs == 2:
                self.hand(which, j).start()
            self.pass_first(which, self.at.across, j).start()

    def finish(self, j):
        if self.pairs == 2:
            self.hand(1 - self.mine, j).wait_recv()
            self.pass_second(1 - self.mine, self.at.across, j).start()

    def close(self):
        for i in range(2):
            self.near(i, self.at.mate).wait_recv()
            self.near(i, self.at.row).wait_send()
        for j in range(4):
            for which in self.held():
                self.over(which, self.at.row, j).wait_send()
                self.pass_first(which, self.at.diag, j).wait_recv()
                self.pass_first(which, self.at.across, j).wait_send()
            if self.pairs == 2:
                self.hand(self.mine, j).wait_send()
                self.pass_second(1 - self.mine, self.at.diag, j).wait_recv()
                self.pass_second(1 - self.mine, self.at.across, j).wait_send()


def weight_gather_sems(pairs):
    dma = pltpu.SemaphoreType.DMA
    lanes = 1 if pairs == 2 else 2
    return [
        dma((2,)), dma((2,)), dma((lanes, 4)), dma((lanes, 4)), dma((4,)), dma((4,)),
        dma((lanes, 4)), dma((lanes, 4)), dma((4,)), dma((4,)),
    ]


class ColSum:
    def __init__(self, at, product, sent, got, extra, sends, recvs, extra_recvs):
        self.at, self.product, self.sent, self.got, self.extra = at, product, sent, got, extra
        self.sends, self.recvs, self.extra_recvs = sends, recvs, extra_recvs
        self.size = product.shape[0] // 4

    def part(self, h):
        return pl.ds(h * self.size, self.size)

    def up(self, s, h):
        return remote(
            self.sent.at[s, self.part(h)], self.got.at[s, self.part(h)],
            self.sends.at[s, h], self.recvs.at[s, h], col=self.at.above,
        )

    def down(self, s, h):
        return remote(
            self.sent.at[s, self.part(h)], self.got.at[s, self.part(h)],
            self.sends.at[s, h], self.recvs.at[s, h], col=self.at.below,
        )

    def last_down(self, s, h):
        return remote(
            self.sent.at[s, self.part(h)], self.extra.at[self.part(h)],
            self.sends.at[s, h], self.extra_recvs.at[h], col=self.at.below,
        )

    def step(self, s, halves=(0, 1)):
        col, product = self.at.col, self.product
        for h in [2 * half + part for half in halves for part in range(2)]:
            @pl.when(((s >= col) & (col > 0)) | ((s < col) & (col < 3)))
            def _():
                self.up(s, h).wait_recv()

                def add(here):
                    product[here, :] += self.got[s, here].astype(F32)

                in_rows(self.size, 64, add, h * self.size)

            @pl.when((s == col) & (col < 3))
            def _():
                self.last_down(s, h).wait_recv()

                def add(here):
                    product[here, :] += self.extra[here].astype(F32)

                in_rows(self.size, 64, add, h * self.size)

            @pl.when(s != col)
            def _():
                def cast(here):
                    self.sent[s, here] = product[here, :].astype(BF16)

                in_rows(self.size, 64, cast, h * self.size)

            pl.when(s > col)(lambda: self.up(s, h).start())
            pl.when(s < col - 1)(lambda: self.down(s, h).start())
            pl.when(s == col - 1)(lambda: self.last_down(s, h).start())

    def close(self):
        def one(s, _):
            for h in range(4):
                pl.when(s != self.at.col)(lambda: self.up(s, h).wait_send())
            return 0

        lax.fori_loop(0, 4, one, 0)


def far_first(col, j):
    first = jnp.where(col < 2, 3, 0)
    near = jnp.where(col < 2, 2, 1)
    partner = jnp.where(lax.rem(col, 2) == 0, col + 1, col - 1)
    end = (col == 0) | (col == 3)
    return (first, jnp.where(end, near, partner), jnp.where(end, partner, near), col)[j]


def near_first(at, j):
    first = jnp.where(at.col < 2, 3, 0)
    near = jnp.where(at.col < 2, 2, 1)
    partner = jnp.where(lax.rem(at.col, 2) == 0, at.col + 1, at.col - 1)
    mine = at.paired
    return (
        jnp.where(mine, partner, first),
        jnp.where(mine, first, near),
        jnp.where(mine, near, partner),
        at.col,
    )[j]


def turn_tables(length):
    rates = THETA ** (-np.arange(HEAD_SIZE // 2) * 2.0 / HEAD_SIZE)
    angles = np.arange(length)[:, None] * rates[None, :]
    cos, sin = np.cos(angles), np.sin(angles)
    return (
        np.concatenate([cos, cos], axis=1).astype(np.float32),
        np.concatenate([-sin, sin], axis=1).astype(np.float32),
    )


def swap_halves(value):
    return pltpu.roll(value, HEAD_SIZE // 2, 1)


def head(ref, index):
    return ref[:, index * HEAD_SIZE : (index + 1) * HEAD_SIZE]


def root_scale(raw):
    return lax.rsqrt(jnp.mean(raw * raw, axis=1, keepdims=True) + EPSILON)


def attend(q_heads, groups, qkv, seg_row, cos, sin, q_gain, k_gain, o, qa, ka, va, probs, done):
    kv = q_heads // groups
    tokens = qkv.shape[0]
    half = tokens // 2
    seg_line = seg_row[...].astype(F32)
    seg_column = jnp.broadcast_to(seg_line, (128, tokens)).T[:, :1]

    def turned(index, gain):
        raw = head(qkv, index)
        normed = raw * root_scale(raw) * gain[...]
        return (normed * cos[...] + swap_halves(normed) * sin[...]).astype(BF16)

    for i in range(q_heads):
        qa[:, i * HEAD_SIZE : (i + 1) * HEAD_SIZE] = turned(i, q_gain)
    for i in range(kv):
        ka[:, i * HEAD_SIZE : (i + 1) * HEAD_SIZE] = turned(q_heads + i, k_gain)
        va[:, i * HEAD_SIZE : (i + 1) * HEAD_SIZE] = head(qkv, q_heads + kv + i).astype(BF16)
    for block in range(2):
        rows = slice(block * half, (block + 1) * half)
        keys = (block + 1) * half
        spot = lax.broadcasted_iota(jnp.int32, (half, keys), 0) + block * half
        other = lax.broadcasted_iota(jnp.int32, (half, keys), 1)
        allowed = (other <= spot) & (seg_column[rows, :] == seg_line[:, :keys])
        for i in range(q_heads):
            j = i // groups
            dots = lax.dot_general(
                head(qa, i)[rows], head(ka, j)[:keys], (((1,), (1,)), ((), ())), preferred_element_type=F32
            ) * (1.0 / math.sqrt(HEAD_SIZE))
            scores = jnp.where(allowed, dots, MASKED)
            expo = jnp.exp(scores - jnp.max(scores, axis=1, keepdims=True))
            p = expo / jnp.sum(expo, axis=1, keepdims=True)
            probs[i, rows, :keys] = p.astype(BF16)
            mixed = jnp.dot(p.astype(BF16), head(va, j)[:keys], preferred_element_type=F32)
            o[rows, i * HEAD_SIZE : (i + 1) * HEAD_SIZE] = mixed.astype(BF16)
        done(block)


def front_kernel(pairs, q_heads, groups, model_width, *refs):
    refs = list(refs)

    def take(count):
        found = refs[:count]
        del refs[:count]
        return found

    (x_ref, seg_row, q_gain, k_gain, gain_one, gain_two) = take(6)
    late = take(8)
    (w_gate, w_up) = take(2)
    (scale_one, hidden, scale_two, ffn_in) = take(4)
    kept_out = take(5)
    (dact_out, xn_out, gy_out, mixed_out, full) = take(5)
    (w_query, w_key, w_value, w_out, w_down, cos, sin) = late_held = take(7)
    (qkv, qa, ka, va, probs) = kept = take(5)
    (dact,) = take(1)
    (x_wide, scales, xn_wide, gy_wide, mixed_wide, mixed, product, chunk, keep) = take(9)
    total_bufs = take(2)
    second_bufs = take(2)
    moved = take(5)
    moved_q = take(5)
    chain = take(3)
    x_sems, gy_sems = take(2), take(2)
    (local,) = take(1)
    moved_sems, moved_q_sems = take(4), take(4)
    mixed_sems = take(7)
    chain_sems = take(3)
    total_sems, second_sems = take(2), take(2)
    full_sems = take(10)
    late_sems, kept_sems, dact_sems = take(3)
    scale_sems = take(2)

    at = Ends()
    gain_spot = pl.ds(pl.multiple_of(at.row * x_ref.shape[1], x_ref.shape[1]), x_ref.shape[1])
    fetch = Fetch([*zip(late[1:], late_held), (late[0], gy_wide.at[at.col])], late_sems)
    fetch.start()
    keep_saved = Fetch(list(zip(kept, kept_out)), kept_sems)
    full_gather = WeightGather(at, pairs, (w_gate, w_up), full, full_sems)
    tokens, feats = x_ref.shape
    first_total = RowTotal(at, *total_bufs, *total_sems)
    second_total = RowTotal(at, *second_bufs, *second_sems)
    x_gather = ColGather(at, x_wide, *x_sems)
    scale_share = LineShare(at, scales, *scale_sems)
    gy_gather = ColGather(at, gy_wide, *gy_sems)
    row_sum = RowSumWhole(at, product, qkv, *moved, *moved_sems)
    quarter_sum = RowSumQuarter(at, chunk, keep, *moved_q, *moved_q_sems)
    half = tokens // 2
    mixes = RowGather(
        at, lambda h: mixed.at[pl.ds(h * half, half)], lambda h, q: mixed_wide.at[q, pl.ds(h * half, half)], mixed_sems
    )
    out_sum = ColSum(at, hidden, *chain, *chain_sems)

    x_wide[at.col] = x_ref[...]
    at.greet(pairs if pairs == 2 else 0, True)
    x_gather.arrive(0)
    stream = x_ref[...].astype(F32)
    first_total.start(jnp.sum(stream * stream, axis=1, keepdims=True))
    full_gather.begin()
    full_gather.send(0)
    scales[at.col] = lax.rsqrt(first_total.total() / model_width + EPSILON)
    scale_share.start()
    scale_one[...] = as_column(scales[at.col])

    def project(s):
        scale_share.wait(s)
        scale = as_column(scales[s])
        xn_wide[s] = (x_wide[s].astype(F32) * scale * gain_one[:, gain_spot]).astype(BF16)
        base = 0
        for w in (w_query, w_key, w_value):
            size = w.shape[1]
            product[:, base : base + size] = jnp.dot(xn_wide[s], w[...], preferred_element_type=F32)
            base += size
        row_sum.give(s)

    def back_down(s):
        size = chunk.shape[1]

        def one(j, _):
            cols = pl.ds(pl.multiple_of(j * size, size), size)
            value = lax.dot_general(
                gy_wide[s], w_down[cols, :], (((1,), (1,)), ((), ())), preferred_element_type=F32
            )
            quarter_sum.split(s, value, cols, dact)
            return 0

        lax.fori_loop(0, w_down.shape[0] // size, one, 0)
        quarter_sum.give(s)

    def keep_dact(s):
        return pltpu.make_async_copy(dact.at[s], dact_out.at[s], dact_sems.at[s])

    def end_down(s):
        quarter_sum.finish(s)

        def add(here):
            dact[s, here] += moved_q[2][s, here].astype(F32) + moved_q[4][s, here].astype(F32)

        in_rows(128, 16, add)
        keep_dact(s).start()

    def send_gy(dist):
        @pl.when((at.col == dist) & (at.col < 3))
        def _():
            gy_gather.send_up()

        @pl.when((at.col == 3 - dist) & (at.col > 0))
        def _():
            gy_gather.send_down()

    def out_step(j, halves=(0, 1)):
        s = near_first(at, j)
        for h in halves:
            rows = pl.ds(h * half, half)
            hidden[rows, :] = jnp.dot(mixed_wide[s, rows, :], w_out[...], preferred_element_type=F32)
        out_sum.step(s, halves)

    mid = jnp.logical_not(at.end)
    fetch.wait()
    send_gy(0)
    x_gather.loop(0, project)
    back_down(at.col)
    full_gather.send(1)
    for dist in range(1, 4):
        x_gather.arrive(dist)
        send_gy(dist)
        x_gather.loop(dist, project)
        if dist == 1:
            full_gather.forward(0)

    @pl.when(mid)
    def _():
        gy_gather.arrive(1)

    row_sum.finish()

    def send_mixed(h):
        mixes.to_across(h).start()
        mixes.near(h)

    attend(q_heads, groups, qkv, seg_row, cos, sin, q_gain, k_gain, mixed, qa, ka, va, probs, send_mixed)
    keep_saved.start()
    full_gather.send(2)
    full_gather.forward(1)

    @pl.when(mid)
    def _():
        gy_gather.arrive(2)

    for h in range(2):
        mixes.wait_near(h)

    @pl.when(at.end)
    def _():
        out_step(0)
        pl.when(jnp.logical_not(at.paired))(lambda: out_step(1))
        gy_gather.arrive(1)

    full_gather.send(3)
    gy_gather.loop(1, back_down)
    for h in range(2):
        mixes.take_across(h)
        mixes.wait_diag(h)

        @pl.when(at.end)
        def _():
            pl.when(at.paired)(lambda: out_step(1, (h,)))
            out_step(2, (h,))

    @pl.when(at.end)
    def _():
        gy_gather.arrive(2)

    paired = mid & at.paired
    unpaired = mid & jnp.logical_not(at.paired)

    @pl.when(paired)
    def _():
        out_step(1, (0,))
        out_step(0, (0,))

    pl.when(unpaired)(lambda: out_step(0))
    gy_gather.loop(2, back_down)
    full_gather.forward(2)

    @pl.when(paired)
    def _():
        out_step(1, (1,))
        out_step(0, (1,))

    pl.when(unpaired)(lambda: out_step(1))

    @pl.when(mid)
    def _():
        full_gather.forward(3)
        out_step(2)

    @pl.when(at.end)
    def _():
        gy_gather.arrive(3)

    gy_gather.loop(3, back_down)
    full_gather.finish(0)
    full_gather.finish(1)
    pl.when(at.end)(lambda: full_gather.forward(3))
    wides = [
        pltpu.make_async_copy(src, dst, local.at[i])
        for i, (src, dst) in enumerate(((xn_wide, xn_out), (gy_wide, gy_out), (mixed_wide, mixed_out)))
    ]
    for copy in wides:
        copy.start()
    full_gather.finish(2)
    for dist in range(3):
        gy_gather.loop(dist, end_down)
    full_gather.finish(3)
    out_step(3)

    def residual(here):
        hidden[here, :] += x_ref[here, :].astype(F32)

    in_rows(tokens, 64, residual)
    value = hidden[...]
    second_total.start(jnp.sum(value * value, axis=1, keepdims=True))
    gy_gather.loop(3, end_down)
    scale = lax.rsqrt(second_total.finish() / model_width + EPSILON)
    scale_two[...] = scale
    ffn_in[...] = (hidden[...] * scale * gain_two[:, gain_spot]).astype(BF16)

    keep_saved.wait()
    for s in range(4):
        keep_dact(s).wait()
    full_gather.close()
    scale_share.close()
    x_gather.close()
    gy_gather.close()
    row_sum.close()
    quarter_sum.close()
    mixes.close(2)
    out_sum.close()
    for copy in wides:
        copy.wait()


def col_gather_sems():
    return [pltpu.SemaphoreType.DMA((2, 4, 2)), pltpu.SemaphoreType.DMA((4, 2))]


def chain_scratch(tokens, feats):
    return [
        pltpu.VMEM((4, tokens, feats), BF16), pltpu.VMEM((4, tokens, feats), BF16), pltpu.VMEM((tokens, feats), BF16),
    ]


def chain_sems():
    dma = pltpu.SemaphoreType.DMA
    return [dma((4, 4)), dma((4, 4)), dma((4,))]


def front(pairs, q_heads, groups, model_width, number, x, gy, weights, segments, tables, gains, ffn_weights):
    tokens, feats = x.shape
    w_query, w_key, w_value, w_out, w_down = weights
    width = w_query.shape[1] + w_key.shape[1] + w_value.shape[1]
    q_width, k_width, ff = w_query.shape[1], w_key.shape[1], w_down.shape[0]
    dma = pltpu.SemaphoreType.DMA
    any_spec, vmem = pl.BlockSpec(memory_space=pl.ANY), pl.BlockSpec(memory_space=pltpu.VMEM)
    shape = jax.ShapeDtypeStruct
    wide = pltpu.VMEM((4, tokens, feats), BF16)
    late = (*weights, *tables[:2])
    kept = [
        shape((tokens, width), F32),
        shape((tokens, q_width), BF16),
        shape((tokens, k_width), BF16),
        shape((tokens, k_width), BF16),
        shape((q_heads, tokens, tokens), BF16),
    ]
    dact = shape((4, tokens // 4, ff), F32)
    return pl.pallas_call(
        functools.partial(front_kernel, pairs, q_heads, groups, model_width),
        out_shape=(
            shape((tokens, 1), F32),
            shape((tokens, feats), F32),
            shape((tokens, 1), F32),
            shape((tokens, feats), BF16),
            *kept,
            dact,
            shape((4, tokens, feats), BF16),
            shape((4, tokens, feats), BF16),
            shape((4, tokens, q_width), BF16),
            shape((2, 4, *ffn_weights[0].shape), BF16),
        ),
        in_specs=[vmem] * 6 + [any_spec] * 10,
        out_specs=tuple([vmem] * 4 + [any_spec] * 10),
        scratch_shapes=[held(array) for array in late]
        + [held(array) for array in kept]
        + [
            held(dact),
            wide,
            pltpu.VMEM((4, 8, tokens), F32),
            wide,
            wide,
            pltpu.VMEM((4, tokens, q_width), BF16),
            pltpu.VMEM((tokens, q_width), BF16),
            pltpu.VMEM((tokens, width), F32),
            pltpu.VMEM((tokens, 512), F32),
            pltpu.VMEM((tokens // 4, ff), F32),
        ]
        + row_total_scratch(tokens) * 2
        + row_sum_scratch(tokens, width)
        + [pltpu.VMEM((4, tokens // 4, ff), BF16)] * 5
        + chain_scratch(tokens, feats)
        + col_gather_sems() * 2
        + [dma((3,))]
        + row_sum_sems()
        + [dma((2, 4)), dma((2, 4)), dma((4,)), dma((4,))]
        + [dma((2,))] * 7
        + chain_sems()
        + row_total_sems() * 2
        + weight_gather_sems(pairs)
        + [dma((8,)), dma((5,)), dma((4,)), dma((3,)), dma((4,))],
        compiler_params=pltpu.CompilerParams(
            collective_id=number, has_side_effects=True, vmem_limit_bytes=VMEM_LIMIT
        ),
        name="front",
    )(x, segments, *tables[2:], *gains, gy, *late, *ffn_weights)


def across_rows(left, right):
    return lax.dot_general(left, right, (((0,), (0,)), ((), ())), preferred_element_type=F32)


def attend_back(
    q_heads, groups, grad, qkv, qa, ka, va, probs, cos, sin, q_gain, k_gain, out, q_part, k_part, dq, dk, dv, done
):
    kv = q_heads // groups
    tokens = qkv.shape[0]
    half = tokens // 2
    scale = 1.0 / math.sqrt(HEAD_SIZE)
    dk[...] = jnp.zeros_like(dk)
    dv[...] = jnp.zeros_like(dv)
    q_part[...] = jnp.zeros_like(q_part)
    k_part[...] = jnp.zeros_like(k_part)

    def back(turned, index, gain, rows):
        raw = head(qkv, index)[rows]
        scales = root_scale(raw)
        normed = turned * cos[rows, :] - swap_halves(turned) * sin[rows, :]
        part = jnp.sum(normed * raw * scales, axis=0, keepdims=True)
        weighted = normed * gain[...]
        inner = jnp.sum(weighted * raw, axis=1, keepdims=True)
        result = scales * weighted - raw * (scales * scales * scales) * inner * (1.0 / HEAD_SIZE)
        out[rows, index * HEAD_SIZE : (index + 1) * HEAD_SIZE] = result.astype(BF16)
        return part

    for block in (1, 0):
        rows = slice(block * half, (block + 1) * half)
        keys = (block + 1) * half
        for i in range(q_heads):
            j = i // groups
            spot = slice(j * HEAD_SIZE, (j + 1) * HEAD_SIZE)
            pb = probs[i, rows, :keys]
            p = pb.astype(F32)
            g = head(grad, i)[rows].astype(BF16)
            dv[:keys, spot] += across_rows(pb, g)
            dp = lax.dot_general(
                g, head(va, j)[:keys], (((1,), (1,)), ((), ())), preferred_element_type=F32
            )
            ds = (p * (dp - jnp.sum(p * dp, axis=1, keepdims=True))).astype(BF16)
            dq[rows, i * HEAD_SIZE : (i + 1) * HEAD_SIZE] = (
                jnp.dot(ds, head(ka, j)[:keys], preferred_element_type=F32) * scale
            )
            dk[:keys, spot] += across_rows(ds, head(qa, i)[rows]) * scale
        q_part[...] += sum(back(head(dq, i)[rows], i, q_gain, rows) for i in range(q_heads))
        k_part[...] += sum(back(head(dk, i)[rows], q_heads + i, k_gain, rows) for i in range(kv))
        for i in range(kv):
            spot = (q_heads + kv + i) * HEAD_SIZE
            out[rows, spot : spot + HEAD_SIZE] = head(dv, i)[rows].astype(BF16)
        done(block)


def act_copy(src, dst, at, j, sem):
    s = far_first(at.col, j)
    if j < 1:
        return pltpu.make_async_copy(src.at[s], dst.at[s], sem)
    return pltpu.make_async_copy(src.at[s, at.row], dst.at[s, at.row], sem)


def weight_grad(out, left, right, send=None):
    def block(here):
        total = None
        for s in range(4):
            term = across_rows(left(s, here), right(s))
            total = term if total is None else total + term
        out[here, :] = total.astype(BF16)
        if send is not None:
            send(here).start()

    in_rows(out.shape[0], 256, block)


def middle_kernel(pairs, *refs):
    refs = list(refs)

    def take(count):
        found = refs[:count]
        del refs[:count]
        return found

    (hn, w_gate, w_up, dact_in, full) = take(5)
    (dhn, act_out, gate_n, up_n) = take(4)
    others = take(1) if pairs == 2 else []
    (hn_wide, hn_full, weights, dact, gate_up, gate_wide, up_wide, act_wide, n_gate, n_up) = take(10)
    chain = take(3)
    hn_sems = take(2)
    (full_sem, share_send, share_recv) = take(3)
    gate_sems, up_sems, act_sems = take(6), take(6), take(6)
    chain_sems_ = take(3)
    (local, y_send, y_recv) = take(3)

    at = Ends()
    ff = w_gate.shape[1]
    quarter = hn.shape[0] // 4
    gather = ColGather(at, hn_wide, *hn_sems)
    loads = [pltpu.make_async_copy(dact_in, dact, full_sem.at[2, 0])]
    for which, own in enumerate((w_gate, w_up)):
        for i, r in enumerate((at.mate, at.across, at.diag, at.row)):
            src = own if i == 3 else full.at[which, r]
            loads.append(pltpu.make_async_copy(src, weights.at[which, r], full_sem.at[which, i]))
    for load in loads:
        load.start()
    gates = RowGather(at, lambda s: gate_wide.at[s, at.row], lambda s, q: gate_wide.at[s, q], gate_sems)
    ups = RowGather(at, lambda s: up_wide.at[s, at.row], lambda s, q: up_wide.at[s, q], up_sems)
    acts = RowGather(at, lambda s: act_wide.at[s, at.row], lambda s, q: act_wide.at[s, q], act_sems)
    back_sum = ColSum(at, dhn, *chain, *chain_sems_)

    hn_wide[at.col] = hn[...]
    at.greet(pairs if pairs == 2 else 0)

    peers = (at.mate, at.across, at.diag)

    def share(s):
        hn_full[s, at.row] = hn_wide[s, pl.ds(pl.multiple_of(at.row * quarter, quarter), quarter)]
        for i, peer in enumerate(peers):
            theirs = hn_wide.at[s, pl.ds(pl.multiple_of(peer * quarter, quarter), quarter)]
            remote(theirs, hn_full.at[s, at.row], share_send.at[s, i], share_recv.at[s, i], row=peer).start()

    def hidden_units(s):
        for i, peer in enumerate(peers):
            here = hn_full.at[s, peer]
            remote(here, here, share_send.at[s, i], share_recv.at[s, i], row=peer).wait_recv()
        size = gate_up.shape[2]

        def some(j, _):
            cols = pl.ds(pl.multiple_of(j * size, size), size)
            for which in range(2):
                total = None
                for r in range(4):
                    term = jnp.dot(hn_full[s, r], weights[which, r, :, cols], preferred_element_type=F32)
                    total = term if total is None else total + term
                gate_up[which] = total

            def one(here):
                gate, up = gate_up[0, here], gate_up[1, here]
                grad = dact[s, here, cols]
                sigmoid = jax.nn.sigmoid(gate)
                silu = gate * sigmoid
                act_wide[s, at.row, here, cols] = (silu * up).astype(BF16)
                gate_wide[s, at.row, here, cols] = (
                    grad * up * (sigmoid * (1.0 + gate * (1.0 - sigmoid)))
                ).astype(BF16)
                up_wide[s, at.row, here, cols] = (grad * silu).astype(BF16)

            in_rows(quarter, 16, one)
            return 0

        lax.fori_loop(0, ff // size, some, 0)
        gates.to_across(s).start()
        gates.near(s)
        ups.near(s)

    def close_share(s):
        for i, peer in enumerate(peers):
            here = hn_full.at[s, peer]
            remote(here, here, share_send.at[s, i], share_recv.at[s, i], row=peer).wait_send()

    def rows_of(ref, s):
        return ref[s].reshape(4 * quarter, ff)

    def back(j):
        s = far_first(at.col, j)
        contract = (((1,), (1,)), ((), ()))
        dhn[...] = lax.dot_general(
            rows_of(gate_wide, s), weights[0, at.row], contract, preferred_element_type=F32
        ) + lax.dot_general(rows_of(up_wide, s), weights[1, at.row], contract, preferred_element_type=F32)

    def arrive(some, j):
        s = far_first(at.col, j)
        some.wait_near(s)
        some.take_across(s)
        some.wait_diag(s)

    def left(s, here):
        return hn_wide[s, :, here]

    mid = jnp.logical_not(at.end)
    gather.arrive(0)
    gather.loop(0, share)
    for load in loads:
        load.wait()
    gather.loop(0, hidden_units)
    gather.arrive(1)
    gather.loop(1, share)
    gather.arrive(2)
    gather.loop(2, share)
    gather.loop(1, hidden_units)
    gather.arrive(3)
    gather.loop(3, share)
    gather.loop(2, hidden_units)
    gather.loop(3, hidden_units)
    for j in range(4):
        ups.to_across(far_first(at.col, j)).start()
    acts.near(far_first(at.col, 0))
    acts.to_across(far_first(at.col, 0)).start()
    keep_acts = [
        act_copy(act_wide, act_out, at, j, local.at[2 + j]) for j in range(4)
    ]
    for copy in keep_acts[1:]:
        copy.start()
    for j in range(4):
        arrive(gates, j)

    def to_other(here=slice(None)):
        return remote(n_gate.at[here], others[0].at[here], y_send.at[0], y_recv.at[0], dp=at.pair(2, 1))

    weight_grad(n_gate, left, lambda s: rows_of(gate_wide, s), to_other if pairs == 2 else None)
    keep_gate = pltpu.make_async_copy(n_gate, gate_n, local.at[0])
    keep_gate.start()
    arrive(ups, 0)
    for j in range(3):
        back(j)
        pl.when(at.end)(lambda: back_sum.step(far_first(at.col, j)))
        arrive(ups, j + 1)
        pl.when(mid)(lambda: back_sum.step(far_first(at.col, j)))
    weight_grad(n_up, left, lambda s: rows_of(up_wide, s))
    keep_up = pltpu.make_async_copy(n_up, up_n, local.at[1])
    keep_up.start()
    back(3)
    arrive(acts, 0)
    keep_acts[0].start()
    back_sum.step(at.col)

    gather.close()
    for dist in range(4):
        gather.loop(dist, close_share)
    gates.close(4)
    ups.close(4)
    acts.close_one(far_first(at.col, 0))
    back_sum.close()
    for copy in keep_acts:
        copy.wait()
    keep_gate.wait()
    keep_up.wait()
    if pairs == 2:
        to_other().wait()


def middle(pairs, number, hn, w_gate, w_up, dact, full):
    tokens, feats = hn.shape
    ff = w_gate.shape[1]
    quarter = tokens // 4
    dma = pltpu.SemaphoreType.DMA
    any_spec, vmem = pl.BlockSpec(memory_space=pl.ANY), pl.BlockSpec(memory_space=pltpu.VMEM)
    shape = jax.ShapeDtypeStruct
    narrow = shape((feats, ff), BF16)
    others = 1 if pairs == 2 else 0
    out = pl.pallas_call(
        functools.partial(middle_kernel, pairs),
        out_shape=tuple(
            [shape((tokens, feats), F32), shape((4, 4, quarter, ff), BF16), narrow, narrow] + [narrow] * others
        ),
        in_specs=[vmem] + [any_spec] * 4,
        out_specs=tuple([vmem] + [any_spec] * (3 + others)),
        scratch_shapes=[
            pltpu.VMEM((4, tokens, feats), BF16),
            pltpu.VMEM((4, 4, quarter, feats), BF16),
            pltpu.VMEM((2, 4, feats, ff), BF16),
            held(dact),
            pltpu.VMEM((2, quarter, 512), F32),
            pltpu.VMEM((4, 4, quarter, ff), BF16),
            pltpu.VMEM((4, 4, quarter, ff), BF16),
            pltpu.VMEM((4, 4, quarter, ff), BF16),
            pltpu.VMEM((feats, ff), BF16),
            pltpu.VMEM((feats, ff), BF16),
        ]
        + chain_scratch(tokens, feats)
        + col_gather_sems()
        + [dma((3, 4)), dma((4, 3)), dma((4, 3))]
        + [dma((4,))] * 18
        + chain_sems()
        + [dma((6,)), dma((1,)), dma((1,))],
        compiler_params=pltpu.CompilerParams(
            collective_id=number, has_side_effects=True, vmem_limit_bytes=VMEM_LIMIT
        ),
        name="middle",
    )(hn, w_gate, w_up, dact, full)
    return out[:4], out[4:]


def tail_kernel(pairs, q_heads, groups, *refs):
    refs = list(refs)

    def take(count):
        found = refs[:count]
        del refs[:count]
        return found

    (w_out, q_gain, k_gain, dhn, hidden, scale_two, gain_two, gy, x_ref, scale_one, gain_one) = take(11)
    late = take(12)
    (gy_wide, mixed_wide, normed_wide, up_n) = take(4)
    (in_grad, layer_out, one_grad, two_grad, q_grad, k_grad) = take(6)
    kept_out = take(5)
    others = take(6) if pairs == 2 else []
    (w_down, w_query, w_key, w_value, qkv, qa, ka, va, probs, cos, sin) = late_held = take(11)
    (da_wide, act_wide, dqkv, dqkv_wide, held_wide, product, grad_mixed, dq, dk, dv, *narrow) = take(15)
    (dh, q_part, k_part, packet, packet_got, by_row, summed) = take(7)
    first_bufs, last_bufs = take(2), take(2)
    moved = take(5)
    down_bufs, dxn_bufs = take(3), take(3)
    (g_send, g_recv, local, y_send, y_recv, late_sems) = take(6)
    moved_sems = take(4)
    act_sems, dqkv_sems = take(6), take(7)
    down_sems, dxn_sems = take(3), take(3)
    first_sems, last_sems = take(2), take(2)
    (p_send, p_recv, r_send, r_recv) = take(4)

    at = Ends()
    feats = dhn.shape[1]
    model_width = 4 * feats
    gain_spot = pl.ds(pl.multiple_of(at.row * feats, feats), feats)
    fetch_acts = [act_copy(late[0], act_wide, at, j, local.at[8 + j]) for j in range(4)]
    for copy in reversed(fetch_acts):
        copy.start()
    fetch = Fetch(list(zip(late[1:], late_held)), late_sems)
    fetch.start()
    first_total = RowTotal(at, *first_bufs, *first_sems)
    last_total = RowTotal(at, *last_bufs, *last_sems)
    at.greet(pairs, True, True)

    def pair_copy(index, here=slice(None)):
        return remote(
            narrow[index].at[here], others[index].at[here], y_send.at[index], y_recv.at[index],
            dp=1 - lax.axis_index("dp"),
        )

    n_down, n_out, n_query, n_key, n_value = narrow
    narrow = [up_n, *narrow]

    def to_pair(index):
        return functools.partial(pair_copy, index) if pairs == 2 else None

    def load(index, src):
        return pltpu.make_async_copy(src, held_wide, local.at[index])

    def keep(index):
        return pltpu.make_async_copy(narrow[index], kept_out[index - 1], local.at[2 + index])

    if pairs == 2:
        pair_copy(0).start()
    load(0, gy_wide).start()
    gather = ColGather(at, da_wide, g_send, g_recv)
    row_sum = RowSumWhole(at, product, grad_mixed, *moved, *moved_sems)
    acts = RowGather(at, lambda s: late[0].at[s, at.row], lambda s, q: act_wide.at[s, q], act_sems)
    half = dqkv.shape[0] // 2
    grads = RowGather(
        at, lambda h: dqkv.at[pl.ds(h * half, half)], lambda h, q: dqkv_wide.at[q, pl.ds(h * half, half)], dqkv_sems
    )
    down_sum = ColSum(at, product, *down_bufs, *down_sems)
    dxn_sum = ColSum(at, product, *dxn_bufs, *dxn_sems)

    weighted = dhn[...] * gain_two[:, gain_spot]
    first_total.start(jnp.sum(weighted * hidden[...], axis=1, keepdims=True))
    for j in range(1, 4):
        acts.to_across(far_first(at.col, j)).start()
        acts.near(far_first(at.col, j))
    scale = scale_two[...]
    packet[...] = jnp.zeros_like(packet)
    packet[1:2, :] = jnp.sum(dhn[...] * hidden[...] * scale, axis=0, keepdims=True)
    inner = first_total.finish()
    dh[...] = (
        gy[...].astype(F32)
        + scale * (dhn[...] * gain_two[:, gain_spot])
        - hidden[...] * (scale * scale * scale * inner * (1.0 / model_width))
    )
    da_wide[at.col] = dh[...].astype(BF16)
    gather.arrive(0)
    for copy in reversed(fetch_acts):
        copy.wait()

    def back_out(s):
        product[...] = lax.dot_general(
            da_wide[s], w_out[...], (((1,), (1,)), ((), ())), preferred_element_type=F32
        )
        row_sum.give(s)

    def take_act(j):
        s = far_first(at.col, j)
        acts.wait_near(s)
        acts.take_across(s)
        acts.wait_diag(s)

    def act_rows(s, cols):
        return act_wide[s, :, :, cols].reshape(product.shape[0], cols.size)

    def down_step(j):
        s = far_first(at.col, j)
        product[...] = jnp.dot(
            act_rows(s, pl.ds(0, act_wide.shape[3])), w_down[...], preferred_element_type=F32
        )
        down_sum.step(s)

    def dxn_step(j, halves=(1, 0)):
        s = near_first(at, j)
        for h in halves:
            rows = pl.ds(h * half, half)
            total, base = None, 0
            for w in (w_query, w_key, w_value):
                size = w.shape[1]
                term = lax.dot_general(
                    dqkv_wide[s, rows, pl.ds(base, size)], w[...], (((1,), (1,)), ((), ())),
                    preferred_element_type=F32,
                )
                total = term if total is None else total + term
                base += size
            product[rows, :] = total
        dxn_sum.step(s, halves)

    def down_weight():
        load(0, gy_wide).wait()
        weight_grad(n_down, act_rows, lambda s: held_wide[s], to_pair(1))
        keep(1).start()
        load(1, mixed_wide).start()

    mid = jnp.logical_not(at.end)
    fetch.wait()
    gather.loop(0, back_out)
    gather.arrive(1)
    gather.loop(1, back_out)
    pl.when(at.end)(lambda: down_step(0))
    gather.arrive(2)
    gather.loop(2, back_out)
    pl.when(mid)(lambda: down_step(0))
    take_act(1)
    pl.when(at.end)(lambda: down_step(1))
    take_act(2)
    take_act(3)
    pl.when(at.end)(lambda: down_step(2))
    down_weight()
    pl.when(mid)(lambda: down_step(1))
    gather.arrive(3)
    gather.loop(3, back_out)
    row_sum.finish()

    def send_grads(h):
        grads.to_across(h).start()
        grads.near(h)

    attend_back(
        q_heads, groups, grad_mixed, qkv, qa, ka, va, probs, cos, sin, q_gain, k_gain,
        dqkv, q_part, k_part, dq, dk, dv, send_grads,
    )
    for h in range(2):
        grads.wait_near(h)

    @pl.when(at.end)
    def _():
        dxn_step(0)
        pl.when(jnp.logical_not(at.paired))(lambda: dxn_step(1))

    @pl.when(mid)
    def _():
        down_step(2)

    load(1, mixed_wide).wait()
    weight_grad(n_out, lambda s, here: held_wide[s, :, here], lambda s: da_wide[s], to_pair(2))
    keep(2).start()
    load(2, normed_wide).start()
    paired = mid & at.paired
    unpaired = mid & jnp.logical_not(at.paired)
    pl.when(unpaired)(lambda: dxn_step(0))
    grads.take_across(1)
    grads.wait_diag(1)

    @pl.when(at.end)
    def _():
        pl.when(at.paired)(lambda: dxn_step(1, (1,)))
        dxn_step(2, (1,))

    @pl.when(paired)
    def _():
        dxn_step(1, (1,))
        dxn_step(0, (1,))

    pl.when(unpaired)(lambda: dxn_step(1, (1,)))
    grads.take_across(0)
    grads.wait_diag(0)

    @pl.when(at.end)
    def _():
        pl.when(at.paired)(lambda: dxn_step(1, (0,)))
        dxn_step(2, (0,))

    pl.when(unpaired)(lambda: dxn_step(1, (0,)))
    load(2, normed_wide).wait()
    base = 0
    for index, some in ((3, n_query), (4, n_key), (5, n_value)):
        spot = pl.ds(base, some.shape[1])
        weight_grad(
            some, lambda s, here: held_wide[s, :, here], lambda s, spot=spot: dqkv_wide[s, :, spot], to_pair(index)
        )
        keep(index).start()
        base += some.shape[1]

    @pl.when(paired)
    def _():
        dxn_step(2, (1,))
        dxn_step(0, (0,))

    @pl.when(paired)
    def _():
        dxn_step(1, (0,))
        dxn_step(2, (0,))

    pl.when(unpaired)(lambda: dxn_step(2))
    down_step(3)
    layer_out[...] = (hidden[...] + product[...]).astype(BF16)
    dxn_step(3)
    scale = scale_one[...]
    last_total.start(
        jnp.sum(product[...] * gain_one[:, gain_spot] * x_ref[...].astype(F32), axis=1, keepdims=True)
    )
    packet[0:1, :] = jnp.sum(product[...] * x_ref[...].astype(F32) * scale, axis=0, keepdims=True)
    packet[2:3, :HEAD_SIZE] = q_part[...]
    packet[2:3, HEAD_SIZE : 2 * HEAD_SIZE] = k_part[...]

    def to_line(step):
        return remote(
            packet, packet_got.at[step - 1], p_send.at[step - 1], p_recv.at[step - 1],
            col=lax.rem(at.col + step, 4),
        )

    def to_group(index, row, step):
        where = dict(row=row) if step == 0 else dict(row=row, dp=at.pair(pairs, step))
        return remote(summed, by_row.at[step, at.row], r_send.at[index], r_recv.at[step, at.row], **where)

    def from_group(index, row, step):
        here = by_row.at[step, row]
        return remote(summed, here, r_send.at[index], r_recv.at[step, row], row=at.mate)

    group = [(row, 0) for row in (at.mate, at.across, at.diag)]
    group += [(row, step) for step in range(1, pairs) for row in range(4)]
    for step in range(1, 4):
        to_line(step).start()
    for step in range(1, 4):
        to_line(step).wait()
    summed[...] = (packet[...] + packet_got[0]) + (packet_got[1] + packet_got[2])
    by_row[0, at.row] = summed[...]
    for index, (row, step) in enumerate(group):
        to_group(index, row, step).start()
    inner = last_total.finish()
    in_grad[...] = (
        dh[...]
        + scale * (product[...] * gain_one[:, gain_spot])
        - x_ref[...].astype(F32) * (scale * scale * scale * inner * (1.0 / model_width))
    )
    for index, (row, step) in enumerate(group):
        from_group(index, row, step).wait_recv()
        to_group(index, row, step).wait_send()
    total = by_row[0]
    for step in range(1, pairs):
        total = total + by_row[step]
    for r in range(4):
        one_grad[:, r * feats : (r + 1) * feats] = total[r, 0:1, :]
        two_grad[:, r * feats : (r + 1) * feats] = total[r, 1:2, :]
    heads = (total[0, 2:3, :] + total[1, 2:3, :]) + (total[2, 2:3, :] + total[3, 2:3, :])
    q_grad[...] = heads[:, :HEAD_SIZE]
    k_grad[...] = heads[:, HEAD_SIZE : 2 * HEAD_SIZE]

    gather.close()
    row_sum.close()
    for j in range(1, 4):
        acts.close_one(far_first(at.col, j))
    grads.close(2)
    down_sum.close()
    dxn_sum.close()
    for index in range(1, 6):
        keep(index).wait()
    if pairs == 2:
        for index in range(6):
            pair_copy(index).wait()


def tail(pairs, q_heads, groups, number, act, weights, saved, tables, norms, wides, narrow):
    tokens, feats = norms[0].shape
    w_out, w_down, w_query, w_key, _ = weights
    ff = w_down.shape[0]
    width = saved[0].shape[1]
    q_width, k_width = saved[1].shape[1], saved[2].shape[1]
    dma = pltpu.SemaphoreType.DMA
    any_spec, vmem = pl.BlockSpec(memory_space=pl.ANY), pl.BlockSpec(memory_space=pltpu.VMEM)
    shape = jax.ShapeDtypeStruct
    shapes = [
        shape((tokens, feats), F32),
        shape((tokens, feats), BF16),
        shape((1, 4 * feats), F32),
        shape((1, 4 * feats), F32),
        shape((1, HEAD_SIZE), F32),
        shape((1, HEAD_SIZE), F32),
    ]
    own = [
        shape((ff, feats), BF16),
        shape((q_width, feats), BF16),
        shape((feats, q_width), BF16),
        shape((feats, k_width), BF16),
        shape((feats, k_width), BF16),
    ]
    others = [shape(n.shape, BF16) for n in narrow] + own if pairs == 2 else []
    packet = pltpu.VMEM((8, feats), F32)
    early = (w_out, *tables[2:], *norms)
    late = (act, *weights[1:], *saved, *tables[:2])
    out = pl.pallas_call(
        functools.partial(tail_kernel, pairs, q_heads, groups),
        out_shape=tuple(shapes + own + others),
        in_specs=[vmem] * len(early) + [any_spec] * (len(late) + 4),
        out_specs=tuple([vmem] * 6 + [any_spec] * (5 + len(others))),
        scratch_shapes=[held(array) for array in late[1:]]
        + [
            pltpu.VMEM((4, tokens, feats), BF16),
            pltpu.VMEM((4, 4, tokens // 4, ff), BF16),
            pltpu.VMEM((tokens, width), BF16),
            pltpu.VMEM((4, tokens, width), BF16),
            pltpu.VMEM((4, tokens, feats), BF16),
            pltpu.VMEM((tokens, feats), F32),
            pltpu.VMEM((tokens, q_width), F32),
            pltpu.VMEM((tokens, q_width), F32),
            pltpu.VMEM((tokens, k_width), F32),
            pltpu.VMEM((tokens, k_width), F32),
        ]
        + [held(array) for array in own]
        + [
            pltpu.VMEM((tokens, feats), F32),
            pltpu.VMEM((1, HEAD_SIZE), F32),
            pltpu.VMEM((1, HEAD_SIZE), F32),
            packet,
            pltpu.VMEM((3, 8, feats), F32),
            pltpu.VMEM((pairs, 4, 8, feats), F32),
            packet,
        ]
        + row_total_scratch(tokens) * 2
        + row_sum_scratch(tokens, q_width)
        + chain_scratch(tokens, feats) * 2
        + col_gather_sems()
        + [dma((12,)), dma((6,)), dma((6,)), dma((12,))]
        + row_sum_sems()
        + [dma((4,))] * 6
        + [dma((2,))] * 7
        + chain_sems() * 2
        + row_total_sems() * 2
        + [dma((3,)), dma((3,)), dma((4 * pairs - 1,)), dma((pairs, 4))],
        compiler_params=pltpu.CompilerParams(
            collective_id=number, has_side_effects=True, vmem_limit_bytes=VMEM_LIMIT
        ),
        name="tail",
    )(*early, *late, *wides, *narrow)
    return out[:6], out[6:11], out[11:]


def finish_kernel(count, *refs):
    parts, others, rest = refs[:count], refs[count : 2 * count], refs[2 * count :]
    kept = len(rest) - count
    for a, b, out in zip(parts, others, rest[kept // 2 :]):
        out[...] = a[...].astype(F32) + b[...].astype(F32)
    for src, dst in zip(rest[: kept // 2], rest[kept // 2 + count :]):
        dst[...] = src[...]


def finish(parts, others, rest, steps=4):
    def spec(array):
        block = (array.shape[0] // steps, array.shape[1]) if array.shape[0] % steps == 0 else array.shape
        index = (lambda i: (i, 0)) if block != array.shape else (lambda i: (0, 0))
        return pl.BlockSpec(block, index)

    outs = [jax.ShapeDtypeStruct(a.shape, F32) for a in parts] + [jax.ShapeDtypeStruct(a.shape, a.dtype) for a in rest]
    operands = (*parts, *others, *rest)
    out = pl.pallas_call(
        functools.partial(finish_kernel, len(parts)),
        grid=(steps,),
        out_shape=tuple(outs),
        in_specs=[spec(a) for a in operands],
        out_specs=tuple(spec(a) for a in outs),
        compiler_params=pltpu.CompilerParams(vmem_limit_bytes=VMEM_LIMIT),
        name="finish",
    )(*operands)
    return out[: len(parts)], out[len(parts) :]


def shards(
    pairs,
    hidden_in,
    segment_ids,
    attn_gain,
    w_query,
    key_projection,
    value_projection,
    query_gain,
    key_norm_gain,
    w_out,
    ffn_gain,
    w_gate,
    w_up,
    w_down,
    out_grad,
):
    tokens = hidden_in.shape[0]
    model_width = attn_gain.shape[0]
    q_width = w_query.shape[1]
    k_width = key_projection.shape[1]
    q_heads = q_width // HEAD_SIZE
    groups = q_width // k_width
    tables = (*turn_tables(tokens), query_gain[None, :], key_norm_gain[None, :])
    (scale_one, hidden, scale_two, ffn_in, qkv, q_turned, k_turned, values, probs, grad_inner, xn_wide, gy_wide, mixed_wide, full) = front(
        pairs, q_heads, groups, model_width, 0, hidden_in, out_grad,
        (w_query, key_projection, value_projection, w_out, w_down),
        segment_ids[None, :],
        tables,
        (attn_gain[None, :], ffn_gain[None, :]),
        (w_gate, w_up),
    )
    (grad_ffn_in, inner_act, gate_n, up_n), other_gate = middle(pairs, 1, ffn_in, w_gate, w_up, grad_inner, full)
    (in_grad, layer_out, one_grad, two_grad, q_gain_grad, k_gain_grad), own, others = tail(
        pairs, q_heads, groups, 2, inner_act,
        (w_out, w_down, w_query, key_projection, value_projection),
        (qkv, q_turned, k_turned, values, probs),
        tables,
        (grad_ffn_in, hidden, scale_two, ffn_gain[None, :], out_grad, hidden_in, scale_one, attn_gain[None, :]),
        (gy_wide, mixed_wide, xn_wide),
        (up_n,),
    )
    parts = (gate_n, up_n, *own)
    if pairs == 2:
        rest = (in_grad, layer_out, one_grad, two_grad, q_gain_grad, k_gain_grad)
        sums, rest = finish(parts, (*other_gate, *others), rest)
        in_grad, layer_out, one_grad, two_grad, q_gain_grad, k_gain_grad = rest
    else:
        sums = lax.psum(tuple(part.astype(F32) for part in parts), "dp")
    gate_grad, up_grad, down_grad, out_weight_grad, query_grad, key_grad, value_grad = sums
    return (
        layer_out,
        in_grad,
        one_grad.reshape(-1),
        query_grad,
        key_grad,
        value_grad,
        q_gain_grad.reshape(-1),
        k_gain_grad.reshape(-1),
        out_weight_grad,
        two_grad.reshape(-1),
        gate_grad,
        up_grad,
        down_grad,
    )


def solution(mesh):
    acts, grid, flip, none = P(("dp", "col"), "row"), P("row", "col"), P("col", "row"), P()
    return jax.shard_map(
        functools.partial(shards, mesh.shape["dp"]),
        mesh=mesh,
        in_specs=(
            acts, P(("dp", "row")), none, grid, grid, grid, none, none, flip, none, grid, grid, flip, acts,
        ),
        out_specs=(
            acts, acts, none, grid, grid, grid, none, none, flip, none, grid, grid, flip,
        ),
        check_vma=False,
    )
```

```python
import functools
import math

import jax
import jax.numpy as jnp
import numpy as np
from jax import lax
from jax.experimental import pallas as pl
from jax.experimental.pallas import tpu as pltpu
from jax.sharding import PartitionSpec as P

HEAD_SIZE = 128
EPSILON = 1e-06
THETA = 1000000.0
MASKED = -1e30
MESH = pl.DeviceIdType.MESH
BF16 = jnp.bfloat16
F32 = jnp.float32
VMEM_LIMIT = 60 << 20


def to(**where):
    return dict(device_id=where, device_id_type=MESH)


class Ends:
    def __init__(self):
        self.row = lax.axis_index("row")
        self.col = lax.axis_index("col")
        self.chip = lax.div(self.row, 2)
        self.core = lax.rem(self.row, 2)
        self.mate = self.chip * 2 + (1 - self.core)
        self.across = (1 - self.chip) * 2 + self.core
        self.diag = (1 - self.chip) * 2 + (1 - self.core)
        self.end = (self.col == 0) | (self.col == 3)
        self.paired = lax.div(self.col, 2) == self.chip
        self.above = jnp.minimum(self.col + 1, 3)
        self.below = jnp.maximum(self.col - 1, 0)

    def greet(self, pairs=0, line=False, rows=False):
        gate = pltpu.get_barrier_semaphore()
        count = 3
        for peer in (self.mate, self.across, self.diag):
            pl.semaphore_signal(gate, inc=1, **to(row=peer))
        for step in range(1, pairs):
            dp = self.pair(pairs, step)
            for row in range(4) if rows else (self.row,):
                pl.semaphore_signal(gate, inc=1, **to(dp=dp, row=row))
                count += 1
        if line:
            for step in range(1, 4):
                pl.semaphore_signal(gate, inc=1, **to(col=lax.rem(self.col + step, 4)))
                count += 1
        else:

            @pl.when(self.col > 0)
            def _():
                pl.semaphore_signal(gate, inc=1, **to(col=self.col - 1))

            @pl.when(self.col < 3)
            def _():
                pl.semaphore_signal(gate, inc=1, **to(col=self.col + 1))

            count += jnp.where(self.col > 0, 1, 0) + jnp.where(self.col < 3, 1, 0)
        pl.semaphore_wait(gate, count)

    def pair(self, pairs, step):
        return lax.rem(lax.axis_index("dp") + step, pairs)


class RowTotal:
    def __init__(self, at, own, got, sends, recvs):
        self.own, self.got = own, got
        self.copies = [
            remote(own, got.at[i], sends.at[i], recvs.at[i], row=peer)
            for i, peer in enumerate((at.mate, at.across, at.diag))
        ]

    def start(self, column):
        self.own[...] = jnp.broadcast_to(column, (column.shape[0], 128)).T[:8, :]
        for copy in self.copies:
            copy.start()

    def total(self):
        for copy in self.copies:
            copy.wait()
        return (self.own[...] + self.got[0]) + (self.got[1] + self.got[2])

    def finish(self):
        return as_column(self.total())


def as_column(lines):
    return jnp.concatenate([lines] * 16, axis=0).T[:, :1]


class LineShare:
    def __init__(self, at, blocks, sends, recvs):
        self.at, self.blocks, self.sends, self.recvs = at, blocks, sends, recvs

    def copy(self, s, step):
        here = self.blocks.at[s]
        col = lax.rem(self.at.col + step, 4)
        return remote(here, here, self.sends.at[step - 1], self.recvs.at[s], col=col)

    def start(self):
        for step in range(1, 4):
            self.copy(self.at.col, step).start()

    def wait(self, s):
        pl.when(s != self.at.col)(lambda: self.copy(s, 1).wait_recv())

    def close(self):
        for step in range(1, 4):
            self.copy(self.at.col, step).wait_send()


def row_total_scratch(tokens):
    return [pltpu.VMEM((8, tokens), F32), pltpu.VMEM((3, 8, tokens), F32)]


def row_total_sems():
    return [pltpu.SemaphoreType.DMA((3,)), pltpu.SemaphoreType.DMA((3,))]


def remote(src, dst, sends, recvs, **where):
    return pltpu.make_async_remote_copy(
        src_ref=src, dst_ref=dst, send_sem=sends, recv_sem=recvs, **to(**where)
    )


class Fetch:
    def __init__(self, pairs, sems):
        self.copies = [
            pltpu.make_async_copy(src, dst, sems.at[i]) for i, (src, dst) in enumerate(pairs)
        ]

    def start(self):
        for copy in self.copies:
            copy.start()

    def wait(self, first=0, last=None):
        for copy in self.copies[first:last]:
            copy.wait()


def held(array):
    return pltpu.VMEM(array.shape, array.dtype)


def in_rows(count, step, body, first=0):
    def one(i, _):
        body(pl.ds(pl.multiple_of(first + i * step, step), step))
        return 0

    lax.fori_loop(0, count // step, one, 0)


class ColGather:
    def __init__(self, at, wide, sends, recvs):
        self.at, self.wide, self.sends, self.recvs = at, wide, sends, recvs
        self.half = wide.shape[1] // 2

    def copy(self, s, h, side, col):
        part = self.wide.at[s, pl.ds(h * self.half, self.half)]
        return remote(part, part, self.sends.at[side, s, h], self.recvs.at[s, h], col=col)

    def up(self, s, h):
        return self.copy(s, h, 0, self.at.above)

    def down(self, s, h):
        return self.copy(s, h, 1, self.at.below)

    def loop(self, dist, body):
        if dist == 0:
            body(self.at.col)
            return

        def one(side, _):
            s = jnp.where(side == 0, self.at.col - dist, self.at.col + dist)
            pl.when((s >= 0) & (s <= 3))(lambda: body(s))
            return 0

        lax.fori_loop(0, 2, one, 0)

    def arrive(self, dist):
        for h in range(2):

            def take(s, h=h):
                if dist:
                    self.up(s, h).wait_recv()

                @pl.when((s <= self.at.col) & (self.at.col < 3))
                def _():
                    self.up(s, h).start()

                @pl.when((s >= self.at.col) & (self.at.col > 0))
                def _():
                    self.down(s, h).start()

            self.loop(dist, take)

    def send_up(self):
        for h in range(2):
            self.up(self.at.col, h).start()

    def send_down(self):
        for h in range(2):
            self.down(self.at.col, h).start()

    def close(self):
        def one(s, _):
            for h in range(2):

                @pl.when((s <= self.at.col) & (self.at.col < 3))
                def _():
                    self.up(s, h).wait_send()

                @pl.when((s >= self.at.col) & (self.at.col > 0))
                def _():
                    self.down(s, h).wait_send()

            return 0

        lax.fori_loop(0, 4, one, 0)


class RowSumWhole:
    def __init__(self, at, product, out, a_send, a_recv, c_recv, d_send, d_recv, m_send, m_recv, x_send, x_recv):
        self.at, self.product, self.out = at, product, out
        self.a_send, self.a_recv, self.c_recv, self.d_send, self.d_recv = a_send, a_recv, c_recv, d_send, d_recv
        self.m_send, self.m_recv, self.x_send, self.x_recv = m_send, m_recv, x_send, x_recv
        self.half = product.shape[0] // 2
        self.d = remote(d_send, d_recv, m_send.at[2], m_recv.at[2], row=at.mate)

    def a(self, i):
        return remote(self.a_send.at[i], self.a_recv.at[i], self.m_send.at[i], self.m_recv.at[i], row=self.at.mate)

    def b(self, i, s):
        core = self.at.core
        return remote(self.a_recv.at[i], self.c_recv.at[core], self.x_send.at[i], self.x_recv.at[core], row=s)

    def part(self, core, here):
        return pl.ds(pl.multiple_of(core * self.half + here.start, here.size), here.size)

    def give(self, s):
        at, product, half = self.at, self.product, self.half
        i = lax.rem(s, 2)
        ours = lax.div(s, 2) == at.chip

        @pl.when(jnp.logical_not(ours))
        def _():
            def cast(here):
                self.a_send[i, here] = product[self.part(1 - at.core, here), :].astype(BF16)

            in_rows(half, 64, cast)
            self.a(i).start()
            self.a(i).wait_recv()

            def add(here):
                total = product[self.part(at.core, here), :] + self.a_recv[i, here].astype(F32)
                self.a_recv[i, here] = total.astype(BF16)

            in_rows(half, 64, add)
            self.b(i, s).start()

        @pl.when(ours & (i != at.core))
        def _():
            def cast(here):
                self.d_send[here] = product[here, :].astype(BF16)

            in_rows(2 * half, 64, cast)
            self.d.start()

        @pl.when(s == at.row)
        def _():
            def store(here):
                self.out[here] = product[here, :]

            in_rows(2 * half, 64, store)

    def finish(self):
        self.d.wait_recv()
        for h in range(2):
            here = self.c_recv.at[h]
            remote(here, here, self.x_send.at[h], self.x_recv.at[h], row=self.at.across).wait_recv()

            def add(rows, h=h):
                spot = pl.ds(pl.multiple_of(h * self.half + rows.start, rows.size), rows.size)
                self.out[spot] += self.d_recv[spot].astype(F32) + self.c_recv[h, rows].astype(F32)

            in_rows(self.half, 64, add)

    def close(self):
        self.d.wait_send()
        for i in range(2):
            self.a(i).wait_send()
            self.b(i, self.at.across).wait_send()


def row_sum_scratch(tokens, width):
    half = pltpu.VMEM((2, tokens // 2, width), BF16)
    full = pltpu.VMEM((tokens, width), BF16)
    return [half, half, half, full, full]


def row_sum_sems():
    dma = pltpu.SemaphoreType.DMA
    return [dma((3,)), dma((3,)), dma((2,)), dma((2,))]


class RowSumQuarter:
    def __init__(self, at, chunk, keep, a_send, a_recv, c_recv, d_send, d_recv, m_send, m_recv, x_send, x_recv):
        self.at, self.chunk, self.keep = at, chunk, keep
        self.a_send, self.a_recv, self.c_recv = a_send, a_recv, c_recv
        self.d_send, self.d_recv = d_send, d_recv
        self.sems = (m_send, m_recv, x_send, x_recv)

    def a(self, s):
        m_send, m_recv, _, _ = self.sems
        return remote(self.a_send.at[s], self.a_recv.at[s], m_send.at[0, s], m_recv.at[0, s], row=self.at.mate)

    def d(self, s):
        m_send, m_recv, _, _ = self.sems
        return remote(self.d_send.at[s], self.d_recv.at[s], m_send.at[1, s], m_recv.at[1, s], row=self.at.mate)

    def b(self, s):
        _, _, x_send, x_recv = self.sems
        return remote(self.a_recv.at[s], self.c_recv.at[s], x_send.at[s], x_recv.at[s], row=self.at.across)

    def split(self, s, value, spot, own):
        at, chunk = self.at, self.chunk
        chunk[...] = value

        def quarter(q):
            return chunk[pl.ds(pl.multiple_of(q * 128, 128), 128), :]

        self.a_send[s, :, spot] = quarter(at.diag).astype(BF16)
        self.keep[:, spot] = quarter(at.across)
        self.d_send[s, :, spot] = quarter(at.mate).astype(BF16)
        own[s, :, spot] = quarter(at.row).astype(own.dtype)

    def give(self, s):
        self.a(s).start()
        self.d(s).start()
        self.a(s).wait_recv()

        def one(here):
            self.a_recv[s, here] = (self.keep[here, :] + self.a_recv[s, here].astype(F32)).astype(BF16)

        in_rows(128, 16, one)
        self.b(s).start()

    def finish(self, s):
        self.d(s).wait_recv()
        self.b(s).wait_recv()

    def close(self):
        def one(s, _):
            self.a(s).wait_send()
            self.b(s).wait_send()
            self.d(s).wait_send()
            return 0

        lax.fori_loop(0, 4, one, 0)


class RowGather:
    def __init__(self, at, own, slot, sems):
        self.at, self.own, self.slot = at, own, slot
        self.m_send, self.m_recv, self.x_send, self.x_recv, self.f_send, self.f_recv, self.local = (*sems, None)[:7]

    def to_mate(self, s):
        return remote(self.own(s), self.slot(s, self.at.row), self.m_send.at[s], self.m_recv.at[s], row=self.at.mate)

    def to_across(self, s):
        return remote(self.own(s), self.slot(s, self.at.row), self.x_send.at[s], self.x_recv.at[s], row=self.at.across)

    def pass_on(self, s):
        here = self.slot(s, self.at.across)
        return remote(here, here, self.f_send.at[s], self.f_recv.at[s], row=self.at.mate)

    def move_own(self, s):
        return pltpu.make_async_copy(self.own(s), self.slot(s, self.at.row), self.local.at[s])

    def near(self, s):
        self.to_mate(s).start()
        if self.local is not None:
            self.move_own(s).start()

    def wait_near(self, s):
        here = self.slot(s, self.at.mate)
        remote(here, here, self.m_send.at[s], self.m_recv.at[s], row=self.at.mate).wait_recv()
        if self.local is not None:
            self.move_own(s).wait()

    def take_across(self, s):
        here = self.slot(s, self.at.across)
        remote(here, here, self.x_send.at[s], self.x_recv.at[s], row=self.at.across).wait_recv()
        self.pass_on(s).start()

    def wait_diag(self, s):
        here = self.slot(s, self.at.diag)
        remote(here, here, self.f_send.at[s], self.f_recv.at[s], row=self.at.mate).wait_recv()

    def close_one(self, s):
        self.to_mate(s).wait_send()
        self.to_across(s).wait_send()
        self.pass_on(s).wait_send()

    def close(self, count):
        def one(s, _):
            self.close_one(s)
            return 0

        lax.fori_loop(0, count, one, 0)


class WeightGather:
    def __init__(self, at, pairs, own, full, sems):
        self.at, self.pairs, self.own, self.full = at, pairs, own, full
        self.m_send, self.m_recv, self.x_send, self.x_recv, self.y_send, self.y_recv = sems[:6]
        self.f_send, self.f_recv, self.g_send, self.g_recv = sems[6:]
        self.step = full.shape[2] // 4
        self.mine = lax.axis_index("dp") if pairs == 2 else None

    def rows(self, j):
        return pl.ds(j * self.step, self.step)

    def piece(self, which, row, j):
        return self.full.at[which, row, self.rows(j)]

    def held(self):
        return (self.mine,) if self.pairs == 2 else (0, 1)

    def near(self, which, row):
        here = self.full.at[which, row]
        return remote(self.own[which], here, self.m_send.at[which], self.m_recv.at[which], row=self.at.mate)

    def over(self, which, row, j, src=None):
        here = self.piece(which, row, j)
        lane = 0 if self.pairs == 2 else which
        src = here if src is None else src
        return remote(src, here, self.x_send.at[lane, j], self.x_recv.at[lane, j], row=self.at.across)

    def hand(self, which, j):
        here = self.piece(which, self.at.across, j)
        return remote(here, here, self.y_send.at[j], self.y_recv.at[j], dp=self.at.pair(2, 1))

    def pass_first(self, which, row, j):
        here = self.piece(which, row, j)
        lane = 0 if self.pairs == 2 else which
        return remote(here, here, self.f_send.at[lane, j], self.f_recv.at[lane, j], row=self.at.mate)

    def pass_second(self, which, row, j):
        here = self.piece(which, row, j)
        return remote(here, here, self.g_send.at[j], self.g_recv.at[j], row=self.at.mate)

    def begin(self):
        for i in range(2):
            self.near(i, self.at.row).start()

    def send(self, j):
        for which in range(2):
            copy = self.over(which, self.at.row, j, self.own[which].at[self.rows(j)])
            if self.pairs == 2:
                pl.when(self.mine == which)(copy.start)
            else:
                copy.start()

    def forward(self, j):
        for which in self.held():
            self.over(which, self.at.across, j).wait_recv()
            if self.pairs == 2:
                self.hand(which, j).start()
            self.pass_first(which, self.at.across, j).start()

    def finish(self, j):
        if self.pairs == 2:
            self.hand(1 - self.mine, j).wait_recv()
            self.pass_second(1 - self.mine, self.at.across, j).start()

    def close(self):
        for i in range(2):
            self.near(i, self.at.mate).wait_recv()
            self.near(i, self.at.row).wait_send()
        for j in range(4):
            for which in self.held():
                self.over(which, self.at.row, j).wait_send()
                self.pass_first(which, self.at.diag, j).wait_recv()
                self.pass_first(which, self.at.across, j).wait_send()
            if self.pairs == 2:
                self.hand(self.mine, j).wait_send()
                self.pass_second(1 - self.mine, self.at.diag, j).wait_recv()
                self.pass_second(1 - self.mine, self.at.across, j).wait_send()


def weight_gather_sems(pairs):
    dma = pltpu.SemaphoreType.DMA
    lanes = 1 if pairs == 2 else 2
    return [
        dma((2,)), dma((2,)), dma((lanes, 4)), dma((lanes, 4)), dma((4,)), dma((4,)),
        dma((lanes, 4)), dma((lanes, 4)), dma((4,)), dma((4,)),
    ]


class ColSum:
    def __init__(self, at, product, sent, got, extra, sends, recvs, extra_recvs):
        self.at, self.product, self.sent, self.got, self.extra = at, product, sent, got, extra
        self.sends, self.recvs, self.extra_recvs = sends, recvs, extra_recvs
        self.size = product.shape[0] // 4

    def part(self, h):
        return pl.ds(h * self.size, self.size)

    def up(self, s, h):
        return remote(
            self.sent.at[s, self.part(h)], self.got.at[s, self.part(h)],
            self.sends.at[s, h], self.recvs.at[s, h], col=self.at.above,
        )

    def down(self, s, h):
        return remote(
            self.sent.at[s, self.part(h)], self.got.at[s, self.part(h)],
            self.sends.at[s, h], self.recvs.at[s, h], col=self.at.below,
        )

    def last_down(self, s, h):
        return remote(
            self.sent.at[s, self.part(h)], self.extra.at[self.part(h)],
            self.sends.at[s, h], self.extra_recvs.at[h], col=self.at.below,
        )

    def step(self, s, halves=(0, 1)):
        col, product = self.at.col, self.product
        for h in [2 * half + part for half in halves for part in range(2)]:
            @pl.when(((s >= col) & (col > 0)) | ((s < col) & (col < 3)))
            def _():
                self.up(s, h).wait_recv()

                def add(here):
                    product[here, :] += self.got[s, here].astype(F32)

                in_rows(self.size, 64, add, h * self.size)

            @pl.when((s == col) & (col < 3))
            def _():
                self.last_down(s, h).wait_recv()

                def add(here):
                    product[here, :] += self.extra[here].astype(F32)

                in_rows(self.size, 64, add, h * self.size)

            @pl.when(s != col)
            def _():
                def cast(here):
                    self.sent[s, here] = product[here, :].astype(BF16)

                in_rows(self.size, 64, cast, h * self.size)

            pl.when(s > col)(lambda: self.up(s, h).start())
            pl.when(s < col - 1)(lambda: self.down(s, h).start())
            pl.when(s == col - 1)(lambda: self.last_down(s, h).start())

    def close(self):
        def one(s, _):
            for h in range(4):
                pl.when(s != self.at.col)(lambda: self.up(s, h).wait_send())
            return 0

        lax.fori_loop(0, 4, one, 0)


def far_first(col, j):
    first = jnp.where(col < 2, 3, 0)
    near = jnp.where(col < 2, 2, 1)
    partner = jnp.where(lax.rem(col, 2) == 0, col + 1, col - 1)
    end = (col == 0) | (col == 3)
    return (first, jnp.where(end, near, partner), jnp.where(end, partner, near), col)[j]


def near_first(at, j):
    first = jnp.where(at.col < 2, 3, 0)
    near = jnp.where(at.col < 2, 2, 1)
    partner = jnp.where(lax.rem(at.col, 2) == 0, at.col + 1, at.col - 1)
    mine = at.paired
    return (
        jnp.where(mine, partner, first),
        jnp.where(mine, first, near),
        jnp.where(mine, near, partner),
        at.col,
    )[j]


def turn_tables(length):
    rates = THETA ** (-np.arange(HEAD_SIZE // 2) * 2.0 / HEAD_SIZE)
    angles = np.arange(length)[:, None] * rates[None, :]
    cos, sin = np.cos(angles), np.sin(angles)
    return (
        np.concatenate([cos, cos], axis=1).astype(np.float32),
        np.concatenate([-sin, sin], axis=1).astype(np.float32),
    )


def swap_halves(value):
    return pltpu.roll(value, HEAD_SIZE // 2, 1)


def head(ref, index):
    return ref[:, index * HEAD_SIZE : (index + 1) * HEAD_SIZE]


def root_scale(raw):
    return lax.rsqrt(jnp.mean(raw * raw, axis=1, keepdims=True) + EPSILON)


def attend(q_heads, groups, qkv, seg_row, cos, sin, q_gain, k_gain, o, qa, ka, va, probs, done):
    kv = q_heads // groups
    tokens = qkv.shape[0]
    half = tokens // 2
    seg_line = seg_row[...].astype(F32)
    seg_column = jnp.broadcast_to(seg_line, (128, tokens)).T[:, :1]

    def turned(index, gain):
        raw = head(qkv, index)
        normed = raw * root_scale(raw) * gain[...]
        return (normed * cos[...] + swap_halves(normed) * sin[...]).astype(BF16)

    for i in range(q_heads):
        qa[:, i * HEAD_SIZE : (i + 1) * HEAD_SIZE] = turned(i, q_gain)
    for i in range(kv):
        ka[:, i * HEAD_SIZE : (i + 1) * HEAD_SIZE] = turned(q_heads + i, k_gain)
        va[:, i * HEAD_SIZE : (i + 1) * HEAD_SIZE] = head(qkv, q_heads + kv + i).astype(BF16)
    for block in range(2):
        rows = slice(block * half, (block + 1) * half)
        keys = (block + 1) * half
        spot = lax.broadcasted_iota(jnp.int32, (half, keys), 0) + block * half
        other = lax.broadcasted_iota(jnp.int32, (half, keys), 1)
        allowed = (other <= spot) & (seg_column[rows, :] == seg_line[:, :keys])
        for i in range(q_heads):
            j = i // groups
            dots = lax.dot_general(
                head(qa, i)[rows], head(ka, j)[:keys], (((1,), (1,)), ((), ())), preferred_element_type=F32
            ) * (1.0 / math.sqrt(HEAD_SIZE))
            scores = jnp.where(allowed, dots, MASKED)
            expo = jnp.exp(scores - jnp.max(scores, axis=1, keepdims=True))
            p = expo / jnp.sum(expo, axis=1, keepdims=True)
            probs[i, rows, :keys] = p.astype(BF16)
            mixed = jnp.dot(p.astype(BF16), head(va, j)[:keys], preferred_element_type=F32)
            o[rows, i * HEAD_SIZE : (i + 1) * HEAD_SIZE] = mixed.astype(BF16)
        done(block)


def front_kernel(pairs, q_heads, groups, model_width, *refs):
    refs = list(refs)

    def take(count):
        found = refs[:count]
        del refs[:count]
        return found

    (x_ref, seg_row, q_gain, k_gain, gain_one, gain_two) = take(6)
    late = take(8)
    (w_gate, w_up) = take(2)
    (scale_one, hidden, scale_two, ffn_in) = take(4)
    kept_out = take(5)
    (dact_out, xn_out, gy_out, mixed_out, full) = take(5)
    (w_query, w_key, w_value, w_out, w_down, cos, sin) = late_held = take(7)
    (qkv, qa, ka, va, probs) = kept = take(5)
    (dact,) = take(1)
    (x_wide, scales, xn_wide, gy_wide, mixed_wide, mixed, product, chunk, keep) = take(9)
    total_bufs = take(2)
    second_bufs = take(2)
    moved = take(5)
    moved_q = take(5)
    chain = take(3)
    x_sems, gy_sems = take(2), take(2)
    (local,) = take(1)
    moved_sems, moved_q_sems = take(4), take(4)
    mixed_sems = take(7)
    chain_sems = take(3)
    total_sems, second_sems = take(2), take(2)
    full_sems = take(10)
    late_sems, kept_sems, dact_sems = take(3)
    scale_sems = take(2)

    at = Ends()
    gain_spot = pl.ds(pl.multiple_of(at.row * x_ref.shape[1], x_ref.shape[1]), x_ref.shape[1])
    fetch = Fetch([*zip(late[1:], late_held), (late[0], gy_wide.at[at.col])], late_sems)
    fetch.start()
    keep_saved = Fetch(list(zip(kept, kept_out)), kept_sems)
    full_gather = WeightGather(at, pairs, (w_gate, w_up), full, full_sems)
    tokens, feats = x_ref.shape
    first_total = RowTotal(at, *total_bufs, *total_sems)
    second_total = RowTotal(at, *second_bufs, *second_sems)
    x_gather = ColGather(at, x_wide, *x_sems)
    scale_share = LineShare(at, scales, *scale_sems)
    gy_gather = ColGather(at, gy_wide, *gy_sems)
    row_sum = RowSumWhole(at, product, qkv, *moved, *moved_sems)
    quarter_sum = RowSumQuarter(at, chunk, keep, *moved_q, *moved_q_sems)
    half = tokens // 2
    mixes = RowGather(
        at, lambda h: mixed.at[pl.ds(h * half, half)], lambda h, q: mixed_wide.at[q, pl.ds(h * half, half)], mixed_sems
    )
    out_sum = ColSum(at, hidden, *chain, *chain_sems)

    x_wide[at.col] = x_ref[...]
    at.greet(pairs if pairs == 2 else 0, True)
    x_gather.arrive(0)
    stream = x_ref[...].astype(F32)
    first_total.start(jnp.sum(stream * stream, axis=1, keepdims=True))
    full_gather.begin()
    full_gather.send(0)
    scales[at.col] = lax.rsqrt(first_total.total() / model_width + EPSILON)
    scale_share.start()
    scale_one[...] = as_column(scales[at.col])

    def project(s):
        scale_share.wait(s)
        scale = as_column(scales[s])
        xn_wide[s] = (x_wide[s].astype(F32) * scale * gain_one[:, gain_spot]).astype(BF16)
        base = 0
        for w in (w_query, w_key, w_value):
            size = w.shape[1]
            product[:, base : base + size] = jnp.dot(xn_wide[s], w[...], preferred_element_type=F32)
            base += size
        row_sum.give(s)

    def back_down(s):
        size = chunk.shape[1]

        def one(j, _):
            cols = pl.ds(pl.multiple_of(j * size, size), size)
            value = lax.dot_general(
                gy_wide[s], w_down[cols, :], (((1,), (1,)), ((), ())), preferred_element_type=F32
            )
            quarter_sum.split(s, value, cols, dact)
            return 0

        lax.fori_loop(0, w_down.shape[0] // size, one, 0)
        quarter_sum.give(s)

    def keep_dact(s):
        return pltpu.make_async_copy(dact.at[s], dact_out.at[s], dact_sems.at[s])

    def end_down(s):
        quarter_sum.finish(s)

        def add(here):
            dact[s, here] += moved_q[2][s, here].astype(F32) + moved_q[4][s, here].astype(F32)

        in_rows(128, 16, add)
        keep_dact(s).start()

    def send_gy(dist):
        @pl.when((at.col == dist) & (at.col < 3))
        def _():
            gy_gather.send_up()

        @pl.when((at.col == 3 - dist) & (at.col > 0))
        def _():
            gy_gather.send_down()

    def out_step(j, halves=(0, 1)):
        s = near_first(at, j)
        for h in halves:
            rows = pl.ds(h * half, half)
            hidden[rows, :] = jnp.dot(mixed_wide[s, rows, :], w_out[...], preferred_element_type=F32)
        out_sum.step(s, halves)

    mid = jnp.logical_not(at.end)
    fetch.wait()
    send_gy(0)
    x_gather.loop(0, project)
    back_down(at.col)
    full_gather.send(1)
    for dist in range(1, 4):
        x_gather.arrive(dist)
        send_gy(dist)
        x_gather.loop(dist, project)
        if dist == 1:
            full_gather.forward(0)

    @pl.when(mid)
    def _():
        gy_gather.arrive(1)

    row_sum.finish()

    def send_mixed(h):
        mixes.to_across(h).start()
        mixes.near(h)

    attend(q_heads, groups, qkv, seg_row, cos, sin, q_gain, k_gain, mixed, qa, ka, va, probs, send_mixed)
    keep_saved.start()
    full_gather.send(2)
    full_gather.forward(1)

    @pl.when(mid)
    def _():
        gy_gather.arrive(2)

    for h in range(2):
        mixes.wait_near(h)

    @pl.when(at.end)
    def _():
        out_step(0)
        pl.when(jnp.logical_not(at.paired))(lambda: out_step(1))
        gy_gather.arrive(1)

    full_gather.send(3)
    gy_gather.loop(1, back_down)
    for h in range(2):
        mixes.take_across(h)
        mixes.wait_diag(h)

        @pl.when(at.end)
        def _():
            pl.when(at.paired)(lambda: out_step(1, (h,)))
            out_step(2, (h,))

    @pl.when(at.end)
    def _():
        gy_gather.arrive(2)

    paired = mid & at.paired
    unpaired = mid & jnp.logical_not(at.paired)

    @pl.when(paired)
    def _():
        out_step(1, (0,))
        out_step(0, (0,))

    pl.when(unpaired)(lambda: out_step(0))
    gy_gather.loop(2, back_down)
    full_gather.forward(2)

    @pl.when(paired)
    def _():
        out_step(1, (1,))
        out_step(0, (1,))

    pl.when(unpaired)(lambda: out_step(1))

    @pl.when(mid)
    def _():
        full_gather.forward(3)
        out_step(2)

    @pl.when(at.end)
    def _():
        gy_gather.arrive(3)

    gy_gather.loop(3, back_down)
    full_gather.finish(0)
    full_gather.finish(1)
    pl.when(at.end)(lambda: full_gather.forward(3))
    wides = [
        pltpu.make_async_copy(src, dst, local.at[i])
        for i, (src, dst) in enumerate(((xn_wide, xn_out), (gy_wide, gy_out), (mixed_wide, mixed_out)))
    ]
    for copy in wides:
        copy.start()
    full_gather.finish(2)
    for dist in range(3):
        gy_gather.loop(dist, end_down)
    full_gather.finish(3)
    out_step(3)

    def residual(here):
        hidden[here, :] += x_ref[here, :].astype(F32)

    in_rows(tokens, 64, residual)
    value = hidden[...]
    second_total.start(jnp.sum(value * value, axis=1, keepdims=True))
    gy_gather.loop(3, end_down)
    scale = lax.rsqrt(second_total.finish() / model_width + EPSILON)
    scale_two[...] = scale
    ffn_in[...] = (hidden[...] * scale * gain_two[:, gain_spot]).astype(BF16)

    keep_saved.wait()
    for s in range(4):
        keep_dact(s).wait()
    full_gather.close()
    scale_share.close()
    x_gather.close()
    gy_gather.close()
    row_sum.close()
    quarter_sum.close()
    mixes.close(2)
    out_sum.close()
    for copy in wides:
        copy.wait()


def col_gather_sems():
    return [pltpu.SemaphoreType.DMA((2, 4, 2)), pltpu.SemaphoreType.DMA((4, 2))]


def chain_scratch(tokens, feats):
    return [
        pltpu.VMEM((4, tokens, feats), BF16), pltpu.VMEM((4, tokens, feats), BF16), pltpu.VMEM((tokens, feats), BF16),
    ]


def chain_sems():
    dma = pltpu.SemaphoreType.DMA
    return [dma((4, 4)), dma((4, 4)), dma((4,))]


def front(pairs, q_heads, groups, model_width, number, x, gy, weights, segments, tables, gains, ffn_weights):
    tokens, feats = x.shape
    w_query, w_key, w_value, w_out, w_down = weights
    width = w_query.shape[1] + w_key.shape[1] + w_value.shape[1]
    q_width, k_width, ff = w_query.shape[1], w_key.shape[1], w_down.shape[0]
    dma = pltpu.SemaphoreType.DMA
    any_spec, vmem = pl.BlockSpec(memory_space=pl.ANY), pl.BlockSpec(memory_space=pltpu.VMEM)
    shape = jax.ShapeDtypeStruct
    wide = pltpu.VMEM((4, tokens, feats), BF16)
    late = (*weights, *tables[:2])
    kept = [
        shape((tokens, width), F32),
        shape((tokens, q_width), BF16),
        shape((tokens, k_width), BF16),
        shape((tokens, k_width), BF16),
        shape((q_heads, tokens, tokens), BF16),
    ]
    dact = shape((4, tokens // 4, ff), F32)
    return pl.pallas_call(
        functools.partial(front_kernel, pairs, q_heads, groups, model_width),
        out_shape=(
            shape((tokens, 1), F32),
            shape((tokens, feats), F32),
            shape((tokens, 1), F32),
            shape((tokens, feats), BF16),
            *kept,
            dact,
            shape((4, tokens, feats), BF16),
            shape((4, tokens, feats), BF16),
            shape((4, tokens, q_width), BF16),
            shape((2, 4, *ffn_weights[0].shape), BF16),
        ),
        in_specs=[vmem] * 6 + [any_spec] * 10,
        out_specs=tuple([vmem] * 4 + [any_spec] * 10),
        scratch_shapes=[held(array) for array in late]
        + [held(array) for array in kept]
        + [
            held(dact),
            wide,
            pltpu.VMEM((4, 8, tokens), F32),
            wide,
            wide,
            pltpu.VMEM((4, tokens, q_width), BF16),
            pltpu.VMEM((tokens, q_width), BF16),
            pltpu.VMEM((tokens, width), F32),
            pltpu.VMEM((tokens, 512), F32),
            pltpu.VMEM((tokens // 4, ff), F32),
        ]
        + row_total_scratch(tokens) * 2
        + row_sum_scratch(tokens, width)
        + [pltpu.VMEM((4, tokens // 4, ff), BF16)] * 5
        + chain_scratch(tokens, feats)
        + col_gather_sems() * 2
        + [dma((3,))]
        + row_sum_sems()
        + [dma((2, 4)), dma((2, 4)), dma((4,)), dma((4,))]
        + [dma((2,))] * 7
        + chain_sems()
        + row_total_sems() * 2
        + weight_gather_sems(pairs)
        + [dma((8,)), dma((5,)), dma((4,)), dma((3,)), dma((4,))],
        compiler_params=pltpu.CompilerParams(
            collective_id=number, has_side_effects=True, vmem_limit_bytes=VMEM_LIMIT
        ),
        name="front",
    )(x, segments, *tables[2:], *gains, gy, *late, *ffn_weights)


def across_rows(left, right):
    return lax.dot_general(left, right, (((0,), (0,)), ((), ())), preferred_element_type=F32)


def attend_back(
    q_heads, groups, grad, qkv, qa, ka, va, probs, cos, sin, q_gain, k_gain, out, q_part, k_part, dq, dk, dv, done
):
    kv = q_heads // groups
    tokens = qkv.shape[0]
    half = tokens // 2
    scale = 1.0 / math.sqrt(HEAD_SIZE)
    dk[...] = jnp.zeros_like(dk)
    dv[...] = jnp.zeros_like(dv)
    q_part[...] = jnp.zeros_like(q_part)
    k_part[...] = jnp.zeros_like(k_part)

    def back(turned, index, gain, rows):
        raw = head(qkv, index)[rows]
        scales = root_scale(raw)
        normed = turned * cos[rows, :] - swap_halves(turned) * sin[rows, :]
        part = jnp.sum(normed * raw * scales, axis=0, keepdims=True)
        weighted = normed * gain[...]
        inner = jnp.sum(weighted * raw, axis=1, keepdims=True)
        result = scales * weighted - raw * (scales * scales * scales) * inner * (1.0 / HEAD_SIZE)
        out[rows, index * HEAD_SIZE : (index + 1) * HEAD_SIZE] = result.astype(BF16)
        return part

    for block in (1, 0):
        rows = slice(block * half, (block + 1) * half)
        keys = (block + 1) * half
        for i in range(q_heads):
            j = i // groups
            spot = slice(j * HEAD_SIZE, (j + 1) * HEAD_SIZE)
            pb = probs[i, rows, :keys]
            p = pb.astype(F32)
            g = head(grad, i)[rows].astype(BF16)
            dv[:keys, spot] += across_rows(pb, g)
            dp = lax.dot_general(
                g, head(va, j)[:keys], (((1,), (1,)), ((), ())), preferred_element_type=F32
            )
            ds = (p * (dp - jnp.sum(p * dp, axis=1, keepdims=True))).astype(BF16)
            dq[rows, i * HEAD_SIZE : (i + 1) * HEAD_SIZE] = (
                jnp.dot(ds, head(ka, j)[:keys], preferred_element_type=F32) * scale
            )
            dk[:keys, spot] += across_rows(ds, head(qa, i)[rows]) * scale
        q_part[...] += sum(back(head(dq, i)[rows], i, q_gain, rows) for i in range(q_heads))
        k_part[...] += sum(back(head(dk, i)[rows], q_heads + i, k_gain, rows) for i in range(kv))
        for i in range(kv):
            spot = (q_heads + kv + i) * HEAD_SIZE
            out[rows, spot : spot + HEAD_SIZE] = head(dv, i)[rows].astype(BF16)
        done(block)


def act_copy(src, dst, at, j, sem):
    s = far_first(at.col, j)
    if j < 1:
        return pltpu.make_async_copy(src.at[s], dst.at[s], sem)
    return pltpu.make_async_copy(src.at[s, at.row], dst.at[s, at.row], sem)


def weight_grad(out, left, right, send=None):
    def block(here):
        total = None
        for s in range(4):
            term = across_rows(left(s, here), right(s))
            total = term if total is None else total + term
        out[here, :] = total.astype(BF16)
        if send is not None:
            send(here).start()

    in_rows(out.shape[0], 256, block)


def middle_kernel(pairs, *refs):
    refs = list(refs)

    def take(count):
        found = refs[:count]
        del refs[:count]
        return found

    (hn, w_gate, w_up, dact_in, full) = take(5)
    (dhn, act_out, gate_n, up_n) = take(4)
    others = take(1) if pairs == 2 else []
    (hn_wide, hn_full, weights, dact, gate_up, gate_wide, up_wide, act_wide, n_gate, n_up) = take(10)
    chain = take(3)
    hn_sems = take(2)
    (full_sem, share_send, share_recv) = take(3)
    gate_sems, up_sems, act_sems = take(6), take(6), take(6)
    chain_sems_ = take(3)
    (local, y_send, y_recv) = take(3)

    at = Ends()
    ff = w_gate.shape[1]
    quarter = hn.shape[0] // 4
    gather = ColGather(at, hn_wide, *hn_sems)
    loads = [pltpu.make_async_copy(dact_in, dact, full_sem.at[2, 0])]
    for which, own in enumerate((w_gate, w_up)):
        for i, r in enumerate((at.mate, at.across, at.diag, at.row)):
            src = own if i == 3 else full.at[which, r]
            loads.append(pltpu.make_async_copy(src, weights.at[which, r], full_sem.at[which, i]))
    for load in loads:
        load.start()
    gates = RowGather(at, lambda s: gate_wide.at[s, at.row], lambda s, q: gate_wide.at[s, q], gate_sems)
    ups = RowGather(at, lambda s: up_wide.at[s, at.row], lambda s, q: up_wide.at[s, q], up_sems)
    acts = RowGather(at, lambda s: act_wide.at[s, at.row], lambda s, q: act_wide.at[s, q], act_sems)
    back_sum = ColSum(at, dhn, *chain, *chain_sems_)

    hn_wide[at.col] = hn[...]
    at.greet(pairs if pairs == 2 else 0)

    peers = (at.mate, at.across, at.diag)

    def share(s):
        hn_full[s, at.row] = hn_wide[s, pl.ds(pl.multiple_of(at.row * quarter, quarter), quarter)]
        for i, peer in enumerate(peers):
            theirs = hn_wide.at[s, pl.ds(pl.multiple_of(peer * quarter, quarter), quarter)]
            remote(theirs, hn_full.at[s, at.row], share_send.at[s, i], share_recv.at[s, i], row=peer).start()

    def hidden_units(s):
        for i, peer in enumerate(peers):
            here = hn_full.at[s, peer]
            remote(here, here, share_send.at[s, i], share_recv.at[s, i], row=peer).wait_recv()
        size = gate_up.shape[2]

        def some(j, _):
            cols = pl.ds(pl.multiple_of(j * size, size), size)
            for which in range(2):
                total = None
                for r in range(4):
                    term = jnp.dot(hn_full[s, r], weights[which, r, :, cols], preferred_element_type=F32)
                    total = term if total is None else total + term
                gate_up[which] = total

            def one(here):
                gate, up = gate_up[0, here], gate_up[1, here]
                grad = dact[s, here, cols]
                sigmoid = jax.nn.sigmoid(gate)
                silu = gate * sigmoid
                act_wide[s, at.row, here, cols] = (silu * up).astype(BF16)
                gate_wide[s, at.row, here, cols] = (
                    grad * up * (sigmoid * (1.0 + gate * (1.0 - sigmoid)))
                ).astype(BF16)
                up_wide[s, at.row, here, cols] = (grad * silu).astype(BF16)

            in_rows(quarter, 16, one)
            return 0

        lax.fori_loop(0, ff // size, some, 0)
        gates.to_across(s).start()
        gates.near(s)
        ups.near(s)

    def close_share(s):
        for i, peer in enumerate(peers):
            here = hn_full.at[s, peer]
            remote(here, here, share_send.at[s, i], share_recv.at[s, i], row=peer).wait_send()

    def rows_of(ref, s):
        return ref[s].reshape(4 * quarter, ff)

    def back(j, halves=(0, 1)):
        s = far_first(at.col, j)
        contract = (((1,), (1,)), ((), ()))
        for h in halves:
            two = pl.ds(2 * h, 2)
            dhn[pl.ds(2 * h * quarter, 2 * quarter), :] = lax.dot_general(
                gate_wide[s, two].reshape(2 * quarter, ff), weights[0, at.row], contract, preferred_element_type=F32
            ) + lax.dot_general(
                up_wide[s, two].reshape(2 * quarter, ff), weights[1, at.row], contract, preferred_element_type=F32
            )

    def back_and_push(j):
        for h in range(2):
            back(j, (h,))
            back_sum.step(far_first(at.col, j), (h,))

    def arrive(some, j):
        s = far_first(at.col, j)
        some.wait_near(s)
        some.take_across(s)
        some.wait_diag(s)

    def left(s, here):
        return hn_wide[s, :, here]

    mid = jnp.logical_not(at.end)
    gather.arrive(0)
    gather.loop(0, share)
    for load in loads:
        load.wait()
    gather.loop(0, hidden_units)
    gather.arrive(1)
    gather.loop(1, share)
    gather.arrive(2)
    gather.loop(2, share)
    gather.loop(1, hidden_units)
    gather.arrive(3)
    gather.loop(3, share)
    gather.loop(2, hidden_units)
    gather.loop(3, hidden_units)
    for j in range(4):
        ups.to_across(far_first(at.col, j)).start()
    acts.near(far_first(at.col, 0))
    acts.to_across(far_first(at.col, 0)).start()
    keep_acts = [
        act_copy(act_wide, act_out, at, j, local.at[2 + j]) for j in range(4)
    ]
    for copy in keep_acts[1:]:
        copy.start()
    for j in range(4):
        arrive(gates, j)

    def to_other(here=slice(None)):
        return remote(n_gate.at[here], others[0].at[here], y_send.at[0], y_recv.at[0], dp=at.pair(2, 1))

    weight_grad(n_gate, left, lambda s: rows_of(gate_wide, s), to_other if pairs == 2 else None)
    keep_gate = pltpu.make_async_copy(n_gate, gate_n, local.at[0])
    keep_gate.start()
    arrive(ups, 0)
    for j in range(3):
        pl.when(at.end)(lambda: back_and_push(j))
        pl.when(mid)(lambda: back(j))
        arrive(ups, j + 1)
        pl.when(mid)(lambda: back_sum.step(far_first(at.col, j)))
    weight_grad(n_up, left, lambda s: rows_of(up_wide, s))
    keep_up = pltpu.make_async_copy(n_up, up_n, local.at[1])
    keep_up.start()
    back(3)
    arrive(acts, 0)
    keep_acts[0].start()
    back_sum.step(at.col)

    gather.close()
    for dist in range(4):
        gather.loop(dist, close_share)
    gates.close(4)
    ups.close(4)
    acts.close_one(far_first(at.col, 0))
    back_sum.close()
    for copy in keep_acts:
        copy.wait()
    keep_gate.wait()
    keep_up.wait()
    if pairs == 2:
        to_other().wait()


def middle(pairs, number, hn, w_gate, w_up, dact, full):
    tokens, feats = hn.shape
    ff = w_gate.shape[1]
    quarter = tokens // 4
    dma = pltpu.SemaphoreType.DMA
    any_spec, vmem = pl.BlockSpec(memory_space=pl.ANY), pl.BlockSpec(memory_space=pltpu.VMEM)
    shape = jax.ShapeDtypeStruct
    narrow = shape((feats, ff), BF16)
    others = 1 if pairs == 2 else 0
    out = pl.pallas_call(
        functools.partial(middle_kernel, pairs),
        out_shape=tuple(
            [shape((tokens, feats), F32), shape((4, 4, quarter, ff), BF16), narrow, narrow] + [narrow] * others
        ),
        in_specs=[vmem] + [any_spec] * 4,
        out_specs=tuple([vmem] + [any_spec] * (3 + others)),
        scratch_shapes=[
            pltpu.VMEM((4, tokens, feats), BF16),
            pltpu.VMEM((4, 4, quarter, feats), BF16),
            pltpu.VMEM((2, 4, feats, ff), BF16),
            held(dact),
            pltpu.VMEM((2, quarter, 512), F32),
            pltpu.VMEM((4, 4, quarter, ff), BF16),
            pltpu.VMEM((4, 4, quarter, ff), BF16),
            pltpu.VMEM((4, 4, quarter, ff), BF16),
            pltpu.VMEM((feats, ff), BF16),
            pltpu.VMEM((feats, ff), BF16),
        ]
        + chain_scratch(tokens, feats)
        + col_gather_sems()
        + [dma((3, 4)), dma((4, 3)), dma((4, 3))]
        + [dma((4,))] * 18
        + chain_sems()
        + [dma((6,)), dma((1,)), dma((1,))],
        compiler_params=pltpu.CompilerParams(
            collective_id=number, has_side_effects=True, vmem_limit_bytes=VMEM_LIMIT
        ),
        name="middle",
    )(hn, w_gate, w_up, dact, full)
    return out[:4], out[4:]


def tail_kernel(pairs, q_heads, groups, *refs):
    refs = list(refs)

    def take(count):
        found = refs[:count]
        del refs[:count]
        return found

    (w_out, q_gain, k_gain, dhn, hidden, scale_two, gain_two, gy, x_ref, scale_one, gain_one) = take(11)
    late = take(12)
    (gy_wide, mixed_wide, normed_wide, up_n) = take(4)
    (in_grad, layer_out, one_grad, two_grad, q_grad, k_grad) = take(6)
    kept_out = take(5)
    others = take(6) if pairs == 2 else []
    (w_down, w_query, w_key, w_value, qkv, qa, ka, va, probs, cos, sin) = late_held = take(11)
    (da_wide, act_wide, dqkv, dqkv_wide, held_wide, product, grad_mixed, dq, dk, dv, *narrow) = take(15)
    (dh, q_part, k_part, packet, packet_got, by_row, summed) = take(7)
    first_bufs, last_bufs = take(2), take(2)
    moved = take(5)
    down_bufs, dxn_bufs = take(3), take(3)
    (g_send, g_recv, local, y_send, y_recv, late_sems) = take(6)
    moved_sems = take(4)
    act_sems, dqkv_sems = take(6), take(7)
    down_sems, dxn_sems = take(3), take(3)
    first_sems, last_sems = take(2), take(2)
    (p_send, p_recv, r_send, r_recv) = take(4)

    at = Ends()
    feats = dhn.shape[1]
    model_width = 4 * feats
    gain_spot = pl.ds(pl.multiple_of(at.row * feats, feats), feats)
    fetch_acts = [act_copy(late[0], act_wide, at, j, local.at[8 + j]) for j in range(4)]
    for copy in reversed(fetch_acts):
        copy.start()
    fetch = Fetch(list(zip(late[1:], late_held)), late_sems)
    fetch.start()
    first_total = RowTotal(at, *first_bufs, *first_sems)
    last_total = RowTotal(at, *last_bufs, *last_sems)
    at.greet(pairs, True, True)

    def pair_copy(index, here=slice(None)):
        return remote(
            narrow[index].at[here], others[index].at[here], y_send.at[index], y_recv.at[index],
            dp=1 - lax.axis_index("dp"),
        )

    n_down, n_out, n_query, n_key, n_value = narrow
    narrow = [up_n, *narrow]

    def to_pair(index):
        return functools.partial(pair_copy, index) if pairs == 2 else None

    def load(index, src):
        return pltpu.make_async_copy(src, held_wide, local.at[index])

    def keep(index):
        return pltpu.make_async_copy(narrow[index], kept_out[index - 1], local.at[2 + index])

    if pairs == 2:
        pair_copy(0).start()
    load(0, gy_wide).start()
    gather = ColGather(at, da_wide, g_send, g_recv)
    row_sum = RowSumWhole(at, product, grad_mixed, *moved, *moved_sems)
    acts = RowGather(at, lambda s: late[0].at[s, at.row], lambda s, q: act_wide.at[s, q], act_sems)
    half = dqkv.shape[0] // 2
    grads = RowGather(
        at, lambda h: dqkv.at[pl.ds(h * half, half)], lambda h, q: dqkv_wide.at[q, pl.ds(h * half, half)], dqkv_sems
    )
    down_sum = ColSum(at, product, *down_bufs, *down_sems)
    dxn_sum = ColSum(at, product, *dxn_bufs, *dxn_sems)

    weighted = dhn[...] * gain_two[:, gain_spot]
    first_total.start(jnp.sum(weighted * hidden[...], axis=1, keepdims=True))
    for j in range(1, 4):
        acts.to_across(far_first(at.col, j)).start()
        acts.near(far_first(at.col, j))
    scale = scale_two[...]
    packet[...] = jnp.zeros_like(packet)
    packet[1:2, :] = jnp.sum(dhn[...] * hidden[...] * scale, axis=0, keepdims=True)
    inner = first_total.finish()
    dh[...] = (
        gy[...].astype(F32)
        + scale * (dhn[...] * gain_two[:, gain_spot])
        - hidden[...] * (scale * scale * scale * inner * (1.0 / model_width))
    )
    da_wide[at.col] = dh[...].astype(BF16)
    gather.arrive(0)
    for copy in reversed(fetch_acts):
        copy.wait()

    def back_out(s):
        product[...] = lax.dot_general(
            da_wide[s], w_out[...], (((1,), (1,)), ((), ())), preferred_element_type=F32
        )
        row_sum.give(s)

    def take_act(j):
        s = far_first(at.col, j)
        acts.wait_near(s)
        acts.take_across(s)
        acts.wait_diag(s)

    def act_rows(s, cols):
        return act_wide[s, :, :, cols].reshape(product.shape[0], cols.size)

    def down_step(j):
        s = far_first(at.col, j)
        product[...] = jnp.dot(
            act_rows(s, pl.ds(0, act_wide.shape[3])), w_down[...], preferred_element_type=F32
        )
        down_sum.step(s)

    def dxn_step(j, halves=(1, 0)):
        s = near_first(at, j)
        for h in halves:
            rows = pl.ds(h * half, half)
            total, base = None, 0
            for w in (w_query, w_key, w_value):
                size = w.shape[1]
                term = lax.dot_general(
                    dqkv_wide[s, rows, pl.ds(base, size)], w[...], (((1,), (1,)), ((), ())),
                    preferred_element_type=F32,
                )
                total = term if total is None else total + term
                base += size
            product[rows, :] = total
        dxn_sum.step(s, halves)

    def down_weight():
        load(0, gy_wide).wait()
        weight_grad(n_down, act_rows, lambda s: held_wide[s], to_pair(1))
        keep(1).start()
        load(1, mixed_wide).start()

    mid = jnp.logical_not(at.end)
    fetch.wait()
    gather.loop(0, back_out)
    gather.arrive(1)
    gather.loop(1, back_out)
    pl.when(at.end)(lambda: down_step(0))
    gather.arrive(2)
    gather.loop(2, back_out)
    pl.when(mid)(lambda: down_step(0))
    take_act(1)
    pl.when(at.end)(lambda: down_step(1))
    take_act(2)
    take_act(3)
    pl.when(at.end)(lambda: down_step(2))
    down_weight()
    pl.when(mid)(lambda: down_step(1))
    gather.arrive(3)
    gather.loop(3, back_out)
    row_sum.finish()

    def send_grads(h):
        grads.to_across(h).start()
        grads.near(h)

    attend_back(
        q_heads, groups, grad_mixed, qkv, qa, ka, va, probs, cos, sin, q_gain, k_gain,
        dqkv, q_part, k_part, dq, dk, dv, send_grads,
    )
    for h in range(2):
        grads.wait_near(h)

    @pl.when(at.end)
    def _():
        dxn_step(0)
        pl.when(jnp.logical_not(at.paired))(lambda: dxn_step(1))

    @pl.when(mid)
    def _():
        down_step(2)

    load(1, mixed_wide).wait()
    weight_grad(n_out, lambda s, here: held_wide[s, :, here], lambda s: da_wide[s], to_pair(2))
    keep(2).start()
    load(2, normed_wide).start()
    paired = mid & at.paired
    unpaired = mid & jnp.logical_not(at.paired)
    pl.when(unpaired)(lambda: dxn_step(0))
    grads.take_across(1)
    grads.wait_diag(1)

    @pl.when(at.end)
    def _():
        pl.when(at.paired)(lambda: dxn_step(1, (1,)))
        dxn_step(2, (1,))

    @pl.when(paired)
    def _():
        dxn_step(1, (1,))
        dxn_step(0, (1,))

    pl.when(unpaired)(lambda: dxn_step(1, (1,)))
    grads.take_across(0)
    grads.wait_diag(0)

    @pl.when(at.end)
    def _():
        pl.when(at.paired)(lambda: dxn_step(1, (0,)))
        dxn_step(2, (0,))

    pl.when(unpaired)(lambda: dxn_step(1, (0,)))
    load(2, normed_wide).wait()
    base = 0
    for index, some in ((3, n_query), (4, n_key), (5, n_value)):
        spot = pl.ds(base, some.shape[1])
        weight_grad(
            some, lambda s, here: held_wide[s, :, here], lambda s, spot=spot: dqkv_wide[s, :, spot], to_pair(index)
        )
        keep(index).start()
        base += some.shape[1]

    @pl.when(paired)
    def _():
        dxn_step(2, (1,))
        dxn_step(0, (0,))

    @pl.when(paired)
    def _():
        dxn_step(1, (0,))
        dxn_step(2, (0,))

    pl.when(unpaired)(lambda: dxn_step(2))
    down_step(3)
    layer_out[...] = (hidden[...] + product[...]).astype(BF16)
    dxn_step(3)
    scale = scale_one[...]
    last_total.start(
        jnp.sum(product[...] * gain_one[:, gain_spot] * x_ref[...].astype(F32), axis=1, keepdims=True)
    )
    packet[0:1, :] = jnp.sum(product[...] * x_ref[...].astype(F32) * scale, axis=0, keepdims=True)
    packet[2:3, :HEAD_SIZE] = q_part[...]
    packet[2:3, HEAD_SIZE : 2 * HEAD_SIZE] = k_part[...]

    def to_line(step):
        return remote(
            packet, packet_got.at[step - 1], p_send.at[step - 1], p_recv.at[step - 1],
            col=lax.rem(at.col + step, 4),
        )

    def to_group(index, row, step):
        where = dict(row=row) if step == 0 else dict(row=row, dp=at.pair(pairs, step))
        return remote(summed, by_row.at[step, at.row], r_send.at[index], r_recv.at[step, at.row], **where)

    def from_group(index, row, step):
        here = by_row.at[step, row]
        return remote(summed, here, r_send.at[index], r_recv.at[step, row], row=at.mate)

    group = [(row, 0) for row in (at.mate, at.across, at.diag)]
    group += [(row, step) for step in range(1, pairs) for row in range(4)]
    for step in range(1, 4):
        to_line(step).start()
    for step in range(1, 4):
        to_line(step).wait()
    summed[...] = (packet[...] + packet_got[0]) + (packet_got[1] + packet_got[2])
    by_row[0, at.row] = summed[...]
    for index, (row, step) in enumerate(group):
        to_group(index, row, step).start()
    inner = last_total.finish()
    in_grad[...] = (
        dh[...]
        + scale * (product[...] * gain_one[:, gain_spot])
        - x_ref[...].astype(F32) * (scale * scale * scale * inner * (1.0 / model_width))
    )
    for index, (row, step) in enumerate(group):
        from_group(index, row, step).wait_recv()
        to_group(index, row, step).wait_send()
    total = by_row[0]
    for step in range(1, pairs):
        total = total + by_row[step]
    for r in range(4):
        one_grad[:, r * feats : (r + 1) * feats] = total[r, 0:1, :]
        two_grad[:, r * feats : (r + 1) * feats] = total[r, 1:2, :]
    heads = (total[0, 2:3, :] + total[1, 2:3, :]) + (total[2, 2:3, :] + total[3, 2:3, :])
    q_grad[...] = heads[:, :HEAD_SIZE]
    k_grad[...] = heads[:, HEAD_SIZE : 2 * HEAD_SIZE]

    gather.close()
    row_sum.close()
    for j in range(1, 4):
        acts.close_one(far_first(at.col, j))
    grads.close(2)
    down_sum.close()
    dxn_sum.close()
    for index in range(1, 6):
        keep(index).wait()
    if pairs == 2:
        for index in range(6):
            pair_copy(index).wait()


def tail(pairs, q_heads, groups, number, act, weights, saved, tables, norms, wides, narrow):
    tokens, feats = norms[0].shape
    w_out, w_down, w_query, w_key, _ = weights
    ff = w_down.shape[0]
    width = saved[0].shape[1]
    q_width, k_width = saved[1].shape[1], saved[2].shape[1]
    dma = pltpu.SemaphoreType.DMA
    any_spec, vmem = pl.BlockSpec(memory_space=pl.ANY), pl.BlockSpec(memory_space=pltpu.VMEM)
    shape = jax.ShapeDtypeStruct
    shapes = [
        shape((tokens, feats), F32),
        shape((tokens, feats), BF16),
        shape((1, 4 * feats), F32),
        shape((1, 4 * feats), F32),
        shape((1, HEAD_SIZE), F32),
        shape((1, HEAD_SIZE), F32),
    ]
    own = [
        shape((ff, feats), BF16),
        shape((q_width, feats), BF16),
        shape((feats, q_width), BF16),
        shape((feats, k_width), BF16),
        shape((feats, k_width), BF16),
    ]
    others = [shape(n.shape, BF16) for n in narrow] + own if pairs == 2 else []
    packet = pltpu.VMEM((8, feats), F32)
    early = (w_out, *tables[2:], *norms)
    late = (act, *weights[1:], *saved, *tables[:2])
    out = pl.pallas_call(
        functools.partial(tail_kernel, pairs, q_heads, groups),
        out_shape=tuple(shapes + own + others),
        in_specs=[vmem] * len(early) + [any_spec] * (len(late) + 4),
        out_specs=tuple([vmem] * 6 + [any_spec] * (5 + len(others))),
        scratch_shapes=[held(array) for array in late[1:]]
        + [
            pltpu.VMEM((4, tokens, feats), BF16),
            pltpu.VMEM((4, 4, tokens // 4, ff), BF16),
            pltpu.VMEM((tokens, width), BF16),
            pltpu.VMEM((4, tokens, width), BF16),
            pltpu.VMEM((4, tokens, feats), BF16),
            pltpu.VMEM((tokens, feats), F32),
            pltpu.VMEM((tokens, q_width), F32),
            pltpu.VMEM((tokens, q_width), F32),
            pltpu.VMEM((tokens, k_width), F32),
            pltpu.VMEM((tokens, k_width), F32),
        ]
        + [held(array) for array in own]
        + [
            pltpu.VMEM((tokens, feats), F32),
            pltpu.VMEM((1, HEAD_SIZE), F32),
            pltpu.VMEM((1, HEAD_SIZE), F32),
            packet,
            pltpu.VMEM((3, 8, feats), F32),
            pltpu.VMEM((pairs, 4, 8, feats), F32),
            packet,
        ]
        + row_total_scratch(tokens) * 2
        + row_sum_scratch(tokens, q_width)
        + chain_scratch(tokens, feats) * 2
        + col_gather_sems()
        + [dma((12,)), dma((6,)), dma((6,)), dma((12,))]
        + row_sum_sems()
        + [dma((4,))] * 6
        + [dma((2,))] * 7
        + chain_sems() * 2
        + row_total_sems() * 2
        + [dma((3,)), dma((3,)), dma((4 * pairs - 1,)), dma((pairs, 4))],
        compiler_params=pltpu.CompilerParams(
            collective_id=number, has_side_effects=True, vmem_limit_bytes=VMEM_LIMIT
        ),
        name="tail",
    )(*early, *late, *wides, *narrow)
    return out[:6], out[6:11], out[11:]


def finish_kernel(count, *refs):
    parts, others, rest = refs[:count], refs[count : 2 * count], refs[2 * count :]
    kept = len(rest) - count
    for a, b, out in zip(parts, others, rest[kept // 2 :]):
        out[...] = a[...].astype(F32) + b[...].astype(F32)
    for src, dst in zip(rest[: kept // 2], rest[kept // 2 + count :]):
        dst[...] = src[...]


def finish(parts, others, rest, steps=4):
    def spec(array):
        block = (array.shape[0] // steps, array.shape[1]) if array.shape[0] % steps == 0 else array.shape
        index = (lambda i: (i, 0)) if block != array.shape else (lambda i: (0, 0))
        return pl.BlockSpec(block, index)

    outs = [jax.ShapeDtypeStruct(a.shape, F32) for a in parts] + [jax.ShapeDtypeStruct(a.shape, a.dtype) for a in rest]
    operands = (*parts, *others, *rest)
    out = pl.pallas_call(
        functools.partial(finish_kernel, len(parts)),
        grid=(steps,),
        out_shape=tuple(outs),
        in_specs=[spec(a) for a in operands],
        out_specs=tuple(spec(a) for a in outs),
        compiler_params=pltpu.CompilerParams(vmem_limit_bytes=VMEM_LIMIT),
        name="finish",
    )(*operands)
    return out[: len(parts)], out[len(parts) :]


def shards(
    pairs,
    hidden_in,
    segment_ids,
    attn_gain,
    w_query,
    key_projection,
    value_projection,
    query_gain,
    key_norm_gain,
    w_out,
    ffn_gain,
    w_gate,
    w_up,
    w_down,
    out_grad,
):
    tokens = hidden_in.shape[0]
    model_width = attn_gain.shape[0]
    q_width = w_query.shape[1]
    k_width = key_projection.shape[1]
    q_heads = q_width // HEAD_SIZE
    groups = q_width // k_width
    tables = (*turn_tables(tokens), query_gain[None, :], key_norm_gain[None, :])
    (scale_one, hidden, scale_two, ffn_in, qkv, q_turned, k_turned, values, probs, grad_inner, xn_wide, gy_wide, mixed_wide, full) = front(
        pairs, q_heads, groups, model_width, 0, hidden_in, out_grad,
        (w_query, key_projection, value_projection, w_out, w_down),
        segment_ids[None, :],
        tables,
        (attn_gain[None, :], ffn_gain[None, :]),
        (w_gate, w_up),
    )
    (grad_ffn_in, inner_act, gate_n, up_n), other_gate = middle(pairs, 1, ffn_in, w_gate, w_up, grad_inner, full)
    (in_grad, layer_out, one_grad, two_grad, q_gain_grad, k_gain_grad), own, others = tail(
        pairs, q_heads, groups, 2, inner_act,
        (w_out, w_down, w_query, key_projection, value_projection),
        (qkv, q_turned, k_turned, values, probs),
        tables,
        (grad_ffn_in, hidden, scale_two, ffn_gain[None, :], out_grad, hidden_in, scale_one, attn_gain[None, :]),
        (gy_wide, mixed_wide, xn_wide),
        (up_n,),
    )
    parts = (gate_n, up_n, *own)
    if pairs == 2:
        rest = (in_grad, layer_out, one_grad, two_grad, q_gain_grad, k_gain_grad)
        sums, rest = finish(parts, (*other_gate, *others), rest)
        in_grad, layer_out, one_grad, two_grad, q_gain_grad, k_gain_grad = rest
    else:
        sums = lax.psum(tuple(part.astype(F32) for part in parts), "dp")
    gate_grad, up_grad, down_grad, out_weight_grad, query_grad, key_grad, value_grad = sums
    return (
        layer_out,
        in_grad,
        one_grad.reshape(-1),
        query_grad,
        key_grad,
        value_grad,
        q_gain_grad.reshape(-1),
        k_gain_grad.reshape(-1),
        out_weight_grad,
        two_grad.reshape(-1),
        gate_grad,
        up_grad,
        down_grad,
    )


def solution(mesh):
    acts, grid, flip, none = P(("dp", "col"), "row"), P("row", "col"), P("col", "row"), P()
    return jax.shard_map(
        functools.partial(shards, mesh.shape["dp"]),
        mesh=mesh,
        in_specs=(
            acts, P(("dp", "row")), none, grid, grid, grid, none, none, flip, none, grid, grid, flip, acts,
        ),
        out_specs=(
            acts, acts, none, grid, grid, grid, none, none, flip, none, grid, grid, flip,
        ),
        check_vma=False,
    )
```
